32 devices in a mesh: dp: 8 (over y, x, core), fsdp: 4 (over z).
Axes of the slice: x: 2, y: 2, z: 4, core: 2. Of those that a mesh axis runs over, the one named last changes fastest.
Arguments:
- tokens_in: bfloat16 [4096, 2048], P(('dp', 'fsdp')), may hold values from -6 to 6
- text_in: bfloat16 [1024, 4096], P(('dp', 'fsdp')), may hold values from -6 to 6
- seg_ids: int32 [32, 128], P(('dp', 'fsdp')), may hold values from 0 to 2, never falling along the last dimension, each value on 1 to 64 neighbouring positions
- capt_ids: int32 [32, 32], P(('dp', 'fsdp')), may hold values from 0 to 2, never falling along the last dimension, each value on 1 to 21 neighbouring positions
- grad_out: bfloat16 [4096, 2048], P(('dp', 'fsdp')), may hold values from -6 to 6
- owner_query: int32 [64, 1], replicated, may hold values from 0 to 7; in each aligned block of 64 rows (0 to 63, 64 to 127, ...) at most 16 rows name the same one
- owner_up: int32 [64, 1], replicated, may hold values from 0 to 7; in each aligned block of 64 rows (0 to 63, 64 to 127, ...) at most 16 rows name the same one
- owner_outs: int32 [32, 1], replicated, may hold values from 0 to 7; in each aligned block of 32 rows (0 to 31, 32 to 63, ...) at most 8 rows name the same one
- owner_text: int32 [64, 1], replicated, may hold values from 0 to 7; in each aligned block of 64 rows (0 to 63, 64 to 127, ...) at most 16 rows name the same one
- owner_down: int32 [64, 1], replicated, may hold values from 0 to 7; in each aligned block of 64 rows (0 to 63, 64 to 127, ...) at most 16 rows name the same one
- w_query: float32 [2048, 16384], P('fsdp', 'dp'), may hold values from -0.125 to 0.125
- m_query: float32 [2048, 16384], P('fsdp', 'dp'), may hold values from -48 to 48
- v_query: float32 [2048, 16384], P('fsdp', 'dp'), may hold values from 5.89824 to 23.59296
- w_up: float32 [2048, 16384], P('fsdp', 'dp'), may hold values from -0.125 to 0.125
- m_up: float32 [2048, 16384], P('fsdp', 'dp'), may hold values from -20 to 20
- v_up: float32 [2048, 16384], P('fsdp', 'dp'), may hold values from 1.024 to 4.096
- w_outs: float32 [2048, 8192], P('fsdp', 'dp'), may hold values from -0.375 to 0.375
- m_outs: float32 [2048, 8192], P('fsdp', 'dp'), may hold values from -16 to 16
- v_outs: float32 [2048, 8192], P('fsdp', 'dp'), may hold values from 0.65536 to 2.62144
- w_text: float32 [2048, 16384], P('fsdp', 'dp'), may hold values from -0.09375 to 0.09375
- m_text: float32 [2048, 16384], P('fsdp', 'dp'), may hold values from -32 to 32
- v_text: float32 [2048, 16384], P('fsdp', 'dp'), may hold values from 2.9696 to 11.8784
- w_down: float32 [2048, 16384], P('fsdp', 'dp'), may hold values from -0.09375 to 0.09375
- m_down: float32 [2048, 16384], P('fsdp', 'dp'), may hold values from -28 to 28
- v_down: float32 [2048, 16384], P('fsdp', 'dp'), may hold values from 1.72032 to 6.9632
- norm_weight: float32 [6, 2048], P(None, 'dp'), may hold values from -1 to 2, as said below
- m_norm: float32 [6, 2048], P(None, 'dp'), may hold values from -64 to 64
- v_norm: float32 [6, 2048], P(None, 'dp'), may hold values from 9.216 to 36.864
Outputs:
- result: bfloat16 [4096, 2048], P(('dp', 'fsdp'))
- grad_in: bfloat16 [4096, 2048], P(('dp', 'fsdp'))
- query_first: float32 [2048, 16384], P('fsdp', 'dp')
- query_second: float32 [2048, 16384], P('fsdp', 'dp')
- query_weight: float32 [2048, 16384], P('fsdp', 'dp')
- up_first: float32 [2048, 16384], P('fsdp', 'dp')
- up_second: float32 [2048, 16384], P('fsdp', 'dp')
- up_weight: float32 [2048, 16384], P('fsdp', 'dp')
- outs_first: float32 [2048, 8192], P('fsdp', 'dp')
- outs_second: float32 [2048, 8192], P('fsdp', 'dp')
- outs_weight: float32 [2048, 8192], P('fsdp', 'dp')
- text_first: float32 [2048, 16384], P('fsdp', 'dp')
- text_second: float32 [2048, 16384], P('fsdp', 'dp')
- text_weight: float32 [2048, 16384], P('fsdp', 'dp')
- down_first: float32 [2048, 16384], P('fsdp', 'dp')
- down_second: float32 [2048, 16384], P('fsdp', 'dp')
- down_weight: float32 [2048, 16384], P('fsdp', 'dp')
- norm_first: float32 [6, 2048], P(None, 'dp')
- norm_second: float32 [6, 2048], P(None, 'dp')
- norm_new: float32 [6, 2048], P(None, 'dp')
The draws below stay inside these ranges and needn't reach their ends.
Inputs may be any that keep to these rules, and one draw needn't show every extreme that they name: `seg_ids`: within one packed row the image numbers never fall; each image holds 1 to 64 tokens, one holds exactly 64, and every image number appears. `capt_ids`: within one packed row the caption numbers never fall; caption n belongs to image n of the same row; each caption holds 1 to 21 text tokens, one holds exactly 21, and every caption number appears. `owner_query`: no dp index owns more than 16 blocks, one owns exactly 16, every index owns at least one. `owner_up`: no dp index owns more than 16 blocks, one owns exactly 16, every index owns at least one. `owner_outs`: no dp index owns more than 8 blocks, one owns exactly 8, every index owns at least one. `owner_text`: no dp index owns more than 16 blocks, one owns exactly 16, every index owns at least one. `owner_down`: no dp index owns more than 16 blocks, one owns exactly 16, every index owns at least one. `norm_weight`: rows 0, 2 and 4 are positive gains, rows 1, 3 and 5 biases.
All inputs are finite; a program needn't handle non-finite values.
Results may differ from the reference program's by a relative error of at most 0.022.
Values may be sent and summed in bfloat16 or wider, within the bound.
A program may use at most 512 MiB of HBM per device.

```python
import math
import jax
import jax.numpy as jnp
import numpy as np
from jax import lax

D = 2048
HEADS = 16
HEAD = 128
FF = 8192
TD = 4096
STEP = 10
BLK = 128
TOK_DEV = 128
TXT_DEV = 32
ROWS = 32
TOKENS = 4096
TEXTS = 1024
SEGS = 3
MOST = 64
CAPT_MOST = 21
NB_BIG = 64
NB_OUT = 32
CAP_BIG = 16
CAP_OUT = 8
SLOT_BIG = 128
SLOT_OUT = 64
N_DP = 8


def draw_norm_weight(key, part):
    key = jax.random.fold_in(key, 7)
    gain_key, bias_key = jax.random.split(key)
    gain_rows = jnp.clip(1.0 + 0.15 * jax.random.normal(gain_key, (3, D), jnp.float32), 0.4, 1.6)
    bias_rows = jnp.clip(0.3 * jax.random.normal(bias_key, (3, D), jnp.float32), -1.0, 1.0)
    return jnp.stack([gain_rows, bias_rows], axis=1).reshape(6, D)


def steps_of(stream_key, extent, shards, low, high):
    factor_of = 1.0
    for axis_at, blocks in shards:
        heights = jax.random.uniform(jax.random.fold_in(jax.random.fold_in(stream_key, 6), axis_at), (blocks,), jnp.float32, low / len(shards), high / len(shards))
        factor_of = factor_of * jnp.repeat(jnp.exp(heights), extent[axis_at] // blocks).reshape((-1,) + (1,) * (len(extent) - 1 - axis_at))
    return factor_of


def split_up(amount, total, limit, slope):
    loads = [(1 << 20) // math.isqrt(grade ** slope) + 1 for grade in range(2, amount + 1)]
    spare, given = total - limit - (amount - 1), [1] * (amount - 1)
    while spare > 0:
        candidates = [i for i in range(amount - 1) if given[i] < limit]
        pool, remaining = sum([loads[i] for i in candidates]), spare
        for i in candidates:
            addition = min(limit - given[i], max(1, remaining * loads[i] // pool), spare)
            given[i] = given[i] + addition
            spare = spare - addition
    return np.array([limit] + given)


def ragged_sizes(rng, amount, total, limit, skew):
    if amount == 2:
        one = jax.random.randint(rng, (), max(1, total - limit), min(limit, total - 1) + 1)
        return jnp.stack([one, total - one])
    lengths = jnp.asarray(split_up(amount, total, limit, skew), jnp.int32)
    pairs = (amount - 1) // 2
    giver, receiver = lengths[1:1 + 2 * pairs:2], lengths[2:2 + 2 * pairs:2]
    slack = jnp.minimum(giver - 1, limit - receiver)
    shifted = jax.random.randint(jax.random.fold_in(rng, 1), (pairs,), 0, 1 << 20) % (slack + 1)
    lengths = lengths.at[1:1 + 2 * pairs:2].set(giver - shifted).at[2:2 + 2 * pairs:2].set(receiver + shifted)
    return lengths[jax.random.permutation(jax.random.fold_in(rng, 2), amount)]


def shared_out(stream_key, own, number, rows, amount, top, bound, lean):
    order = jax.random.permutation(stream_key, amount)
    packed, common = load_shares(amount, rows * top, bound, lean, True), load_shares(amount, rows * top, bound, lean, False)
    places = jnp.arange(amount)

    def named(sizes, offset_by):
        used = int((sizes > 0).sum())
        fixed = max(1, used // 4)
        passed = fixed + (places - fixed + offset_by * (used - fixed)) % max(1, amount - fixed)
        return jnp.zeros((amount,), jnp.int32).at[order[jnp.where(places < fixed, places, passed)]].set(jnp.asarray(sizes, jnp.int32))

    sizes = jnp.where(number % 4 == 0, named(packed, number // 4), named(common, number - number // 4 - 1))
    mixed = jax.random.permutation(jax.random.fold_in(own, 3), amount)
    giver, receiver = mixed[0:amount // 2 * 2:2], mixed[1:amount // 2 * 2:2]
    room = jnp.minimum(sizes[giver] - 1, bound - sizes[receiver]) // 2
    room = jnp.where((giver == order[0]) | (receiver == order[0]) | (sizes[receiver] == 0), 0, jnp.maximum(room, 0))
    passed = jax.random.randint(jax.random.fold_in(own, 4), (amount // 2,), 0, 1 << 20) % (room + 1)
    sizes = sizes.at[giver].add(-passed).at[receiver].add(passed)
    members = jnp.searchsorted(jnp.cumsum(sizes), jnp.arange(rows * top), side="right").astype(jnp.int32)
    grid = members.reshape(top, rows).T
    grid = grid[jax.random.permutation(jax.random.fold_in(own, 1), rows)]
    offset_by = jax.random.randint(jax.random.fold_in(own, 2), (rows, 1), 0, top)
    return jnp.take_along_axis(grid, (jnp.arange(top)[None, :] + offset_by) % top, axis=1)


def load_shares(number_of, total, most, slope, full):
    portions = [(1 << 20) // math.isqrt(rank ** slope) + 1 for rank in range(1, number_of + 1)]
    largest = most if full else min(most, max(-(-total // number_of), total * portions[0] // sum(portions)))
    least = 1 if total - largest >= number_of - 1 else 0
    counts, surplus = [largest] + [least] * (number_of - 1), total - largest - least * (number_of - 1)
    while surplus > 0:
        candidates = [i for i in range(1, number_of) if counts[i] < largest] or [i for i in range(1, number_of) if counts[i] < most]
        whole, remaining = sum([portions[i] for i in candidates]), surplus
        for i in candidates:
            more = min(most - counts[i], max(1, remaining * portions[i] // whole), surplus)
            counts[i] = counts[i] + more
            surplus = surplus - more
    return np.array(counts)


def centred(key, shape, width, most, cuts=(), held_as=jnp.bfloat16):
    result = width * jax.random.normal(key, shape, jnp.float32)
    if cuts:
        result = result * steps_of(key, shape, cuts, -0.22, 0.18)
    return jnp.clip(result, -most, most).astype(held_as)


def setup_inputs(seed: int = 0) -> dict:
    splits = jax.random.split(jax.random.key(seed), 29)
    tokens_in = centred(splits[0], (TOKENS, D), 1.0, 6.0, ((0, 32),))
    text_in = centred(splits[1], (TEXTS, TD), 1.0, 6.0, ((0, 32),))
    seg_ids = jax.vmap(lambda own: jnp.searchsorted(jnp.cumsum(ragged_sizes(own, SEGS, TOK_DEV, MOST, 2)), jnp.arange(TOK_DEV), side="right"))(jax.random.split(splits[2], ROWS)).reshape((ROWS, TOK_DEV)).astype(jnp.int32)
    capt_ids = jax.vmap(lambda own: jnp.searchsorted(jnp.cumsum(ragged_sizes(own, SEGS, TXT_DEV, CAPT_MOST, 2)), jnp.arange(TXT_DEV), side="right"))(jax.random.split(splits[3], ROWS)).reshape((ROWS, TXT_DEV)).astype(jnp.int32)
    grad_out = centred(splits[4], (TOKENS, D), 1.0, 6.0, ((0, 32),))
    owner_query_keys = jax.random.split(jax.random.fold_in(splits[5], 1), NB_BIG // NB_BIG)
    owner_query_turns = jax.random.permutation(jax.random.fold_in(splits[5], 3), NB_BIG // NB_BIG)
    owner_query = jax.vmap(lambda own, number: shared_out(jax.random.fold_in(splits[5], 2), own, number, NB_BIG, N_DP, 1, CAP_BIG, 2))(owner_query_keys, owner_query_turns).reshape((NB_BIG, 1))
    owner_up_keys = jax.random.split(jax.random.fold_in(splits[6], 1), NB_BIG // NB_BIG)
    owner_up_turns = jax.random.permutation(jax.random.fold_in(splits[6], 3), NB_BIG // NB_BIG)
    owner_up = jax.vmap(lambda own, number: shared_out(jax.random.fold_in(splits[6], 2), own, number, NB_BIG, N_DP, 1, CAP_BIG, 2))(owner_up_keys, owner_up_turns).reshape((NB_BIG, 1))
    owner_outs_keys = jax.random.split(jax.random.fold_in(splits[7], 1), NB_OUT // NB_OUT)
    owner_outs_turns = jax.random.permutation(jax.random.fold_in(splits[7], 3), NB_OUT // NB_OUT)
    owner_outs = jax.vmap(lambda own, number: shared_out(jax.random.fold_in(splits[7], 2), own, number, NB_OUT, N_DP, 1, CAP_OUT, 2))(owner_outs_keys, owner_outs_turns).reshape((NB_OUT, 1))
    owner_text_keys = jax.random.split(jax.random.fold_in(splits[8], 1), NB_BIG // NB_BIG)
    owner_text_turns = jax.random.permutation(jax.random.fold_in(splits[8], 3), NB_BIG // NB_BIG)
    owner_text = jax.vmap(lambda own, number: shared_out(jax.random.fold_in(splits[8], 2), own, number, NB_BIG, N_DP, 1, CAP_BIG, 2))(owner_text_keys, owner_text_turns).reshape((NB_BIG, 1))
    owner_down_keys = jax.random.split(jax.random.fold_in(splits[9], 1), NB_BIG // NB_BIG)
    owner_down_turns = jax.random.permutation(jax.random.fold_in(splits[9], 3), NB_BIG // NB_BIG)
    owner_down = jax.vmap(lambda own, number: shared_out(jax.random.fold_in(splits[9], 2), own, number, NB_BIG, N_DP, 1, CAP_BIG, 2))(owner_down_keys, owner_down_turns).reshape((NB_BIG, 1))
    w_query = centred(splits[10], (D, SLOT_BIG * BLK), D ** -0.5, 0.125, ((0, 4), (1, 8)), jnp.float32)
    m_query = centred(splits[11], (D, SLOT_BIG * BLK), (0.133 * TOKENS ** 0.5), 48.0, ((0, 4), (1, 8)), jnp.float32)
    v_query = jnp.clip(jnp.exp(math.log(23.59296) - 1.3862944 * jax.random.uniform(splits[12], (D, SLOT_BIG * BLK), jnp.float32) ** steps_of(splits[12], (D, SLOT_BIG * BLK), ((0, 4), (1, 8)), -0.2, 0.2)), 5.89824, 23.59296)
    w_up = centred(splits[13], (D, SLOT_BIG * BLK), D ** -0.5, 0.125, ((0, 4), (1, 8)), jnp.float32)
    m_up = centred(splits[14], (D, SLOT_BIG * BLK), (0.056 * TOKENS ** 0.5), 20.0, ((0, 4), (1, 8)), jnp.float32)
    v_up = jnp.clip(jnp.exp(math.log(4.096) - 1.3862944 * jax.random.uniform(splits[15], (D, SLOT_BIG * BLK), jnp.float32) ** steps_of(splits[15], (D, SLOT_BIG * BLK), ((0, 4), (1, 8)), -0.2, 0.2)), 1.024, 4.096)
    w_outs = centred(splits[16], (D, SLOT_OUT * BLK), (D // 8) ** -0.5, 0.375, ((0, 4), (1, 8)), jnp.float32)
    m_outs = centred(splits[17], (D, SLOT_OUT * BLK), (0.044 * TOKENS ** 0.5), 16.0, ((0, 4), (1, 8)), jnp.float32)
    v_outs = jnp.clip(jnp.exp(math.log(2.62144) - 1.3862944 * jax.random.uniform(splits[18], (D, SLOT_OUT * BLK), jnp.float32) ** steps_of(splits[18], (D, SLOT_OUT * BLK), ((0, 4), (1, 8)), -0.2, 0.2)), 0.65536, 2.62144)
    w_text = centred(splits[19], (D, SLOT_BIG * BLK), TD ** -0.5, 0.09375, ((0, 4), (1, 8)), jnp.float32)
    m_text = centred(splits[20], (D, SLOT_BIG * BLK), (0.19 * TEXTS ** 0.5), 32.0, ((0, 4), (1, 8)), jnp.float32)
    v_text = jnp.clip(jnp.exp(math.log(11.8784) - 1.3862944 * jax.random.uniform(splits[21], (D, SLOT_BIG * BLK), jnp.float32) ** steps_of(splits[21], (D, SLOT_BIG * BLK), ((0, 4), (1, 8)), -0.2, 0.2)), 2.9696, 11.8784)
    w_down = centred(splits[22], (D, SLOT_BIG * BLK), (FF // 2) ** -0.5, 0.09375, ((0, 4), (1, 8)), jnp.float32)
    m_down = centred(splits[23], (D, SLOT_BIG * BLK), (0.072 * TOKENS ** 0.5), 28.0, ((0, 4), (1, 8)), jnp.float32)
    v_down = jnp.clip(jnp.exp(math.log(6.9632) - 1.39812884 * jax.random.uniform(splits[24], (D, SLOT_BIG * BLK), jnp.float32) ** steps_of(splits[24], (D, SLOT_BIG * BLK), ((0, 4), (1, 8)), -0.2, 0.2)), 1.72032, 6.9632)
    norm_weight = draw_norm_weight(jax.random.fold_in(splits[28], 71), 0)
    m_norm = centred(splits[26], (6, D), (0.167 * TOKENS ** 0.5), 64.0, ((1, 8),), jnp.float32)
    v_norm = jnp.clip(jnp.exp(math.log(36.864) - 1.3862944 * jax.random.uniform(splits[27], (6, D), jnp.float32) ** steps_of(splits[27], (6, D), ((1, 8),), -0.2, 0.2)), 9.216, 36.864)
    return {"tokens_in": tokens_in, "text_in": text_in, "seg_ids": seg_ids, "capt_ids": capt_ids, "grad_out": grad_out, "owner_query": owner_query, "owner_up": owner_up, "owner_outs": owner_outs, "owner_text": owner_text, "owner_down": owner_down, "w_query": w_query, "m_query": m_query, "v_query": v_query, "w_up": w_up, "m_up": m_up, "v_up": v_up, "w_outs": w_outs, "m_outs": m_outs, "v_outs": v_outs, "w_text": w_text, "m_text": m_text, "v_text": v_text, "w_down": w_down, "m_down": m_down, "v_down": v_down, "norm_weight": norm_weight, "m_norm": m_norm, "v_norm": v_norm}


beta_first = 0.9
beta_second = 0.999
adam_eps = 1e-08
decay_rate = 0.01
rate_query = 0.04
rate_up = 0.04
rate_outs = 0.12
rate_text = 0.03
rate_down = 0.03
rate_norm = 0.5
norm_eps = 1e-05
score_floor = -1e+30

@jax.custom_vjp
def low(v):
    return lax.optimization_barrier(v.astype(jnp.bfloat16)).astype(jnp.float32)

@jax.custom_vjp
def low_back(v):
    return v

def low_keep(v):
    return (low(v), None)

def low_pass(kept, grad):
    return (grad,)

def back_keep(v):
    return (v, None)

def back_low(kept, grad):
    return (low(grad),)
low.defvjp(low_keep, low_pass)
low_back.defvjp(back_keep, back_low)

def normalize(values):
    centered = values - lax.optimization_barrier(jnp.mean(values, axis=-1, keepdims=True))
    inverse_std = lax.rsqrt(lax.optimization_barrier(jnp.mean(centered * centered, axis=-1, keepdims=True)) + norm_eps)
    return centered * inverse_std

def matmul(left, right):
    return jnp.dot(left, right, precision=lax.Precision.HIGHEST)

def attend(query_part, key_part, value_part, allowed):
    query_heads = query_part.reshape(-1, HEADS, HEAD)
    key_heads = key_part.reshape(-1, HEADS, HEAD)
    value_heads = value_part.reshape(-1, HEADS, HEAD)
    raw_scores = jnp.einsum('qhd,khd->hqk', query_heads, key_heads, precision=lax.Precision.HIGHEST) * HEAD ** (-0.5)
    scores = low_back(raw_scores)
    scores = jnp.where(allowed[None], scores, score_floor)
    row_peak = lax.optimization_barrier(jnp.max(scores, axis=-1, keepdims=True))
    powers = jnp.exp(scores - row_peak)
    shares = low(powers / lax.optimization_barrier(jnp.sum(powers, axis=-1, keepdims=True)))
    attended = jnp.einsum('hqk,khd->qhd', shares, value_heads, precision=lax.Precision.HIGHEST)
    return low(low_back(attended.reshape(-1, HEADS * HEAD)))

def one_row(token_row, text_row, row_seg, row_capt, query_low, up_low, outs_low, text_map, down_map, norm_master):
    hidden1 = low(normalize(token_row) * norm_master[0] + norm_master[1])
    projected = low(low_back(matmul(hidden1, query_low[:, :3 * D])))
    self_allowed = row_seg[:, None] == row_seg[None, :]
    attended1 = attend(projected[:, :D], projected[:, D:2 * D], projected[:, 2 * D:], self_allowed)
    middle1 = token_row + low_back(matmul(attended1, outs_low[:, :D]))
    hidden2 = low(normalize(middle1) * norm_master[2] + norm_master[3])
    cross_query = low(low_back(matmul(hidden2, query_low[:, 3 * D:])))
    text_pairs = low(low_back(matmul(text_row, text_map)))
    cross_allowed = row_seg[:, None] == row_capt[None, :]
    attended2 = attend(cross_query, text_pairs[:, :D], text_pairs[:, D:], cross_allowed)
    middle2 = middle1 + low_back(matmul(attended2, outs_low[:, D:]))
    hidden3 = low(normalize(middle2) * norm_master[4] + norm_master[5])
    up_values = low_back(matmul(hidden3, up_low))
    activated = low(jax.nn.gelu(up_values, approximate=False))
    return middle2 + low_back(matmul(activated, down_map))

def slot_index(owner_list, capacity):
    owner_column = owner_list[:, 0].astype(jnp.int32)
    block_count = owner_column.shape[0]
    same_owner = owner_column[:, None] == owner_column[None, :]
    earlier = jnp.arange(block_count, dtype=jnp.int32)[None, :] < jnp.arange(block_count, dtype=jnp.int32)[:, None]
    position = lax.optimization_barrier(jnp.sum(jnp.logical_and(same_owner, earlier).astype(jnp.int32), axis=1))
    return (owner_column * capacity + position).astype(jnp.int32)

def unslot(slot_array, slot_list):
    row_count = slot_array.shape[0]
    return slot_array.reshape(row_count, -1, BLK)[:, slot_list, :].reshape(row_count, -1)

def to_slots(gradient, slot_list, capacity):
    row_count = gradient.shape[0]
    empty_slots = jnp.zeros((row_count, capacity * N_DP, BLK), jnp.float32)
    return empty_slots.at[:, slot_list, :].set(gradient.reshape(row_count, -1, BLK)).reshape(row_count, -1)

def adamw_update(weight, first, second, gradient, rate, decay):
    first_new = beta_first * first + (1.0 - beta_first) * gradient
    second_new = beta_second * second + (1.0 - beta_second) * gradient * gradient
    first_hat = first_new / (1.0 - beta_first ** STEP)
    second_hat = second_new / (1.0 - beta_second ** STEP)
    weight_new = weight - rate * (first_hat / (jnp.sqrt(second_hat) + adam_eps) + decay * weight)
    return (first_new, second_new, weight_new)

def reference(tokens_in, text_in, seg_ids, capt_ids, grad_out, owner_query, owner_up, owner_outs, owner_text, owner_down, w_query, m_query, v_query, w_up, m_up, v_up, w_outs, m_outs, v_outs, w_text, m_text, v_text, w_down, m_down, v_down, norm_weight, m_norm, v_norm):
    slot_query = slot_index(owner_query, CAP_BIG)
    slot_up = slot_index(owner_up, CAP_BIG)
    slot_outs = slot_index(owner_outs, CAP_OUT)
    slot_text = slot_index(owner_text, CAP_BIG)
    slot_down = slot_index(owner_down, CAP_BIG)
    text_rows = text_in.astype(jnp.float32).reshape(ROWS, TXT_DEV, TD)

    def layer_forward(token_block, query_master, up_master, outs_master, text_master, down_master, norm_master):
        query_low = low(query_master)
        up_low = low(up_master)
        outs_low = low(outs_master)
        text_map = low(text_master).reshape(D, 2, 2 * D).transpose(1, 0, 2).reshape(TD, 2 * D)
        down_map = low(down_master).reshape(D, 4, D).transpose(1, 0, 2).reshape(FF, D)
        row_function = jax.checkpoint(one_row)

        def row_step(running, row_items):
            token_row, text_row, row_seg, row_capt = row_items
            return (running, row_function(token_row, text_row, row_seg, row_capt, query_low, up_low, outs_low, text_map, down_map, norm_master))
        stacked = token_block.reshape(ROWS, TOK_DEV, D)
        final_state, result_rows = lax.scan(row_step, jnp.zeros((), jnp.float32), (stacked, text_rows, seg_ids, capt_ids))
        return result_rows.reshape(TOKENS, D)
    outputs, pullback = jax.vjp(layer_forward, tokens_in.astype(jnp.float32), unslot(w_query, slot_query), unslot(w_up, slot_up), unslot(w_outs, slot_outs), unslot(w_text, slot_text), unslot(w_down, slot_down), norm_weight)
    gradients = pullback(grad_out.astype(jnp.float32))
    query_first, query_second, query_weight = adamw_update(w_query, m_query, v_query, to_slots(gradients[1], slot_query, CAP_BIG), rate_query, decay_rate)
    up_first, up_second, up_weight = adamw_update(w_up, m_up, v_up, to_slots(gradients[2], slot_up, CAP_BIG), rate_up, decay_rate)
    outs_first, outs_second, outs_weight = adamw_update(w_outs, m_outs, v_outs, to_slots(gradients[3], slot_outs, CAP_OUT), rate_outs, decay_rate)
    text_first, text_second, text_weight = adamw_update(w_text, m_text, v_text, to_slots(gradients[4], slot_text, CAP_BIG), rate_text, decay_rate)
    down_first, down_second, down_weight = adamw_update(w_down, m_down, v_down, to_slots(gradients[5], slot_down, CAP_BIG), rate_down, decay_rate)
    norm_first, norm_second, norm_new = adamw_update(norm_weight, m_norm, v_norm, gradients[6], rate_norm, 0.0)
    return (outputs.astype(jnp.bfloat16), gradients[0].astype(jnp.bfloat16), query_first, query_second, query_weight, up_first, up_second, up_weight, outs_first, outs_second, outs_weight, text_first, text_second, text_weight, down_first, down_second, down_weight, norm_first, norm_second, norm_new)
```

```python
import functools

import jax
import jax.numpy as jnp
from jax import lax
from jax.experimental import pallas as pl
from jax.experimental.pallas import tpu as pltpu
from jax.sharding import PartitionSpec as P

HEADS = 16
HEAD = 128
STEP = 10
BLK = 128


beta_first = 0.9
beta_second = 0.999
adam_eps = 1e-08
decay_rate = 0.01
rate_query = 0.04
rate_up = 0.04
rate_outs = 0.12
rate_text = 0.03
rate_down = 0.03
rate_norm = 0.5
norm_eps = 1e-05
score_floor = -1e30
bf16 = jnp.bfloat16
f32 = jnp.float32


def normalize(values):
    centered = values - jnp.mean(values, axis=-1, keepdims=True)
    inverse_std = lax.rsqrt(jnp.mean(centered * centered, axis=-1, keepdims=True) + norm_eps)
    return (centered * inverse_std, inverse_std)


def norm_back(back_hidden, normed, inverse_std, gain_row):
    back_normed = back_hidden * gain_row
    return inverse_std * (
        back_normed
        - jnp.mean(back_normed, axis=-1, keepdims=True)
        - normed * jnp.mean(back_normed * normed, axis=-1, keepdims=True)
    )


def exact_gelu(values):
    return jax.nn.gelu(values, approximate=False)


def adamw_update(weight, first, second, gradient, rate, decay):
    first_new = beta_first * first + (1.0 - beta_first) * gradient
    second_new = beta_second * second + (1.0 - beta_second) * gradient * gradient
    first_hat = first_new / (1.0 - beta_first**STEP)
    second_hat = second_new / (1.0 - beta_second**STEP)
    weight_new = weight - rate * (first_hat / (jnp.sqrt(second_hat) + adam_eps) + decay * weight)
    return (first_new, second_new, weight_new)


def dot(left, right):
    return jnp.dot(left, right, preferred_element_type=f32)


def dot_nt(left, right):
    return lax.dot_general(left, right, (((1,), (1,)), ((), ())), preferred_element_type=f32)


def dot_tn(left, right):
    return lax.dot_general(left, right, (((0,), (0,)), ((), ())), preferred_element_type=f32)


def split_place(block, per_part, parts):
    group, rest = divmod(block, per_part * parts)
    part, inner = divmod(rest, per_part)
    return part, group * per_part + inner


def flat_place(block):
    return 0, block


def compact_kernel(places, n_dp, owner_ref, slots_ref, out_ref, count_ref):
    for index in range(n_dp):
        count_ref[index] = 0
    for block, (part, column) in enumerate(places):
        owner = owner_ref[block]
        position = count_ref[owner]
        count_ref[owner] = position + 1
        start = pl.multiple_of(position * BLK, BLK)
        out_ref[part, :, column * BLK : (column + 1) * BLK] = slots_ref[
            owner, :, pl.ds(start, BLK)
        ]


def compact(slots, owner, places, parts):
    n_dp, rows, _ = slots.shape
    columns = len(places) // parts * BLK
    return pl.pallas_call(
        functools.partial(compact_kernel, places, n_dp),
        out_shape=jax.ShapeDtypeStruct((parts, rows, columns), slots.dtype),
        in_specs=[
            pl.BlockSpec(memory_space=pltpu.SMEM),
            pl.BlockSpec(memory_space=pltpu.VMEM),
        ],
        out_specs=pl.BlockSpec(memory_space=pltpu.VMEM),
        scratch_shapes=[pltpu.SMEM((n_dp,), jnp.int32)],
        compiler_params=pltpu.CompilerParams(vmem_limit_bytes=32 * 1024 * 1024),
        cost_estimate=pl.CostEstimate(
            flops=0, bytes_accessed=2 * (slots.size + len(places) * BLK * rows), transcendentals=0
        ),
    )(owner, slots)


def expand_kernel(places, n_dp, owner_ref, grad_ref, out_ref, count_ref):
    for index in range(n_dp):
        count_ref[index] = 0
    out_ref[...] = jnp.zeros_like(out_ref)
    for block, (part, column) in enumerate(places):
        owner = owner_ref[block]
        position = count_ref[owner]
        count_ref[owner] = position + 1
        start = pl.multiple_of(position * BLK, BLK)
        out_ref[owner, :, pl.ds(start, BLK)] = grad_ref[
            part, :, column * BLK : (column + 1) * BLK
        ]


def expand(grad, owner, places, n_dp, capacity):
    rows = grad.shape[1]
    return pl.pallas_call(
        functools.partial(expand_kernel, places, n_dp),
        out_shape=jax.ShapeDtypeStruct((n_dp, rows, capacity * BLK), grad.dtype),
        in_specs=[
            pl.BlockSpec(memory_space=pltpu.SMEM),
            pl.BlockSpec(memory_space=pltpu.VMEM),
        ],
        out_specs=pl.BlockSpec(memory_space=pltpu.VMEM),
        scratch_shapes=[pltpu.SMEM((n_dp,), jnp.int32)],
        compiler_params=pltpu.CompilerParams(vmem_limit_bytes=32 * 1024 * 1024),
        cost_estimate=pl.CostEstimate(
            flops=0,
            bytes_accessed=2 * (grad.size + n_dp * capacity * BLK * rows),
            transcendentals=0,
        ),
    )(owner, grad)


def swap(values, axis):
    return lax.all_to_all(values, axis, 0, 0, tiled=True)


def z_gather(values):
    return lax.all_gather(values, "fsdp", axis=0, tiled=True)


def z_reduce(values):
    return lax.psum_scatter(values.astype(bf16), "fsdp", scatter_dimension=0, tiled=True).astype(
        f32
    )


def attend_forward(queries, keys, values, allowed):
    packed = allowed.shape[0]
    heads = queries.shape[1] // HEAD
    query_heads = queries.reshape(packed, -1, heads, HEAD)
    key_heads = keys.reshape(packed, -1, heads, HEAD)
    value_heads = values.reshape(packed, -1, heads, HEAD)
    scores = jnp.einsum(
        "pqhd,pkhd->phqk", query_heads, key_heads, preferred_element_type=f32
    ) * HEAD ** (-0.5)
    scores = jnp.where(allowed[:, None], scores, score_floor)
    powers = jnp.exp(scores - jnp.max(scores, axis=-1, keepdims=True))
    shares = powers / jnp.sum(powers, axis=-1, keepdims=True)
    attended = jnp.einsum(
        "phqk,pkhd->pqhd", shares.astype(bf16), value_heads, preferred_element_type=f32
    )
    return attended.reshape(queries.shape).astype(bf16), shares


def attend_backward(queries, keys, values, shares, back_attended):
    packed = shares.shape[0]
    heads = queries.shape[1] // HEAD
    query_heads = queries.reshape(packed, -1, heads, HEAD)
    key_heads = keys.reshape(packed, -1, heads, HEAD)
    value_heads = values.reshape(packed, -1, heads, HEAD)
    back_heads = back_attended.reshape(packed, -1, heads, HEAD)
    score_scale = HEAD ** (-0.5)
    back_shares = jnp.einsum(
        "pqhd,pkhd->phqk", back_heads, value_heads, preferred_element_type=f32
    )
    inner_sum = jnp.sum(shares * back_shares, axis=-1, keepdims=True)
    back_scores = (shares * (back_shares - inner_sum)).astype(bf16)
    query_grad = (
        jnp.einsum("phqk,pkhd->pqhd", back_scores, key_heads, preferred_element_type=f32)
        * score_scale
    )
    key_grad = (
        jnp.einsum("phqk,pqhd->pkhd", back_scores, query_heads, preferred_element_type=f32)
        * score_scale
    )
    value_grad = jnp.einsum(
        "phqk,pqhd->pkhd", shares.astype(bf16), back_heads, preferred_element_type=f32
    )
    return (
        query_grad.reshape(queries.shape).astype(bf16),
        key_grad.reshape(keys.shape).astype(bf16),
        value_grad.reshape(values.shape).astype(bf16),
    )


def body(
    tokens_in,
    text_in,
    seg_ids,
    capt_ids,
    grad_out,
    owner_query,
    owner_up,
    owner_outs,
    owner_text,
    owner_down,
    w_query,
    m_query,
    v_query,
    w_up,
    m_up,
    v_up,
    w_outs,
    m_outs,
    v_outs,
    w_text,
    m_text,
    v_text,
    w_down,
    m_down,
    v_down,
    norm_weight,
    m_norm,
    v_norm,
):
    n_dp = lax.axis_size("dp")
    n_z = lax.axis_size("fsdp")
    width = tokens_in.shape[1]
    own_rows = w_query.shape[0]
    chunk = own_rows // n_dp
    cap_big = w_query.shape[1] // BLK
    cap_out = w_outs.shape[1] // BLK
    heads_z = HEADS // n_z
    share = width // n_z
    owner_query, owner_up, owner_outs, owner_text, owner_down = (
        owner[:, 0] for owner in (owner_query, owner_up, owner_outs, owner_text, owner_down)
    )
    split_places = [split_place(b, heads_z, n_z) for b in range(owner_query.shape[0])]
    big_places = [flat_place(b) for b in range(owner_down.shape[0])]
    out_places = [flat_place(b) for b in range(owner_outs.shape[0])]

    def shuffled(values):
        lead = values.shape[:-1]
        folds = values.shape[-1] // width
        cut = values.reshape(lead[0], folds, n_z, n_dp, chunk)
        return cut.transpose(0, 1, 3, 2, 4).reshape(values.shape)

    def unshuffled(values):
        cut = values.reshape(values.shape[0], n_dp, n_z, chunk)
        return cut.transpose(0, 2, 1, 3).reshape(values.shape)

    def fetch(weight, owner, places, parts):
        slots = swap(weight.astype(bf16), "dp").reshape(n_dp, chunk, -1)
        rows = compact(slots, owner, places, parts)
        if parts > 1:
            rows = swap(rows, "fsdp")
        rows = rows.reshape(parts * chunk, -1)
        return lax.all_gather(rows, "dp", axis=0, tiled=True)

    def settle(pieces, owner, places, parts, capacity):
        summed = [
            lax.psum_scatter(piece, "dp", scatter_dimension=0, tiled=True) for piece in pieces
        ]
        summed = summed[0] if len(summed) == 1 else jnp.concatenate(summed, axis=1)
        rows = summed.reshape(parts, chunk, -1)
        if parts > 1:
            rows = swap(rows, "fsdp")
        slots = expand(rows, owner, places, n_dp, capacity)
        return swap(slots, "dp").reshape(n_dp * chunk, -1).astype(f32)

    norm_full = lax.all_gather(norm_weight, "dp", axis=1, tiled=True)
    marks = lax.all_gather(jnp.concatenate([seg_ids, capt_ids], axis=1), "fsdp", axis=0, tiled=True)
    token_count = tokens_in.shape[0]
    segment = marks[:, :token_count]
    caption = marks[:, token_count:]
    self_mask = segment[:, :, None] == segment[:, None, :]
    cross_mask = segment[:, :, None] == caption[:, None, :]

    query_z = fetch(w_query, owner_query, split_places, n_z)
    outs_z = fetch(w_outs, owner_outs, out_places, 1)
    text_z = fetch(w_text, owner_text, split_places, n_z)
    up_z = fetch(w_up, owner_up, split_places, n_z)
    down_z = fetch(w_down, owner_down, big_places, 1)

    inputs = tokens_in.astype(f32)
    normed1, inverse1 = normalize(inputs)
    hidden1 = z_gather(shuffled((normed1 * norm_full[0] + norm_full[1]).astype(bf16)))
    text_all = z_gather(shuffled(text_in))
    grad_all = z_gather(grad_out)

    projected = dot(hidden1, query_z[:, : 3 * share]).astype(bf16)
    self_query = projected[:, :share]
    self_key = projected[:, share : 2 * share]
    self_value = projected[:, 2 * share :]
    attended1, shares1 = attend_forward(self_query, self_key, self_value, self_mask)
    middle1 = inputs + z_reduce(dot(attended1, outs_z[:, :width]))
    normed2, inverse2 = normalize(middle1)
    hidden2 = z_gather(shuffled((normed2 * norm_full[2] + norm_full[3]).astype(bf16)))
    cross_query = dot(hidden2, query_z[:, 3 * share :]).astype(bf16)
    text_pairs = (
        dot(text_all[:, :width], text_z[:, : 2 * share])
        + dot(text_all[:, width:], text_z[:, 2 * share :])
    ).astype(bf16)
    text_key = text_pairs[:, :share]
    text_value = text_pairs[:, share:]
    attended2, shares2 = attend_forward(cross_query, text_key, text_value, cross_mask)
    middle2 = middle1 + z_reduce(dot(attended2, outs_z[:, width:]))
    normed3, inverse3 = normalize(middle2)
    hidden3 = z_gather(shuffled((normed3 * norm_full[4] + norm_full[5]).astype(bf16)))
    up_values = dot(hidden3, up_z)
    gelu_values, gelu_pull = jax.vjp(exact_gelu, up_values)
    activated = gelu_values.astype(bf16)
    branch3 = sum(
        dot(activated[:, f * share : (f + 1) * share], down_z[:, f * width : (f + 1) * width])
        for f in range(4)
    )
    result = (middle2 + z_reduce(branch3)).astype(bf16)

    down_part = jnp.concatenate(
        [dot_tn(activated[:, f * share : (f + 1) * share], grad_all).astype(bf16) for f in range(4)],
        axis=1,
    )
    down_grad = settle([down_part], owner_down, big_places, 1, cap_big)
    back_act = jnp.concatenate(
        [dot_nt(grad_all, down_z[:, f * width : (f + 1) * width]) for f in range(4)], axis=1
    )
    back_up = gelu_pull(back_act)[0].astype(bf16)
    back_hidden3 = unshuffled(z_reduce(dot_nt(back_up, up_z)))
    up_part = dot_tn(hidden3, back_up).astype(bf16)
    up_grad = settle([up_part], owner_up, split_places, n_z, cap_big)
    at_middle2 = grad_out.astype(f32) + norm_back(back_hidden3, normed3, inverse3, norm_full[4])
    carry2 = z_gather(at_middle2.astype(bf16))
    back_att2 = dot_nt(carry2, outs_z[:, width:]).astype(bf16)
    outs_part2 = dot_tn(attended2, carry2).astype(bf16)
    back_cross, text_kgrad, text_vgrad = attend_backward(
        cross_query, text_key, text_value, shares2, back_att2
    )
    back_pairs = jnp.concatenate([text_kgrad, text_vgrad], axis=1)
    back_hidden2 = unshuffled(z_reduce(dot_nt(back_cross, query_z[:, 3 * share :])))
    text_part = jnp.concatenate(
        [dot_tn(text_all[:, f * width : (f + 1) * width], back_pairs).astype(bf16) for f in range(2)],
        axis=1,
    )
    text_grad = settle([text_part], owner_text, split_places, n_z, cap_big)
    query_part2 = dot_tn(hidden2, back_cross).astype(bf16)
    at_middle1 = at_middle2 + norm_back(back_hidden2, normed2, inverse2, norm_full[2])
    carry1 = z_gather(at_middle1.astype(bf16))
    back_att1 = dot_nt(carry1, outs_z[:, :width]).astype(bf16)
    outs_part1 = dot_tn(attended1, carry1).astype(bf16)
    outs_grad = settle([outs_part1, outs_part2], owner_outs, out_places, 1, cap_out)
    back_projected = jnp.concatenate(
        attend_backward(self_query, self_key, self_value, shares1, back_att1), axis=1
    )
    query_part1 = dot_tn(hidden1, back_projected).astype(bf16)
    query_grad = settle([query_part1, query_part2], owner_query, split_places, n_z, cap_big)
    back_hidden1 = unshuffled(z_reduce(dot_nt(back_projected, query_z[:, : 3 * share])))
    grad_in = (at_middle1 + norm_back(back_hidden1, normed1, inverse1, norm_full[0])).astype(bf16)

    norm_term = jnp.stack(
        [
            jnp.sum(back_hidden1 * normed1, axis=0),
            jnp.sum(back_hidden1, axis=0),
            jnp.sum(back_hidden2 * normed2, axis=0),
            jnp.sum(back_hidden2, axis=0),
            jnp.sum(back_hidden3 * normed3, axis=0),
            jnp.sum(back_hidden3, axis=0),
        ]
    )
    norm_total = lax.psum(norm_term, ("dp", "fsdp"))
    norm_share = width // n_dp
    norm_grad = lax.dynamic_slice_in_dim(
        norm_total, lax.axis_index("dp") * norm_share, norm_share, 1
    )
    query_new = adamw_update(w_query, m_query, v_query, query_grad, rate_query, decay_rate)
    up_new = adamw_update(w_up, m_up, v_up, up_grad, rate_up, decay_rate)
    outs_new = adamw_update(w_outs, m_outs, v_outs, outs_grad, rate_outs, decay_rate)
    text_new = adamw_update(w_text, m_text, v_text, text_grad, rate_text, decay_rate)
    down_new = adamw_update(w_down, m_down, v_down, down_grad, rate_down, decay_rate)
    norm_new = adamw_update(norm_weight, m_norm, v_norm, norm_grad, rate_norm, 0.0)
    return (
        result,
        grad_in,
        *query_new,
        *up_new,
        *outs_new,
        *text_new,
        *down_new,
        *norm_new,
    )


def solution(mesh):
    rows = P(("dp", "fsdp"), None)
    slots = P("fsdp", "dp")
    norms = P(None, "dp")
    in_specs = (rows,) * 5 + (P(),) * 5 + (slots,) * 15 + (norms,) * 3
    out_specs = (rows,) * 2 + (slots,) * 15 + (norms,) * 3
    return jax.shard_map(body, mesh=mesh, in_specs=in_specs, out_specs=out_specs, check_vma=False)
```

```python
import functools

import jax
import jax.numpy as jnp
from jax import lax
from jax.experimental import pallas as pl
from jax.experimental.pallas import tpu as pltpu
from jax.sharding import PartitionSpec as P

HEADS = 16
HEAD = 128
STEP = 10
BLK = 128


beta_first = 0.9
beta_second = 0.999
adam_eps = 1e-08
decay_rate = 0.01
rate_query = 0.04
rate_up = 0.04
rate_outs = 0.12
rate_text = 0.03
rate_down = 0.03
rate_norm = 0.5
norm_eps = 1e-05
score_floor = -1e30
bf16 = jnp.bfloat16
f32 = jnp.float32


def normalize(values):
    centered = values - jnp.mean(values, axis=-1, keepdims=True)
    inverse_std = lax.rsqrt(jnp.mean(centered * centered, axis=-1, keepdims=True) + norm_eps)
    return (centered * inverse_std, inverse_std)


def norm_back(back_hidden, normed, inverse_std, gain_row):
    back_normed = back_hidden * gain_row
    return inverse_std * (
        back_normed
        - jnp.mean(back_normed, axis=-1, keepdims=True)
        - normed * jnp.mean(back_normed * normed, axis=-1, keepdims=True)
    )


def exact_gelu(values):
    return jax.nn.gelu(values, approximate=False)


def adamw_update(weight, first, second, gradient, rate, decay):
    first_new = beta_first * first + (1.0 - beta_first) * gradient
    second_new = beta_second * second + (1.0 - beta_second) * gradient * gradient
    first_hat = first_new / (1.0 - beta_first**STEP)
    second_hat = second_new / (1.0 - beta_second**STEP)
    weight_new = weight - rate * (first_hat / (jnp.sqrt(second_hat) + adam_eps) + decay * weight)
    return (first_new, second_new, weight_new)


def dot(left, right):
    return jnp.dot(left, right, preferred_element_type=f32)


def dot_nt(left, right):
    return lax.dot_general(left, right, (((1,), (1,)), ((), ())), preferred_element_type=f32)


def dot_tn(left, right):
    return lax.dot_general(left, right, (((0,), (0,)), ((), ())), preferred_element_type=f32)


def split_place(block, per_part, parts):
    group, rest = divmod(block, per_part * parts)
    part, inner = divmod(rest, per_part)
    return part, group * per_part + inner


def flat_place(block):
    return 0, block


def compact_kernel(places, n_dp, owner_ref, slots_ref, out_ref, count_ref):
    for index in range(n_dp):
        count_ref[index] = 0
    for block, (part, column) in enumerate(places):
        owner = owner_ref[block]
        position = count_ref[owner]
        count_ref[owner] = position + 1
        start = pl.multiple_of(position * BLK, BLK)
        out_ref[part, :, column * BLK : (column + 1) * BLK] = slots_ref[
            owner, :, pl.ds(start, BLK)
        ]


def compact(slots, owner, places, parts):
    n_dp, rows, _ = slots.shape
    columns = len(places) // parts * BLK
    return pl.pallas_call(
        functools.partial(compact_kernel, places, n_dp),
        out_shape=jax.ShapeDtypeStruct((parts, rows, columns), slots.dtype),
        in_specs=[
            pl.BlockSpec(memory_space=pltpu.SMEM),
            pl.BlockSpec(memory_space=pltpu.VMEM),
        ],
        out_specs=pl.BlockSpec(memory_space=pltpu.VMEM),
        scratch_shapes=[pltpu.SMEM((n_dp,), jnp.int32)],
        compiler_params=pltpu.CompilerParams(vmem_limit_bytes=32 * 1024 * 1024),
        cost_estimate=pl.CostEstimate(
            flops=0, bytes_accessed=2 * (slots.size + len(places) * BLK * rows), transcendentals=0
        ),
    )(owner, slots)


def expand_kernel(places, n_dp, owner_ref, grad_ref, out_ref, count_ref):
    for index in range(n_dp):
        count_ref[index] = 0
    out_ref[...] = jnp.zeros_like(out_ref)
    for block, (part, column) in enumerate(places):
        owner = owner_ref[block]
        position = count_ref[owner]
        count_ref[owner] = position + 1
        start = pl.multiple_of(position * BLK, BLK)
        out_ref[owner, :, pl.ds(start, BLK)] = grad_ref[
            part, :, column * BLK : (column + 1) * BLK
        ]


def expand(grad, owner, places, n_dp, capacity):
    rows = grad.shape[1]
    return pl.pallas_call(
        functools.partial(expand_kernel, places, n_dp),
        out_shape=jax.ShapeDtypeStruct((n_dp, rows, capacity * BLK), grad.dtype),
        in_specs=[
            pl.BlockSpec(memory_space=pltpu.SMEM),
            pl.BlockSpec(memory_space=pltpu.VMEM),
        ],
        out_specs=pl.BlockSpec(memory_space=pltpu.VMEM),
        scratch_shapes=[pltpu.SMEM((n_dp,), jnp.int32)],
        compiler_params=pltpu.CompilerParams(vmem_limit_bytes=32 * 1024 * 1024),
        cost_estimate=pl.CostEstimate(
            flops=0,
            bytes_accessed=2 * (grad.size + n_dp * capacity * BLK * rows),
            transcendentals=0,
        ),
    )(owner, grad)


def swap(values, axis):
    return lax.all_to_all(values, axis, 0, 0, tiled=True)


SUBS = 4


class Line:
    def __init__(self, n, rows, step):
        self.n, self.rows, self.step = n, rows, step
        self.at = lax.axis_index("fsdp")

    def has(self, way):
        return self.at < self.n - 1 if way == 0 else self.at > 0

    def peer(self, way):
        index = jnp.clip(self.at + (1 if way == 0 else -1), 0, self.n - 1)
        return {"fsdp": index}

    def greet(self, others=0):
        barrier = pltpu.get_barrier_semaphore()
        for way in (0, 1):

            @pl.when(self.has(way))
            def _():
                pl.semaphore_signal(
                    barrier, inc=1, device_id=self.peer(way), device_id_type=pl.DeviceIdType.MESH
                )

        pl.semaphore_wait(
            barrier, others + self.has(0).astype(jnp.int32) + self.has(1).astype(jnp.int32)
        )

    def copy(self, source, target, send, recv, way):
        return pltpu.make_async_remote_copy(
            src_ref=source,
            dst_ref=target,
            send_sem=send,
            recv_sem=recv,
            device_id=self.peer(way),
            device_id_type=pl.DeviceIdType.MESH,
        )

    def part(self, sub):
        return pl.ds(sub * self.step, self.step)


class Sums:
    def __init__(self, line, part, held, send, recv):
        self.line, self.part, self.held, self.send, self.recv = line, part, held, send, recv

    def move(self, way, target, sub, source):
        line = self.line
        rows = line.part(sub)
        return line.copy(
            source,
            self.held.at[way, target, rows],
            self.send.at[way, target, sub],
            self.recv.at[way, target, sub],
            way,
        )

    def targets(self, way):
        n = self.line.n
        return range(n - 1, 0, -1) if way == 0 else range(n - 1)

    def beyond(self, way, target):
        return self.line.at < target if way == 0 else self.line.at > target

    def forward(self, sub):
        line = self.line
        rows = line.part(sub)
        for step in range(line.n - 1):
            for way in (0, 1):
                target = self.targets(way)[step]
                inner = jnp.logical_and(self.beyond(way, target), line.has(1 - way))
                outer = jnp.logical_and(
                    self.beyond(way, target), jnp.logical_not(line.has(1 - way))
                )

                @pl.when(outer)
                def _():
                    self.move(way, target, sub, self.part.at[target, rows]).start()

                @pl.when(inner)
                def _():
                    held = self.held.at[way, target, rows]
                    self.move(way, target, sub, held).wait_recv()
                    total = held[...].astype(f32) + self.part[target, rows].astype(f32)
                    held[...] = total.astype(bf16)
                    self.move(way, target, sub, held).start()

    def total(self, sub, sum_ref):
        line = self.line
        rows = line.part(sub)
        sum_ref[...] = self.part[line.at, rows].astype(f32)
        for way in (0, 1):

            @pl.when(line.has(1 - way))
            def _():
                held = self.held.at[way, line.at, rows]
                self.move(way, line.at, sub, held).wait_recv()
                sum_ref[...] += held[...].astype(f32)

    def finish(self):
        for way in (0, 1):
            for target in self.targets(way):

                @pl.when(self.beyond(way, target))
                def _():
                    for sub in range(self.line.rows // self.line.step):
                        held = self.held.at[way, target, self.line.part(sub)]
                        self.move(way, target, sub, held).wait_send()


class Blocks:
    def __init__(self, line, full, send, recv):
        self.line, self.full, self.send, self.recv = line, full, send, recv

    def move(self, way, source, sub):
        line = self.line
        held = self.full.at[source, line.part(sub)]
        return line.copy(
            held, held, self.send.at[way, source, sub], self.recv.at[way, source, sub], way
        )

    def sources(self, way):
        n = self.line.n
        return range(n - 2, -1, -1) if way == 0 else range(1, n)

    def behind(self, way, source):
        return self.line.at > source if way == 0 else self.line.at < source

    def start(self, sub):
        for way in (0, 1):

            @pl.when(self.line.has(way))
            def _():
                self.move(way, self.line.at, sub).start()

    def forward(self, sub):
        line = self.line
        for step in range(line.n - 1):
            for way in (0, 1):
                source = self.sources(way)[step]

                @pl.when(self.behind(way, source))
                def _():
                    self.move(way, source, sub).wait_recv()

                    @pl.when(line.has(way))
                    def _():
                        self.move(way, source, sub).start()

    def finish(self):
        line = self.line
        for way in (0, 1):
            for source in range(line.n):
                ours = jnp.logical_or(self.behind(way, source), line.at == source)

                @pl.when(jnp.logical_and(ours, line.has(way)))
                def _():
                    for sub in range(line.rows // line.step):
                        self.move(way, source, sub).wait_send()


def lane_moves(width, order):
    moves = []
    piece = width // len(order)
    for group in range(width // BLK):
        parts = []
        for offset in range(0, BLK, piece):
            start = order[(group * BLK + offset) // piece] * piece
            parts.append((offset, start // BLK, start % BLK))
        moves.append(parts)
    return piece, moves


def reorder(load, store, rows, width, order):
    piece, moves = lane_moves(width, order)
    lane = lax.broadcasted_iota(jnp.int32, (rows, BLK), 1)
    for group, parts in enumerate(moves):
        value = None
        for offset, source, start in parts:
            block = load(source)
            if start != offset:
                block = pltpu.roll(block, (offset - start) % BLK, 1)
            value = block if value is None else jnp.where(lane >= offset, block, value)
        store(group, value)


def shuffle_order(n_z, n_dp):
    return [z * n_dp + i for i in range(n_dp) for z in range(n_z)]


def unshuffle_order(n_z, n_dp):
    return [i * n_z + z for z in range(n_z) for i in range(n_dp)]


def by_tiles(columns, tile, run):
    def one(index, carry):
        run(pl.ds(pl.multiple_of(index * tile, tile), tile))
        return carry

    lax.fori_loop(0, columns // tile, one, 0)


def start_kernel(n, n_dp, order, tokens, text, grad, marks, norms, *rest):
    h_full, text_full, grad_full, marks_full, norm_full = rest[:5]
    parts, work, n_send, n_recv = rest[5:9]
    sems = rest[9:]
    rows, width = tokens.shape
    step = rows // SUBS
    me = lax.axis_index("dp")
    line = Line(n, rows, step)
    barrier = pltpu.get_barrier_semaphore()
    for jump in range(1, n_dp):
        pl.semaphore_signal(
            barrier,
            inc=1,
            device_id={"dp": lax.rem(me + jump, n_dp)},
            device_id_type=pl.DeviceIdType.MESH,
        )
    line.greet(n_dp - 1)

    def norm_copy(jump):
        return pltpu.make_async_remote_copy(
            src_ref=norms,
            dst_ref=parts.at[me],
            send_sem=n_send.at[jump],
            recv_sem=n_recv.at[me],
            device_id={"dp": lax.rem(me + jump, n_dp)},
            device_id_type=pl.DeviceIdType.MESH,
        )

    def norm_arrival(jump):
        source = lax.rem(me + jump, n_dp)
        return pltpu.make_async_remote_copy(
            src_ref=norms,
            dst_ref=parts.at[source],
            send_sem=n_send.at[jump],
            recv_sem=n_recv.at[source],
            device_id={"dp": source},
            device_id_type=pl.DeviceIdType.MESH,
        )

    for jump in range(1, n_dp):
        norm_copy(jump).start()
    text_rows = text.shape[0]
    text_line = Line(n, text_rows, text_rows)
    mark_line = Line(n, marks.shape[0], marks.shape[0])
    hidden = Blocks(line, h_full, sems[0], sems[1])
    texts = Blocks(text_line, text_full, sems[2], sems[3])
    grads = Blocks(line, grad_full, sems[4], sems[5])
    places = Blocks(mark_line, marks_full, sems[6], sems[7])
    marks_full[line.at] = marks[...]
    places.start(0)
    parts[me] = norms[...]
    for jump in range(1, n_dp):
        norm_arrival(jump).wait_recv()
    share = width // n_dp
    for index in range(n_dp):
        norm_full[:, index * share : (index + 1) * share] = parts[index]
    for sub in range(SUBS):
        here = line.part(sub)
        normed, _ = normalize(tokens[here].astype(f32))
        work[...] = normed * norm_full[0:1] + norm_full[1:2]

        def load(group):
            return work[:, group * BLK : (group + 1) * BLK]

        def store(group, value):
            h_full[line.at, here, group * BLK : (group + 1) * BLK] = value.astype(bf16)

        reorder(load, store, step, width, order)
        hidden.start(sub)

    def load_text(group):
        return text[:, group * BLK : (group + 1) * BLK].astype(f32)

    def store_text(group, value):
        text_full[line.at, :, group * BLK : (group + 1) * BLK] = value.astype(bf16)

    folds = text.shape[1] // width
    text_order = [fold * len(order) + piece for fold in range(folds) for piece in order]
    reorder(load_text, store_text, text_rows, folds * width, text_order)
    texts.start(0)
    for sub in range(SUBS):
        here = line.part(sub)
        grad_full[line.at, here] = grad[here]
        grads.start(sub)
    places.forward(0)
    for sub in range(SUBS):
        hidden.forward(sub)
    texts.forward(0)
    for sub in range(SUBS):
        grads.forward(sub)
    for blocks in (hidden, texts, grads, places):
        blocks.finish()
    for jump in range(1, n_dp):
        norm_copy(jump).wait_send()


def fetch_columns(source, index, target, sem):
    columns = target.shape[1]
    return pltpu.make_async_copy(source.at[:, pl.ds(index * columns, columns)], target, sem)


def forward_kernel(n, order, half, wide, att_ref, outs_hbm, base_ref, norm_ref, *rest):
    if wide:
        next_hbm, middle_ref, full_ref, result_ref = rest[:4]
        *rest, next_ref, next_sem = rest[4:]
    else:
        middle_ref, full_ref = rest[:2]
        rest = rest[2:]
    part, held, work, s_send, s_recv, b_send, b_recv, outs_ref, outs_sem = rest
    rows, width = base_ref.shape
    step = rows // SUBS
    load_outs = fetch_columns(outs_hbm, half, outs_ref, outs_sem)
    load_outs.start()
    if wide:
        load_next = fetch_columns(next_hbm, 3, next_ref, next_sem)
        load_next.start()
    line = Line(n, rows, step)
    line.greet()
    load_outs.wait()
    sums = Sums(line, part, held, s_send, s_recv)
    blocks = Blocks(line, full_ref, b_send, b_recv)

    def multiply(columns):
        product = dot(att_ref[...], outs_ref[:, columns]).astype(bf16)
        part[:, :, columns] = product.reshape(n, rows, -1)

    by_tiles(width, 256, multiply)
    for time in range(SUBS + 2):
        if time < SUBS:
            sums.forward(time)
        if 0 <= time - 1 < SUBS:
            sub = time - 1
            here = line.part(sub)
            sums.total(sub, work)
            middle = base_ref[here].astype(f32) + work[...]
            middle_ref[here] = middle
            normed, _ = normalize(middle)
            work[...] = normed * norm_ref[0:1] + norm_ref[1:2]

            def load(group):
                return work[:, group * BLK : (group + 1) * BLK]

            def store(group, value):
                full_ref[line.at, here, group * BLK : (group + 1) * BLK] = value.astype(bf16)

            reorder(load, store, step, width, order)
            blocks.start(sub)
        if 0 <= time - 2 < SUBS:
            blocks.forward(time - 2)
    sums.finish()
    blocks.finish()
    if wide:
        load_next.wait()

        def multiply_next(columns):
            whole = full_ref[...].reshape(n * rows, width)
            result_ref[:, columns] = dot(whole, next_ref[:, columns]).astype(bf16)

        by_tiles(result_ref.shape[1], 256, multiply_next)


def carry_back(work, plain, order, step, width, middle, base, gain, term_ref, first):
    def load(group):
        return work[:, group * BLK : (group + 1) * BLK]

    def store(group, value):
        plain[:, group * BLK : (group + 1) * BLK] = value

    reorder(load, store, step, width, order)
    back_hidden = plain[...]
    normed, inverse = normalize(middle)
    gain_term = jnp.sum(back_hidden * normed, axis=0, keepdims=True)
    bias_term = jnp.sum(back_hidden, axis=0, keepdims=True)
    if first:
        term_ref[0:1] = gain_term
        term_ref[1:2] = bias_term
    else:
        term_ref[0:1] += gain_term
        term_ref[1:2] += bias_term
    return base + norm_back(back_hidden, normed, inverse, gain)


def back_kernel(
    n, order, column, half, dy_ref, w_hbm, base_ref, middle_ref, norm_ref, outs_hbm, *rest
):
    carry_ref, full_ref, att_ref, term_ref = rest[:4]
    part, held, work, plain, s_send, s_recv, b_send, b_recv = rest[4:12]
    w_ref, w_sem, outs_ref, outs_sem = rest[12:]
    rows, width = base_ref.shape
    step = rows // SUBS
    load_w = fetch_columns(w_hbm, column, w_ref, w_sem)
    load_w.start()
    load_outs = fetch_columns(outs_hbm, half, outs_ref, outs_sem)
    load_outs.start()
    line = Line(n, rows, step)
    line.greet()
    load_w.wait()
    sums = Sums(line, part, held, s_send, s_recv)
    blocks = Blocks(line, full_ref, b_send, b_recv)

    def multiply(columns):
        product = dot_nt(dy_ref[...], w_ref[columns]).astype(bf16)
        part[:, :, columns] = product.reshape(n, rows, -1)

    by_tiles(width, 256, multiply)
    for time in range(SUBS + 2):
        if time < SUBS:
            sums.forward(time)
        if 0 <= time - 1 < SUBS:
            sub = time - 1
            here = line.part(sub)
            sums.total(sub, work)
            carry = carry_back(
                work,
                plain,
                order,
                step,
                width,
                middle_ref[here].astype(f32),
                base_ref[here].astype(f32),
                norm_ref[0:1],
                term_ref,
                sub == 0,
            )
            carry_ref[here] = carry
            full_ref[line.at, here] = carry.astype(bf16)
            blocks.start(sub)
        if 0 <= time - 2 < SUBS:
            blocks.forward(time - 2)
    sums.finish()
    blocks.finish()
    load_outs.wait()

    def multiply_next(columns):
        whole = full_ref[...].reshape(n * rows, width)
        att_ref[:, columns] = dot_nt(whole, outs_ref[columns]).astype(bf16)

    by_tiles(att_ref.shape[1], 256, multiply_next)


def last_kernel(n, order, dy_ref, w_hbm, base_ref, tokens, norm_ref, branch, middle, *rest):
    grad_ref, result_ref, term_ref = rest[:3]
    part, held, held2, work, plain, s_send, s_recv, r_send, r_recv, w_ref, w_sem = rest[3:]
    rows, width = base_ref.shape
    step = rows // SUBS
    load_w = fetch_columns(w_hbm, 0, w_ref, w_sem)
    load_w.start()
    line = Line(n, rows, step)
    line.greet()
    load_w.wait()
    sums = Sums(line, part, held, s_send, s_recv)
    results = Sums(line, branch, held2, r_send, r_recv)

    def multiply(columns):
        product = dot_nt(dy_ref[...], w_ref[columns]).astype(bf16)
        part[:, :, columns] = product.reshape(n, rows, -1)

    by_tiles(width, 256, multiply)
    for time in range(SUBS + 1):
        if time < SUBS:
            sums.forward(time)
            results.forward(time)
        if 0 <= time - 1 < SUBS:
            sub = time - 1
            here = line.part(sub)
            sums.total(sub, work)
            carry = carry_back(
                work,
                plain,
                order,
                step,
                width,
                tokens[here].astype(f32),
                base_ref[here],
                norm_ref[0:1],
                term_ref,
                sub == 0,
            )
            grad_ref[here] = carry.astype(bf16)
            results.total(sub, work)
            result_ref[here] = (middle[here] + work[...]).astype(bf16)
    sums.finish()
    results.finish()


VMEM_CAP = 52 * 1024 * 1024


def in_place():
    return pl.BlockSpec(memory_space=pl.ANY)


def whole_vmem():
    return pl.BlockSpec(memory_space=pltpu.VMEM)


def sem_pair(n, subs):
    return [pltpu.SemaphoreType.DMA((2, n, subs)), pltpu.SemaphoreType.DMA((2, n, subs))]


def line_call(kernel, name, ident, outs, specs, scratch, flops, moved):
    return pl.pallas_call(
        kernel,
        name=name,
        out_shape=outs,
        in_specs=specs,
        out_specs=jax.tree.map(lambda _: whole_vmem(), outs),
        scratch_shapes=scratch,
        compiler_params=pltpu.CompilerParams(
            collective_id=ident, has_side_effects=True, vmem_limit_bytes=VMEM_CAP
        ),
        cost_estimate=pl.CostEstimate(flops=flops, bytes_accessed=moved, transcendentals=0),
    )


def shape(dims, kind):
    return jax.ShapeDtypeStruct(dims, kind)


LINK_COST = 120_000_000


def start_call(tokens, text, grad, marks, norms, n, n_dp):
    rows, width = tokens.shape
    outs = (
        shape((n, *tokens.shape), bf16),
        shape((n, *text.shape), bf16),
        shape((n, *grad.shape), bf16),
        shape((n, *marks.shape), jnp.int32),
        shape((norms.shape[0], width), f32),
    )
    scratch = [
        pltpu.VMEM((n_dp, *norms.shape), f32),
        pltpu.VMEM((rows // SUBS, width), f32),
        pltpu.SemaphoreType.DMA((n_dp,)),
        pltpu.SemaphoreType.DMA((n_dp,)),
        *sem_pair(n, SUBS),
        *sem_pair(n, 1),
        *sem_pair(n, SUBS),
        *sem_pair(n, 1),
    ]
    kernel = functools.partial(start_kernel, n, n_dp, shuffle_order(n, n_dp))
    call = line_call(kernel, "start", 0, outs, [whole_vmem()] * 5, scratch, 0, LINK_COST)
    return call(tokens, text, grad, marks, norms)


def forward_call(attended, outs_z, half, base, norm_rows, after, n, n_dp, ident):
    rows, width = base.shape
    share = outs_z.shape[0]
    outs = [shape((rows, width), f32), shape((n, rows, width), bf16)]
    specs = [whole_vmem(), in_place(), whole_vmem(), whole_vmem()]
    args = [attended, outs_z, base, norm_rows]
    scratch = [
        pltpu.VMEM((n, rows, width), bf16),
        pltpu.VMEM((2, n, rows, width), bf16),
        pltpu.VMEM((rows // SUBS, width), f32),
        *sem_pair(n, SUBS),
        *sem_pair(n, SUBS),
        pltpu.VMEM((share, width), bf16),
        pltpu.SemaphoreType.DMA,
    ]
    if after is not None:
        outs.append(shape((n * rows, share), bf16))
        specs.append(in_place())
        args.append(after)
        scratch += [pltpu.VMEM((width, share), bf16), pltpu.SemaphoreType.DMA]
    kernel = functools.partial(forward_kernel, n, shuffle_order(n, n_dp), half, after is not None)
    call = line_call(kernel, f"forward{half}", ident, outs, specs, scratch, 0, LINK_COST)
    return call(*args)


def back_call(dy, weight, column, base, middle, norm_rows, outs_z, half, n, n_dp, ident):
    rows, width = base.shape
    share = outs_z.shape[0]
    outs = [
        shape((rows, width), f32),
        shape((n, rows, width), bf16),
        shape((n * rows, share), bf16),
        shape((8, width), f32),
    ]
    specs = [
        whole_vmem(),
        in_place(),
        whole_vmem(),
        whole_vmem(),
        whole_vmem(),
        in_place(),
    ]
    scratch = [
        pltpu.VMEM((n, rows, width), bf16),
        pltpu.VMEM((2, n, rows, width), bf16),
        pltpu.VMEM((rows // SUBS, width), f32),
        pltpu.VMEM((rows // SUBS, width), f32),
        *sem_pair(n, SUBS),
        *sem_pair(n, SUBS),
        pltpu.VMEM((width, dy.shape[1]), bf16),
        pltpu.SemaphoreType.DMA,
        pltpu.VMEM((share, width), bf16),
        pltpu.SemaphoreType.DMA,
    ]
    kernel = functools.partial(back_kernel, n, unshuffle_order(n, n_dp), column, half)
    call = line_call(kernel, f"back{half}", ident, outs, specs, scratch, 0, LINK_COST)
    return call(dy, weight, base, middle, norm_rows, outs_z)


def last_call(dy, weight, base, tokens, norm_rows, branch, middle, n, n_dp, ident):
    rows, width = base.shape
    outs = [
        shape((rows, width), bf16),
        shape((rows, width), bf16),
        shape((8, width), f32),
    ]
    specs = [whole_vmem(), in_place()] + [whole_vmem()] * 5
    scratch = [
        pltpu.VMEM((n, rows, width), bf16),
        pltpu.VMEM((2, n, rows, width), bf16),
        pltpu.VMEM((2, n, rows, width), bf16),
        pltpu.VMEM((rows // SUBS, width), f32),
        pltpu.VMEM((rows // SUBS, width), f32),
        *sem_pair(n, SUBS),
        *sem_pair(n, SUBS),
        pltpu.VMEM((width, dy.shape[1]), bf16),
        pltpu.SemaphoreType.DMA,
    ]
    kernel = functools.partial(last_kernel, n, unshuffle_order(n, n_dp))
    call = line_call(kernel, "last", ident, outs, specs, scratch, 0, LINK_COST)
    return call(dy, weight, base, tokens, norm_rows, branch, middle)


def attend_forward(queries, keys, values, allowed):
    packed = allowed.shape[0]
    heads = queries.shape[1] // HEAD
    query_heads = queries.reshape(packed, -1, heads, HEAD)
    key_heads = keys.reshape(packed, -1, heads, HEAD)
    value_heads = values.reshape(packed, -1, heads, HEAD)
    scores = jnp.einsum(
        "pqhd,pkhd->phqk", query_heads, key_heads, preferred_element_type=f32
    ) * HEAD ** (-0.5)
    scores = jnp.where(allowed[:, None], scores, score_floor)
    powers = jnp.exp(scores - jnp.max(scores, axis=-1, keepdims=True))
    shares = powers / jnp.sum(powers, axis=-1, keepdims=True)
    attended = jnp.einsum(
        "phqk,pkhd->pqhd", shares.astype(bf16), value_heads, preferred_element_type=f32
    )
    return attended.reshape(queries.shape).astype(bf16), shares


def attend_backward(queries, keys, values, shares, back_attended):
    packed = shares.shape[0]
    heads = queries.shape[1] // HEAD
    query_heads = queries.reshape(packed, -1, heads, HEAD)
    key_heads = keys.reshape(packed, -1, heads, HEAD)
    value_heads = values.reshape(packed, -1, heads, HEAD)
    back_heads = back_attended.reshape(packed, -1, heads, HEAD)
    score_scale = HEAD ** (-0.5)
    back_shares = jnp.einsum(
        "pqhd,pkhd->phqk", back_heads, value_heads, preferred_element_type=f32
    )
    inner_sum = jnp.sum(shares * back_shares, axis=-1, keepdims=True)
    back_scores = (shares * (back_shares - inner_sum)).astype(bf16)
    query_grad = (
        jnp.einsum("phqk,pkhd->pqhd", back_scores, key_heads, preferred_element_type=f32)
        * score_scale
    )
    key_grad = (
        jnp.einsum("phqk,pqhd->pkhd", back_scores, query_heads, preferred_element_type=f32)
        * score_scale
    )
    value_grad = jnp.einsum(
        "phqk,pqhd->pkhd", shares.astype(bf16), back_heads, preferred_element_type=f32
    )
    return (
        query_grad.reshape(queries.shape).astype(bf16),
        key_grad.reshape(keys.shape).astype(bf16),
        value_grad.reshape(values.shape).astype(bf16),
    )


def body(
    tokens_in,
    text_in,
    seg_ids,
    capt_ids,
    grad_out,
    owner_query,
    owner_up,
    owner_outs,
    owner_text,
    owner_down,
    w_query,
    m_query,
    v_query,
    w_up,
    m_up,
    v_up,
    w_outs,
    m_outs,
    v_outs,
    w_text,
    m_text,
    v_text,
    w_down,
    m_down,
    v_down,
    norm_weight,
    m_norm,
    v_norm,
):
    n_dp = lax.axis_size("dp")
    n_z = lax.axis_size("fsdp")
    width = tokens_in.shape[1]
    own_rows = w_query.shape[0]
    chunk = own_rows // n_dp
    cap_big = w_query.shape[1] // BLK
    cap_out = w_outs.shape[1] // BLK
    heads_z = HEADS // n_z
    share = width // n_z
    owner_query, owner_up, owner_outs, owner_text, owner_down = (
        owner[:, 0] for owner in (owner_query, owner_up, owner_outs, owner_text, owner_down)
    )
    split_places = [split_place(b, heads_z, n_z) for b in range(owner_query.shape[0])]
    big_places = [flat_place(b) for b in range(owner_down.shape[0])]
    out_places = [flat_place(b) for b in range(owner_outs.shape[0])]

    def fetch(weight, owner, places, parts):
        slots = swap(weight.astype(bf16), "dp").reshape(n_dp, chunk, -1)
        rows = compact(slots, owner, places, parts)
        if parts > 1:
            rows = swap(rows, "fsdp")
        rows = rows.reshape(parts * chunk, -1)
        return lax.all_gather(rows, "dp", axis=0, tiled=True)

    def settle(pieces, owner, places, parts, capacity):
        summed = [
            lax.psum_scatter(piece, "dp", scatter_dimension=0, tiled=True) for piece in pieces
        ]
        summed = summed[0] if len(summed) == 1 else jnp.concatenate(summed, axis=1)
        rows = summed.reshape(parts, chunk, -1)
        if parts > 1:
            rows = swap(rows, "fsdp")
        slots = expand(rows, owner, places, n_dp, capacity)
        return swap(slots, "dp").reshape(n_dp * chunk, -1).astype(f32)

    query_z = fetch(w_query, owner_query, split_places, n_z)
    outs_z = fetch(w_outs, owner_outs, out_places, 1)
    text_z = fetch(w_text, owner_text, split_places, n_z)
    up_z = fetch(w_up, owner_up, split_places, n_z)
    down_z = fetch(w_down, owner_down, big_places, 1)

    token_count = tokens_in.shape[0]
    marks = jnp.concatenate([seg_ids, capt_ids], axis=1)
    marks = jnp.pad(marks, ((0, 7), (0, 256 - marks.shape[1])))
    norms = jnp.pad(norm_weight, ((0, 2), (0, 0)))
    hidden1, text_all, grad_all, marks, norm_full = start_call(
        tokens_in, text_in, grad_out, marks, norms, n_z, n_dp
    )
    hidden1, text_all, grad_all = (
        values.reshape(-1, values.shape[-1]) for values in (hidden1, text_all, grad_all)
    )
    segment = marks[:, 0, :token_count]
    caption = marks[:, 0, token_count : token_count + capt_ids.shape[1]]
    self_mask = segment[:, :, None] == segment[:, None, :]
    cross_mask = segment[:, :, None] == caption[:, None, :]

    projected = dot(hidden1, query_z[:, : 3 * share]).astype(bf16)
    self_query = projected[:, :share]
    self_key = projected[:, share : 2 * share]
    self_value = projected[:, 2 * share :]
    attended1, shares1 = attend_forward(self_query, self_key, self_value, self_mask)
    middle1, hidden2, cross_query = forward_call(
        attended1, outs_z, 0, tokens_in, norm_full[2:4], query_z, n_z, n_dp, 1
    )
    hidden2 = hidden2.reshape(-1, width)
    text_pairs = (
        dot(text_all[:, :width], text_z[:, : 2 * share])
        + dot(text_all[:, width:], text_z[:, 2 * share :])
    ).astype(bf16)
    text_key = text_pairs[:, :share]
    text_value = text_pairs[:, share:]
    attended2, shares2 = attend_forward(cross_query, text_key, text_value, cross_mask)
    middle2, hidden3 = forward_call(
        attended2, outs_z, 1, middle1, norm_full[4:6], None, n_z, n_dp, 2
    )
    hidden3 = hidden3.reshape(-1, width)
    up_values = dot(hidden3, up_z)
    gelu_values, gelu_pull = jax.vjp(exact_gelu, up_values)
    activated = gelu_values.astype(bf16)
    branch3 = sum(
        dot(activated[:, f * share : (f + 1) * share], down_z[:, f * width : (f + 1) * width])
        for f in range(4)
    )
    branch3 = branch3.astype(bf16).reshape(n_z, token_count, width)

    down_part = jnp.concatenate(
        [dot_tn(activated[:, f * share : (f + 1) * share], grad_all).astype(bf16) for f in range(4)],
        axis=1,
    )
    down_grad = settle([down_part], owner_down, big_places, 1, cap_big)
    back_act = jnp.concatenate(
        [dot_nt(grad_all, down_z[:, f * width : (f + 1) * width]) for f in range(4)], axis=1
    )
    back_up = gelu_pull(back_act)[0].astype(bf16)
    up_part = dot_tn(hidden3, back_up).astype(bf16)
    up_grad = settle([up_part], owner_up, split_places, n_z, cap_big)
    at_middle2, carry2, back_att2, term3 = back_call(
        back_up, up_z, 0, grad_out, middle2, norm_full[4:6], outs_z, 1, n_z, n_dp, 3
    )
    carry2 = carry2.reshape(-1, width)
    outs_part2 = dot_tn(attended2, carry2).astype(bf16)
    back_cross, text_kgrad, text_vgrad = attend_backward(
        cross_query, text_key, text_value, shares2, back_att2
    )
    back_pairs = jnp.concatenate([text_kgrad, text_vgrad], axis=1)
    text_part = jnp.concatenate(
        [dot_tn(text_all[:, f * width : (f + 1) * width], back_pairs).astype(bf16) for f in range(2)],
        axis=1,
    )
    text_grad = settle([text_part], owner_text, split_places, n_z, cap_big)
    query_part2 = dot_tn(hidden2, back_cross).astype(bf16)
    at_middle1, carry1, back_att1, term2 = back_call(
        back_cross, query_z, 3, at_middle2, middle1, norm_full[2:4], outs_z, 0, n_z, n_dp, 4
    )
    carry1 = carry1.reshape(-1, width)
    outs_part1 = dot_tn(attended1, carry1).astype(bf16)
    outs_grad = settle([outs_part1, outs_part2], owner_outs, out_places, 1, cap_out)
    back_projected = jnp.concatenate(
        attend_backward(self_query, self_key, self_value, shares1, back_att1), axis=1
    )
    query_part1 = dot_tn(hidden1, back_projected).astype(bf16)
    query_grad = settle([query_part1, query_part2], owner_query, split_places, n_z, cap_big)
    grad_in, result, term1 = last_call(
        back_projected,
        query_z,
        at_middle1,
        tokens_in,
        norm_full[0:2],
        branch3,
        middle2,
        n_z,
        n_dp,
        5,
    )
    norm_term = jnp.concatenate([term1[:2], term2[:2], term3[:2]], axis=0)
    norm_total = lax.psum(norm_term, ("dp", "fsdp"))
    norm_share = width // n_dp
    norm_grad = lax.dynamic_slice_in_dim(
        norm_total, lax.axis_index("dp") * norm_share, norm_share, 1
    )
    query_new = adamw_update(w_query, m_query, v_query, query_grad, rate_query, decay_rate)
    up_new = adamw_update(w_up, m_up, v_up, up_grad, rate_up, decay_rate)
    outs_new = adamw_update(w_outs, m_outs, v_outs, outs_grad, rate_outs, decay_rate)
    text_new = adamw_update(w_text, m_text, v_text, text_grad, rate_text, decay_rate)
    down_new = adamw_update(w_down, m_down, v_down, down_grad, rate_down, decay_rate)
    norm_new = adamw_update(norm_weight, m_norm, v_norm, norm_grad, rate_norm, 0.0)
    return (
        result,
        grad_in,
        *query_new,
        *up_new,
        *outs_new,
        *text_new,
        *down_new,
        *norm_new,
    )


def solution(mesh):
    rows = P(("dp", "fsdp"), None)
    slots = P("fsdp", "dp")
    norms = P(None, "dp")
    in_specs = (rows,) * 5 + (P(),) * 5 + (slots,) * 15 + (norms,) * 3
    out_specs = (rows,) * 2 + (slots,) * 15 + (norms,) * 3
    return jax.shard_map(body, mesh=mesh, in_specs=in_specs, out_specs=out_specs, check_vma=False)
```

```python
import functools

import jax
import jax.numpy as jnp
from jax import lax
from jax.experimental import pallas as pl
from jax.experimental.pallas import tpu as pltpu
from jax.sharding import PartitionSpec as P

HEADS = 16
HEAD = 128
STEP = 10
BLK = 128


beta_first = 0.9
beta_second = 0.999
adam_eps = 1e-08
decay_rate = 0.01
rate_query = 0.04
rate_up = 0.04
rate_outs = 0.12
rate_text = 0.03
rate_down = 0.03
rate_norm = 0.5
norm_eps = 1e-05
score_floor = -1e30
bf16 = jnp.bfloat16
f32 = jnp.float32


def normalize(values):
    centered = values - jnp.mean(values, axis=-1, keepdims=True)
    inverse_std = lax.rsqrt(jnp.mean(centered * centered, axis=-1, keepdims=True) + norm_eps)
    return (centered * inverse_std, inverse_std)


def norm_back(back_hidden, normed, inverse_std, gain_row):
    back_normed = back_hidden * gain_row
    return inverse_std * (
        back_normed
        - jnp.mean(back_normed, axis=-1, keepdims=True)
        - normed * jnp.mean(back_normed * normed, axis=-1, keepdims=True)
    )


def exact_gelu(values):
    return jax.nn.gelu(values, approximate=False)


def adamw_update(weight, first, second, gradient, rate, decay):
    first_new = beta_first * first + (1.0 - beta_first) * gradient
    second_new = beta_second * second + (1.0 - beta_second) * gradient * gradient
    first_hat = first_new / (1.0 - beta_first**STEP)
    second_hat = second_new / (1.0 - beta_second**STEP)
    weight_new = weight - rate * (first_hat / (jnp.sqrt(second_hat) + adam_eps) + decay * weight)
    return (first_new, second_new, weight_new)


def dot(left, right):
    return jnp.dot(left, right, preferred_element_type=f32)


def dot_nt(left, right):
    return lax.dot_general(left, right, (((1,), (1,)), ((), ())), preferred_element_type=f32)


def dot_tn(left, right):
    return lax.dot_general(left, right, (((0,), (0,)), ((), ())), preferred_element_type=f32)


def split_place(block, per_part, parts):
    group, rest = divmod(block, per_part * parts)
    part, inner = divmod(rest, per_part)
    return part, group * per_part + inner


def flat_place(block):
    return 0, block


MESH = pl.DeviceIdType.MESH


SUBS = 4


class Line:
    def __init__(self, n, rows, step):
        self.n, self.rows, self.step = n, rows, step
        self.at = lax.axis_index("fsdp")

    def has(self, way):
        return self.at < self.n - 1 if way == 0 else self.at > 0

    def peer(self, way):
        index = jnp.clip(self.at + (1 if way == 0 else -1), 0, self.n - 1)
        return {"fsdp": index}

    def greet(self, others=0):
        barrier = pltpu.get_barrier_semaphore()
        for way in (0, 1):

            @pl.when(self.has(way))
            def _():
                pl.semaphore_signal(
                    barrier, inc=1, device_id=self.peer(way), device_id_type=pl.DeviceIdType.MESH
                )

        pl.semaphore_wait(
            barrier, others + self.has(0).astype(jnp.int32) + self.has(1).astype(jnp.int32)
        )

    def copy(self, source, target, send, recv, way):
        return pltpu.make_async_remote_copy(
            src_ref=source,
            dst_ref=target,
            send_sem=send,
            recv_sem=recv,
            device_id=self.peer(way),
            device_id_type=pl.DeviceIdType.MESH,
        )

    def part(self, sub):
        return pl.ds(sub * self.step, self.step)


class Sums:
    def __init__(self, line, part, held, send, recv):
        self.line, self.part, self.held, self.send, self.recv = line, part, held, send, recv

    def move(self, way, target, sub, source):
        line = self.line
        rows = line.part(sub)
        return line.copy(
            source,
            self.held.at[way, target, rows],
            self.send.at[way, target, sub],
            self.recv.at[way, target, sub],
            way,
        )

    def target(self, way, time):
        n, at = self.line.n, self.line.at
        return n - 1 - (time - at) if way == 0 else time - (n - 1 - at)

    def passes(self, way, target):
        n, at = self.line.n, self.line.at
        if way == 0:
            return jnp.logical_and(target > at, target < n)
        return jnp.logical_and(target < at, target >= 0)

    def forward(self, sub, time):
        line = self.line
        rows = line.part(sub)
        for way in (0, 1):
            target = self.target(way, time)
            passes = self.passes(way, target)
            inner = jnp.logical_and(passes, line.has(1 - way))
            outer = jnp.logical_and(passes, jnp.logical_not(line.has(1 - way)))

            @pl.when(outer)
            def _():
                self.move(way, target, sub, self.part.at[target, rows]).start()

            @pl.when(inner)
            def _():
                held = self.held.at[way, target, rows]
                self.move(way, target, sub, held).wait_recv()
                total = held[...].astype(f32) + self.part[target, rows].astype(f32)
                held[...] = total.astype(bf16)
                self.move(way, target, sub, held).start()

    def total(self, sub, sum_ref):
        line = self.line
        rows = line.part(sub)
        sum_ref[...] = self.part[line.at, rows].astype(f32)
        for way in (0, 1):

            @pl.when(line.has(1 - way))
            def _():
                held = self.held.at[way, line.at, rows]
                self.move(way, line.at, sub, held).wait_recv()
                sum_ref[...] += held[...].astype(f32)

    def finish(self):
        line = self.line
        for way in (0, 1):
            for time in range(line.n - 1):
                target = self.target(way, time)

                @pl.when(self.passes(way, target))
                def _():
                    for sub in range(line.rows // line.step):
                        held = self.held.at[way, target, line.part(sub)]
                        self.move(way, target, sub, held).wait_send()


def relay(n, sums, blocks, settle):
    for slot in range((SUBS + 2) * (n - 1)):
        sub, time = divmod(slot, n - 1)
        if sub < SUBS:
            for one in sums:
                one.forward(sub, time)
        if time == 0 and 0 <= sub - 1 < SUBS:
            settle(sub - 1)
        if blocks is not None:
            if time == n - 2 and 0 <= sub - 1 < SUBS:
                blocks.forward(sub - 1, 1)
            if time < n - 2 and 0 <= sub - 2 < SUBS:
                blocks.forward(sub - 2, time + 2)
    for one in sums:
        one.finish()
    if blocks is not None:
        blocks.finish()


class Blocks:
    def __init__(self, line, full, send, recv):
        self.line, self.full, self.send, self.recv = line, full, send, recv

    def move(self, way, source, sub):
        line = self.line
        held = self.full.at[source, line.part(sub)]
        return line.copy(
            held, held, self.send.at[way, source, sub], self.recv.at[way, source, sub], way
        )

    def behind(self, way, source):
        return self.line.at > source if way == 0 else self.line.at < source

    def start(self, sub):
        for way in (0, 1):

            @pl.when(self.line.has(way))
            def _():
                self.move(way, self.line.at, sub).start()

    def forward(self, sub, step):
        line = self.line
        for way in (0, 1):
            source = line.at - step if way == 0 else line.at + step

            @pl.when(jnp.logical_and(source >= 0, source < line.n))
            def _():
                self.move(way, source, sub).wait_recv()

                @pl.when(line.has(way))
                def _():
                    self.move(way, source, sub).start()

    def forward_all(self, sub):
        for step in range(1, self.line.n):
            self.forward(sub, step)

    def finish(self):
        line = self.line
        for way in (0, 1):
            for source in range(line.n):
                ours = jnp.logical_or(self.behind(way, source), line.at == source)

                @pl.when(jnp.logical_and(ours, line.has(way)))
                def _():
                    for sub in range(line.rows // line.step):
                        self.move(way, source, sub).wait_send()


def lane_moves(width, order):
    moves = []
    piece = width // len(order)
    for group in range(width // BLK):
        parts = []
        for offset in range(0, BLK, piece):
            start = order[(group * BLK + offset) // piece] * piece
            parts.append((offset, start // BLK, start % BLK))
        moves.append(parts)
    return piece, moves


def reorder(load, store, rows, width, order):
    piece, moves = lane_moves(width, order)
    lane = lax.broadcasted_iota(jnp.int32, (rows, BLK), 1)
    for group, parts in enumerate(moves):
        value = None
        for offset, source, start in parts:
            block = load(source)
            if start != offset:
                block = pltpu.roll(block, (offset - start) % BLK, 1)
            value = block if value is None else jnp.where(lane >= offset, block, value)
        store(group, value)


def shuffle_order(n_z, n_dp):
    return [z * n_dp + i for i in range(n_dp) for z in range(n_z)]


def unshuffle_order(n_z, n_dp):
    return [i * n_z + z for z in range(n_z) for i in range(n_dp)]


def by_tiles(columns, tile, run):
    def one(index, carry):
        run(pl.ds(pl.multiple_of(index * tile, tile), tile))
        return carry

    lax.fori_loop(0, columns // tile, one, 0)


class Swap:
    def __init__(self, axis, source, target, send, recv):
        self.axis, self.source, self.target = axis, source, target
        self.send, self.recv = send, recv
        self.n = lax.axis_size(axis)
        self.me = lax.axis_index(axis)

    def copy(self, jump, arrival=False):
        peer = lax.rem(self.me + jump, self.n)
        slot = peer if arrival else self.me
        return pltpu.make_async_remote_copy(
            src_ref=self.source.at[peer],
            dst_ref=self.target.at[slot],
            send_sem=self.send.at[jump],
            recv_sem=self.recv.at[slot],
            device_id={self.axis: peer},
            device_id_type=MESH,
        )

    def start(self):
        for jump in range(1, self.n):
            self.copy(jump).start()

    def keep(self):
        self.target[self.me] = self.source[self.me]

    def wait(self):
        for jump in range(1, self.n):
            self.copy(jump, True).wait_recv()

    def finish(self):
        for jump in range(1, self.n):
            self.copy(jump).wait_send()


def greet_all():
    barrier = pltpu.get_barrier_semaphore()
    count = 0
    for axis in ("dp", "fsdp"):
        n, me = lax.axis_size(axis), lax.axis_index(axis)
        count += n - 1
        for jump in range(1, n):
            pl.semaphore_signal(
                barrier, inc=1, device_id={axis: lax.rem(me + jump, n)}, device_id_type=MESH
            )
    pl.semaphore_wait(barrier, count)


class Refs:
    def __init__(self, refs):
        self.refs = list(refs)

    def take(self, count=None):
        taken = self.refs[: 1 if count is None else count]
        self.refs = self.refs[len(taken) :]
        return taken[0] if count is None else taken


def enter_kernel(weights, gathers, order, normed, hidden, *refs):
    refs = Refs(refs)
    n_dp, n_z = lax.axis_size("dp"), lax.axis_size("fsdp")
    slots_ref = refs.take()
    w_refs = refs.take(len(weights))
    in_refs = refs.take(len(gathers))
    norm_in = refs.take() if normed or hidden else None
    row_refs = refs.take(len(weights))
    full_refs = refs.take(len(gathers))
    norm_out = refs.take() if normed else None
    loads = []
    for w_ref in w_refs:
        stage, sem = refs.take(2)
        load = pltpu.make_async_copy(w_ref, stage, sem)
        load.start()
        loads.append((stage, load))
    greet_all()
    if normed:
        parts, *sems = refs.take(3)
        norm_swap = Spread("dp", norm_in, parts, *sems)
        norm_swap.start()
    lines = []
    for in_ref, full_ref in zip(in_refs, full_refs):
        rows = in_ref.shape[0]
        step = rows // SUBS if rows >= 16 * SUBS else rows
        lines.append(Blocks(Line(n_z, rows, step), full_ref, *refs.take(2)))
    swaps = []
    for (stage, load), (places, split, _) in zip(loads, weights):
        source, target, *sems = refs.take(4)
        swap = Swap("dp", source, target, *sems)
        load.wait()
        chunk = source.shape[2]
        for jump in range(n_dp):
            peer = lax.rem(swap.me + jump, n_dp)
            into = source if jump else target
            for slot in range(source.shape[1]):
                here = pl.ds(pl.multiple_of(peer * chunk, chunk), chunk)
                piece = stage[here, slot * BLK : (slot + 1) * BLK]
                into[peer, slot] = piece.astype(bf16)
            if jump:
                swap.copy(jump).start()
        swaps.append(swap)
    work = refs.take()
    for index, (in_ref, full_ref, blocks) in enumerate(zip(in_refs, full_refs, lines)):
        line = blocks.line
        if hidden and index == 0:
            for sub in range(line.rows // line.step):
                here = line.part(sub)
                values, _ = normalize(in_ref[here].astype(f32))
                work[...] = values * norm_in[0:1] + norm_in[1:2]
                store_shuffled(work, full_ref, line, here, order)
                blocks.start(sub)
        elif in_ref.dtype == bf16 and gathers[index]:
            work2 = refs.take()
            work2[...] = in_ref[...].astype(f32)
            store_shuffled(work2, full_ref, line, line.part(0), order)
            blocks.start(0)
        else:
            for sub in range(line.rows // line.step):
                here = line.part(sub)
                full_ref[line.at, here] = in_ref[here]
                blocks.start(sub)
    if normed:
        parts[norm_swap.me] = norm_in[...]
        norm_swap.wait()
        share = norm_in.shape[1]
        for index in range(n_dp):
            norm_out[:, index * share : (index + 1) * share] = parts[index]
    shares = []
    for swap, row_ref, (places, split, first) in zip(swaps, row_refs, weights):
        swap.wait()
        if split:
            cut, *sems = refs.take(3)
            share = Swap("fsdp", cut, row_ref, *sems)
            shares.append(share)
        else:
            cut = row_ref
        for block, (part, column) in enumerate(places):
            owner, slot = slots_ref[0, first + block], slots_ref[1, first + block]
            cut[part, :, column * BLK : (column + 1) * BLK] = swap.target[owner, slot]
        if split:
            share.start()
            share.keep()
    for blocks in lines:
        for sub in range(blocks.line.rows // blocks.line.step):
            blocks.forward_all(sub)
    for share in shares:
        share.wait()
    for one in [*swaps, *shares, *lines]:
        one.finish()
    if normed:
        norm_swap.finish()


class Spread(Swap):
    def copy(self, jump, arrival=False):
        peer = lax.rem(self.me + jump, self.n)
        slot = peer if arrival else self.me
        return pltpu.make_async_remote_copy(
            src_ref=self.source,
            dst_ref=self.target.at[slot],
            send_sem=self.send.at[jump],
            recv_sem=self.recv.at[slot],
            device_id={self.axis: peer},
            device_id_type=MESH,
        )


def store_shuffled(work, full_ref, line, here, order):
    rows, width = work.shape
    folds = width // order.width
    pieces = len(order.pieces)
    orders = [fold * pieces + piece for fold in range(folds) for piece in order.pieces]

    def load(group):
        return work[:, group * BLK : (group + 1) * BLK]

    def store(group, value):
        full_ref[line.at, here, group * BLK : (group + 1) * BLK] = value.astype(bf16)

    reorder(load, store, rows, width, orders)


def leave_kernel(weights, summed, *refs):
    refs = Refs(refs)
    n_dp = lax.axis_size("dp")
    slots_ref = refs.take()
    row_refs = refs.take(len(weights))
    term_ref = refs.take() if summed else None
    out_refs = refs.take(len(weights))
    sum_ref = refs.take() if summed else None
    greet_all()
    if summed:
        cut, parts, send, recv, total, others, send2, recv2 = refs.take(8)
        share = cut.shape[2]
        for index in range(n_dp):
            cut[index] = term_ref[:, index * share : (index + 1) * share]
        term_swap = Swap("dp", cut, parts, send, recv)
        term_swap.start()
        term_swap.keep()
    shares = []
    for row_ref, (split, _, _) in zip(row_refs, weights):
        if split:
            held, *sems = refs.take(3)
            share = Swap("fsdp", row_ref, held, *sems)
            share.start()
            share.keep()
            shares.append(share)
        else:
            shares.append(None)
    if summed:
        term_swap.wait()
        total[...] = jnp.sum(parts[...], axis=0)
        total_spread = Spread("fsdp", total, others, send2, recv2)
        total_spread.start()
        others[total_spread.me] = total[...]
    swaps = []
    for row_ref, out_ref, share, (split, capacity, first) in zip(
        row_refs, out_refs, shares, weights
    ):
        if split:
            share.wait()
        rows = share.target if split else row_ref
        cut, *sems, blocks = refs.take(4)
        columns = rows.shape[2] // BLK
        for part in range(rows.shape[0]):
            for column in range(columns):
                blocks[part * columns + column] = rows[part, :, column * BLK : (column + 1) * BLK]
        swap = Swap("dp", cut, out_ref, *sems)
        for owner in range(n_dp):

            for position in range(capacity):
                slot = first + owner * capacity + position
                value = blocks[slots_ref[0, slot]].astype(f32)
                live = slots_ref[1, slot].astype(f32)
                cut[owner, :, position * BLK : (position + 1) * BLK] = (value * live).astype(bf16)
        swap.start()
        swap.keep()
        swaps.append(swap)
    if summed:
        total_spread.wait()
        sum_ref[...] = jnp.sum(others[...], axis=0)
    for swap in swaps:
        swap.wait()
    for one in [*swaps, *shares]:
        if one is not None:
            one.finish()
    if summed:
        term_swap.finish()
        total_spread.finish()


def fetch_columns(source, index, target, sem):
    columns = target.shape[1]
    return pltpu.make_async_copy(source.at[:, pl.ds(index * columns, columns)], target, sem)


def forward_kernel(n, order, half, wide, att_ref, outs_hbm, base_ref, norm_ref, *rest):
    if wide:
        next_hbm, middle_ref, full_ref, result_ref = rest[:4]
        *rest, next_ref, next_sem = rest[4:]
    else:
        middle_ref, full_ref = rest[:2]
        rest = rest[2:]
    part, held, work, s_send, s_recv, b_send, b_recv, outs_ref, outs_sem = rest
    rows, width = base_ref.shape
    step = rows // SUBS
    load_outs = fetch_columns(outs_hbm, half, outs_ref, outs_sem)
    load_outs.start()
    if wide:
        load_next = fetch_columns(next_hbm, 3, next_ref, next_sem)
        load_next.start()
    line = Line(n, rows, step)
    line.greet()
    load_outs.wait()
    sums = Sums(line, part, held, s_send, s_recv)
    blocks = Blocks(line, full_ref, b_send, b_recv)

    def multiply(columns):
        product = dot(att_ref[...], outs_ref[:, columns]).astype(bf16)
        part[:, :, columns] = product.reshape(n, rows, -1)

    by_tiles(width, 256, multiply)

    def settle(sub):
        here = line.part(sub)
        sums.total(sub, work)
        middle = base_ref[here].astype(f32) + work[...]
        middle_ref[here] = middle
        normed, _ = normalize(middle)
        work[...] = normed * norm_ref[0:1] + norm_ref[1:2]

        def load(group):
            return work[:, group * BLK : (group + 1) * BLK]

        def store(group, value):
            full_ref[line.at, here, group * BLK : (group + 1) * BLK] = value.astype(bf16)

        reorder(load, store, step, width, order)
        blocks.start(sub)

    relay(n, [sums], blocks, settle)
    if wide:
        load_next.wait()

        def multiply_next(columns):
            whole = full_ref[...].reshape(n * rows, width)
            result_ref[:, columns] = dot(whole, next_ref[:, columns]).astype(bf16)

        by_tiles(result_ref.shape[1], 256, multiply_next)


def carry_back(work, plain, order, step, width, middle, base, gain, term_ref, first):
    def load(group):
        return work[:, group * BLK : (group + 1) * BLK]

    def store(group, value):
        plain[:, group * BLK : (group + 1) * BLK] = value

    reorder(load, store, step, width, order)
    back_hidden = plain[...]
    normed, inverse = normalize(middle)
    gain_term = jnp.sum(back_hidden * normed, axis=0, keepdims=True)
    bias_term = jnp.sum(back_hidden, axis=0, keepdims=True)
    if first:
        term_ref[...] = jnp.zeros_like(term_ref)
        term_ref[0:1] = gain_term
        term_ref[1:2] = bias_term
    else:
        term_ref[0:1] += gain_term
        term_ref[1:2] += bias_term
    return base + norm_back(back_hidden, normed, inverse, gain)


def back_kernel(
    n, order, column, half, dy_ref, w_hbm, base_ref, middle_ref, norm_ref, outs_hbm, *rest
):
    carry_ref, full_ref, att_ref, term_ref = rest[:4]
    part, held, work, plain, s_send, s_recv, b_send, b_recv = rest[4:12]
    w_ref, w_sem, outs_ref, outs_sem = rest[12:]
    rows, width = base_ref.shape
    step = rows // SUBS
    load_w = fetch_columns(w_hbm, column, w_ref, w_sem)
    load_w.start()
    load_outs = fetch_columns(outs_hbm, half, outs_ref, outs_sem)
    load_outs.start()
    line = Line(n, rows, step)
    line.greet()
    load_w.wait()
    sums = Sums(line, part, held, s_send, s_recv)
    blocks = Blocks(line, full_ref, b_send, b_recv)

    def multiply(columns):
        product = dot_nt(dy_ref[...], w_ref[columns]).astype(bf16)
        part[:, :, columns] = product.reshape(n, rows, -1)

    by_tiles(width, 256, multiply)

    def settle(sub):
        here = line.part(sub)
        sums.total(sub, work)
        carry = carry_back(
            work,
            plain,
            order,
            step,
            width,
            middle_ref[here].astype(f32),
            base_ref[here].astype(f32),
            norm_ref[0:1],
            term_ref,
            sub == 0,
        )
        carry_ref[here] = carry
        full_ref[line.at, here] = carry.astype(bf16)
        blocks.start(sub)

    relay(n, [sums], blocks, settle)
    load_outs.wait()

    def multiply_next(columns):
        whole = full_ref[...].reshape(n * rows, width)
        att_ref[:, columns] = dot_nt(whole, outs_ref[columns]).astype(bf16)

    by_tiles(att_ref.shape[1], 256, multiply_next)


def last_kernel(n, order, dy_ref, w_hbm, base_ref, tokens, norm_ref, branch, middle, *rest):
    grad_ref, result_ref, term_ref = rest[:3]
    part, held, held2, work, plain, s_send, s_recv, r_send, r_recv, w_ref, w_sem = rest[3:]
    rows, width = base_ref.shape
    step = rows // SUBS
    load_w = fetch_columns(w_hbm, 0, w_ref, w_sem)
    load_w.start()
    line = Line(n, rows, step)
    line.greet()
    load_w.wait()
    sums = Sums(line, part, held, s_send, s_recv)
    results = Sums(line, branch, held2, r_send, r_recv)

    def multiply(columns):
        product = dot_nt(dy_ref[...], w_ref[columns]).astype(bf16)
        part[:, :, columns] = product.reshape(n, rows, -1)

    by_tiles(width, 256, multiply)

    def settle(sub):
        here = line.part(sub)
        sums.total(sub, work)
        carry = carry_back(
            work,
            plain,
            order,
            step,
            width,
            tokens[here].astype(f32),
            base_ref[here],
            norm_ref[0:1],
            term_ref,
            sub == 0,
        )
        grad_ref[here] = carry.astype(bf16)
        results.total(sub, work)
        result_ref[here] = (middle[here] + work[...]).astype(bf16)

    relay(n, [sums, results], None, settle)


VMEM_CAP = 52 * 1024 * 1024


def in_place():
    return pl.BlockSpec(memory_space=pl.ANY)


def whole_vmem():
    return pl.BlockSpec(memory_space=pltpu.VMEM)


def sem_pair(n, subs):
    return [pltpu.SemaphoreType.DMA((2, n, subs)), pltpu.SemaphoreType.DMA((2, n, subs))]


def line_call(kernel, name, ident, outs, specs, scratch, flops, moved):
    return pl.pallas_call(
        kernel,
        name=name,
        out_shape=outs,
        in_specs=specs,
        out_specs=jax.tree.map(lambda _: whole_vmem(), outs),
        scratch_shapes=scratch,
        compiler_params=pltpu.CompilerParams(
            collective_id=ident, has_side_effects=True, vmem_limit_bytes=VMEM_CAP
        ),
        cost_estimate=pl.CostEstimate(flops=flops, bytes_accessed=moved, transcendentals=0),
    )


def shape(dims, kind):
    return jax.ShapeDtypeStruct(dims, kind)


LINK_COST = 120_000_000


class Order:
    def __init__(self, pieces, width):
        self.pieces, self.width = pieces, width


def swap_sems(n):
    return [pltpu.SemaphoreType.DMA((n,)), pltpu.SemaphoreType.DMA((n,))]


def enter_call(name, ident, slots, weights, gathers, norms, normed, hidden, n, n_dp, width):
    chunk = weights[0][0].shape[0] // n_dp
    outs, scratch = [], []
    for array, places, split, _ in weights:
        parts = n if split else 1
        outs.append(shape((parts, chunk, len(places) // parts * BLK), bf16))
        scratch += [pltpu.VMEM(array.shape, f32), pltpu.SemaphoreType.DMA]
    if normed:
        scratch += [pltpu.VMEM((n_dp, *norms.shape), f32), *swap_sems(n_dp)]
    for array, _ in gathers:
        rows = array.shape[0]
        outs.append(shape((n, *array.shape), array.dtype))
        scratch += sem_pair(n, SUBS if rows >= 16 * SUBS else 1)
    if normed:
        outs.append(shape((norms.shape[0], n_dp * norms.shape[1]), f32))
    for array, _, _, _ in weights:
        slots_shape = (n_dp, array.shape[1] // BLK, chunk, BLK)
        scratch += [pltpu.VMEM(slots_shape, bf16)] * 2 + swap_sems(n_dp)
    rows = gathers[0][0].shape[0]
    scratch.append(pltpu.VMEM((rows // SUBS if hidden else 8, width), f32))
    for array, moved in gathers[1 if hidden else 0 :]:
        if moved:
            scratch.append(pltpu.VMEM(array.shape, f32))
    for index, (_, places, split, _) in enumerate(weights):
        if split:
            scratch += [pltpu.VMEM(outs[index].shape, bf16), *swap_sems(n)]
    args = [slots, *(weight[0] for weight in weights), *(gather[0] for gather in gathers)]
    specs = [pl.BlockSpec(memory_space=pltpu.SMEM)] + [in_place()] * len(weights)
    specs += [whole_vmem()] * len(gathers)
    if normed or hidden:
        args.append(norms)
        specs.append(whole_vmem())
    kernel = functools.partial(
        enter_kernel,
        [weight[1:] for weight in weights],
        [gather[1] for gather in gathers],
        Order(shuffle_order(n, n_dp), width),
        normed,
        hidden,
    )
    return line_call(kernel, name, ident, outs, specs, scratch, 0, LINK_COST)(*args)


def leave_call(name, ident, slots, weights, term, n, n_dp):
    outs, scratch = [], []
    specs = [pl.BlockSpec(memory_space=pltpu.SMEM)] + [whole_vmem()] * len(weights)
    args = [slots, *(weight[0] for weight in weights)]
    chunk = weights[0][0].shape[1]
    if term is not None:
        args.append(term)
        specs.append(whole_vmem())
        block = (term.shape[0], term.shape[1] // n_dp)
        scratch += [pltpu.VMEM((n_dp, *block), f32)] * 2 + swap_sems(n_dp)
        scratch += [pltpu.VMEM(block, f32), pltpu.VMEM((n, *block), f32), *swap_sems(n)]
    for rows, split, _, _ in weights:
        if split:
            scratch += [pltpu.VMEM(rows.shape, bf16), *swap_sems(n)]
    for rows, _, capacity, _ in weights:
        slots_shape = (n_dp, chunk, capacity * BLK)
        outs.append(shape(slots_shape, bf16))
        scratch += [pltpu.VMEM(slots_shape, bf16), *swap_sems(n_dp)]
        blocks = rows.shape[0] * rows.shape[2] // BLK
        scratch.append(pltpu.VMEM((blocks, chunk, BLK), bf16))
    if term is not None:
        outs.append(shape(block, f32))
    kernel = functools.partial(
        leave_kernel, [weight[1:] for weight in weights], term is not None
    )
    return line_call(kernel, name, ident, outs, specs, scratch, 0, LINK_COST)(*args)


def forward_call(attended, outs_z, half, base, norm_rows, after, n, n_dp, ident):
    rows, width = base.shape
    share = outs_z.shape[0]
    outs = [shape((rows, width), f32), shape((n, rows, width), bf16)]
    specs = [whole_vmem(), in_place(), whole_vmem(), whole_vmem()]
    args = [attended, outs_z, base, norm_rows]
    scratch = [
        pltpu.VMEM((n, rows, width), bf16),
        pltpu.VMEM((2, n, rows, width), bf16),
        pltpu.VMEM((rows // SUBS, width), f32),
        *sem_pair(n, SUBS),
        *sem_pair(n, SUBS),
        pltpu.VMEM((share, width), bf16),
        pltpu.SemaphoreType.DMA,
    ]
    if after is not None:
        outs.append(shape((n * rows, share), bf16))
        specs.append(in_place())
        args.append(after)
        scratch += [pltpu.VMEM((width, share), bf16), pltpu.SemaphoreType.DMA]
    kernel = functools.partial(forward_kernel, n, shuffle_order(n, n_dp), half, after is not None)
    call = line_call(kernel, f"forward{half}", ident, outs, specs, scratch, 0, LINK_COST)
    return call(*args)


def back_call(dy, weight, column, base, middle, norm_rows, outs_z, half, n, n_dp, ident):
    rows, width = base.shape
    share = outs_z.shape[0]
    outs = [
        shape((rows, width), f32),
        shape((n, rows, width), bf16),
        shape((n * rows, share), bf16),
        shape((8, width), f32),
    ]
    specs = [
        whole_vmem(),
        in_place(),
        whole_vmem(),
        whole_vmem(),
        whole_vmem(),
        in_place(),
    ]
    scratch = [
        pltpu.VMEM((n, rows, width), bf16),
        pltpu.VMEM((2, n, rows, width), bf16),
        pltpu.VMEM((rows // SUBS, width), f32),
        pltpu.VMEM((rows // SUBS, width), f32),
        *sem_pair(n, SUBS),
        *sem_pair(n, SUBS),
        pltpu.VMEM((width, dy.shape[1]), bf16),
        pltpu.SemaphoreType.DMA,
        pltpu.VMEM((share, width), bf16),
        pltpu.SemaphoreType.DMA,
    ]
    kernel = functools.partial(back_kernel, n, unshuffle_order(n, n_dp), column, half)
    call = line_call(kernel, f"back{half}", ident, outs, specs, scratch, 0, LINK_COST)
    return call(dy, weight, base, middle, norm_rows, outs_z)


def last_call(dy, weight, base, tokens, norm_rows, branch, middle, n, n_dp, ident):
    rows, width = base.shape
    outs = [
        shape((rows, width), bf16),
        shape((rows, width), bf16),
        shape((8, width), f32),
    ]
    specs = [whole_vmem(), in_place()] + [whole_vmem()] * 5
    scratch = [
        pltpu.VMEM((n, rows, width), bf16),
        pltpu.VMEM((2, n, rows, width), bf16),
        pltpu.VMEM((2, n, rows, width), bf16),
        pltpu.VMEM((rows // SUBS, width), f32),
        pltpu.VMEM((rows // SUBS, width), f32),
        *sem_pair(n, SUBS),
        *sem_pair(n, SUBS),
        pltpu.VMEM((width, dy.shape[1]), bf16),
        pltpu.SemaphoreType.DMA,
    ]
    kernel = functools.partial(last_kernel, n, unshuffle_order(n, n_dp))
    call = line_call(kernel, "last", ident, outs, specs, scratch, 0, LINK_COST)
    return call(dy, weight, base, tokens, norm_rows, branch, middle)


def attend_forward(queries, keys, values, allowed):
    packed = allowed.shape[0]
    heads = queries.shape[1] // HEAD
    query_heads = queries.reshape(packed, -1, heads, HEAD)
    key_heads = keys.reshape(packed, -1, heads, HEAD)
    value_heads = values.reshape(packed, -1, heads, HEAD)
    scores = jnp.einsum(
        "pqhd,pkhd->phqk", query_heads, key_heads, preferred_element_type=f32
    ) * HEAD ** (-0.5)
    scores = jnp.where(allowed[:, None], scores, score_floor)
    powers = jnp.exp(scores - jnp.max(scores, axis=-1, keepdims=True))
    shares = powers / jnp.sum(powers, axis=-1, keepdims=True)
    attended = jnp.einsum(
        "phqk,pkhd->pqhd", shares.astype(bf16), value_heads, preferred_element_type=f32
    )
    return attended.reshape(queries.shape).astype(bf16), shares


def attend_backward(queries, keys, values, shares, back_attended):
    packed = shares.shape[0]
    heads = queries.shape[1] // HEAD
    query_heads = queries.reshape(packed, -1, heads, HEAD)
    key_heads = keys.reshape(packed, -1, heads, HEAD)
    value_heads = values.reshape(packed, -1, heads, HEAD)
    back_heads = back_attended.reshape(packed, -1, heads, HEAD)
    score_scale = HEAD ** (-0.5)
    back_shares = jnp.einsum(
        "pqhd,pkhd->phqk", back_heads, value_heads, preferred_element_type=f32
    )
    inner_sum = jnp.sum(shares * back_shares, axis=-1, keepdims=True)
    back_scores = (shares * (back_shares - inner_sum)).astype(bf16)
    query_grad = (
        jnp.einsum("phqk,pkhd->pqhd", back_scores, key_heads, preferred_element_type=f32)
        * score_scale
    )
    key_grad = (
        jnp.einsum("phqk,pqhd->pkhd", back_scores, query_heads, preferred_element_type=f32)
        * score_scale
    )
    value_grad = jnp.einsum(
        "phqk,pqhd->pkhd", shares.astype(bf16), back_heads, preferred_element_type=f32
    )
    return (
        query_grad.reshape(queries.shape).astype(bf16),
        key_grad.reshape(keys.shape).astype(bf16),
        value_grad.reshape(values.shape).astype(bf16),
    )


def block_slots(owners):
    owner = jnp.concatenate(owners)
    weight = jnp.concatenate([jnp.full(one.shape, at, jnp.int32) for at, one in enumerate(owners)])
    mark = owner + weight * 1024
    count = mark.shape[0]
    earlier = lax.broadcasted_iota(jnp.int32, (count, count), 1) < lax.broadcasted_iota(
        jnp.int32, (count, count), 0
    )
    same = jnp.logical_and(mark[:, None] == mark[None, :], earlier)
    return jnp.stack([owner, jnp.sum(same.astype(jnp.int32), axis=1)])


def slot_contents(owners, slots, places, capacities, firsts, n_dp):
    rows = []
    for owner, place, capacity, first in zip(owners, places, capacities, firsts):
        count = owner.shape[0]
        at = owner * capacity + slots[1, first : first + count]
        hit = at[None, :] == lax.broadcasted_iota(jnp.int32, (n_dp * capacity, count), 0)
        block = lax.broadcasted_iota(jnp.int32, (n_dp * capacity, count), 1)
        per_group, per_part, split = place_rule(place)
        part = block % per_group // per_part if split else block * 0
        column = block // per_group * per_part + block % per_part if split else block
        index = part * (count // (per_group // per_part)) + column if split else column
        rows.append(
            jnp.stack([jnp.sum(jnp.where(hit, value, 0), axis=1) for value in (index, block * 0 + 1)])
        )
    return jnp.concatenate(rows, axis=1)


def place_rule(place):
    parts = 1 + max(part for part, _ in place)
    if parts == 1:
        return 0, 0, False
    per_part = sum(1 for part, _ in place[:HEADS] if part == 0)
    return per_part * parts, per_part, True


def after(small, first):
    return lax.optimization_barrier((small, first))[0]


def body(
    tokens_in,
    text_in,
    seg_ids,
    capt_ids,
    grad_out,
    owner_query,
    owner_up,
    owner_outs,
    owner_text,
    owner_down,
    w_query,
    m_query,
    v_query,
    w_up,
    m_up,
    v_up,
    w_outs,
    m_outs,
    v_outs,
    w_text,
    m_text,
    v_text,
    w_down,
    m_down,
    v_down,
    norm_weight,
    m_norm,
    v_norm,
):
    n_dp = lax.axis_size("dp")
    n_z = lax.axis_size("fsdp")
    width = tokens_in.shape[1]
    own_rows = w_query.shape[0]
    chunk = own_rows // n_dp
    cap_big = w_query.shape[1] // BLK
    cap_out = w_outs.shape[1] // BLK
    heads_z = HEADS // n_z
    share = width // n_z
    owner_query, owner_up, owner_outs, owner_text, owner_down = (
        owner[:, 0] for owner in (owner_query, owner_up, owner_outs, owner_text, owner_down)
    )
    split_places = [split_place(b, heads_z, n_z) for b in range(owner_query.shape[0])]
    big_places = [flat_place(b) for b in range(owner_down.shape[0])]
    out_places = [flat_place(b) for b in range(owner_outs.shape[0])]
    owners = (owner_query, owner_outs, owner_text, owner_up, owner_down)
    places = (split_places, out_places, split_places, split_places, big_places)
    capacities = (cap_big, cap_out, cap_big, cap_big, cap_big)
    firsts = [sum(len(one) for one in places[:index]) for index in range(5)]
    slot_firsts = [sum(capacities[:index]) * n_dp for index in range(5)]
    slots = block_slots(owners)
    contents = slot_contents(owners, slots, places, capacities, firsts, n_dp)

    def spread(rows):
        return lax.all_gather(rows.reshape(-1, rows.shape[-1]), "dp", axis=0, tiled=True)

    def gather_sum(piece, parts):
        summed = lax.psum_scatter(piece, "dp", scatter_dimension=0, tiled=True)
        return summed.reshape(parts, chunk, -1)

    token_count = tokens_in.shape[0]
    marks = jnp.concatenate([seg_ids, capt_ids], axis=1)
    marks = jnp.pad(marks, ((0, 7), (0, 256 - marks.shape[1])))
    norms = jnp.pad(norm_weight, ((0, 2), (0, 0)))
    query_rows, marks, norm_full = enter_call(
        "enter_query",
        0,
        slots,
        [(w_query, split_places, True, firsts[0])],
        [(marks, False)],
        norms,
        True,
        False,
        n_z,
        n_dp,
        width,
    )
    outs_rows, text_rows, hidden1, text_all = enter_call(
        "enter_text",
        6,
        slots,
        [(w_outs, out_places, False, firsts[1]), (w_text, split_places, True, firsts[2])],
        [(tokens_in, True), (text_in, True)],
        norm_full[0:2],
        False,
        True,
        n_z,
        n_dp,
        width,
    )
    query_z, outs_z, text_z = spread(query_rows), spread(outs_rows), spread(text_rows)
    hidden1 = hidden1.reshape(-1, width)
    text_all = text_all.reshape(-1, text_in.shape[1])
    segment = marks[:, 0, :token_count]
    caption = marks[:, 0, token_count : token_count + capt_ids.shape[1]]
    self_mask = segment[:, :, None] == segment[:, None, :]
    cross_mask = segment[:, :, None] == caption[:, None, :]

    projected = dot(hidden1, query_z[:, : 3 * share]).astype(bf16)
    self_query = projected[:, :share]
    self_key = projected[:, share : 2 * share]
    self_value = projected[:, 2 * share :]
    attended1, shares1 = attend_forward(self_query, self_key, self_value, self_mask)
    up_rows, down_rows, grad_all = enter_call(
        "enter_up",
        7,
        after(slots, attended1),
        [(w_up, split_places, True, firsts[3]), (w_down, big_places, False, firsts[4])],
        [(grad_out, False)],
        None,
        False,
        False,
        n_z,
        n_dp,
        width,
    )
    grad_all = grad_all.reshape(-1, width)
    up_z, down_z = spread(up_rows), spread(down_rows)
    middle1, hidden2, cross_query = forward_call(
        attended1, outs_z, 0, tokens_in, after(norm_full[2:4], up_rows), query_z, n_z, n_dp, 1
    )
    hidden2 = hidden2.reshape(-1, width)
    text_pairs = (
        dot(text_all[:, :width], text_z[:, : 2 * share])
        + dot(text_all[:, width:], text_z[:, 2 * share :])
    ).astype(bf16)
    text_key = text_pairs[:, :share]
    text_value = text_pairs[:, share:]
    attended2, shares2 = attend_forward(cross_query, text_key, text_value, cross_mask)
    middle2, hidden3 = forward_call(
        attended2, outs_z, 1, middle1, norm_full[4:6], None, n_z, n_dp, 2
    )
    hidden3 = hidden3.reshape(-1, width)
    up_values = dot(hidden3, up_z)
    gelu_values, gelu_pull = jax.vjp(exact_gelu, up_values)
    activated = gelu_values.astype(bf16)
    branch3 = sum(
        dot(activated[:, f * share : (f + 1) * share], down_z[:, f * width : (f + 1) * width])
        for f in range(4)
    )
    branch3 = branch3.astype(bf16).reshape(n_z, token_count, width)

    down_part = jnp.concatenate(
        [dot_tn(activated[:, f * share : (f + 1) * share], grad_all).astype(bf16) for f in range(4)],
        axis=1,
    )
    down_sum = gather_sum(down_part, 1)
    back_act = jnp.concatenate(
        [dot_nt(grad_all, down_z[:, f * width : (f + 1) * width]) for f in range(4)], axis=1
    )
    back_up = gelu_pull(back_act)[0].astype(bf16)
    up_part = dot_tn(hidden3, back_up).astype(bf16)
    up_sum = gather_sum(up_part, n_z)
    at_middle2, carry2, back_att2, term3 = back_call(
        back_up, up_z, 0, grad_out, middle2, norm_full[4:6], outs_z, 1, n_z, n_dp, 3
    )
    carry2 = carry2.reshape(-1, width)
    outs_part2 = dot_tn(attended2, carry2).astype(bf16)
    back_cross, text_kgrad, text_vgrad = attend_backward(
        cross_query, text_key, text_value, shares2, back_att2
    )
    back_pairs = jnp.concatenate([text_kgrad, text_vgrad], axis=1)
    text_part = jnp.concatenate(
        [dot_tn(text_all[:, f * width : (f + 1) * width], back_pairs).astype(bf16) for f in range(2)],
        axis=1,
    )
    text_sum = gather_sum(text_part, n_z)
    query_part2 = dot_tn(hidden2, back_cross).astype(bf16)
    at_middle1, carry1, back_att1, term2 = back_call(
        back_cross, query_z, 3, at_middle2, middle1, norm_full[2:4], outs_z, 0, n_z, n_dp, 4
    )
    carry1 = carry1.reshape(-1, width)
    outs_part1 = dot_tn(attended1, carry1).astype(bf16)
    outs_sum = gather_sum(jnp.concatenate([outs_part1, outs_part2], axis=1), 1)
    back_projected = jnp.concatenate(
        attend_backward(self_query, self_key, self_value, shares1, back_att1), axis=1
    )
    query_part1 = dot_tn(hidden1, back_projected).astype(bf16)
    query_sum = gather_sum(jnp.concatenate([query_part1, query_part2], axis=1), n_z)
    text_grad, up_grad, down_grad = leave_call(
        "leave_up",
        8,
        after(contents, back_projected),
        [
            (text_sum, True, cap_big, slot_firsts[2]),
            (up_sum, True, cap_big, slot_firsts[3]),
            (down_sum, False, cap_big, slot_firsts[4]),
        ],
        None,
        n_z,
        n_dp,
    )
    grad_in, result, term1 = last_call(
        back_projected,
        query_z,
        at_middle1,
        tokens_in,
        after(norm_full[0:2], text_grad),
        branch3,
        middle2,
        n_z,
        n_dp,
        5,
    )
    norm_term = jnp.concatenate([term1[:2], term2[:2], term3[:4]], axis=0)
    query_grad, outs_grad, norm_grad = leave_call(
        "leave_query",
        9,
        contents,
        [
            (query_sum, True, cap_big, slot_firsts[0]),
            (outs_sum, False, cap_out, slot_firsts[1]),
        ],
        norm_term,
        n_z,
        n_dp,
    )
    norm_grad = norm_grad[:6]
    query_grad, outs_grad, text_grad, up_grad, down_grad = (
        grad.reshape(own_rows, -1).astype(f32)
        for grad in (query_grad, outs_grad, text_grad, up_grad, down_grad)
    )
    query_new = adamw_update(w_query, m_query, v_query, query_grad, rate_query, decay_rate)
    up_new = adamw_update(w_up, m_up, v_up, up_grad, rate_up, decay_rate)
    outs_new = adamw_update(w_outs, m_outs, v_outs, outs_grad, rate_outs, decay_rate)
    text_new = adamw_update(w_text, m_text, v_text, text_grad, rate_text, decay_rate)
    down_new = adamw_update(w_down, m_down, v_down, down_grad, rate_down, decay_rate)
    norm_new = adamw_update(norm_weight, m_norm, v_norm, norm_grad, rate_norm, 0.0)
    return (
        result,
        grad_in,
        *query_new,
        *up_new,
        *outs_new,
        *text_new,
        *down_new,
        *norm_new,
    )


def solution(mesh):
    rows = P(("dp", "fsdp"), None)
    slots = P("fsdp", "dp")
    norms = P(None, "dp")
    in_specs = (rows,) * 5 + (P(),) * 5 + (slots,) * 15 + (norms,) * 3
    out_specs = (rows,) * 2 + (slots,) * 15 + (norms,) * 3
    return jax.shard_map(body, mesh=mesh, in_specs=in_specs, out_specs=out_specs, check_vma=False)
```

```python
import functools

import jax
import jax.numpy as jnp
from jax import lax
from jax.experimental import pallas as pl
from jax.experimental.pallas import tpu as pltpu
from jax.sharding import PartitionSpec as P

HEADS = 16
HEAD = 128
STEP = 10
BLK = 128


beta_first = 0.9
beta_second = 0.999
adam_eps = 1e-08
decay_rate = 0.01
rate_query = 0.04
rate_up = 0.04
rate_outs = 0.12
rate_text = 0.03
rate_down = 0.03
rate_norm = 0.5
norm_eps = 1e-05
score_floor = -1e30
bf16 = jnp.bfloat16
f32 = jnp.float32


def normalize(values):
    centered = values - jnp.mean(values, axis=-1, keepdims=True)
    inverse_std = lax.rsqrt(jnp.mean(centered * centered, axis=-1, keepdims=True) + norm_eps)
    return (centered * inverse_std, inverse_std)


def norm_back(back_hidden, normed, inverse_std, gain_row):
    back_normed = back_hidden * gain_row
    return inverse_std * (
        back_normed
        - jnp.mean(back_normed, axis=-1, keepdims=True)
        - normed * jnp.mean(back_normed * normed, axis=-1, keepdims=True)
    )


def adamw_update(weight, first, second, gradient, rate, decay):
    first_new = beta_first * first + (1.0 - beta_first) * gradient
    second_new = beta_second * second + (1.0 - beta_second) * gradient * gradient
    first_hat = first_new / (1.0 - beta_first**STEP)
    second_hat = second_new / (1.0 - beta_second**STEP)
    weight_new = weight - rate * (first_hat / (jnp.sqrt(second_hat) + adam_eps) + decay * weight)
    return (first_new, second_new, weight_new)


def dot(left, right):
    return jnp.dot(left, right, preferred_element_type=f32)


def dot_nt(left, right):
    return lax.dot_general(left, right, (((1,), (1,)), ((), ())), preferred_element_type=f32)


def dot_tn(left, right):
    return lax.dot_general(left, right, (((0,), (0,)), ((), ())), preferred_element_type=f32)


def split_place(block, per_part, parts):
    group, rest = divmod(block, per_part * parts)
    part, inner = divmod(rest, per_part)
    return part, group * per_part + inner


def flat_place(block):
    return 0, block


MESH = pl.DeviceIdType.MESH


SUBS = 4


class Line:
    def __init__(self, n, rows, step):
        self.n, self.rows, self.step = n, rows, step
        self.at = lax.axis_index("fsdp")

    def has(self, way):
        return self.at < self.n - 1 if way == 0 else self.at > 0

    def peer(self, way):
        index = jnp.clip(self.at + (1 if way == 0 else -1), 0, self.n - 1)
        return {"fsdp": index}

    def greet(self, others=0):
        barrier = pltpu.get_barrier_semaphore()
        for way in (0, 1):

            @pl.when(self.has(way))
            def _():
                pl.semaphore_signal(
                    barrier, inc=1, device_id=self.peer(way), device_id_type=pl.DeviceIdType.MESH
                )

        pl.semaphore_wait(
            barrier, others + self.has(0).astype(jnp.int32) + self.has(1).astype(jnp.int32)
        )

    def copy(self, source, target, send, recv, way):
        return pltpu.make_async_remote_copy(
            src_ref=source,
            dst_ref=target,
            send_sem=send,
            recv_sem=recv,
            device_id=self.peer(way),
            device_id_type=pl.DeviceIdType.MESH,
        )

    def part(self, sub):
        return pl.ds(sub * self.step, self.step)


class Sums:
    def __init__(self, line, part, held, send, recv):
        self.line, self.part, self.held, self.send, self.recv = line, part, held, send, recv

    def move(self, way, target, sub, source):
        line = self.line
        rows = line.part(sub)
        return line.copy(
            source,
            self.held.at[way, target, rows],
            self.send.at[way, target, sub],
            self.recv.at[way, target, sub],
            way,
        )

    def target(self, way, time):
        n, at = self.line.n, self.line.at
        return n - 1 - (time - at) if way == 0 else time - (n - 1 - at)

    def passes(self, way, target):
        n, at = self.line.n, self.line.at
        if way == 0:
            return jnp.logical_and(target > at, target < n)
        return jnp.logical_and(target < at, target >= 0)

    def forward(self, sub, time):
        line = self.line
        rows = line.part(sub)
        for way in (0, 1):
            target = self.target(way, time)
            passes = self.passes(way, target)
            inner = jnp.logical_and(passes, line.has(1 - way))
            outer = jnp.logical_and(passes, jnp.logical_not(line.has(1 - way)))

            @pl.when(outer)
            def _():
                self.move(way, target, sub, self.part.at[target, rows]).start()

            @pl.when(inner)
            def _():
                held = self.held.at[way, target, rows]
                self.move(way, target, sub, held).wait_recv()
                total = held[...].astype(f32) + self.part[target, rows].astype(f32)
                held[...] = total.astype(bf16)
                self.move(way, target, sub, held).start()

    def total(self, sub, sum_ref):
        line = self.line
        rows = line.part(sub)
        sum_ref[...] = self.part[line.at, rows].astype(f32)
        for way in (0, 1):

            @pl.when(line.has(1 - way))
            def _():
                held = self.held.at[way, line.at, rows]
                self.move(way, line.at, sub, held).wait_recv()
                sum_ref[...] += held[...].astype(f32)

    def finish(self):
        line = self.line
        for way in (0, 1):
            for time in range(line.n - 1):
                target = self.target(way, time)

                @pl.when(self.passes(way, target))
                def _():
                    for sub in range(line.rows // line.step):
                        held = self.held.at[way, target, line.part(sub)]
                        self.move(way, target, sub, held).wait_send()


def relay(n, sums, blocks, settle):
    for slot in range((SUBS + 2) * (n - 1)):
        sub, time = divmod(slot, n - 1)
        if sub < SUBS:
            for one in sums:
                one.forward(sub, time)
        if time == 0 and 0 <= sub - 1 < SUBS:
            settle(sub - 1)
        if blocks is not None:
            if time == n - 2 and 0 <= sub - 1 < SUBS:
                blocks.forward(sub - 1, 1)
            if time < n - 2 and 0 <= sub - 2 < SUBS:
                blocks.forward(sub - 2, time + 2)
    for one in sums:
        one.finish()
    if blocks is not None:
        blocks.finish()


class Blocks:
    def __init__(self, line, full, send, recv):
        self.line, self.full, self.send, self.recv = line, full, send, recv

    def move(self, way, source, sub):
        line = self.line
        held = self.full.at[source, line.part(sub)]
        return line.copy(
            held, held, self.send.at[way, source, sub], self.recv.at[way, source, sub], way
        )

    def behind(self, way, source):
        return self.line.at > source if way == 0 else self.line.at < source

    def start(self, sub):
        for way in (0, 1):

            @pl.when(self.line.has(way))
            def _():
                self.move(way, self.line.at, sub).start()

    def forward(self, sub, step):
        line = self.line
        for way in (0, 1):
            source = line.at - step if way == 0 else line.at + step

            @pl.when(jnp.logical_and(source >= 0, source < line.n))
            def _():
                self.move(way, source, sub).wait_recv()

                @pl.when(line.has(way))
                def _():
                    self.move(way, source, sub).start()

    def forward_all(self, sub):
        for step in range(1, self.line.n):
            self.forward(sub, step)

    def finish(self):
        line = self.line
        for way in (0, 1):
            for source in range(line.n):
                ours = jnp.logical_or(self.behind(way, source), line.at == source)

                @pl.when(jnp.logical_and(ours, line.has(way)))
                def _():
                    for sub in range(line.rows // line.step):
                        self.move(way, source, sub).wait_send()


def lane_moves(width, order):
    moves = []
    piece = width // len(order)
    for group in range(width // BLK):
        parts = []
        for offset in range(0, BLK, piece):
            start = order[(group * BLK + offset) // piece] * piece
            parts.append((offset, start // BLK, start % BLK))
        moves.append(parts)
    return piece, moves


def reorder(load, store, rows, width, order):
    piece, moves = lane_moves(width, order)
    lane = lax.broadcasted_iota(jnp.int32, (rows, BLK), 1)
    for group, parts in enumerate(moves):
        value = None
        for offset, source, start in parts:
            block = load(source)
            if start != offset:
                block = pltpu.roll(block, (offset - start) % BLK, 1)
            value = block if value is None else jnp.where(lane >= offset, block, value)
        store(group, value)


def shuffle_order(n_z, n_dp):
    return [z * n_dp + i for i in range(n_dp) for z in range(n_z)]


def unshuffle_order(n_z, n_dp):
    return [i * n_z + z for z in range(n_z) for i in range(n_dp)]


def by_tiles(columns, tile, run):
    def one(index, carry):
        run(pl.ds(pl.multiple_of(index * tile, tile), tile))
        return carry

    lax.fori_loop(0, columns // tile, one, 0)


class Swap:
    def __init__(self, axis, source, target, send, recv):
        self.axis, self.source, self.target = axis, source, target
        self.send, self.recv = send, recv
        self.n = lax.axis_size(axis)
        self.me = lax.axis_index(axis)

    def copy(self, jump, arrival=False):
        peer = lax.rem(self.me + jump, self.n)
        slot = peer if arrival else self.me
        return pltpu.make_async_remote_copy(
            src_ref=self.source.at[peer],
            dst_ref=self.target.at[slot],
            send_sem=self.send.at[jump],
            recv_sem=self.recv.at[slot],
            device_id={self.axis: peer},
            device_id_type=MESH,
        )

    def start(self):
        for jump in range(1, self.n):
            self.copy(jump).start()

    def keep(self):
        self.target[self.me] = self.source[self.me]

    def wait(self):
        for jump in range(1, self.n):
            self.copy(jump, True).wait_recv()

    def finish(self):
        for jump in range(1, self.n):
            self.copy(jump).wait_send()


def greet_all():
    barrier = pltpu.get_barrier_semaphore()
    count = 0
    for axis in ("dp", "fsdp"):
        n, me = lax.axis_size(axis), lax.axis_index(axis)
        count += n - 1
        for jump in range(1, n):
            pl.semaphore_signal(
                barrier, inc=1, device_id={axis: lax.rem(me + jump, n)}, device_id_type=MESH
            )
    pl.semaphore_wait(barrier, count)


class Refs:
    def __init__(self, refs):
        self.refs = list(refs)

    def take(self, count=None):
        taken = self.refs[: 1 if count is None else count]
        self.refs = self.refs[len(taken) :]
        return taken[0] if count is None else taken


def enter_kernel(weights, gathers, order, normed, hidden, *refs):
    refs = Refs(refs)
    n_dp, n_z = lax.axis_size("dp"), lax.axis_size("fsdp")
    slots_ref = refs.take()
    w_refs = refs.take(len(weights))
    in_refs = refs.take(len(gathers))
    norm_in = refs.take() if normed or hidden else None
    row_refs = refs.take(len(weights))
    full_refs = refs.take(len(gathers))
    norm_out = refs.take() if normed else None
    loads = []
    for w_ref in w_refs:
        stage, sem = refs.take(2)
        load = pltpu.make_async_copy(w_ref, stage, sem)
        load.start()
        loads.append((stage, load))
    greet_all()
    if normed:
        parts, *sems = refs.take(3)
        norm_swap = Spread("dp", norm_in, parts, *sems)
        norm_swap.start()
    lines = []
    for in_ref, full_ref in zip(in_refs, full_refs):
        rows = in_ref.shape[0]
        step = rows // SUBS if rows >= 16 * SUBS else rows
        lines.append(Blocks(Line(n_z, rows, step), full_ref, *refs.take(2)))
    swaps = []
    for (stage, load), (places, split, _) in zip(loads, weights):
        source, target, *sems = refs.take(4)
        swap = Swap("dp", source, target, *sems)
        load.wait()
        chunk = source.shape[2]
        for jump in range(n_dp):
            peer = lax.rem(swap.me + jump, n_dp)
            into = source if jump else target
            for slot in range(source.shape[1]):
                here = pl.ds(pl.multiple_of(peer * chunk, chunk), chunk)
                piece = stage[here, slot * BLK : (slot + 1) * BLK]
                into[peer, slot] = piece.astype(bf16)
            if jump:
                swap.copy(jump).start()
        swaps.append(swap)
    work = refs.take()
    for index, (in_ref, full_ref, blocks) in enumerate(zip(in_refs, full_refs, lines)):
        line = blocks.line
        if hidden and index == 0:
            for sub in range(line.rows // line.step):
                here = line.part(sub)
                values, _ = normalize(in_ref[here].astype(f32))
                work[...] = values * norm_in[0:1] + norm_in[1:2]
                store_shuffled(work, full_ref, line, here, order)
                blocks.start(sub)
        elif in_ref.dtype == bf16 and gathers[index]:
            work2 = refs.take()
            work2[...] = in_ref[...].astype(f32)
            store_shuffled(work2, full_ref, line, line.part(0), order)
            blocks.start(0)
        else:
            for sub in range(line.rows // line.step):
                here = line.part(sub)
                full_ref[line.at, here] = in_ref[here]
                blocks.start(sub)
    if normed:
        parts[norm_swap.me] = norm_in[...]
        norm_swap.wait()
        share = norm_in.shape[1]
        for index in range(n_dp):
            norm_out[:, index * share : (index + 1) * share] = parts[index]
    shares = []
    for swap, row_ref, (places, split, first) in zip(swaps, row_refs, weights):
        swap.wait()
        if split:
            cut, *sems = refs.take(3)
            share = Swap("fsdp", cut, row_ref, *sems)
            shares.append(share)
        else:
            cut = row_ref
        for block, (part, column) in enumerate(places):
            owner, slot = slots_ref[0, first + block], slots_ref[1, first + block]
            cut[part, :, column * BLK : (column + 1) * BLK] = swap.target[owner, slot]
        if split:
            share.start()
            share.keep()
    for blocks in lines:
        for sub in range(blocks.line.rows // blocks.line.step):
            blocks.forward_all(sub)
    for share in shares:
        share.wait()
    for one in [*swaps, *shares, *lines]:
        one.finish()
    if normed:
        norm_swap.finish()


class Spread(Swap):
    def copy(self, jump, arrival=False):
        peer = lax.rem(self.me + jump, self.n)
        slot = peer if arrival else self.me
        return pltpu.make_async_remote_copy(
            src_ref=self.source,
            dst_ref=self.target.at[slot],
            send_sem=self.send.at[jump],
            recv_sem=self.recv.at[slot],
            device_id={self.axis: peer},
            device_id_type=MESH,
        )


def store_shuffled(work, full_ref, line, here, order):
    rows, width = work.shape
    folds = width // order.width
    pieces = len(order.pieces)
    orders = [fold * pieces + piece for fold in range(folds) for piece in order.pieces]

    def load(group):
        return work[:, group * BLK : (group + 1) * BLK]

    def store(group, value):
        full_ref[line.at, here, group * BLK : (group + 1) * BLK] = value.astype(bf16)

    reorder(load, store, rows, width, orders)


def leave_kernel(weights, summed, *refs):
    refs = Refs(refs)
    n_dp = lax.axis_size("dp")
    slots_ref = refs.take()
    row_refs = refs.take(len(weights))
    term_ref = refs.take() if summed else None
    out_refs = refs.take(len(weights))
    sum_ref = refs.take() if summed else None
    greet_all()
    if summed:
        cut, parts, send, recv, total, others, send2, recv2 = refs.take(8)
        share = cut.shape[2]
        for index in range(n_dp):
            cut[index] = term_ref[:, index * share : (index + 1) * share]
        term_swap = Swap("dp", cut, parts, send, recv)
        term_swap.start()
        term_swap.keep()
    shares = []
    for row_ref, (split, _, _) in zip(row_refs, weights):
        if split:
            held, *sems = refs.take(3)
            share = Swap("fsdp", row_ref, held, *sems)
            share.start()
            share.keep()
            shares.append(share)
        else:
            shares.append(None)
    if summed:
        term_swap.wait()
        total[...] = jnp.sum(parts[...], axis=0)
        total_spread = Spread("fsdp", total, others, send2, recv2)
        total_spread.start()
        others[total_spread.me] = total[...]
    swaps = []
    for row_ref, out_ref, share, (split, capacity, first) in zip(
        row_refs, out_refs, shares, weights
    ):
        if split:
            share.wait()
        rows = share.target if split else row_ref
        cut, *sems, blocks = refs.take(4)
        columns = rows.shape[2] // BLK
        for part in range(rows.shape[0]):
            for column in range(columns):
                blocks[part * columns + column] = rows[part, :, column * BLK : (column + 1) * BLK]
        swap = Swap("dp", cut, out_ref, *sems)
        for owner in range(n_dp):

            for position in range(capacity):
                slot = first + owner * capacity + position
                value = blocks[slots_ref[0, slot]].astype(f32)
                live = slots_ref[1, slot].astype(f32)
                cut[owner, :, position * BLK : (position + 1) * BLK] = (value * live).astype(bf16)
        swap.start()
        swap.keep()
        swaps.append(swap)
    if summed:
        total_spread.wait()
        sum_ref[...] = jnp.sum(others[...], axis=0)
    for swap in swaps:
        swap.wait()
    for one in [*swaps, *shares]:
        if one is not None:
            one.finish()
    if summed:
        term_swap.finish()
        total_spread.finish()


def fetch_columns(source, index, target, sem):
    columns = target.shape[1]
    return pltpu.make_async_copy(source.at[:, pl.ds(index * columns, columns)], target, sem)


def forward_kernel(n, order, half, wide, att_ref, outs_hbm, base_ref, norm_ref, *rest):
    if wide:
        next_hbm, middle_ref, full_ref, result_ref = rest[:4]
        *rest, next_ref, next_sem = rest[4:]
    else:
        middle_ref, full_ref = rest[:2]
        rest = rest[2:]
    part, held, work, s_send, s_recv, b_send, b_recv, outs_ref, outs_sem = rest
    rows, width = base_ref.shape
    step = rows // SUBS
    load_outs = fetch_columns(outs_hbm, half, outs_ref, outs_sem)
    load_outs.start()
    if wide:
        load_next = fetch_columns(next_hbm, 3, next_ref, next_sem)
        load_next.start()
    line = Line(n, rows, step)
    line.greet()
    load_outs.wait()
    sums = Sums(line, part, held, s_send, s_recv)
    blocks = Blocks(line, full_ref, b_send, b_recv)

    def multiply(columns):
        product = dot(att_ref[...], outs_ref[:, columns]).astype(bf16)
        part[:, :, columns] = product.reshape(n, rows, -1)

    by_tiles(width, 256, multiply)

    def settle(sub):
        here = line.part(sub)
        sums.total(sub, work)
        middle = base_ref[here].astype(f32) + work[...]
        middle_ref[here] = middle
        normed, _ = normalize(middle)
        work[...] = normed * norm_ref[0:1] + norm_ref[1:2]

        def load(group):
            return work[:, group * BLK : (group + 1) * BLK]

        def store(group, value):
            full_ref[line.at, here, group * BLK : (group + 1) * BLK] = value.astype(bf16)

        reorder(load, store, step, width, order)
        blocks.start(sub)

    relay(n, [sums], blocks, settle)
    if wide:
        load_next.wait()

        def multiply_next(columns):
            whole = full_ref[...].reshape(n * rows, width)
            result_ref[:, columns] = dot(whole, next_ref[:, columns]).astype(bf16)

        by_tiles(result_ref.shape[1], 256, multiply_next)


def carry_back(work, plain, order, step, width, middle, base, gain, term_ref, first):
    def load(group):
        return work[:, group * BLK : (group + 1) * BLK]

    def store(group, value):
        plain[:, group * BLK : (group + 1) * BLK] = value

    reorder(load, store, step, width, order)
    back_hidden = plain[...]
    normed, inverse = normalize(middle)
    gain_term = jnp.sum(back_hidden * normed, axis=0, keepdims=True)
    bias_term = jnp.sum(back_hidden, axis=0, keepdims=True)
    if first:
        term_ref[...] = jnp.zeros_like(term_ref)
        term_ref[0:1] = gain_term
        term_ref[1:2] = bias_term
    else:
        term_ref[0:1] += gain_term
        term_ref[1:2] += bias_term
    return base + norm_back(back_hidden, normed, inverse, gain)


def back_kernel(
    n, order, column, half, dy_ref, w_hbm, base_ref, middle_ref, norm_ref, outs_hbm, *rest
):
    carry_ref, full_ref, att_ref, term_ref = rest[:4]
    part, held, work, plain, s_send, s_recv, b_send, b_recv = rest[4:12]
    w_ref, w_sem, outs_ref, outs_sem = rest[12:]
    rows, width = base_ref.shape
    step = rows // SUBS
    load_w = fetch_columns(w_hbm, column, w_ref, w_sem)
    load_w.start()
    load_outs = fetch_columns(outs_hbm, half, outs_ref, outs_sem)
    load_outs.start()
    line = Line(n, rows, step)
    line.greet()
    load_w.wait()
    sums = Sums(line, part, held, s_send, s_recv)
    blocks = Blocks(line, full_ref, b_send, b_recv)

    def multiply(columns):
        product = dot_nt(dy_ref[...], w_ref[columns]).astype(bf16)
        part[:, :, columns] = product.reshape(n, rows, -1)

    by_tiles(width, 256, multiply)

    def settle(sub):
        here = line.part(sub)
        sums.total(sub, work)
        carry = carry_back(
            work,
            plain,
            order,
            step,
            width,
            middle_ref[here].astype(f32),
            base_ref[here].astype(f32),
            norm_ref[0:1],
            term_ref,
            sub == 0,
        )
        carry_ref[here] = carry
        full_ref[line.at, here] = carry.astype(bf16)
        blocks.start(sub)

    relay(n, [sums], blocks, settle)
    load_outs.wait()

    def multiply_next(columns):
        whole = full_ref[...].reshape(n * rows, width)
        att_ref[:, columns] = dot_nt(whole, outs_ref[columns]).astype(bf16)

    by_tiles(att_ref.shape[1], 256, multiply_next)


def last_kernel(n, order, dy_ref, w_hbm, base_ref, tokens, norm_ref, branch, middle, *rest):
    grad_ref, result_ref, term_ref = rest[:3]
    part, held, held2, work, plain, s_send, s_recv, r_send, r_recv, w_ref, w_sem = rest[3:]
    rows, width = base_ref.shape
    step = rows // SUBS
    load_w = fetch_columns(w_hbm, 0, w_ref, w_sem)
    load_w.start()
    line = Line(n, rows, step)
    line.greet()
    load_w.wait()
    sums = Sums(line, part, held, s_send, s_recv)
    results = Sums(line, branch, held2, r_send, r_recv)

    def multiply(columns):
        product = dot_nt(dy_ref[...], w_ref[columns]).astype(bf16)
        part[:, :, columns] = product.reshape(n, rows, -1)

    by_tiles(width, 256, multiply)

    def settle(sub):
        here = line.part(sub)
        sums.total(sub, work)
        carry = carry_back(
            work,
            plain,
            order,
            step,
            width,
            tokens[here].astype(f32),
            base_ref[here],
            norm_ref[0:1],
            term_ref,
            sub == 0,
        )
        grad_ref[here] = carry.astype(bf16)
        results.total(sub, work)
        result_ref[here] = (middle[here] + work[...]).astype(bf16)

    relay(n, [sums, results], None, settle)


VMEM_CAP = 52 * 1024 * 1024


def in_place():
    return pl.BlockSpec(memory_space=pl.ANY)


def whole_vmem():
    return pl.BlockSpec(memory_space=pltpu.VMEM)


def sem_pair(n, subs):
    return [pltpu.SemaphoreType.DMA((2, n, subs)), pltpu.SemaphoreType.DMA((2, n, subs))]


def line_call(kernel, name, ident, outs, specs, scratch, flops, moved):
    return pl.pallas_call(
        kernel,
        name=name,
        out_shape=outs,
        in_specs=specs,
        out_specs=jax.tree.map(lambda _: whole_vmem(), outs),
        scratch_shapes=scratch,
        compiler_params=pltpu.CompilerParams(
            collective_id=ident, has_side_effects=True, vmem_limit_bytes=VMEM_CAP
        ),
        cost_estimate=pl.CostEstimate(flops=flops, bytes_accessed=moved, transcendentals=0),
    )


def shape(dims, kind):
    return jax.ShapeDtypeStruct(dims, kind)


LINK_COST = 120_000_000


class Order:
    def __init__(self, pieces, width):
        self.pieces, self.width = pieces, width


def swap_sems(n):
    return [pltpu.SemaphoreType.DMA((n,)), pltpu.SemaphoreType.DMA((n,))]


def enter_call(name, ident, slots, weights, gathers, norms, normed, hidden, n, n_dp, width):
    chunk = weights[0][0].shape[0] // n_dp
    outs, scratch = [], []
    for array, places, split, _ in weights:
        parts = n if split else 1
        outs.append(shape((parts, chunk, len(places) // parts * BLK), bf16))
        scratch += [pltpu.VMEM(array.shape, f32), pltpu.SemaphoreType.DMA]
    if normed:
        scratch += [pltpu.VMEM((n_dp, *norms.shape), f32), *swap_sems(n_dp)]
    for array, _ in gathers:
        rows = array.shape[0]
        outs.append(shape((n, *array.shape), array.dtype))
        scratch += sem_pair(n, SUBS if rows >= 16 * SUBS else 1)
    if normed:
        outs.append(shape((norms.shape[0], n_dp * norms.shape[1]), f32))
    for array, _, _, _ in weights:
        slots_shape = (n_dp, array.shape[1] // BLK, chunk, BLK)
        scratch += [pltpu.VMEM(slots_shape, bf16)] * 2 + swap_sems(n_dp)
    rows = gathers[0][0].shape[0]
    scratch.append(pltpu.VMEM((rows // SUBS if hidden else 8, width), f32))
    for array, moved in gathers[1 if hidden else 0 :]:
        if moved:
            scratch.append(pltpu.VMEM(array.shape, f32))
    for index, (_, places, split, _) in enumerate(weights):
        if split:
            scratch += [pltpu.VMEM(outs[index].shape, bf16), *swap_sems(n)]
    args = [slots, *(weight[0] for weight in weights), *(gather[0] for gather in gathers)]
    specs = [pl.BlockSpec(memory_space=pltpu.SMEM)] + [in_place()] * len(weights)
    specs += [whole_vmem()] * len(gathers)
    if normed or hidden:
        args.append(norms)
        specs.append(whole_vmem())
    kernel = functools.partial(
        enter_kernel,
        [weight[1:] for weight in weights],
        [gather[1] for gather in gathers],
        Order(shuffle_order(n, n_dp), width),
        normed,
        hidden,
    )
    return line_call(kernel, name, ident, outs, specs, scratch, 0, LINK_COST)(*args)


def leave_call(name, ident, slots, weights, term, n, n_dp):
    outs, scratch = [], []
    specs = [pl.BlockSpec(memory_space=pltpu.SMEM)] + [whole_vmem()] * len(weights)
    args = [slots, *(weight[0] for weight in weights)]
    chunk = weights[0][0].shape[1]
    if term is not None:
        args.append(term)
        specs.append(whole_vmem())
        block = (term.shape[0], term.shape[1] // n_dp)
        scratch += [pltpu.VMEM((n_dp, *block), f32)] * 2 + swap_sems(n_dp)
        scratch += [pltpu.VMEM(block, f32), pltpu.VMEM((n, *block), f32), *swap_sems(n)]
    for rows, split, _, _ in weights:
        if split:
            scratch += [pltpu.VMEM(rows.shape, bf16), *swap_sems(n)]
    for rows, _, capacity, _ in weights:
        slots_shape = (n_dp, chunk, capacity * BLK)
        outs.append(shape(slots_shape, bf16))
        scratch += [pltpu.VMEM(slots_shape, bf16), *swap_sems(n_dp)]
        blocks = rows.shape[0] * rows.shape[2] // BLK
        scratch.append(pltpu.VMEM((blocks, chunk, BLK), bf16))
    if term is not None:
        outs.append(shape(block, f32))
    kernel = functools.partial(
        leave_kernel, [weight[1:] for weight in weights], term is not None
    )
    return line_call(kernel, name, ident, outs, specs, scratch, 0, LINK_COST)(*args)


def forward_call(attended, outs_z, half, base, norm_rows, after, n, n_dp, ident):
    rows, width = base.shape
    share = outs_z.shape[0]
    outs = [shape((rows, width), f32), shape((n, rows, width), bf16)]
    specs = [whole_vmem(), in_place(), whole_vmem(), whole_vmem()]
    args = [attended, outs_z, base, norm_rows]
    scratch = [
        pltpu.VMEM((n, rows, width), bf16),
        pltpu.VMEM((2, n, rows, width), bf16),
        pltpu.VMEM((rows // SUBS, width), f32),
        *sem_pair(n, SUBS),
        *sem_pair(n, SUBS),
        pltpu.VMEM((share, width), bf16),
        pltpu.SemaphoreType.DMA,
    ]
    if after is not None:
        outs.append(shape((n * rows, share), bf16))
        specs.append(in_place())
        args.append(after)
        scratch += [pltpu.VMEM((width, share), bf16), pltpu.SemaphoreType.DMA]
    kernel = functools.partial(forward_kernel, n, shuffle_order(n, n_dp), half, after is not None)
    call = line_call(kernel, f"forward{half}", ident, outs, specs, scratch, 0, LINK_COST)
    return call(*args)


def back_call(dy, weight, column, base, middle, norm_rows, outs_z, half, n, n_dp, ident):
    rows, width = base.shape
    share = outs_z.shape[0]
    outs = [
        shape((rows, width), f32),
        shape((n, rows, width), bf16),
        shape((n * rows, share), bf16),
        shape((8, width), f32),
    ]
    specs = [
        whole_vmem(),
        in_place(),
        whole_vmem(),
        whole_vmem(),
        whole_vmem(),
        in_place(),
    ]
    scratch = [
        pltpu.VMEM((n, rows, width), bf16),
        pltpu.VMEM((2, n, rows, width), bf16),
        pltpu.VMEM((rows // SUBS, width), f32),
        pltpu.VMEM((rows // SUBS, width), f32),
        *sem_pair(n, SUBS),
        *sem_pair(n, SUBS),
        pltpu.VMEM((width, dy.shape[1]), bf16),
        pltpu.SemaphoreType.DMA,
        pltpu.VMEM((share, width), bf16),
        pltpu.SemaphoreType.DMA,
    ]
    kernel = functools.partial(back_kernel, n, unshuffle_order(n, n_dp), column, half)
    call = line_call(kernel, f"back{half}", ident, outs, specs, scratch, 0, LINK_COST)
    return call(dy, weight, base, middle, norm_rows, outs_z)


def last_call(dy, weight, base, tokens, norm_rows, branch, middle, n, n_dp, ident):
    rows, width = base.shape
    outs = [
        shape((rows, width), bf16),
        shape((rows, width), bf16),
        shape((8, width), f32),
    ]
    specs = [whole_vmem(), in_place()] + [whole_vmem()] * 5
    scratch = [
        pltpu.VMEM((n, rows, width), bf16),
        pltpu.VMEM((2, n, rows, width), bf16),
        pltpu.VMEM((2, n, rows, width), bf16),
        pltpu.VMEM((rows // SUBS, width), f32),
        pltpu.VMEM((rows // SUBS, width), f32),
        *sem_pair(n, SUBS),
        *sem_pair(n, SUBS),
        pltpu.VMEM((width, dy.shape[1]), bf16),
        pltpu.SemaphoreType.DMA,
    ]
    kernel = functools.partial(last_kernel, n, unshuffle_order(n, n_dp))
    call = line_call(kernel, "last", ident, outs, specs, scratch, 0, LINK_COST)
    return call(dy, weight, base, tokens, norm_rows, branch, middle)


def attend_forward(query, keys, values, mask_ref, keyed, att_ref, share_ref):
    packed, rows, _ = mask_ref.shape
    heads = att_ref.shape[1] // HEAD
    for p in range(packed):
        here = slice(p * rows, (p + 1) * rows)
        there = here if keyed else slice(None)
        for h in range(heads):
            columns = slice(h * HEAD, (h + 1) * HEAD)
            scores = dot_nt(query[here, columns], keys[there, columns]) * HEAD ** (-0.5)
            scores = jnp.where(mask_ref[p] > 0, scores, score_floor)
            powers = jnp.exp(scores - jnp.max(scores, axis=-1, keepdims=True))
            shares = powers / jnp.sum(powers, axis=-1, keepdims=True)
            share_ref[p * heads + h] = shares
            att_ref[here, columns] = dot(shares.astype(bf16), values[there, columns]).astype(bf16)


def attend_backward(query, keys, values, share_ref, back_ref, rows, keyed, put_query, put_pair):
    heads = back_ref.shape[1] // HEAD
    packed = back_ref.shape[0] // rows
    score_scale = HEAD ** (-0.5)
    for h in range(heads):
        columns = slice(h * HEAD, (h + 1) * HEAD)
        key_grad = value_grad = None
        for p in range(packed):
            here = slice(p * rows, (p + 1) * rows)
            there = here if keyed else slice(None)
            shares = share_ref[p * heads + h]
            back = back_ref[here, columns]
            back_shares = dot_nt(back, values[there, columns])
            inner_sum = jnp.sum(shares * back_shares, axis=-1, keepdims=True)
            back_scores = (shares * (back_shares - inner_sum)).astype(bf16)
            put_query(here, columns, dot(back_scores, keys[there, columns]) * score_scale)
            key_term = dot_tn(back_scores, query[here, columns]) * score_scale
            value_term = dot_tn(shares.astype(bf16), back)
            if keyed:
                put_pair(there, columns, key_term, value_term)
            else:
                key_grad = key_term if key_grad is None else key_grad + key_term
                value_grad = value_term if value_grad is None else value_grad + value_term
        if not keyed:
            put_pair(slice(None), columns, key_grad, value_grad)


def self_forward_kernel(h_ref, w_ref, mask_ref, proj_ref, att_ref, share_ref):
    tile = pl.program_id(0)
    proj_ref[tile] = dot(h_ref[...], w_ref[...]).astype(bf16)

    @pl.when(tile == 2)
    def _():
        attend_forward(
            proj_ref.at[0], proj_ref.at[1], proj_ref.at[2], mask_ref, True, att_ref, share_ref
        )


def cross_forward_kernel(cq_ref, text_ref, w_ref, mask_ref, kv_ref, att_ref, share_ref, total):
    tile = pl.program_id(0)
    product = dot(text_ref[...], w_ref[...])

    @pl.when(tile < 2)
    def _():
        total[tile] = product

    @pl.when(tile >= 2)
    def _():
        kv_ref[tile - 2] = (total[tile - 2] + product).astype(bf16)

    @pl.when(tile == 3)
    def _():
        attend_forward(cq_ref, kv_ref.at[0], kv_ref.at[1], mask_ref, False, att_ref, share_ref)


def ffn_kernel(h_ref, up_ref, down_ref, grad_ref, du_ref, branch_ref, gup_ref, gdown_ref, total):
    tile = pl.program_id(0)
    up_values = dot(h_ref[...], up_ref[...])
    chance = 0.5 * (1.0 + lax.erf(up_values * 0.5**0.5))
    density = jnp.exp(-0.5 * up_values * up_values) * 0.3989422804014327
    activated = (up_values * chance).astype(bf16)
    back_act = dot_nt(grad_ref[...], down_ref[...])
    back_up = (back_act * (chance + up_values * density)).astype(bf16)
    du_ref[...] = back_up
    gup_ref[...] = dot_tn(h_ref[...], back_up).astype(bf16)
    gdown_ref[...] = dot_tn(activated, grad_ref[...]).astype(bf16)

    @pl.when(tile == 0)
    def _():
        total[...] = dot(activated, down_ref[...])

    @pl.when(tile > 0)
    def _():
        total[...] += dot(activated, down_ref[...])

    @pl.when(tile == 3)
    def _():
        branch_ref[...] = total[...].astype(bf16)


def cross_back_kernel(
    rows, back_ref, cq_ref, kv_ref, share_ref, text_ref, dcq_ref, grad_ref, pairs
):
    share = cq_ref.shape[1]

    @pl.when(pl.program_id(0) == 0)
    def _():
        def put_query(here, columns, value):
            dcq_ref[here, columns] = value.astype(bf16)

        def put_pair(there, columns, key_grad, value_grad):
            pairs[there, columns] = key_grad.astype(bf16)
            after_keys = slice(share + columns.start, share + columns.stop)
            pairs[there, after_keys] = value_grad.astype(bf16)

        attend_backward(
            cq_ref, kv_ref.at[0], kv_ref.at[1], share_ref, back_ref, rows, False, put_query, put_pair
        )

    grad_ref[...] = dot_tn(text_ref[...], pairs[...]).astype(bf16)


def outs_grad_kernel(att1_ref, carry1_ref, att2_ref, carry2_ref, grad_ref):
    tile = pl.program_id(0)

    @pl.when(tile == 0)
    def _():
        grad_ref[...] = dot_tn(att1_ref[...], carry1_ref[...]).astype(bf16)

    @pl.when(tile == 1)
    def _():
        grad_ref[...] = dot_tn(att2_ref[...], carry2_ref[...]).astype(bf16)


def self_back_kernel(
    rows, back_ref, proj_ref, share_ref, h1_ref, h2_ref, dcq_ref, dproj_ref, grad_ref, parts
):
    tile = pl.program_id(0)
    share = dcq_ref.shape[1]

    @pl.when(tile == 0)
    def _():
        def put(part, here, columns, value):
            value = value.astype(bf16)
            parts[part, here, columns] = value
            dproj_ref[here, part * share + columns.start : part * share + columns.stop] = value

        def put_query(here, columns, value):
            put(0, here, columns, value)

        def put_pair(there, columns, key_grad, value_grad):
            put(1, there, columns, key_grad)
            put(2, there, columns, value_grad)

        attend_backward(
            proj_ref.at[0],
            proj_ref.at[1],
            proj_ref.at[2],
            share_ref,
            back_ref,
            rows,
            True,
            put_query,
            put_pair,
        )

    @pl.when(tile < 3)
    def _():
        grad_ref[...] = dot_tn(h1_ref[...], parts[tile]).astype(bf16)

    @pl.when(tile == 3)
    def _():
        grad_ref[...] = dot_tn(h2_ref[...], dcq_ref[...]).astype(bf16)


def fixed(dims):
    return pl.BlockSpec(dims, lambda t: (0,) * len(dims))


def moving(dims, index):
    return pl.BlockSpec(dims, lambda t: (0, index(t)))


def local_call(kernel, name, tiles, outs, specs, out_specs, scratch, flops, moved):
    return pl.pallas_call(
        kernel,
        name=name,
        grid=(tiles,),
        out_shape=outs,
        in_specs=specs,
        out_specs=out_specs,
        scratch_shapes=scratch,
        compiler_params=pltpu.CompilerParams(vmem_limit_bytes=VMEM_CAP),
        cost_estimate=pl.CostEstimate(flops=flops, bytes_accessed=moved, transcendentals=0),
    )


def self_forward(hidden, query_z, mask):
    tokens, width = hidden.shape
    share = query_z.shape[1] // 4
    packed, rows, _ = mask.shape
    pairs = (packed * share // HEAD, rows, rows)
    return local_call(
        self_forward_kernel,
        "self_forward",
        3,
        (shape((3, tokens, share), bf16), shape((tokens, share), bf16), shape(pairs, f32)),
        [fixed(hidden.shape), moving((width, share), lambda t: t), fixed(mask.shape)],
        (fixed((3, tokens, share)), fixed((tokens, share)), fixed(pairs)),
        [],
        6 * tokens * width * share,
        20_000_000,
    )(hidden, query_z, mask)


def cross_forward(cross_query, text_all, text_z, mask):
    tokens, share = cross_query.shape
    texts = text_all.shape[0]
    width = text_z.shape[0]
    packed, rows, _ = mask.shape
    pairs = (packed * share // HEAD, rows, texts)
    return local_call(
        cross_forward_kernel,
        "cross_forward",
        4,
        (shape((2, texts, share), bf16), shape((tokens, share), bf16), shape(pairs, f32)),
        [
            fixed(cross_query.shape),
            moving((texts, width), lambda t: t // 2),
            moving((width, share), lambda t: t),
            fixed(mask.shape),
        ],
        (fixed((2, texts, share)), fixed((tokens, share)), fixed(pairs)),
        [pltpu.VMEM((2, texts, share), f32)],
        8 * texts * width * share,
        20_000_000,
    )(cross_query, text_all, text_z, mask)


def ffn(hidden, up_z, down_z, grad_all):
    tokens, width = hidden.shape
    share = down_z.shape[0]
    return local_call(
        ffn_kernel,
        "ffn",
        4,
        (
            shape((tokens, 4 * share), bf16),
            shape((tokens, width), bf16),
            shape(up_z.shape, bf16),
            shape(down_z.shape, bf16),
        ),
        [
            fixed(hidden.shape),
            moving((width, share), lambda t: t),
            moving((share, width), lambda t: t),
            fixed(grad_all.shape),
        ],
        (
            moving((tokens, share), lambda t: t),
            fixed((tokens, width)),
            moving((width, share), lambda t: t),
            moving((share, width), lambda t: t),
        ),
        [pltpu.VMEM((tokens, width), f32)],
        40 * tokens * width * share,
        60_000_000,
    )(hidden, up_z, down_z, grad_all)


def cross_back(back_attended, cross_query, text_pairs, shares, text_all, rows):
    tokens, share = cross_query.shape
    texts = text_all.shape[0]
    width = text_all.shape[1] // 2
    return local_call(
        functools.partial(cross_back_kernel, rows),
        "cross_back",
        2,
        (shape((tokens, share), bf16), shape((width, 4 * share), bf16)),
        [
            fixed(back_attended.shape),
            fixed(cross_query.shape),
            fixed(text_pairs.shape),
            fixed(shares.shape),
            moving((texts, width), lambda t: t),
        ],
        (fixed((tokens, share)), moving((width, 2 * share), lambda t: t)),
        [pltpu.VMEM((texts, 2 * share), bf16)],
        8 * texts * width * share,
        20_000_000,
    )(back_attended, cross_query, text_pairs, shares, text_all)


def outs_grad(attended1, carry1, attended2, carry2):
    tokens, share = attended1.shape
    width = carry1.shape[1]
    return local_call(
        outs_grad_kernel,
        "outs_grad",
        2,
        shape((share, 2 * width), bf16),
        [fixed((tokens, share)), fixed((tokens, width))] * 2,
        moving((share, width), lambda t: t),
        [],
        4 * tokens * width * share,
        10_000_000,
    )(attended1, carry1, attended2, carry2)


def self_back(back_attended, projected, shares, hidden1, hidden2, back_cross, rows):
    tokens, width = hidden1.shape
    share = back_cross.shape[1]
    return local_call(
        functools.partial(self_back_kernel, rows),
        "self_back",
        4,
        (shape((tokens, 3 * share), bf16), shape((width, 4 * share), bf16)),
        [
            fixed(back_attended.shape),
            fixed(projected.shape),
            fixed(shares.shape),
            fixed(hidden1.shape),
            fixed(hidden2.shape),
            fixed(back_cross.shape),
        ],
        (fixed((tokens, 3 * share)), moving((width, share), lambda t: t)),
        [pltpu.VMEM((3, tokens, share), bf16)],
        8 * tokens * width * share,
        25_000_000,
    )(back_attended, projected, shares, hidden1, hidden2, back_cross)


def block_slots(owners):
    owner = jnp.concatenate(owners)
    weight = jnp.concatenate([jnp.full(one.shape, at, jnp.int32) for at, one in enumerate(owners)])
    mark = owner + weight * 1024
    count = mark.shape[0]
    earlier = lax.broadcasted_iota(jnp.int32, (count, count), 1) < lax.broadcasted_iota(
        jnp.int32, (count, count), 0
    )
    same = jnp.logical_and(mark[:, None] == mark[None, :], earlier)
    return jnp.stack([owner, jnp.sum(same.astype(jnp.int32), axis=1)])


def slot_contents(owners, slots, places, capacities, firsts, n_dp):
    rows = []
    for owner, place, capacity, first in zip(owners, places, capacities, firsts):
        count = owner.shape[0]
        at = owner * capacity + slots[1, first : first + count]
        hit = at[None, :] == lax.broadcasted_iota(jnp.int32, (n_dp * capacity, count), 0)
        block = lax.broadcasted_iota(jnp.int32, (n_dp * capacity, count), 1)
        per_group, per_part, split = place_rule(place)
        part = block % per_group // per_part if split else block * 0
        column = block // per_group * per_part + block % per_part if split else block
        index = part * (count // (per_group // per_part)) + column if split else column
        rows.append(
            jnp.stack([jnp.sum(jnp.where(hit, value, 0), axis=1) for value in (index, block * 0 + 1)])
        )
    return jnp.concatenate(rows, axis=1)


def place_rule(place):
    parts = 1 + max(part for part, _ in place)
    if parts == 1:
        return 0, 0, False
    per_part = sum(1 for part, _ in place[:HEADS] if part == 0)
    return per_part * parts, per_part, True


def after(small, first):
    return lax.optimization_barrier((small, first))[0]


def body(
    tokens_in,
    text_in,
    seg_ids,
    capt_ids,
    grad_out,
    owner_query,
    owner_up,
    owner_outs,
    owner_text,
    owner_down,
    w_query,
    m_query,
    v_query,
    w_up,
    m_up,
    v_up,
    w_outs,
    m_outs,
    v_outs,
    w_text,
    m_text,
    v_text,
    w_down,
    m_down,
    v_down,
    norm_weight,
    m_norm,
    v_norm,
):
    n_dp = lax.axis_size("dp")
    n_z = lax.axis_size("fsdp")
    width = tokens_in.shape[1]
    own_rows = w_query.shape[0]
    chunk = own_rows // n_dp
    cap_big = w_query.shape[1] // BLK
    cap_out = w_outs.shape[1] // BLK
    heads_z = HEADS // n_z
    share = width // n_z
    owner_query, owner_up, owner_outs, owner_text, owner_down = (
        owner[:, 0] for owner in (owner_query, owner_up, owner_outs, owner_text, owner_down)
    )
    split_places = [split_place(b, heads_z, n_z) for b in range(owner_query.shape[0])]
    big_places = [flat_place(b) for b in range(owner_down.shape[0])]
    out_places = [flat_place(b) for b in range(owner_outs.shape[0])]
    owners = (owner_query, owner_outs, owner_text, owner_up, owner_down)
    places = (split_places, out_places, split_places, split_places, big_places)
    capacities = (cap_big, cap_out, cap_big, cap_big, cap_big)
    firsts = [sum(len(one) for one in places[:index]) for index in range(5)]
    slot_firsts = [sum(capacities[:index]) * n_dp for index in range(5)]
    slots = block_slots(owners)
    contents = slot_contents(owners, slots, places, capacities, firsts, n_dp)

    def spread(rows):
        return lax.all_gather(rows.reshape(-1, rows.shape[-1]), "dp", axis=0, tiled=True)

    def gather_sum(piece, parts):
        summed = lax.psum_scatter(piece, "dp", scatter_dimension=0, tiled=True)
        return summed.reshape(parts, chunk, -1)

    token_count = tokens_in.shape[0]
    marks = jnp.concatenate([seg_ids, capt_ids], axis=1)
    marks = jnp.pad(marks, ((0, 7), (0, 256 - marks.shape[1])))
    norms = jnp.pad(norm_weight, ((0, 2), (0, 0)))
    query_rows, marks, norm_full = enter_call(
        "enter_query",
        0,
        slots,
        [(w_query, split_places, True, firsts[0])],
        [(marks, False)],
        norms,
        True,
        False,
        n_z,
        n_dp,
        width,
    )
    outs_rows, text_rows, hidden1, text_all = enter_call(
        "enter_text",
        6,
        slots,
        [(w_outs, out_places, False, firsts[1]), (w_text, split_places, True, firsts[2])],
        [(tokens_in, True), (text_in, True)],
        norm_full[0:2],
        False,
        True,
        n_z,
        n_dp,
        width,
    )
    query_z, outs_z, text_z = spread(query_rows), spread(outs_rows), spread(text_rows)
    hidden1 = hidden1.reshape(-1, width)
    text_all = text_all.reshape(-1, text_in.shape[1])
    segment = marks[:, 0, :token_count]
    caption = marks[:, 0, token_count : token_count + capt_ids.shape[1]]
    self_mask = (segment[:, :, None] == segment[:, None, :]).astype(jnp.int32)
    text_row = lax.broadcasted_iota(jnp.int32, caption.shape, 0).reshape(1, 1, -1)
    packed_row = lax.broadcasted_iota(jnp.int32, (n_z, 1, 1), 0)
    cross_mask = jnp.logical_and(
        segment[:, :, None] == caption.reshape(1, 1, -1), packed_row == text_row
    ).astype(jnp.int32)

    projected, attended1, shares1 = self_forward(hidden1, query_z, self_mask)
    up_rows, down_rows, grad_all = enter_call(
        "enter_up",
        7,
        after(slots, attended1),
        [(w_up, split_places, True, firsts[3]), (w_down, big_places, False, firsts[4])],
        [(grad_out, False)],
        None,
        False,
        False,
        n_z,
        n_dp,
        width,
    )
    grad_all = grad_all.reshape(-1, width)
    up_z, down_z = spread(up_rows), spread(down_rows)
    middle1, hidden2, cross_query = forward_call(
        attended1, outs_z, 0, tokens_in, after(norm_full[2:4], up_rows), query_z, n_z, n_dp, 1
    )
    hidden2 = hidden2.reshape(-1, width)
    text_pairs, attended2, shares2 = cross_forward(cross_query, text_all, text_z, cross_mask)
    middle2, hidden3 = forward_call(
        attended2, outs_z, 1, middle1, norm_full[4:6], None, n_z, n_dp, 2
    )
    hidden3 = hidden3.reshape(-1, width)
    back_up, branch3, up_part, down_part = ffn(hidden3, up_z, down_z, grad_all)
    branch3 = branch3.reshape(n_z, token_count, width)
    down_sum = gather_sum(down_part, 1)
    up_sum = gather_sum(up_part, n_z)
    at_middle2, carry2, back_att2, term3 = back_call(
        back_up, up_z, 0, grad_out, middle2, norm_full[4:6], outs_z, 1, n_z, n_dp, 3
    )
    carry2 = carry2.reshape(-1, width)
    back_cross, text_part = cross_back(
        back_att2, cross_query, text_pairs, shares2, text_all, token_count
    )
    text_sum = gather_sum(text_part, n_z)
    at_middle1, carry1, back_att1, term2 = back_call(
        back_cross, query_z, 3, at_middle2, middle1, norm_full[2:4], outs_z, 0, n_z, n_dp, 4
    )
    carry1 = carry1.reshape(-1, width)
    outs_sum = gather_sum(outs_grad(attended1, carry1, attended2, carry2), 1)
    back_projected, query_part = self_back(
        back_att1, projected, shares1, hidden1, hidden2, back_cross, token_count
    )
    query_sum = gather_sum(query_part, n_z)
    text_grad, up_grad, down_grad = leave_call(
        "leave_up",
        8,
        after(contents, back_projected),
        [
            (text_sum, True, cap_big, slot_firsts[2]),
            (up_sum, True, cap_big, slot_firsts[3]),
            (down_sum, False, cap_big, slot_firsts[4]),
        ],
        None,
        n_z,
        n_dp,
    )
    grad_in, result, term1 = last_call(
        back_projected,
        query_z,
        at_middle1,
        tokens_in,
        after(norm_full[0:2], text_grad),
        branch3,
        middle2,
        n_z,
        n_dp,
        5,
    )
    norm_term = jnp.concatenate([term1[:2], term2[:2], term3[:4]], axis=0)
    query_grad, outs_slots, norm_grad = leave_call(
        "leave_query",
        9,
        contents,
        [
            (query_sum, True, cap_big, slot_firsts[0]),
            (outs_sum, False, cap_out, slot_firsts[1]),
        ],
        norm_term,
        n_z,
        n_dp,
    )
    norm_grad = norm_grad[:6]
    query_grad, outs_slots, text_grad, up_grad, down_grad = (
        grad.reshape(own_rows, -1).astype(f32)
        for grad in (query_grad, outs_slots, text_grad, up_grad, down_grad)
    )
    query_new = adamw_update(w_query, m_query, v_query, query_grad, rate_query, decay_rate)
    up_new = adamw_update(w_up, m_up, v_up, up_grad, rate_up, decay_rate)
    outs_new = adamw_update(w_outs, m_outs, v_outs, outs_slots, rate_outs, decay_rate)
    text_new = adamw_update(w_text, m_text, v_text, text_grad, rate_text, decay_rate)
    down_new = adamw_update(w_down, m_down, v_down, down_grad, rate_down, decay_rate)
    norm_new = adamw_update(norm_weight, m_norm, v_norm, norm_grad, rate_norm, 0.0)
    return (
        result,
        grad_in,
        *query_new,
        *up_new,
        *outs_new,
        *text_new,
        *down_new,
        *norm_new,
    )


def solution(mesh):
    rows = P(("dp", "fsdp"), None)
    slots = P("fsdp", "dp")
    norms = P(None, "dp")
    in_specs = (rows,) * 5 + (P(),) * 5 + (slots,) * 15 + (norms,) * 3
    out_specs = (rows,) * 2 + (slots,) * 15 + (norms,) * 3
    return jax.shard_map(body, mesh=mesh, in_specs=in_specs, out_specs=out_specs, check_vma=False)
```

```python
import functools

import jax
import jax.numpy as jnp
from jax import lax
from jax.experimental import pallas as pl
from jax.experimental.pallas import tpu as pltpu
from jax.sharding import PartitionSpec as P

HEADS = 16
HEAD = 128
STEP = 10
BLK = 128


beta_first = 0.9
beta_second = 0.999
adam_eps = 1e-08
decay_rate = 0.01
rate_query = 0.04
rate_up = 0.04
rate_outs = 0.12
rate_text = 0.03
rate_down = 0.03
rate_norm = 0.5
norm_eps = 1e-05
score_floor = -1e30
bf16 = jnp.bfloat16
f32 = jnp.float32


def normalize(values):
    centered = values - jnp.mean(values, axis=-1, keepdims=True)
    inverse_std = lax.rsqrt(jnp.mean(centered * centered, axis=-1, keepdims=True) + norm_eps)
    return (centered * inverse_std, inverse_std)


def norm_back(back_hidden, normed, inverse_std, gain_row):
    back_normed = back_hidden * gain_row
    return inverse_std * (
        back_normed
        - jnp.mean(back_normed, axis=-1, keepdims=True)
        - normed * jnp.mean(back_normed * normed, axis=-1, keepdims=True)
    )


def adamw_update(weight, first, second, gradient, rate, decay):
    first_new = beta_first * first + (1.0 - beta_first) * gradient
    second_new = beta_second * second + (1.0 - beta_second) * gradient * gradient
    first_hat = first_new / (1.0 - beta_first**STEP)
    second_hat = second_new / (1.0 - beta_second**STEP)
    weight_new = weight - rate * (first_hat / (jnp.sqrt(second_hat) + adam_eps) + decay * weight)
    return (first_new, second_new, weight_new)


def dot(left, right):
    return jnp.dot(left, right, preferred_element_type=f32)


def dot_nt(left, right):
    return lax.dot_general(left, right, (((1,), (1,)), ((), ())), preferred_element_type=f32)


def dot_tn(left, right):
    return lax.dot_general(left, right, (((0,), (0,)), ((), ())), preferred_element_type=f32)


def split_place(block, per_part, parts):
    group, rest = divmod(block, per_part * parts)
    part, inner = divmod(rest, per_part)
    return part, group * per_part + inner


def flat_place(block):
    return 0, block


MESH = pl.DeviceIdType.MESH


SUBS = 4


class Line:
    def __init__(self, n, rows, step):
        self.n, self.rows, self.step = n, rows, step
        self.at = lax.axis_index("fsdp")

    def has(self, way):
        return self.at < self.n - 1 if way == 0 else self.at > 0

    def peer(self, way):
        index = jnp.clip(self.at + (1 if way == 0 else -1), 0, self.n - 1)
        return {"fsdp": index}

    def greet(self, others=0):
        barrier = pltpu.get_barrier_semaphore()
        for way in (0, 1):

            @pl.when(self.has(way))
            def _():
                pl.semaphore_signal(
                    barrier, inc=1, device_id=self.peer(way), device_id_type=pl.DeviceIdType.MESH
                )

        pl.semaphore_wait(
            barrier, others + self.has(0).astype(jnp.int32) + self.has(1).astype(jnp.int32)
        )

    def copy(self, source, target, send, recv, way):
        return pltpu.make_async_remote_copy(
            src_ref=source,
            dst_ref=target,
            send_sem=send,
            recv_sem=recv,
            device_id=self.peer(way),
            device_id_type=pl.DeviceIdType.MESH,
        )

    def part(self, sub):
        return pl.ds(sub * self.step, self.step)


class Sums:
    def __init__(self, line, part, held, send, recv):
        self.line, self.part, self.held, self.send, self.recv = line, part, held, send, recv

    def move(self, way, target, sub, source):
        line = self.line
        rows = line.part(sub)
        return line.copy(
            source,
            self.held.at[way, target, rows],
            self.send.at[way, target, sub],
            self.recv.at[way, target, sub],
            way,
        )

    def target(self, way, time):
        n, at = self.line.n, self.line.at
        return n - 1 - (time - at) if way == 0 else time - (n - 1 - at)

    def passes(self, way, target):
        n, at = self.line.n, self.line.at
        if way == 0:
            return jnp.logical_and(target > at, target < n)
        return jnp.logical_and(target < at, target >= 0)

    def forward(self, sub, time):
        line = self.line
        rows = line.part(sub)
        for way in (0, 1):
            target = self.target(way, time)
            passes = self.passes(way, target)
            inner = jnp.logical_and(passes, line.has(1 - way))
            outer = jnp.logical_and(passes, jnp.logical_not(line.has(1 - way)))

            @pl.when(outer)
            def _():
                self.move(way, target, sub, self.part.at[target, rows]).start()

            @pl.when(inner)
            def _():
                held = self.held.at[way, target, rows]
                self.move(way, target, sub, held).wait_recv()
                total = held[...].astype(f32) + self.part[target, rows].astype(f32)
                held[...] = total.astype(bf16)
                self.move(way, target, sub, held).start()

    def total(self, sub, sum_ref):
        line = self.line
        rows = line.part(sub)
        sum_ref[...] = self.part[line.at, rows].astype(f32)
        for way in (0, 1):

            @pl.when(line.has(1 - way))
            def _():
                held = self.held.at[way, line.at, rows]
                self.move(way, line.at, sub, held).wait_recv()
                sum_ref[...] += held[...].astype(f32)

    def finish(self):
        line = self.line
        for way in (0, 1):
            for time in range(line.n - 1):
                target = self.target(way, time)

                @pl.when(self.passes(way, target))
                def _():
                    for sub in range(line.rows // line.step):
                        held = self.held.at[way, target, line.part(sub)]
                        self.move(way, target, sub, held).wait_send()


def relay(n, sums, blocks, settle):
    for slot in range((SUBS + 2) * (n - 1)):
        sub, time = divmod(slot, n - 1)
        if sub < SUBS:
            for one in sums:
                one.forward(sub, time)
        if time == 0 and 0 <= sub - 1 < SUBS:
            settle(sub - 1)
        if blocks is not None:
            if time == n - 2 and 0 <= sub - 1 < SUBS:
                blocks.forward(sub - 1, 1)
            if time < n - 2 and 0 <= sub - 2 < SUBS:
                blocks.forward(sub - 2, time + 2)
    for one in sums:
        one.finish()
    if blocks is not None:
        blocks.finish()


class Blocks:
    def __init__(self, line, full, send, recv):
        self.line, self.full, self.send, self.recv = line, full, send, recv

    def move(self, way, source, sub):
        line = self.line
        held = self.full.at[source, line.part(sub)]
        return line.copy(
            held, held, self.send.at[way, source, sub], self.recv.at[way, source, sub], way
        )

    def behind(self, way, source):
        return self.line.at > source if way == 0 else self.line.at < source

    def start(self, sub):
        for way in (0, 1):

            @pl.when(self.line.has(way))
            def _():
                self.move(way, self.line.at, sub).start()

    def forward(self, sub, step):
        line = self.line
        for way in (0, 1):
            source = line.at - step if way == 0 else line.at + step

            @pl.when(jnp.logical_and(source >= 0, source < line.n))
            def _():
                self.move(way, source, sub).wait_recv()

                @pl.when(line.has(way))
                def _():
                    self.move(way, source, sub).start()

    def forward_all(self, sub):
        for step in range(1, self.line.n):
            self.forward(sub, step)

    def finish(self):
        line = self.line
        for way in (0, 1):
            for source in range(line.n):
                ours = jnp.logical_or(self.behind(way, source), line.at == source)

                @pl.when(jnp.logical_and(ours, line.has(way)))
                def _():
                    for sub in range(line.rows // line.step):
                        self.move(way, source, sub).wait_send()


def lane_moves(width, order):
    moves = []
    piece = width // len(order)
    for group in range(width // BLK):
        parts = []
        for offset in range(0, BLK, piece):
            start = order[(group * BLK + offset) // piece] * piece
            parts.append((offset, start // BLK, start % BLK))
        moves.append(parts)
    return piece, moves


def reorder(load, store, rows, width, order):
    piece, moves = lane_moves(width, order)
    lane = lax.broadcasted_iota(jnp.int32, (rows, BLK), 1)
    for group, parts in enumerate(moves):
        value = None
        for offset, source, start in parts:
            block = load(source)
            if start != offset:
                block = pltpu.roll(block, (offset - start) % BLK, 1)
            value = block if value is None else jnp.where(lane >= offset, block, value)
        store(group, value)


def shuffle_order(n_z, n_dp):
    return [z * n_dp + i for i in range(n_dp) for z in range(n_z)]


def unshuffle_order(n_z, n_dp):
    return [i * n_z + z for z in range(n_z) for i in range(n_dp)]


def by_tiles(columns, tile, run):
    def one(index, carry):
        run(pl.ds(pl.multiple_of(index * tile, tile), tile))
        return carry

    lax.fori_loop(0, columns // tile, one, 0)


class Swap:
    def __init__(self, axis, source, target, send, recv):
        self.axis, self.source, self.target = axis, source, target
        self.send, self.recv = send, recv
        self.n = lax.axis_size(axis)
        self.me = lax.axis_index(axis)

    def copy(self, jump, arrival=False):
        peer = lax.rem(self.me + jump, self.n)
        slot = peer if arrival else self.me
        return pltpu.make_async_remote_copy(
            src_ref=self.source.at[peer],
            dst_ref=self.target.at[slot],
            send_sem=self.send.at[jump],
            recv_sem=self.recv.at[slot],
            device_id={self.axis: peer},
            device_id_type=MESH,
        )

    def start(self):
        for jump in range(1, self.n):
            self.copy(jump).start()

    def keep(self):
        self.target[self.me] = self.source[self.me]

    def wait(self):
        for jump in range(1, self.n):
            self.copy(jump, True).wait_recv()

    def finish(self):
        for jump in range(1, self.n):
            self.copy(jump).wait_send()


def greet_all():
    barrier = pltpu.get_barrier_semaphore()
    count = 0
    for axis in ("dp", "fsdp"):
        n, me = lax.axis_size(axis), lax.axis_index(axis)
        count += n - 1
        for jump in range(1, n):
            pl.semaphore_signal(
                barrier, inc=1, device_id={axis: lax.rem(me + jump, n)}, device_id_type=MESH
            )
    pl.semaphore_wait(barrier, count)


class Refs:
    def __init__(self, refs):
        self.refs = list(refs)

    def take(self, count=None):
        taken = self.refs[: 1 if count is None else count]
        self.refs = self.refs[len(taken) :]
        return taken[0] if count is None else taken


def enter_kernel(weights, gathers, order, normed, hidden, *refs):
    refs = Refs(refs)
    n_dp, n_z = lax.axis_size("dp"), lax.axis_size("fsdp")
    slots_ref = refs.take()
    w_refs = refs.take(len(weights))
    in_refs = refs.take(len(gathers))
    norm_in = refs.take() if normed or hidden else None
    row_refs = refs.take(len(weights))
    full_refs = refs.take(len(gathers))
    norm_out = refs.take() if normed else None
    loads = []
    for w_ref in w_refs:
        stage, sem = refs.take(2)
        load = pltpu.make_async_copy(w_ref, stage, sem)
        load.start()
        loads.append((stage, load))
    greet_all()
    if normed:
        parts, *sems = refs.take(3)
        norm_swap = Spread("dp", norm_in, parts, *sems)
        norm_swap.start()
    lines = []
    for in_ref, full_ref in zip(in_refs, full_refs):
        rows = in_ref.shape[0]
        step = rows // SUBS if rows >= 16 * SUBS else rows
        lines.append(Blocks(Line(n_z, rows, step), full_ref, *refs.take(2)))
    swaps = []
    for (stage, load), (places, split, _) in zip(loads, weights):
        source, target, *sems = refs.take(4)
        swap = Swap("dp", source, target, *sems)
        load.wait()
        chunk = source.shape[2]
        for jump in range(n_dp):
            peer = lax.rem(swap.me + jump, n_dp)
            into = source if jump else target
            for slot in range(source.shape[1]):
                here = pl.ds(pl.multiple_of(peer * chunk, chunk), chunk)
                piece = stage[here, slot * BLK : (slot + 1) * BLK]
                into[peer, slot] = piece.astype(bf16)
            if jump:
                swap.copy(jump).start()
        swaps.append(swap)
    work = refs.take()
    for index, (in_ref, full_ref, blocks) in enumerate(zip(in_refs, full_refs, lines)):
        line = blocks.line
        if hidden and index == 0:
            for sub in range(line.rows // line.step):
                here = line.part(sub)
                values, _ = normalize(in_ref[here].astype(f32))
                work[...] = values * norm_in[0:1] + norm_in[1:2]
                store_shuffled(work, full_ref, line, here, order)
                blocks.start(sub)
        elif in_ref.dtype == bf16 and gathers[index]:
            work2 = refs.take()
            work2[...] = in_ref[...].astype(f32)
            store_shuffled(work2, full_ref, line, line.part(0), order)
            blocks.start(0)
        else:
            for sub in range(line.rows // line.step):
                here = line.part(sub)
                full_ref[line.at, here] = in_ref[here]
                blocks.start(sub)
    if normed:
        parts[norm_swap.me] = norm_in[...]
        norm_swap.wait()
        share = norm_in.shape[1]
        for index in range(n_dp):
            norm_out[:, index * share : (index + 1) * share] = parts[index]
    shares = []
    for swap, row_ref, (places, split, first) in zip(swaps, row_refs, weights):
        swap.wait()
        if split:
            cut, *sems = refs.take(3)
            share = Swap("fsdp", cut, row_ref, *sems)
            shares.append(share)
        else:
            cut = row_ref
        for block, (part, column) in enumerate(places):
            owner, slot = slots_ref[0, first + block], slots_ref[1, first + block]
            cut[part, :, column * BLK : (column + 1) * BLK] = swap.target[owner, slot]
        if split:
            share.start()
            share.keep()
    for blocks in lines:
        for sub in range(blocks.line.rows // blocks.line.step):
            blocks.forward_all(sub)
    for share in shares:
        share.wait()
    for one in [*swaps, *shares, *lines]:
        one.finish()
    if normed:
        norm_swap.finish()


class Spread(Swap):
    def copy(self, jump, arrival=False):
        peer = lax.rem(self.me + jump, self.n)
        slot = peer if arrival else self.me
        return pltpu.make_async_remote_copy(
            src_ref=self.source,
            dst_ref=self.target.at[slot],
            send_sem=self.send.at[jump],
            recv_sem=self.recv.at[slot],
            device_id={self.axis: peer},
            device_id_type=MESH,
        )


def store_shuffled(work, full_ref, line, here, order):
    rows, width = work.shape
    folds = width // order.width
    pieces = len(order.pieces)
    orders = [fold * pieces + piece for fold in range(folds) for piece in order.pieces]

    def load(group):
        return work[:, group * BLK : (group + 1) * BLK]

    def store(group, value):
        full_ref[line.at, here, group * BLK : (group + 1) * BLK] = value.astype(bf16)

    reorder(load, store, rows, width, orders)


def leave_kernel(weights, summed, inner, inner_counts, *refs):
    refs = Refs(refs)
    n_dp = lax.axis_size("dp")
    slots_ref = refs.take()
    row_refs = refs.take(len(weights))
    term_ref = refs.take() if summed else None
    inner_refs = refs.take(inner_counts[0])
    out_refs = refs.take(len(weights))
    sum_ref = refs.take() if summed else None
    inner_refs += refs.take(inner_counts[1])
    inner_refs += refs.take(inner_counts[2])
    greet_all()
    if summed:
        cut, parts, send, recv, total, others, send2, recv2 = refs.take(8)
        share = cut.shape[2]
        for index in range(n_dp):
            cut[index] = term_ref[:, index * share : (index + 1) * share]
        term_swap = Swap("dp", cut, parts, send, recv)
        term_swap.start()
        term_swap.keep()
    shares = []
    for row_ref, (split, _, _) in zip(row_refs, weights):
        if split:
            held, *sems = refs.take(3)
            share = Swap("fsdp", row_ref, held, *sems)
            share.start()
            share.keep()
            shares.append(share)
        else:
            shares.append(None)
    if summed:
        term_swap.wait()
        total[...] = jnp.sum(parts[...], axis=0)
        total_spread = Spread("fsdp", total, others, send2, recv2)
        total_spread.start()
        others[total_spread.me] = total[...]
    swaps = []
    for row_ref, out_ref, share, (split, capacity, first) in zip(
        row_refs, out_refs, shares, weights
    ):
        if split:
            share.wait()
        rows = share.target if split else row_ref
        cut, *sems, blocks = refs.take(4)
        columns = rows.shape[2] // BLK
        for part in range(rows.shape[0]):
            for column in range(columns):
                blocks[part * columns + column] = rows[part, :, column * BLK : (column + 1) * BLK]
        swap = Swap("dp", cut, out_ref, *sems)
        for owner in range(n_dp):

            for position in range(capacity):
                slot = first + owner * capacity + position
                value = blocks[slots_ref[0, slot]].astype(f32)
                live = slots_ref[1, slot].astype(f32)
                cut[owner, :, position * BLK : (position + 1) * BLK] = (value * live).astype(bf16)
        swap.start()
        swap.keep()
        swaps.append(swap)
    if inner is not None:
        inner(*inner_refs)
    if summed:
        total_spread.wait()
        sum_ref[...] = jnp.sum(others[...], axis=0)
    for swap in swaps:
        swap.wait()
    for one in [*swaps, *shares]:
        if one is not None:
            one.finish()
    if summed:
        term_swap.finish()
        total_spread.finish()


def fetch_columns(source, index, target, sem):
    columns = target.shape[1]
    return pltpu.make_async_copy(source.at[:, pl.ds(index * columns, columns)], target, sem)


def forward_kernel(n, order, half, wide, att_ref, outs_hbm, base_ref, norm_ref, *rest):
    if wide:
        next_hbm, middle_ref, full_ref, result_ref = rest[:4]
        *rest, next_ref, next_sem = rest[4:]
    else:
        middle_ref, full_ref = rest[:2]
        rest = rest[2:]
    part, held, work, s_send, s_recv, b_send, b_recv, outs_ref, outs_sem = rest
    rows, width = base_ref.shape
    step = rows // SUBS
    load_outs = fetch_columns(outs_hbm, half, outs_ref, outs_sem)
    load_outs.start()
    if wide:
        load_next = fetch_columns(next_hbm, 3, next_ref, next_sem)
        load_next.start()
    line = Line(n, rows, step)
    line.greet()
    load_outs.wait()
    sums = Sums(line, part, held, s_send, s_recv)
    blocks = Blocks(line, full_ref, b_send, b_recv)

    def multiply(columns):
        product = dot(att_ref[...], outs_ref[:, columns]).astype(bf16)
        part[:, :, columns] = product.reshape(n, rows, -1)

    by_tiles(width, 256, multiply)

    def settle(sub):
        here = line.part(sub)
        sums.total(sub, work)
        middle = base_ref[here].astype(f32) + work[...]
        middle_ref[here] = middle
        normed, _ = normalize(middle)
        work[...] = normed * norm_ref[0:1] + norm_ref[1:2]

        def load(group):
            return work[:, group * BLK : (group + 1) * BLK]

        def store(group, value):
            full_ref[line.at, here, group * BLK : (group + 1) * BLK] = value.astype(bf16)

        reorder(load, store, step, width, order)
        blocks.start(sub)

    relay(n, [sums], blocks, settle)
    if wide:
        load_next.wait()

        def multiply_next(columns):
            whole = full_ref[...].reshape(n * rows, width)
            result_ref[:, columns] = dot(whole, next_ref[:, columns]).astype(bf16)

        by_tiles(result_ref.shape[1], 256, multiply_next)


def carry_back(work, plain, order, step, width, middle, base, gain, term_ref, first):
    def load(group):
        return work[:, group * BLK : (group + 1) * BLK]

    def store(group, value):
        plain[:, group * BLK : (group + 1) * BLK] = value

    reorder(load, store, step, width, order)
    back_hidden = plain[...]
    normed, inverse = normalize(middle)
    gain_term = jnp.sum(back_hidden * normed, axis=0, keepdims=True)
    bias_term = jnp.sum(back_hidden, axis=0, keepdims=True)
    if first:
        term_ref[...] = jnp.zeros_like(term_ref)
        term_ref[0:1] = gain_term
        term_ref[1:2] = bias_term
    else:
        term_ref[0:1] += gain_term
        term_ref[1:2] += bias_term
    return base + norm_back(back_hidden, normed, inverse, gain)


def back_kernel(
    n, order, column, half, dy_ref, w_hbm, base_ref, middle_ref, norm_ref, outs_hbm, *rest
):
    carry_ref, full_ref, att_ref, term_ref = rest[:4]
    part, held, work, plain, s_send, s_recv, b_send, b_recv = rest[4:12]
    w_ref, w_sem, outs_ref, outs_sem = rest[12:]
    rows, width = base_ref.shape
    step = rows // SUBS
    load_w = fetch_columns(w_hbm, column, w_ref, w_sem)
    load_w.start()
    load_outs = fetch_columns(outs_hbm, half, outs_ref, outs_sem)
    load_outs.start()
    line = Line(n, rows, step)
    line.greet()
    load_w.wait()
    sums = Sums(line, part, held, s_send, s_recv)
    blocks = Blocks(line, full_ref, b_send, b_recv)

    def multiply(columns):
        product = dot_nt(dy_ref[...], w_ref[columns]).astype(bf16)
        part[:, :, columns] = product.reshape(n, rows, -1)

    by_tiles(width, 256, multiply)

    def settle(sub):
        here = line.part(sub)
        sums.total(sub, work)
        carry = carry_back(
            work,
            plain,
            order,
            step,
            width,
            middle_ref[here].astype(f32),
            base_ref[here].astype(f32),
            norm_ref[0:1],
            term_ref,
            sub == 0,
        )
        carry_ref[here] = carry
        full_ref[line.at, here] = carry.astype(bf16)
        blocks.start(sub)

    relay(n, [sums], blocks, settle)
    load_outs.wait()

    def multiply_next(columns):
        whole = full_ref[...].reshape(n * rows, width)
        att_ref[:, columns] = dot_nt(whole, outs_ref[columns]).astype(bf16)

    by_tiles(att_ref.shape[1], 256, multiply_next)


def last_kernel(n, order, dy_ref, w_hbm, base_ref, tokens, norm_ref, branch, middle, *rest):
    grad_ref, result_ref, term_ref = rest[:3]
    part, held, held2, work, plain, s_send, s_recv, r_send, r_recv, w_ref, w_sem = rest[3:]
    rows, width = base_ref.shape
    step = rows // SUBS
    load_w = fetch_columns(w_hbm, 0, w_ref, w_sem)
    load_w.start()
    line = Line(n, rows, step)
    load_w.wait()
    sums = Sums(line, part, held, s_send, s_recv)
    results = Sums(line, branch, held2, r_send, r_recv)

    def multiply(columns):
        product = dot_nt(dy_ref[...], w_ref[columns]).astype(bf16)
        part[:, :, columns] = product.reshape(n, rows, -1)

    by_tiles(width, 256, multiply)

    def settle(sub):
        here = line.part(sub)
        sums.total(sub, work)
        carry = carry_back(
            work,
            plain,
            order,
            step,
            width,
            tokens[here].astype(f32),
            base_ref[here],
            norm_ref[0:1],
            term_ref,
            sub == 0,
        )
        grad_ref[here] = carry.astype(bf16)
        results.total(sub, work)
        result_ref[here] = (middle[here] + work[...]).astype(bf16)

    relay(n, [sums, results], None, settle)


VMEM_CAP = 52 * 1024 * 1024


def in_place():
    return pl.BlockSpec(memory_space=pl.ANY)


def whole_vmem():
    return pl.BlockSpec(memory_space=pltpu.VMEM)


def sem_pair(n, subs):
    return [pltpu.SemaphoreType.DMA((2, n, subs)), pltpu.SemaphoreType.DMA((2, n, subs))]


def line_call(kernel, name, ident, outs, specs, scratch, flops, moved):
    return pl.pallas_call(
        kernel,
        name=name,
        out_shape=outs,
        in_specs=specs,
        out_specs=jax.tree.map(lambda _: whole_vmem(), outs),
        scratch_shapes=scratch,
        compiler_params=pltpu.CompilerParams(
            collective_id=ident, has_side_effects=True, vmem_limit_bytes=VMEM_CAP
        ),
        cost_estimate=pl.CostEstimate(flops=flops, bytes_accessed=moved, transcendentals=0),
    )


def shape(dims, kind):
    return jax.ShapeDtypeStruct(dims, kind)


LINK_COST = 4_000_000


class Order:
    def __init__(self, pieces, width):
        self.pieces, self.width = pieces, width


def swap_sems(n):
    return [pltpu.SemaphoreType.DMA((n,)), pltpu.SemaphoreType.DMA((n,))]


def enter_call(name, ident, slots, weights, gathers, norms, normed, hidden, n, n_dp, width):
    chunk = weights[0][0].shape[0] // n_dp
    outs, scratch = [], []
    for array, places, split, _ in weights:
        parts = n if split else 1
        outs.append(shape((parts, chunk, len(places) // parts * BLK), bf16))
        scratch += [pltpu.VMEM(array.shape, f32), pltpu.SemaphoreType.DMA]
    if normed:
        scratch += [pltpu.VMEM((n_dp, *norms.shape), f32), *swap_sems(n_dp)]
    for array, _ in gathers:
        rows = array.shape[0]
        outs.append(shape((n, *array.shape), array.dtype))
        scratch += sem_pair(n, SUBS if rows >= 16 * SUBS else 1)
    if normed:
        outs.append(shape((norms.shape[0], n_dp * norms.shape[1]), f32))
    for array, _, _, _ in weights:
        slots_shape = (n_dp, array.shape[1] // BLK, chunk, BLK)
        scratch += [pltpu.VMEM(slots_shape, bf16)] * 2 + swap_sems(n_dp)
    rows = gathers[0][0].shape[0]
    scratch.append(pltpu.VMEM((rows // SUBS if hidden else 8, width), f32))
    for array, moved in gathers[1 if hidden else 0 :]:
        if moved:
            scratch.append(pltpu.VMEM(array.shape, f32))
    for index, (_, places, split, _) in enumerate(weights):
        if split:
            scratch += [pltpu.VMEM(outs[index].shape, bf16), *swap_sems(n)]
    args = [slots, *(weight[0] for weight in weights), *(gather[0] for gather in gathers)]
    specs = [pl.BlockSpec(memory_space=pltpu.SMEM)] + [in_place()] * len(weights)
    specs += [whole_vmem()] * len(gathers)
    if normed or hidden:
        args.append(norms)
        specs.append(whole_vmem())
    kernel = functools.partial(
        enter_kernel,
        [weight[1:] for weight in weights],
        [gather[1] for gather in gathers],
        Order(shuffle_order(n, n_dp), width),
        normed,
        hidden,
    )
    return line_call(kernel, name, ident, outs, specs, scratch, 0, LINK_COST)(*args)


def leave_call(name, ident, slots, weights, term, n, n_dp, inner=None):
    outs, scratch = [], []
    specs = [pl.BlockSpec(memory_space=pltpu.SMEM)] + [whole_vmem()] * len(weights)
    args = [slots, *(weight[0] for weight in weights)]
    chunk = weights[0][0].shape[1]
    if term is not None:
        args.append(term)
        specs.append(whole_vmem())
        block = (term.shape[0], term.shape[1] // n_dp)
    counts = (0, 0, 0)
    run = None
    if inner is not None:
        run, inner_args, inner_specs, inner_outs, inner_scratch = inner
        counts = (len(inner_args), len(inner_outs), len(inner_scratch))
        args += inner_args
        specs += inner_specs
        scratch += inner_scratch
    if term is not None:
        scratch += [pltpu.VMEM((n_dp, *block), f32)] * 2 + swap_sems(n_dp)
        scratch += [pltpu.VMEM(block, f32), pltpu.VMEM((n, *block), f32), *swap_sems(n)]
    for rows, split, _, _ in weights:
        if split:
            scratch += [pltpu.VMEM(rows.shape, bf16), *swap_sems(n)]
    for rows, _, capacity, _ in weights:
        slots_shape = (n_dp, chunk, capacity * BLK)
        outs.append(shape(slots_shape, bf16))
        scratch += [pltpu.VMEM(slots_shape, bf16), *swap_sems(n_dp)]
        blocks = rows.shape[0] * rows.shape[2] // BLK
        scratch.append(pltpu.VMEM((blocks, chunk, BLK), bf16))
    if term is not None:
        outs.append(shape(block, f32))
    if inner is not None:
        outs += inner_outs
    kernel = functools.partial(
        leave_kernel, [weight[1:] for weight in weights], term is not None, run, counts
    )
    return line_call(kernel, name, ident, outs, specs, scratch, 0, LINK_COST)(*args)


def forward_call(attended, outs_z, half, base, norm_rows, after, n, n_dp, ident):
    rows, width = base.shape
    share = outs_z.shape[0]
    outs = [shape((rows, width), f32), shape((n, rows, width), bf16)]
    specs = [whole_vmem(), in_place(), whole_vmem(), whole_vmem()]
    args = [attended, outs_z, base, norm_rows]
    scratch = [
        pltpu.VMEM((n, rows, width), bf16),
        pltpu.VMEM((2, n, rows, width), bf16),
        pltpu.VMEM((rows // SUBS, width), f32),
        *sem_pair(n, SUBS),
        *sem_pair(n, SUBS),
        pltpu.VMEM((share, width), bf16),
        pltpu.SemaphoreType.DMA,
    ]
    if after is not None:
        outs.append(shape((n * rows, share), bf16))
        specs.append(in_place())
        args.append(after)
        scratch += [pltpu.VMEM((width, share), bf16), pltpu.SemaphoreType.DMA]
    kernel = functools.partial(forward_kernel, n, shuffle_order(n, n_dp), half, after is not None)
    call = line_call(kernel, f"forward{half}", ident, outs, specs, scratch, 0, LINK_COST)
    return call(*args)


def back_call(dy, weight, column, base, middle, norm_rows, outs_z, half, n, n_dp, ident):
    rows, width = base.shape
    share = outs_z.shape[0]
    outs = [
        shape((rows, width), f32),
        shape((n, rows, width), bf16),
        shape((n * rows, share), bf16),
        shape((8, width), f32),
    ]
    specs = [
        whole_vmem(),
        in_place(),
        whole_vmem(),
        whole_vmem(),
        whole_vmem(),
        in_place(),
    ]
    scratch = [
        pltpu.VMEM((n, rows, width), bf16),
        pltpu.VMEM((2, n, rows, width), bf16),
        pltpu.VMEM((rows // SUBS, width), f32),
        pltpu.VMEM((rows // SUBS, width), f32),
        *sem_pair(n, SUBS),
        *sem_pair(n, SUBS),
        pltpu.VMEM((width, dy.shape[1]), bf16),
        pltpu.SemaphoreType.DMA,
        pltpu.VMEM((share, width), bf16),
        pltpu.SemaphoreType.DMA,
    ]
    kernel = functools.partial(back_kernel, n, unshuffle_order(n, n_dp), column, half)
    call = line_call(kernel, f"back{half}", ident, outs, specs, scratch, 0, LINK_COST)
    return call(dy, weight, base, middle, norm_rows, outs_z)


def last_parts(dy, weight, base, tokens, norm_rows, branch, middle, n, n_dp):
    rows, width = base.shape
    outs = [
        shape((rows, width), bf16),
        shape((rows, width), bf16),
        shape((8, width), f32),
    ]
    specs = [whole_vmem(), in_place()] + [whole_vmem()] * 5
    scratch = [
        pltpu.VMEM((n, rows, width), bf16),
        pltpu.VMEM((2, n, rows, width), bf16),
        pltpu.VMEM((2, n, rows, width), bf16),
        pltpu.VMEM((rows // SUBS, width), f32),
        pltpu.VMEM((rows // SUBS, width), f32),
        *sem_pair(n, SUBS),
        *sem_pair(n, SUBS),
        pltpu.VMEM((width, dy.shape[1]), bf16),
        pltpu.SemaphoreType.DMA,
    ]
    kernel = functools.partial(last_kernel, n, unshuffle_order(n, n_dp))
    return kernel, [dy, weight, base, tokens, norm_rows, branch, middle], specs, outs, scratch


def attend_forward(query, keys, values, mask_ref, keyed, att_ref, share_ref):
    packed, rows, _ = mask_ref.shape
    heads = att_ref.shape[1] // HEAD
    for p in range(packed):
        here = slice(p * rows, (p + 1) * rows)
        there = here if keyed else slice(None)
        for h in range(heads):
            columns = slice(h * HEAD, (h + 1) * HEAD)
            scores = dot_nt(query[here, columns], keys[there, columns]) * HEAD ** (-0.5)
            scores = jnp.where(mask_ref[p] > 0, scores, score_floor)
            powers = jnp.exp(scores - jnp.max(scores, axis=-1, keepdims=True))
            shares = powers / jnp.sum(powers, axis=-1, keepdims=True)
            share_ref[p * heads + h] = shares
            att_ref[here, columns] = dot(shares.astype(bf16), values[there, columns]).astype(bf16)


def attend_backward(query, keys, values, share_ref, back_ref, rows, keyed, put_query, put_pair):
    heads = back_ref.shape[1] // HEAD
    packed = back_ref.shape[0] // rows
    score_scale = HEAD ** (-0.5)
    for h in range(heads):
        columns = slice(h * HEAD, (h + 1) * HEAD)
        key_grad = value_grad = None
        for p in range(packed):
            here = slice(p * rows, (p + 1) * rows)
            there = here if keyed else slice(None)
            shares = share_ref[p * heads + h]
            back = back_ref[here, columns]
            back_shares = dot_nt(back, values[there, columns])
            inner_sum = jnp.sum(shares * back_shares, axis=-1, keepdims=True)
            back_scores = (shares * (back_shares - inner_sum)).astype(bf16)
            put_query(here, columns, dot(back_scores, keys[there, columns]) * score_scale)
            key_term = dot_tn(back_scores, query[here, columns]) * score_scale
            value_term = dot_tn(shares.astype(bf16), back)
            if keyed:
                put_pair(there, columns, key_term, value_term)
            else:
                key_grad = key_term if key_grad is None else key_grad + key_term
                value_grad = value_term if value_grad is None else value_grad + value_term
        if not keyed:
            put_pair(slice(None), columns, key_grad, value_grad)


def self_forward_kernel(h_ref, w_ref, mask_ref, proj_ref, att_ref, share_ref):
    tile = pl.program_id(0)
    proj_ref[tile] = dot(h_ref[...], w_ref[...]).astype(bf16)

    @pl.when(tile == 2)
    def _():
        attend_forward(
            proj_ref.at[0], proj_ref.at[1], proj_ref.at[2], mask_ref, True, att_ref, share_ref
        )


def cross_forward_kernel(cq_ref, text_ref, w_ref, mask_ref, kv_ref, att_ref, share_ref, total):
    tile = pl.program_id(0)
    product = dot(text_ref[...], w_ref[...])

    @pl.when(tile < 2)
    def _():
        total[tile] = product

    @pl.when(tile >= 2)
    def _():
        kv_ref[tile - 2] = (total[tile - 2] + product).astype(bf16)

    @pl.when(tile == 3)
    def _():
        attend_forward(cq_ref, kv_ref.at[0], kv_ref.at[1], mask_ref, False, att_ref, share_ref)


def ffn_kernel(h_ref, up_ref, down_ref, grad_ref, du_ref, branch_ref, gup_ref, gdown_ref, total):
    tile = pl.program_id(0)
    up_values = dot(h_ref[...], up_ref[...])
    chance = 0.5 * (1.0 + lax.erf(up_values * 0.5**0.5))
    density = jnp.exp(-0.5 * up_values * up_values) * 0.3989422804014327
    activated = (up_values * chance).astype(bf16)
    back_act = dot_nt(grad_ref[...], down_ref[...])
    back_up = (back_act * (chance + up_values * density)).astype(bf16)
    du_ref[...] = back_up
    gup_ref[...] = dot_tn(h_ref[...], back_up).astype(bf16)
    gdown_ref[...] = dot_tn(activated, grad_ref[...]).astype(bf16)

    @pl.when(tile == 0)
    def _():
        total[...] = dot(activated, down_ref[...])

    @pl.when(tile > 0)
    def _():
        total[...] += dot(activated, down_ref[...])

    @pl.when(tile == 3)
    def _():
        branch_ref[...] = total[...].astype(bf16)


def cross_back_kernel(
    rows, back_ref, cq_ref, kv_ref, share_ref, text_ref, dcq_ref, grad_ref, pairs
):
    share = cq_ref.shape[1]

    @pl.when(pl.program_id(0) == 0)
    def _():
        def put_query(here, columns, value):
            dcq_ref[here, columns] = value.astype(bf16)

        def put_pair(there, columns, key_grad, value_grad):
            pairs[there, columns] = key_grad.astype(bf16)
            after_keys = slice(share + columns.start, share + columns.stop)
            pairs[there, after_keys] = value_grad.astype(bf16)

        attend_backward(
            cq_ref, kv_ref.at[0], kv_ref.at[1], share_ref, back_ref, rows, False, put_query, put_pair
        )

    grad_ref[...] = dot_tn(text_ref[...], pairs[...]).astype(bf16)


def outs_grad_kernel(att1_ref, carry1_ref, att2_ref, carry2_ref, grad_ref):
    tile = pl.program_id(0)

    @pl.when(tile == 0)
    def _():
        grad_ref[...] = dot_tn(att1_ref[...], carry1_ref[...]).astype(bf16)

    @pl.when(tile == 1)
    def _():
        grad_ref[...] = dot_tn(att2_ref[...], carry2_ref[...]).astype(bf16)


def self_back_kernel(
    rows, back_ref, proj_ref, share_ref, h1_ref, h2_ref, dcq_ref, dproj_ref, grad_ref, parts
):
    tile = pl.program_id(0)
    share = dcq_ref.shape[1]

    @pl.when(tile == 0)
    def _():
        def put(part, here, columns, value):
            value = value.astype(bf16)
            parts[part, here, columns] = value
            dproj_ref[here, part * share + columns.start : part * share + columns.stop] = value

        def put_query(here, columns, value):
            put(0, here, columns, value)

        def put_pair(there, columns, key_grad, value_grad):
            put(1, there, columns, key_grad)
            put(2, there, columns, value_grad)

        attend_backward(
            proj_ref.at[0],
            proj_ref.at[1],
            proj_ref.at[2],
            share_ref,
            back_ref,
            rows,
            True,
            put_query,
            put_pair,
        )

    @pl.when(tile < 3)
    def _():
        grad_ref[...] = dot_tn(h1_ref[...], parts[tile]).astype(bf16)

    @pl.when(tile == 3)
    def _():
        grad_ref[...] = dot_tn(h2_ref[...], dcq_ref[...]).astype(bf16)


def fixed(dims):
    return pl.BlockSpec(dims, lambda t: (0,) * len(dims))


def moving(dims, index):
    return pl.BlockSpec(dims, lambda t: (0, index(t)))


def local_call(kernel, name, tiles, outs, specs, out_specs, scratch, flops, moved):
    return pl.pallas_call(
        kernel,
        name=name,
        grid=(tiles,),
        out_shape=outs,
        in_specs=specs,
        out_specs=out_specs,
        scratch_shapes=scratch,
        compiler_params=pltpu.CompilerParams(vmem_limit_bytes=VMEM_CAP),
        cost_estimate=pl.CostEstimate(
            flops=flops // 8, bytes_accessed=moved // 8, transcendentals=0
        ),
    )


def self_forward(hidden, query_z, mask):
    tokens, width = hidden.shape
    share = query_z.shape[1] // 4
    packed, rows, _ = mask.shape
    pairs = (packed * share // HEAD, rows, rows)
    return local_call(
        self_forward_kernel,
        "self_forward",
        3,
        (shape((3, tokens, share), bf16), shape((tokens, share), bf16), shape(pairs, f32)),
        [fixed(hidden.shape), moving((width, share), lambda t: t), fixed(mask.shape)],
        (fixed((3, tokens, share)), fixed((tokens, share)), fixed(pairs)),
        [],
        6 * tokens * width * share,
        20_000_000,
    )(hidden, query_z, mask)


def cross_forward(cross_query, text_all, text_z, mask):
    tokens, share = cross_query.shape
    texts = text_all.shape[0]
    width = text_z.shape[0]
    packed, rows, _ = mask.shape
    pairs = (packed * share // HEAD, rows, texts)
    return local_call(
        cross_forward_kernel,
        "cross_forward",
        4,
        (shape((2, texts, share), bf16), shape((tokens, share), bf16), shape(pairs, f32)),
        [
            fixed(cross_query.shape),
            moving((texts, width), lambda t: t // 2),
            moving((width, share), lambda t: t),
            fixed(mask.shape),
        ],
        (fixed((2, texts, share)), fixed((tokens, share)), fixed(pairs)),
        [pltpu.VMEM((2, texts, share), f32)],
        8 * texts * width * share,
        20_000_000,
    )(cross_query, text_all, text_z, mask)


def ffn(hidden, up_z, down_z, grad_all):
    tokens, width = hidden.shape
    share = down_z.shape[0]
    return local_call(
        ffn_kernel,
        "ffn",
        4,
        (
            shape((tokens, 4 * share), bf16),
            shape((tokens, width), bf16),
            shape(up_z.shape, bf16),
            shape(down_z.shape, bf16),
        ),
        [
            fixed(hidden.shape),
            moving((width, share), lambda t: t),
            moving((share, width), lambda t: t),
            fixed(grad_all.shape),
        ],
        (
            moving((tokens, share), lambda t: t),
            fixed((tokens, width)),
            moving((width, share), lambda t: t),
            moving((share, width), lambda t: t),
        ),
        [pltpu.VMEM((tokens, width), f32)],
        40 * tokens * width * share,
        60_000_000,
    )(hidden, up_z, down_z, grad_all)


def cross_back(back_attended, cross_query, text_pairs, shares, text_all, rows):
    tokens, share = cross_query.shape
    texts = text_all.shape[0]
    width = text_all.shape[1] // 2
    return local_call(
        functools.partial(cross_back_kernel, rows),
        "cross_back",
        2,
        (shape((tokens, share), bf16), shape((width, 4 * share), bf16)),
        [
            fixed(back_attended.shape),
            fixed(cross_query.shape),
            fixed(text_pairs.shape),
            fixed(shares.shape),
            moving((texts, width), lambda t: t),
        ],
        (fixed((tokens, share)), moving((width, 2 * share), lambda t: t)),
        [pltpu.VMEM((texts, 2 * share), bf16)],
        8 * texts * width * share,
        20_000_000,
    )(back_attended, cross_query, text_pairs, shares, text_all)


def outs_grad(attended1, carry1, attended2, carry2):
    tokens, share = attended1.shape
    width = carry1.shape[1]
    return local_call(
        outs_grad_kernel,
        "outs_grad",
        2,
        shape((share, 2 * width), bf16),
        [fixed((tokens, share)), fixed((tokens, width))] * 2,
        moving((share, width), lambda t: t),
        [],
        4 * tokens * width * share,
        10_000_000,
    )(attended1, carry1, attended2, carry2)


def self_back(back_attended, projected, shares, hidden1, hidden2, back_cross, rows):
    tokens, width = hidden1.shape
    share = back_cross.shape[1]
    return local_call(
        functools.partial(self_back_kernel, rows),
        "self_back",
        4,
        (shape((tokens, 3 * share), bf16), shape((width, 4 * share), bf16)),
        [
            fixed(back_attended.shape),
            fixed(projected.shape),
            fixed(shares.shape),
            fixed(hidden1.shape),
            fixed(hidden2.shape),
            fixed(back_cross.shape),
        ],
        (fixed((tokens, 3 * share)), moving((width, share), lambda t: t)),
        [pltpu.VMEM((3, tokens, share), bf16)],
        8 * tokens * width * share,
        25_000_000,
    )(back_attended, projected, shares, hidden1, hidden2, back_cross)


def block_slots(owners):
    owner = jnp.concatenate(owners)
    weight = jnp.concatenate([jnp.full(one.shape, at, jnp.int32) for at, one in enumerate(owners)])
    mark = owner + weight * 1024
    count = mark.shape[0]
    earlier = lax.broadcasted_iota(jnp.int32, (count, count), 1) < lax.broadcasted_iota(
        jnp.int32, (count, count), 0
    )
    same = jnp.logical_and(mark[:, None] == mark[None, :], earlier)
    return jnp.stack([owner, jnp.sum(same.astype(jnp.int32), axis=1)])


def slot_contents(owners, slots, places, capacities, firsts, n_dp):
    rows = []
    for owner, place, capacity, first in zip(owners, places, capacities, firsts):
        count = owner.shape[0]
        at = owner * capacity + slots[1, first : first + count]
        hit = at[None, :] == lax.broadcasted_iota(jnp.int32, (n_dp * capacity, count), 0)
        block = lax.broadcasted_iota(jnp.int32, (n_dp * capacity, count), 1)
        per_group, per_part, split = place_rule(place)
        part = block % per_group // per_part if split else block * 0
        column = block // per_group * per_part + block % per_part if split else block
        index = part * (count // (per_group // per_part)) + column if split else column
        rows.append(
            jnp.stack([jnp.sum(jnp.where(hit, value, 0), axis=1) for value in (index, block * 0 + 1)])
        )
    return jnp.concatenate(rows, axis=1)


def place_rule(place):
    parts = 1 + max(part for part, _ in place)
    if parts == 1:
        return 0, 0, False
    per_part = sum(1 for part, _ in place[:HEADS] if part == 0)
    return per_part * parts, per_part, True


def after(small, first):
    return lax.optimization_barrier((small, first))[0]


def body(
    tokens_in,
    text_in,
    seg_ids,
    capt_ids,
    grad_out,
    owner_query,
    owner_up,
    owner_outs,
    owner_text,
    owner_down,
    w_query,
    m_query,
    v_query,
    w_up,
    m_up,
    v_up,
    w_outs,
    m_outs,
    v_outs,
    w_text,
    m_text,
    v_text,
    w_down,
    m_down,
    v_down,
    norm_weight,
    m_norm,
    v_norm,
):
    n_dp = lax.axis_size("dp")
    n_z = lax.axis_size("fsdp")
    width = tokens_in.shape[1]
    own_rows = w_query.shape[0]
    chunk = own_rows // n_dp
    cap_big = w_query.shape[1] // BLK
    cap_out = w_outs.shape[1] // BLK
    heads_z = HEADS // n_z
    share = width // n_z
    owner_query, owner_up, owner_outs, owner_text, owner_down = (
        owner[:, 0] for owner in (owner_query, owner_up, owner_outs, owner_text, owner_down)
    )
    split_places = [split_place(b, heads_z, n_z) for b in range(owner_query.shape[0])]
    big_places = [flat_place(b) for b in range(owner_down.shape[0])]
    out_places = [flat_place(b) for b in range(owner_outs.shape[0])]
    owners = (owner_query, owner_outs, owner_text, owner_up, owner_down)
    places = (split_places, out_places, split_places, split_places, big_places)
    capacities = (cap_big, cap_out, cap_big, cap_big, cap_big)
    firsts = [sum(len(one) for one in places[:index]) for index in range(5)]
    slot_firsts = [sum(capacities[:index]) * n_dp for index in range(5)]
    slots = block_slots(owners)
    contents = slot_contents(owners, slots, places, capacities, firsts, n_dp)

    def spread(rows):
        return lax.all_gather(rows.reshape(-1, rows.shape[-1]), "dp", axis=0, tiled=True)

    def gather_sum(piece, parts):
        summed = lax.psum_scatter(piece, "dp", scatter_dimension=0, tiled=True)
        return summed.reshape(parts, chunk, -1)

    token_count = tokens_in.shape[0]
    marks = jnp.concatenate([seg_ids, capt_ids], axis=1)
    marks = jnp.pad(marks, ((0, 7), (0, 256 - marks.shape[1])))
    norms = jnp.pad(norm_weight, ((0, 2), (0, 0)))
    query_rows, marks, norm_full = enter_call(
        "enter_query",
        0,
        slots,
        [(w_query, split_places, True, firsts[0])],
        [(marks, False)],
        norms,
        True,
        False,
        n_z,
        n_dp,
        width,
    )
    outs_rows, hidden1, text_all = enter_call(
        "enter_outs",
        6,
        slots,
        [(w_outs, out_places, False, firsts[1])],
        [(tokens_in, True), (text_in, True)],
        norm_full[0:2],
        False,
        True,
        n_z,
        n_dp,
        width,
    )
    query_z, outs_z = spread(query_rows), spread(outs_rows)
    hidden1 = hidden1.reshape(-1, width)
    text_all = text_all.reshape(-1, text_in.shape[1])
    segment = marks[:, 0, :token_count]
    caption = marks[:, 0, token_count : token_count + capt_ids.shape[1]]
    self_mask = (segment[:, :, None] == segment[:, None, :]).astype(jnp.int32)
    text_row = lax.broadcasted_iota(jnp.int32, caption.shape, 0).reshape(1, 1, -1)
    packed_row = lax.broadcasted_iota(jnp.int32, (n_z, 1, 1), 0)
    cross_mask = jnp.logical_and(
        segment[:, :, None] == caption.reshape(1, 1, -1), packed_row == text_row
    ).astype(jnp.int32)

    projected, attended1, shares1 = self_forward(hidden1, query_z, self_mask)
    text_rows, up_rows, down_rows, grad_all = enter_call(
        "enter_rest",
        7,
        after(slots, attended1),
        [
            (w_text, split_places, True, firsts[2]),
            (w_up, split_places, True, firsts[3]),
            (w_down, big_places, False, firsts[4]),
        ],
        [(grad_out, False)],
        None,
        False,
        False,
        n_z,
        n_dp,
        width,
    )
    grad_all = grad_all.reshape(-1, width)
    text_z, up_z, down_z = spread(text_rows), spread(up_rows), spread(down_rows)
    middle1, hidden2, cross_query = forward_call(
        attended1, outs_z, 0, tokens_in, after(norm_full[2:4], up_rows), query_z, n_z, n_dp, 1
    )
    hidden2 = hidden2.reshape(-1, width)
    text_pairs, attended2, shares2 = cross_forward(cross_query, text_all, text_z, cross_mask)
    middle2, hidden3 = forward_call(
        attended2, outs_z, 1, middle1, norm_full[4:6], None, n_z, n_dp, 2
    )
    hidden3 = hidden3.reshape(-1, width)
    back_up, branch3, up_part, down_part = ffn(hidden3, up_z, down_z, grad_all)
    branch3 = branch3.reshape(n_z, token_count, width)
    down_sum = gather_sum(down_part, 1)
    up_sum = gather_sum(up_part, n_z)
    at_middle2, carry2, back_att2, term3 = back_call(
        back_up, up_z, 0, grad_out, middle2, norm_full[4:6], outs_z, 1, n_z, n_dp, 3
    )
    carry2 = carry2.reshape(-1, width)
    back_cross, text_part = cross_back(
        back_att2, cross_query, text_pairs, shares2, text_all, token_count
    )
    text_sum = gather_sum(text_part, n_z)
    at_middle1, carry1, back_att1, term2 = back_call(
        back_cross, query_z, 3, at_middle2, middle1, norm_full[2:4], outs_z, 0, n_z, n_dp, 4
    )
    carry1 = carry1.reshape(-1, width)
    outs_sum = gather_sum(outs_grad(attended1, carry1, attended2, carry2), 1)
    back_projected, query_part = self_back(
        back_att1, projected, shares1, hidden1, hidden2, back_cross, token_count
    )
    query_sum = gather_sum(query_part, n_z)
    down_grad, up_grad, grad_in, result, term1 = leave_call(
        "leave_up",
        8,
        contents,
        [
            (down_sum, False, cap_big, slot_firsts[4]),
            (up_sum, True, cap_big, slot_firsts[3]),
        ],
        None,
        n_z,
        n_dp,
        last_parts(
            back_projected,
            query_z,
            at_middle1,
            tokens_in,
            norm_full[0:2],
            branch3,
            middle2,
            n_z,
            n_dp,
        ),
    )
    (text_grad,) = leave_call(
        "leave_text",
        5,
        after(contents, term1),
        [(text_sum, True, cap_big, slot_firsts[2])],
        None,
        n_z,
        n_dp,
    )
    text_grad, up_grad, down_grad = (
        grad.reshape(own_rows, -1).astype(f32) for grad in (text_grad, up_grad, down_grad)
    )
    up_new = adamw_update(w_up, m_up, v_up, up_grad, rate_up, decay_rate)
    text_new = adamw_update(w_text, m_text, v_text, text_grad, rate_text, decay_rate)
    down_new = adamw_update(w_down, m_down, v_down, down_grad, rate_down, decay_rate)
    norm_term = jnp.concatenate([term1[:2], term2[:2], term3[:4]], axis=0)
    query_grad, outs_slots, norm_grad = leave_call(
        "leave_query",
        9,
        after(contents, (up_new, down_new, text_new)),
        [
            (query_sum, True, cap_big, slot_firsts[0]),
            (outs_sum, False, cap_out, slot_firsts[1]),
        ],
        norm_term,
        n_z,
        n_dp,
    )
    norm_grad = norm_grad[:6]
    query_grad, outs_slots = (
        grad.reshape(own_rows, -1).astype(f32) for grad in (query_grad, outs_slots)
    )
    query_new = adamw_update(w_query, m_query, v_query, query_grad, rate_query, decay_rate)
    outs_new = adamw_update(w_outs, m_outs, v_outs, outs_slots, rate_outs, decay_rate)
    norm_new = adamw_update(norm_weight, m_norm, v_norm, norm_grad, rate_norm, 0.0)
    return (
        result,
        grad_in,
        *query_new,
        *up_new,
        *outs_new,
        *text_new,
        *down_new,
        *norm_new,
    )


def solution(mesh):
    rows = P(("dp", "fsdp"), None)
    slots = P("fsdp", "dp")
    norms = P(None, "dp")
    in_specs = (rows,) * 5 + (P(),) * 5 + (slots,) * 15 + (norms,) * 3
    out_specs = (rows,) * 2 + (slots,) * 15 + (norms,) * 3
    return jax.shard_map(body, mesh=mesh, in_specs=in_specs, out_specs=out_specs, check_vma=False)
```

```python
import functools

import jax
import jax.numpy as jnp
from jax import lax
from jax.experimental import pallas as pl
from jax.experimental.pallas import tpu as pltpu
from jax.sharding import PartitionSpec as P

HEADS = 16
HEAD = 128
STEP = 10
BLK = 128


beta_first = 0.9
beta_second = 0.999
adam_eps = 1e-08
decay_rate = 0.01
rate_query = 0.04
rate_up = 0.04
rate_outs = 0.12
rate_text = 0.03
rate_down = 0.03
rate_norm = 0.5
norm_eps = 1e-05
score_floor = -1e30
bf16 = jnp.bfloat16
f32 = jnp.float32


def normalize(values):
    centered = values - jnp.mean(values, axis=-1, keepdims=True)
    inverse_std = lax.rsqrt(jnp.mean(centered * centered, axis=-1, keepdims=True) + norm_eps)
    return (centered * inverse_std, inverse_std)


def norm_back(back_hidden, normed, inverse_std, gain_row):
    back_normed = back_hidden * gain_row
    return inverse_std * (
        back_normed
        - jnp.mean(back_normed, axis=-1, keepdims=True)
        - normed * jnp.mean(back_normed * normed, axis=-1, keepdims=True)
    )


def adamw_update(weight, first, second, gradient, rate, decay):
    first_new = beta_first * first + (1.0 - beta_first) * gradient
    second_new = beta_second * second + (1.0 - beta_second) * gradient * gradient
    first_hat = first_new / (1.0 - beta_first**STEP)
    second_hat = second_new / (1.0 - beta_second**STEP)
    weight_new = weight - rate * (first_hat / (jnp.sqrt(second_hat) + adam_eps) + decay * weight)
    return (first_new, second_new, weight_new)


def dot(left, right):
    return jnp.dot(left, right, preferred_element_type=f32)


def dot_nt(left, right):
    return lax.dot_general(left, right, (((1,), (1,)), ((), ())), preferred_element_type=f32)


def dot_tn(left, right):
    return lax.dot_general(left, right, (((0,), (0,)), ((), ())), preferred_element_type=f32)


def split_place(block, per_part, parts):
    group, rest = divmod(block, per_part * parts)
    part, inner = divmod(rest, per_part)
    return part, group * per_part + inner


def flat_place(block):
    return 0, block


MESH = pl.DeviceIdType.MESH


SUBS = 4


class Line:
    def __init__(self, n, rows, step):
        self.n, self.rows, self.step = n, rows, step
        self.at = lax.axis_index("fsdp")

    def has(self, way):
        return self.at < self.n - 1 if way == 0 else self.at > 0

    def peer(self, way):
        index = jnp.clip(self.at + (1 if way == 0 else -1), 0, self.n - 1)
        return {"fsdp": index}

    def greet(self, others=0):
        barrier = pltpu.get_barrier_semaphore()
        for way in (0, 1):

            @pl.when(self.has(way))
            def _():
                pl.semaphore_signal(
                    barrier, inc=1, device_id=self.peer(way), device_id_type=pl.DeviceIdType.MESH
                )

        pl.semaphore_wait(
            barrier, others + self.has(0).astype(jnp.int32) + self.has(1).astype(jnp.int32)
        )

    def copy(self, source, target, send, recv, way):
        return pltpu.make_async_remote_copy(
            src_ref=source,
            dst_ref=target,
            send_sem=send,
            recv_sem=recv,
            device_id=self.peer(way),
            device_id_type=pl.DeviceIdType.MESH,
        )

    def part(self, sub):
        return pl.ds(sub * self.step, self.step)


class Sums:
    def __init__(self, line, part, held, send, recv):
        self.line, self.part, self.held, self.send, self.recv = line, part, held, send, recv

    def move(self, way, target, sub, source):
        line = self.line
        rows = line.part(sub)
        return line.copy(
            source,
            self.held.at[way, target, rows],
            self.send.at[way, target, sub],
            self.recv.at[way, target, sub],
            way,
        )

    def target(self, way, time):
        n, at = self.line.n, self.line.at
        return n - 1 - (time - at) if way == 0 else time - (n - 1 - at)

    def passes(self, way, target):
        n, at = self.line.n, self.line.at
        if way == 0:
            return jnp.logical_and(target > at, target < n)
        return jnp.logical_and(target < at, target >= 0)

    def forward(self, sub, time):
        line = self.line
        rows = line.part(sub)
        for way in (0, 1):
            target = self.target(way, time)
            passes = self.passes(way, target)
            inner = jnp.logical_and(passes, line.has(1 - way))
            outer = jnp.logical_and(passes, jnp.logical_not(line.has(1 - way)))

            @pl.when(outer)
            def _():
                self.move(way, target, sub, self.part.at[target, rows]).start()

            @pl.when(inner)
            def _():
                held = self.held.at[way, target, rows]
                self.move(way, target, sub, held).wait_recv()
                total = held[...].astype(f32) + self.part[target, rows].astype(f32)
                held[...] = total.astype(bf16)
                self.move(way, target, sub, held).start()

    def total(self, sub, sum_ref):
        line = self.line
        rows = line.part(sub)
        sum_ref[...] = self.part[line.at, rows].astype(f32)
        for way in (0, 1):

            @pl.when(line.has(1 - way))
            def _():
                held = self.held.at[way, line.at, rows]
                self.move(way, line.at, sub, held).wait_recv()
                sum_ref[...] += held[...].astype(f32)

    def finish(self):
        line = self.line
        for way in (0, 1):
            for time in range(line.n - 1):
                target = self.target(way, time)

                @pl.when(self.passes(way, target))
                def _():
                    for sub in range(line.rows // line.step):
                        held = self.held.at[way, target, line.part(sub)]
                        self.move(way, target, sub, held).wait_send()


def relay(n, sums, blocks, settle):
    for slot in range((SUBS + 2) * (n - 1)):
        sub, time = divmod(slot, n - 1)
        if sub < SUBS:
            for one in sums:
                one.forward(sub, time)
        if time == 0 and 0 <= sub - 1 < SUBS:
            settle(sub - 1)
        if blocks is not None:
            if time == n - 2 and 0 <= sub - 1 < SUBS:
                blocks.forward(sub - 1, 1)
            if time < n - 2 and 0 <= sub - 2 < SUBS:
                blocks.forward(sub - 2, time + 2)
    for one in sums:
        one.finish()
    if blocks is not None:
        blocks.finish()


class Blocks:
    def __init__(self, line, full, send, recv):
        self.line, self.full, self.send, self.recv = line, full, send, recv

    def move(self, way, source, sub):
        line = self.line
        held = self.full.at[source, line.part(sub)]
        return line.copy(
            held, held, self.send.at[way, source, sub], self.recv.at[way, source, sub], way
        )

    def behind(self, way, source):
        return self.line.at > source if way == 0 else self.line.at < source

    def start(self, sub):
        for way in (0, 1):

            @pl.when(self.line.has(way))
            def _():
                self.move(way, self.line.at, sub).start()

    def forward(self, sub, step):
        line = self.line
        for way in (0, 1):
            source = line.at - step if way == 0 else line.at + step

            @pl.when(jnp.logical_and(source >= 0, source < line.n))
            def _():
                self.move(way, source, sub).wait_recv()

                @pl.when(line.has(way))
                def _():
                    self.move(way, source, sub).start()

    def forward_all(self, sub):
        for step in range(1, self.line.n):
            self.forward(sub, step)

    def finish(self):
        line = self.line
        for way in (0, 1):
            for source in range(line.n):
                ours = jnp.logical_or(self.behind(way, source), line.at == source)

                @pl.when(jnp.logical_and(ours, line.has(way)))
                def _():
                    for sub in range(line.rows // line.step):
                        self.move(way, source, sub).wait_send()


def lane_moves(width, order):
    moves = []
    piece = width // len(order)
    for group in range(width // BLK):
        parts = []
        for offset in range(0, BLK, piece):
            start = order[(group * BLK + offset) // piece] * piece
            parts.append((offset, start // BLK, start % BLK))
        moves.append(parts)
    return piece, moves


def reorder(load, store, rows, width, order):
    piece, moves = lane_moves(width, order)
    lane = lax.broadcasted_iota(jnp.int32, (rows, BLK), 1)
    for group, parts in enumerate(moves):
        value = None
        for offset, source, start in parts:
            block = load(source)
            if start != offset:
                block = pltpu.roll(block, (offset - start) % BLK, 1)
            value = block if value is None else jnp.where(lane >= offset, block, value)
        store(group, value)


def shuffle_order(n_z, n_dp):
    return [z * n_dp + i for i in range(n_dp) for z in range(n_z)]


def unshuffle_order(n_z, n_dp):
    return [i * n_z + z for z in range(n_z) for i in range(n_dp)]


def by_tiles(columns, tile, run):
    def one(index, carry):
        run(pl.ds(pl.multiple_of(index * tile, tile), tile))
        return carry

    lax.fori_loop(0, columns // tile, one, 0)


class Swap:
    def __init__(self, axis, source, target, send, recv):
        self.axis, self.source, self.target = axis, source, target
        self.send, self.recv = send, recv
        self.n = lax.axis_size(axis)
        self.me = lax.axis_index(axis)

    def copy(self, jump, arrival=False):
        peer = lax.rem(self.me + jump, self.n)
        slot = peer if arrival else self.me
        return pltpu.make_async_remote_copy(
            src_ref=self.source.at[peer],
            dst_ref=self.target.at[slot],
            send_sem=self.send.at[jump],
            recv_sem=self.recv.at[slot],
            device_id={self.axis: peer},
            device_id_type=MESH,
        )

    def start(self):
        for jump in range(1, self.n):
            self.copy(jump).start()

    def keep(self):
        self.target[self.me] = self.source[self.me]

    def wait(self):
        for jump in range(1, self.n):
            self.copy(jump, True).wait_recv()

    def finish(self):
        for jump in range(1, self.n):
            self.copy(jump).wait_send()


def greet_all():
    barrier = pltpu.get_barrier_semaphore()
    count = 0
    for axis in ("dp", "fsdp"):
        n, me = lax.axis_size(axis), lax.axis_index(axis)
        count += n - 1
        for jump in range(1, n):
            pl.semaphore_signal(
                barrier, inc=1, device_id={axis: lax.rem(me + jump, n)}, device_id_type=MESH
            )
    pl.semaphore_wait(barrier, count)


class Refs:
    def __init__(self, refs):
        self.refs = list(refs)

    def take(self, count=None):
        taken = self.refs[: 1 if count is None else count]
        self.refs = self.refs[len(taken) :]
        return taken[0] if count is None else taken


def enter_kernel(weights, gathers, order, normed, hidden, inner, inner_counts, *refs):
    refs = Refs(refs)
    n_dp, n_z = lax.axis_size("dp"), lax.axis_size("fsdp")
    slots_ref = refs.take()
    w_refs = refs.take(len(weights))
    in_refs = refs.take(len(gathers))
    norm_in = refs.take() if normed or hidden else None
    inner_refs = refs.take(inner_counts[0])
    row_refs = refs.take(len(weights))
    full_refs = refs.take(len(gathers))
    norm_out = refs.take() if normed else None
    inner_refs += refs.take(inner_counts[1])
    inner_refs += refs.take(inner_counts[2])
    loads = []
    for w_ref in w_refs:
        stage, sem = refs.take(2)
        load = pltpu.make_async_copy(w_ref, stage, sem)
        load.start()
        loads.append((stage, load))
    greet_all()
    if normed:
        parts, *sems = refs.take(3)
        norm_swap = Spread("dp", norm_in, parts, *sems)
        norm_swap.start()
    lines = []
    for in_ref, full_ref in zip(in_refs, full_refs):
        rows = in_ref.shape[0]
        step = rows // pieces_of(rows)
        lines.append(Blocks(Line(n_z, rows, step), full_ref, *refs.take(2)))
    swaps = []
    for (stage, load), (places, split, _) in zip(loads, weights):
        source, target, *sems = refs.take(4)
        swap = Swap("dp", source, target, *sems)
        load.wait()
        chunk = source.shape[2]
        for jump in range(n_dp):
            peer = lax.rem(swap.me + jump, n_dp)
            into = source if jump else target
            for slot in range(source.shape[1]):
                here = pl.ds(pl.multiple_of(peer * chunk, chunk), chunk)
                piece = stage[here, slot * BLK : (slot + 1) * BLK]
                into[peer, slot] = piece.astype(bf16)
            if jump:
                swap.copy(jump).start()
        swaps.append(swap)
    if hidden:
        work = refs.take()
    for index, (in_ref, full_ref, blocks) in enumerate(zip(in_refs, full_refs, lines)):
        line = blocks.line
        if hidden and index == 0:
            for sub in range(line.rows // line.step):
                here = line.part(sub)
                values, _ = normalize(in_ref[here].astype(f32))
                work[...] = values * norm_in[0:1] + norm_in[1:2]
                store_shuffled(work, full_ref, line, here, order)
                blocks.start(sub)
        elif in_ref.dtype == bf16 and gathers[index]:
            work2 = refs.take()
            work2[...] = in_ref[...].astype(f32)
            store_shuffled(work2, full_ref, line, line.part(0), order)
            blocks.start(0)
        else:
            for sub in range(line.rows // line.step):
                here = line.part(sub)
                full_ref[line.at, here] = in_ref[here]
                blocks.start(sub)
    if normed:
        parts[norm_swap.me] = norm_in[...]
        norm_swap.wait()
        share = norm_in.shape[1]
        for index in range(n_dp):
            norm_out[:, index * share : (index + 1) * share] = parts[index]
    if inner is not None:
        inner(*inner_refs)
    shares = []
    for blocks in lines:
        for sub in range(blocks.line.rows // blocks.line.step):
            blocks.forward_all(sub)
    for swap, row_ref, (places, split, first) in zip(swaps, row_refs, weights):
        swap.wait()
        if split:
            cut, *sems = refs.take(3)
            share = Swap("fsdp", cut, row_ref, *sems)
            shares.append(share)
        else:
            cut = row_ref
        for block, (part, column) in enumerate(places):
            owner, slot = slots_ref[0, first + block], slots_ref[1, first + block]
            cut[part, :, column * BLK : (column + 1) * BLK] = swap.target[owner, slot]
        if split:
            share.start()
            share.keep()
    for share in shares:
        share.wait()
    for one in [*swaps, *shares, *lines]:
        one.finish()
    if normed:
        norm_swap.finish()


class Spread(Swap):
    def copy(self, jump, arrival=False):
        peer = lax.rem(self.me + jump, self.n)
        slot = peer if arrival else self.me
        return pltpu.make_async_remote_copy(
            src_ref=self.source,
            dst_ref=self.target.at[slot],
            send_sem=self.send.at[jump],
            recv_sem=self.recv.at[slot],
            device_id={self.axis: peer},
            device_id_type=MESH,
        )


def store_shuffled(work, full_ref, line, here, order):
    rows, width = work.shape
    folds = width // order.width
    pieces = len(order.pieces)
    orders = [fold * pieces + piece for fold in range(folds) for piece in order.pieces]

    def load(group):
        return work[:, group * BLK : (group + 1) * BLK]

    def store(group, value):
        full_ref[line.at, here, group * BLK : (group + 1) * BLK] = value.astype(bf16)

    reorder(load, store, rows, width, orders)


def leave_kernel(weights, summed, inner, inner_counts, *refs):
    refs = Refs(refs)
    n_dp = lax.axis_size("dp")
    slots_ref = refs.take()
    row_refs = refs.take(len(weights))
    term_ref = refs.take() if summed else None
    inner_refs = refs.take(inner_counts[0])
    out_refs = refs.take(len(weights))
    sum_ref = refs.take() if summed else None
    inner_refs += refs.take(inner_counts[1])
    inner_refs += refs.take(inner_counts[2])
    greet_all()
    if summed:
        cut, parts, send, recv, total, others, send2, recv2 = refs.take(8)
        share = cut.shape[2]
        for index in range(n_dp):
            cut[index] = term_ref[:, index * share : (index + 1) * share]
        term_swap = Swap("dp", cut, parts, send, recv)
        term_swap.start()
        term_swap.keep()
    shares = []
    for row_ref, (split, _, _) in zip(row_refs, weights):
        if split:
            held, *sems = refs.take(3)
            share = Swap("fsdp", row_ref, held, *sems)
            share.start()
            share.keep()
            shares.append(share)
        else:
            shares.append(None)
    if summed:
        term_swap.wait()
        total[...] = jnp.sum(parts[...], axis=0)
        total_spread = Spread("fsdp", total, others, send2, recv2)
        total_spread.start()
        others[total_spread.me] = total[...]
    swaps = []
    for row_ref, out_ref, share, (split, capacity, first) in zip(
        row_refs, out_refs, shares, weights
    ):
        if split:
            share.wait()
        rows = share.target if split else row_ref
        cut, *sems, blocks = refs.take(4)
        columns = rows.shape[2] // BLK
        for part in range(rows.shape[0]):
            for column in range(columns):
                blocks[part * columns + column] = rows[part, :, column * BLK : (column + 1) * BLK]
        swap = Swap("dp", cut, out_ref, *sems)
        for owner in range(n_dp):

            for position in range(capacity):
                slot = first + owner * capacity + position
                value = blocks[slots_ref[0, slot]].astype(f32)
                live = slots_ref[1, slot].astype(f32)
                cut[owner, :, position * BLK : (position + 1) * BLK] = (value * live).astype(bf16)
        swap.start()
        swap.keep()
        swaps.append(swap)
    if inner is not None:
        inner(*inner_refs)
    if summed:
        total_spread.wait()
        sum_ref[...] = jnp.sum(others[...], axis=0)
    for swap in swaps:
        swap.wait()
    for one in [*swaps, *shares]:
        if one is not None:
            one.finish()
    if summed:
        term_swap.finish()
        total_spread.finish()


def fetch_columns(source, index, target, sem):
    columns = target.shape[1]
    return pltpu.make_async_copy(source.at[:, pl.ds(index * columns, columns)], target, sem)


def forward_kernel(n, order, half, wide, alone, att_ref, outs_hbm, base_ref, norm_ref, *rest):
    if wide:
        next_hbm, middle_ref, full_ref, result_ref = rest[:4]
        *rest, next_ref, next_sem = rest[4:]
    else:
        middle_ref, full_ref = rest[:2]
        rest = rest[2:]
    part, held, work, s_send, s_recv, b_send, b_recv, outs_ref, outs_sem = rest
    rows, width = base_ref.shape
    step = rows // SUBS
    load_outs = fetch_columns(outs_hbm, half, outs_ref, outs_sem)
    load_outs.start()
    if wide:
        load_next = fetch_columns(next_hbm, 3, next_ref, next_sem)
        load_next.start()
    line = Line(n, rows, step)
    if alone:
        line.greet()
    load_outs.wait()
    sums = Sums(line, part, held, s_send, s_recv)
    blocks = Blocks(line, full_ref, b_send, b_recv)

    def multiply(columns):
        product = dot(att_ref[...], outs_ref[:, columns]).astype(bf16)
        part[:, :, columns] = product.reshape(n, rows, -1)

    by_tiles(width, 256, multiply)

    def settle(sub):
        here = line.part(sub)
        sums.total(sub, work)
        middle = base_ref[here].astype(f32) + work[...]
        middle_ref[here] = middle
        normed, _ = normalize(middle)
        work[...] = normed * norm_ref[0:1] + norm_ref[1:2]

        def load(group):
            return work[:, group * BLK : (group + 1) * BLK]

        def store(group, value):
            full_ref[line.at, here, group * BLK : (group + 1) * BLK] = value.astype(bf16)

        reorder(load, store, step, width, order)
        blocks.start(sub)

    relay(n, [sums], blocks, settle)
    if wide:
        load_next.wait()

        def multiply_next(columns):
            whole = full_ref[...].reshape(n * rows, width)
            result_ref[:, columns] = dot(whole, next_ref[:, columns]).astype(bf16)

        by_tiles(result_ref.shape[1], 256, multiply_next)


def carry_back(work, plain, order, step, width, middle, base, gain, term_ref, first):
    def load(group):
        return work[:, group * BLK : (group + 1) * BLK]

    def store(group, value):
        plain[:, group * BLK : (group + 1) * BLK] = value

    reorder(load, store, step, width, order)
    back_hidden = plain[...]
    normed, inverse = normalize(middle)
    gain_term = jnp.sum(back_hidden * normed, axis=0, keepdims=True)
    bias_term = jnp.sum(back_hidden, axis=0, keepdims=True)
    if first:
        term_ref[...] = jnp.zeros_like(term_ref)
        term_ref[0:1] = gain_term
        term_ref[1:2] = bias_term
    else:
        term_ref[0:1] += gain_term
        term_ref[1:2] += bias_term
    return base + norm_back(back_hidden, normed, inverse, gain)


def back_kernel(
    n, order, column, half, dy_ref, w_hbm, base_ref, middle_ref, norm_ref, outs_hbm, *rest
):
    carry_ref, full_ref, att_ref, term_ref = rest[:4]
    part, held, work, plain, s_send, s_recv, b_send, b_recv = rest[4:12]
    w_ref, w_sem, outs_ref, outs_sem = rest[12:]
    rows, width = base_ref.shape
    step = rows // SUBS
    load_w = fetch_columns(w_hbm, column, w_ref, w_sem)
    load_w.start()
    load_outs = fetch_columns(outs_hbm, half, outs_ref, outs_sem)
    load_outs.start()
    line = Line(n, rows, step)
    line.greet()
    load_w.wait()
    sums = Sums(line, part, held, s_send, s_recv)
    blocks = Blocks(line, full_ref, b_send, b_recv)

    def multiply(columns):
        product = dot_nt(dy_ref[...], w_ref[columns]).astype(bf16)
        part[:, :, columns] = product.reshape(n, rows, -1)

    by_tiles(width, 256, multiply)

    def settle(sub):
        here = line.part(sub)
        sums.total(sub, work)
        carry = carry_back(
            work,
            plain,
            order,
            step,
            width,
            middle_ref[here].astype(f32),
            base_ref[here].astype(f32),
            norm_ref[0:1],
            term_ref,
            sub == 0,
        )
        carry_ref[here] = carry
        full_ref[line.at, here] = carry.astype(bf16)
        blocks.start(sub)

    relay(n, [sums], blocks, settle)
    load_outs.wait()

    def multiply_next(columns):
        whole = full_ref[...].reshape(n * rows, width)
        att_ref[:, columns] = dot_nt(whole, outs_ref[columns]).astype(bf16)

    by_tiles(att_ref.shape[1], 256, multiply_next)


def last_kernel(n, order, dy_ref, w_hbm, base_ref, tokens, norm_ref, branch, middle, *rest):
    grad_ref, result_ref, term_ref = rest[:3]
    part, held, held2, work, plain, s_send, s_recv, r_send, r_recv, w_ref, w_sem = rest[3:]
    rows, width = base_ref.shape
    step = rows // SUBS
    load_w = fetch_columns(w_hbm, 0, w_ref, w_sem)
    load_w.start()
    line = Line(n, rows, step)
    load_w.wait()
    sums = Sums(line, part, held, s_send, s_recv)
    results = Sums(line, branch, held2, r_send, r_recv)

    def multiply(columns):
        product = dot_nt(dy_ref[...], w_ref[columns]).astype(bf16)
        part[:, :, columns] = product.reshape(n, rows, -1)

    by_tiles(width, 256, multiply)

    def settle(sub):
        here = line.part(sub)
        sums.total(sub, work)
        carry = carry_back(
            work,
            plain,
            order,
            step,
            width,
            tokens[here].astype(f32),
            base_ref[here],
            norm_ref[0:1],
            term_ref,
            sub == 0,
        )
        grad_ref[here] = carry.astype(bf16)
        results.total(sub, work)
        result_ref[here] = (middle[here] + work[...]).astype(bf16)

    relay(n, [sums, results], None, settle)


VMEM_CAP = 52 * 1024 * 1024


def in_place():
    return pl.BlockSpec(memory_space=pl.ANY)


def whole_vmem():
    return pl.BlockSpec(memory_space=pltpu.VMEM)


def sem_pair(n, subs):
    return [pltpu.SemaphoreType.DMA((2, n, subs)), pltpu.SemaphoreType.DMA((2, n, subs))]


def line_call(kernel, name, ident, outs, specs, scratch, flops, moved):
    return pl.pallas_call(
        kernel,
        name=name,
        out_shape=outs,
        in_specs=specs,
        out_specs=jax.tree.map(lambda _: whole_vmem(), outs),
        scratch_shapes=scratch,
        compiler_params=pltpu.CompilerParams(
            collective_id=ident, has_side_effects=True, vmem_limit_bytes=VMEM_CAP
        ),
        cost_estimate=pl.CostEstimate(flops=flops, bytes_accessed=moved, transcendentals=0),
    )


def shape(dims, kind):
    return jax.ShapeDtypeStruct(dims, kind)


LINK_COST = 4_000_000


def pieces_of(rows):
    return max(1, rows * SUBS // 128)


class Order:
    def __init__(self, pieces, width):
        self.pieces, self.width = pieces, width


def swap_sems(n):
    return [pltpu.SemaphoreType.DMA((n,)), pltpu.SemaphoreType.DMA((n,))]


def enter_call(
    name, ident, slots, weights, gathers, norms, normed, hidden, n, n_dp, width, inner=None
):
    chunk = weights[0][0].shape[0] // n_dp
    run, inner_args, inner_specs, inner_outs, scratch = inner or (None, [], [], [], [])
    counts = (len(inner_args), len(inner_outs), len(scratch))
    outs, scratch = [], list(scratch)
    for array, places, split, _ in weights:
        parts = n if split else 1
        outs.append(shape((parts, chunk, len(places) // parts * BLK), bf16))
        scratch += [pltpu.VMEM(array.shape, f32), pltpu.SemaphoreType.DMA]
    if normed:
        scratch += [pltpu.VMEM((n_dp, *norms.shape), f32), *swap_sems(n_dp)]
    for array, _ in gathers:
        rows = array.shape[0]
        outs.append(shape((n, *array.shape), array.dtype))
        scratch += sem_pair(n, pieces_of(rows))
    if normed:
        outs.append(shape((norms.shape[0], n_dp * norms.shape[1]), f32))
    for array, _, _, _ in weights:
        slots_shape = (n_dp, array.shape[1] // BLK, chunk, BLK)
        scratch += [pltpu.VMEM(slots_shape, bf16)] * 2 + swap_sems(n_dp)
    if hidden:
        scratch.append(pltpu.VMEM((gathers[0][0].shape[0] // SUBS, width), f32))
    for array, moved in gathers[1 if hidden else 0 :]:
        if moved:
            scratch.append(pltpu.VMEM(array.shape, f32))
    for index, (_, places, split, _) in enumerate(weights):
        if split:
            scratch += [pltpu.VMEM(outs[index].shape, bf16), *swap_sems(n)]
    args = [slots, *(weight[0] for weight in weights), *(gather[0] for gather in gathers)]
    specs = [pl.BlockSpec(memory_space=pltpu.SMEM)] + [in_place()] * len(weights)
    specs += [whole_vmem()] * len(gathers)
    if normed or hidden:
        args.append(norms)
        specs.append(whole_vmem())
    args += inner_args
    specs += inner_specs
    outs += inner_outs
    kernel = functools.partial(
        enter_kernel,
        [weight[1:] for weight in weights],
        [gather[1] for gather in gathers],
        Order(shuffle_order(n, n_dp), width),
        normed,
        hidden,
        run,
        counts,
    )
    return line_call(kernel, name, ident, outs, specs, scratch, 0, LINK_COST)(*args)


def leave_call(name, ident, slots, weights, term, n, n_dp, inner=None):
    outs, scratch = [], []
    specs = [pl.BlockSpec(memory_space=pltpu.SMEM)] + [whole_vmem()] * len(weights)
    args = [slots, *(weight[0] for weight in weights)]
    chunk = weights[0][0].shape[1]
    if term is not None:
        args.append(term)
        specs.append(whole_vmem())
        block = (term.shape[0], term.shape[1] // n_dp)
    counts = (0, 0, 0)
    run = None
    if inner is not None:
        run, inner_args, inner_specs, inner_outs, inner_scratch = inner
        counts = (len(inner_args), len(inner_outs), len(inner_scratch))
        args += inner_args
        specs += inner_specs
        scratch += inner_scratch
    if term is not None:
        scratch += [pltpu.VMEM((n_dp, *block), f32)] * 2 + swap_sems(n_dp)
        scratch += [pltpu.VMEM(block, f32), pltpu.VMEM((n, *block), f32), *swap_sems(n)]
    for rows, split, _, _ in weights:
        if split:
            scratch += [pltpu.VMEM(rows.shape, bf16), *swap_sems(n)]
    for rows, _, capacity, _ in weights:
        slots_shape = (n_dp, chunk, capacity * BLK)
        outs.append(shape(slots_shape, bf16))
        scratch += [pltpu.VMEM(slots_shape, bf16), *swap_sems(n_dp)]
        blocks = rows.shape[0] * rows.shape[2] // BLK
        scratch.append(pltpu.VMEM((blocks, chunk, BLK), bf16))
    if term is not None:
        outs.append(shape(block, f32))
    if inner is not None:
        outs += inner_outs
    kernel = functools.partial(
        leave_kernel, [weight[1:] for weight in weights], term is not None, run, counts
    )
    return line_call(kernel, name, ident, outs, specs, scratch, 0, LINK_COST)(*args)


def forward_parts(attended, outs_z, half, base, norm_rows, after, n, n_dp, alone):
    rows, width = base.shape
    share = outs_z.shape[0]
    outs = [shape((rows, width), f32), shape((n, rows, width), bf16)]
    specs = [whole_vmem(), in_place(), whole_vmem(), whole_vmem()]
    args = [attended, outs_z, base, norm_rows]
    scratch = [
        pltpu.VMEM((n, rows, width), bf16),
        pltpu.VMEM((2, n, rows, width), bf16),
        pltpu.VMEM((rows // SUBS, width), f32),
        *sem_pair(n, SUBS),
        *sem_pair(n, SUBS),
        pltpu.VMEM((share, width), bf16),
        pltpu.SemaphoreType.DMA,
    ]
    if after is not None:
        outs.append(shape((n * rows, share), bf16))
        specs.append(in_place())
        args.append(after)
        scratch += [pltpu.VMEM((width, share), bf16), pltpu.SemaphoreType.DMA]
    kernel = functools.partial(
        forward_kernel, n, shuffle_order(n, n_dp), half, after is not None, alone
    )
    return kernel, args, specs, outs, scratch


def forward_call(attended, outs_z, half, base, norm_rows, after, n, n_dp, ident):
    kernel, args, specs, outs, scratch = forward_parts(
        attended, outs_z, half, base, norm_rows, after, n, n_dp, True
    )
    call = line_call(kernel, f"forward{half}", ident, outs, specs, scratch, 0, LINK_COST)
    return call(*args)


def back_call(dy, weight, column, base, middle, norm_rows, outs_z, half, n, n_dp, ident):
    rows, width = base.shape
    share = outs_z.shape[0]
    outs = [
        shape((rows, width), f32),
        shape((n, rows, width), bf16),
        shape((n * rows, share), bf16),
        shape((8, width), f32),
    ]
    specs = [
        whole_vmem(),
        in_place(),
        whole_vmem(),
        whole_vmem(),
        whole_vmem(),
        in_place(),
    ]
    scratch = [
        pltpu.VMEM((n, rows, width), bf16),
        pltpu.VMEM((2, n, rows, width), bf16),
        pltpu.VMEM((rows // SUBS, width), f32),
        pltpu.VMEM((rows // SUBS, width), f32),
        *sem_pair(n, SUBS),
        *sem_pair(n, SUBS),
        pltpu.VMEM((width, dy.shape[1]), bf16),
        pltpu.SemaphoreType.DMA,
        pltpu.VMEM((share, width), bf16),
        pltpu.SemaphoreType.DMA,
    ]
    kernel = functools.partial(back_kernel, n, unshuffle_order(n, n_dp), column, half)
    call = line_call(kernel, f"back{half}", ident, outs, specs, scratch, 0, LINK_COST)
    return call(dy, weight, base, middle, norm_rows, outs_z)


def last_parts(dy, weight, base, tokens, norm_rows, branch, middle, n, n_dp):
    rows, width = base.shape
    outs = [
        shape((rows, width), bf16),
        shape((rows, width), bf16),
        shape((8, width), f32),
    ]
    specs = [whole_vmem(), in_place()] + [whole_vmem()] * 5
    scratch = [
        pltpu.VMEM((n, rows, width), bf16),
        pltpu.VMEM((2, n, rows, width), bf16),
        pltpu.VMEM((2, n, rows, width), bf16),
        pltpu.VMEM((rows // SUBS, width), f32),
        pltpu.VMEM((rows // SUBS, width), f32),
        *sem_pair(n, SUBS),
        *sem_pair(n, SUBS),
        pltpu.VMEM((width, dy.shape[1]), bf16),
        pltpu.SemaphoreType.DMA,
    ]
    kernel = functools.partial(last_kernel, n, unshuffle_order(n, n_dp))
    return kernel, [dy, weight, base, tokens, norm_rows, branch, middle], specs, outs, scratch


def attend_forward(query, keys, values, mask_ref, keyed, att_ref, share_ref):
    packed, rows, _ = mask_ref.shape
    heads = att_ref.shape[1] // HEAD
    for p in range(packed):
        here = slice(p * rows, (p + 1) * rows)
        there = here if keyed else slice(None)
        for h in range(heads):
            columns = slice(h * HEAD, (h + 1) * HEAD)
            scores = dot_nt(query[here, columns], keys[there, columns]) * HEAD ** (-0.5)
            scores = jnp.where(mask_ref[p] > 0, scores, score_floor)
            powers = jnp.exp(scores - jnp.max(scores, axis=-1, keepdims=True))
            shares = powers / jnp.sum(powers, axis=-1, keepdims=True)
            share_ref[p * heads + h] = shares
            att_ref[here, columns] = dot(shares.astype(bf16), values[there, columns]).astype(bf16)


def attend_backward(query, keys, values, share_ref, back_ref, rows, keyed, put_query, put_pair):
    heads = back_ref.shape[1] // HEAD
    packed = back_ref.shape[0] // rows
    score_scale = HEAD ** (-0.5)
    for h in range(heads):
        columns = slice(h * HEAD, (h + 1) * HEAD)
        key_grad = value_grad = None
        for p in range(packed):
            here = slice(p * rows, (p + 1) * rows)
            there = here if keyed else slice(None)
            shares = share_ref[p * heads + h]
            back = back_ref[here, columns]
            back_shares = dot_nt(back, values[there, columns])
            inner_sum = jnp.sum(shares * back_shares, axis=-1, keepdims=True)
            back_scores = (shares * (back_shares - inner_sum)).astype(bf16)
            put_query(here, columns, dot(back_scores, keys[there, columns]) * score_scale)
            key_term = dot_tn(back_scores, query[here, columns]) * score_scale
            value_term = dot_tn(shares.astype(bf16), back)
            if keyed:
                put_pair(there, columns, key_term, value_term)
            else:
                key_grad = key_term if key_grad is None else key_grad + key_term
                value_grad = value_term if value_grad is None else value_grad + value_term
        if not keyed:
            put_pair(slice(None), columns, key_grad, value_grad)


def self_forward_kernel(h_ref, w_ref, mask_ref, proj_ref, att_ref, share_ref):
    tile = pl.program_id(0)
    proj_ref[tile] = dot(h_ref[...], w_ref[...]).astype(bf16)

    @pl.when(tile == 2)
    def _():
        attend_forward(
            proj_ref.at[0], proj_ref.at[1], proj_ref.at[2], mask_ref, True, att_ref, share_ref
        )


def cross_forward_kernel(cq_ref, text_ref, w_ref, mask_ref, kv_ref, att_ref, share_ref, total):
    tile = pl.program_id(0)
    product = dot(text_ref[...], w_ref[...])

    @pl.when(tile < 2)
    def _():
        total[tile] = product

    @pl.when(tile >= 2)
    def _():
        kv_ref[tile - 2] = (total[tile - 2] + product).astype(bf16)

    @pl.when(tile == 3)
    def _():
        attend_forward(cq_ref, kv_ref.at[0], kv_ref.at[1], mask_ref, False, att_ref, share_ref)


def ffn_kernel(h_ref, up_ref, grad_ref, act_ref, slope_ref, gdown_ref):
    up_values = dot(h_ref[...], up_ref[...])
    chance = 0.5 * (1.0 + lax.erf(up_values * 0.5**0.5))
    density = jnp.exp(-0.5 * up_values * up_values) * 0.3989422804014327
    activated = (up_values * chance).astype(bf16)
    act_ref[...] = activated
    slope_ref[...] = chance + up_values * density
    gdown_ref[...] = dot_tn(activated, grad_ref[...]).astype(bf16)


def ffn_back_kernel(
    h_ref, down_ref, grad_ref, act_ref, slope_ref, du_ref, branch_ref, gup_ref, total
):
    tile = pl.program_id(0)
    back_act = dot_nt(grad_ref[...], down_ref[...])
    back_up = (back_act * slope_ref[...]).astype(bf16)
    du_ref[...] = back_up
    gup_ref[...] = dot_tn(h_ref[...], back_up).astype(bf16)

    @pl.when(tile == 0)
    def _():
        total[...] = dot(act_ref[...], down_ref[...])

    @pl.when(tile > 0)
    def _():
        total[...] += dot(act_ref[...], down_ref[...])

    @pl.when(tile == 3)
    def _():
        branch_ref[...] = total[...].astype(bf16)


def cross_back_kernel(
    rows, back_ref, cq_ref, kv_ref, share_ref, text_ref, dcq_ref, grad_ref, pairs
):
    share = cq_ref.shape[1]

    @pl.when(pl.program_id(0) == 0)
    def _():
        def put_query(here, columns, value):
            dcq_ref[here, columns] = value.astype(bf16)

        def put_pair(there, columns, key_grad, value_grad):
            pairs[there, columns] = key_grad.astype(bf16)
            after_keys = slice(share + columns.start, share + columns.stop)
            pairs[there, after_keys] = value_grad.astype(bf16)

        attend_backward(
            cq_ref, kv_ref.at[0], kv_ref.at[1], share_ref, back_ref, rows, False, put_query, put_pair
        )

    grad_ref[...] = dot_tn(text_ref[...], pairs[...]).astype(bf16)


def outs_grad_kernel(att1_ref, carry1_ref, att2_ref, carry2_ref, grad_ref):
    tile = pl.program_id(0)

    @pl.when(tile == 0)
    def _():
        grad_ref[...] = dot_tn(att1_ref[...], carry1_ref[...]).astype(bf16)

    @pl.when(tile == 1)
    def _():
        grad_ref[...] = dot_tn(att2_ref[...], carry2_ref[...]).astype(bf16)


def self_back_kernel(
    rows, back_ref, proj_ref, share_ref, h1_ref, h2_ref, dcq_ref, dproj_ref, grad_ref, parts
):
    tile = pl.program_id(0)
    share = dcq_ref.shape[1]

    @pl.when(tile == 0)
    def _():
        def put(part, here, columns, value):
            value = value.astype(bf16)
            parts[part, here, columns] = value
            dproj_ref[here, part * share + columns.start : part * share + columns.stop] = value

        def put_query(here, columns, value):
            put(0, here, columns, value)

        def put_pair(there, columns, key_grad, value_grad):
            put(1, there, columns, key_grad)
            put(2, there, columns, value_grad)

        attend_backward(
            proj_ref.at[0],
            proj_ref.at[1],
            proj_ref.at[2],
            share_ref,
            back_ref,
            rows,
            True,
            put_query,
            put_pair,
        )

    @pl.when(tile < 3)
    def _():
        grad_ref[...] = dot_tn(h1_ref[...], parts[tile]).astype(bf16)

    @pl.when(tile == 3)
    def _():
        grad_ref[...] = dot_tn(h2_ref[...], dcq_ref[...]).astype(bf16)


def fixed(dims):
    return pl.BlockSpec(dims, lambda t: (0,) * len(dims))


def moving(dims, index):
    return pl.BlockSpec(dims, lambda t: (0, index(t)))


def local_call(kernel, name, tiles, outs, specs, out_specs, scratch, flops, moved):
    return pl.pallas_call(
        kernel,
        name=name,
        grid=(tiles,),
        out_shape=outs,
        in_specs=specs,
        out_specs=out_specs,
        scratch_shapes=scratch,
        compiler_params=pltpu.CompilerParams(vmem_limit_bytes=VMEM_CAP),
        cost_estimate=pl.CostEstimate(
            flops=flops // 8, bytes_accessed=moved // 8, transcendentals=0
        ),
    )


def self_forward(hidden, query_z, mask):
    tokens, width = hidden.shape
    share = query_z.shape[1] // 4
    packed, rows, _ = mask.shape
    pairs = (packed * share // HEAD, rows, rows)
    return local_call(
        self_forward_kernel,
        "self_forward",
        3,
        (shape((3, tokens, share), bf16), shape((tokens, share), bf16), shape(pairs, f32)),
        [fixed(hidden.shape), moving((width, share), lambda t: t), fixed(mask.shape)],
        (fixed((3, tokens, share)), fixed((tokens, share)), fixed(pairs)),
        [],
        6 * tokens * width * share,
        20_000_000,
    )(hidden, query_z, mask)


def cross_forward(cross_query, text_all, text_z, mask):
    tokens, share = cross_query.shape
    texts = text_all.shape[0]
    width = text_z.shape[0]
    packed, rows, _ = mask.shape
    pairs = (packed * share // HEAD, rows, texts)
    return local_call(
        cross_forward_kernel,
        "cross_forward",
        4,
        (shape((2, texts, share), bf16), shape((tokens, share), bf16), shape(pairs, f32)),
        [
            fixed(cross_query.shape),
            moving((texts, width), lambda t: t // 2),
            moving((width, share), lambda t: t),
            fixed(mask.shape),
        ],
        (fixed((2, texts, share)), fixed((tokens, share)), fixed(pairs)),
        [pltpu.VMEM((2, texts, share), f32)],
        8 * texts * width * share,
        20_000_000,
    )(cross_query, text_all, text_z, mask)


def ffn(hidden, up_z, grad_all):
    tokens, width = hidden.shape
    share = up_z.shape[1] // 4
    return local_call(
        ffn_kernel,
        "ffn",
        4,
        (
            shape((tokens, 4 * share), bf16),
            shape((tokens, 4 * share), f32),
            shape((share, 4 * width), bf16),
        ),
        [fixed(hidden.shape), moving((width, share), lambda t: t), fixed(grad_all.shape)],
        (
            moving((tokens, share), lambda t: t),
            moving((tokens, share), lambda t: t),
            moving((share, width), lambda t: t),
        ),
        [],
        16 * tokens * width * share,
        30_000_000,
    )(hidden, up_z, grad_all)


def ffn_back(hidden, down_z, grad_all, activated, slope):
    tokens, width = hidden.shape
    share = down_z.shape[0]
    return local_call(
        ffn_back_kernel,
        "ffn_back",
        4,
        (
            shape((tokens, 4 * share), bf16),
            shape((tokens, width), bf16),
            shape((width, 4 * share), bf16),
        ),
        [
            fixed(hidden.shape),
            moving((share, width), lambda t: t),
            fixed(grad_all.shape),
            moving((tokens, share), lambda t: t),
            moving((tokens, share), lambda t: t),
        ],
        (
            moving((tokens, share), lambda t: t),
            fixed((tokens, width)),
            moving((width, share), lambda t: t),
        ),
        [pltpu.VMEM((tokens, width), f32)],
        24 * tokens * width * share,
        40_000_000,
    )(hidden, down_z, grad_all, activated, slope)


def cross_back(back_attended, cross_query, text_pairs, shares, text_all, rows):
    tokens, share = cross_query.shape
    texts = text_all.shape[0]
    width = text_all.shape[1] // 2
    return local_call(
        functools.partial(cross_back_kernel, rows),
        "cross_back",
        2,
        (shape((tokens, share), bf16), shape((width, 4 * share), bf16)),
        [
            fixed(back_attended.shape),
            fixed(cross_query.shape),
            fixed(text_pairs.shape),
            fixed(shares.shape),
            moving((texts, width), lambda t: t),
        ],
        (fixed((tokens, share)), moving((width, 2 * share), lambda t: t)),
        [pltpu.VMEM((texts, 2 * share), bf16)],
        8 * texts * width * share,
        20_000_000,
    )(back_attended, cross_query, text_pairs, shares, text_all)


def outs_grad(attended1, carry1, attended2, carry2):
    tokens, share = attended1.shape
    width = carry1.shape[1]
    return local_call(
        outs_grad_kernel,
        "outs_grad",
        2,
        shape((share, 2 * width), bf16),
        [fixed((tokens, share)), fixed((tokens, width))] * 2,
        moving((share, width), lambda t: t),
        [],
        4 * tokens * width * share,
        10_000_000,
    )(attended1, carry1, attended2, carry2)


def self_back(back_attended, projected, shares, hidden1, hidden2, back_cross, rows):
    tokens, width = hidden1.shape
    share = back_cross.shape[1]
    return local_call(
        functools.partial(self_back_kernel, rows),
        "self_back",
        4,
        (shape((tokens, 3 * share), bf16), shape((width, 4 * share), bf16)),
        [
            fixed(back_attended.shape),
            fixed(projected.shape),
            fixed(shares.shape),
            fixed(hidden1.shape),
            fixed(hidden2.shape),
            fixed(back_cross.shape),
        ],
        (fixed((tokens, 3 * share)), moving((width, share), lambda t: t)),
        [pltpu.VMEM((3, tokens, share), bf16)],
        8 * tokens * width * share,
        25_000_000,
    )(back_attended, projected, shares, hidden1, hidden2, back_cross)


def block_slots(owners):
    owner = jnp.concatenate(owners)
    weight = jnp.concatenate([jnp.full(one.shape, at, jnp.int32) for at, one in enumerate(owners)])
    mark = owner + weight * 1024
    count = mark.shape[0]
    earlier = lax.broadcasted_iota(jnp.int32, (count, count), 1) < lax.broadcasted_iota(
        jnp.int32, (count, count), 0
    )
    same = jnp.logical_and(mark[:, None] == mark[None, :], earlier)
    return jnp.stack([owner, jnp.sum(same.astype(jnp.int32), axis=1)])


def slot_contents(owners, slots, places, capacities, firsts, n_dp):
    rows = []
    for owner, place, capacity, first in zip(owners, places, capacities, firsts):
        count = owner.shape[0]
        at = owner * capacity + slots[1, first : first + count]
        hit = at[None, :] == lax.broadcasted_iota(jnp.int32, (n_dp * capacity, count), 0)
        block = lax.broadcasted_iota(jnp.int32, (n_dp * capacity, count), 1)
        per_group, per_part, split = place_rule(place)
        part = block % per_group // per_part if split else block * 0
        column = block // per_group * per_part + block % per_part if split else block
        index = part * (count // (per_group // per_part)) + column if split else column
        rows.append(
            jnp.stack([jnp.sum(jnp.where(hit, value, 0), axis=1) for value in (index, block * 0 + 1)])
        )
    return jnp.concatenate(rows, axis=1)


def place_rule(place):
    parts = 1 + max(part for part, _ in place)
    if parts == 1:
        return 0, 0, False
    per_part = sum(1 for part, _ in place[:HEADS] if part == 0)
    return per_part * parts, per_part, True


def after(small, first):
    return lax.optimization_barrier((small, first))[0]


def body(
    tokens_in,
    text_in,
    seg_ids,
    capt_ids,
    grad_out,
    owner_query,
    owner_up,
    owner_outs,
    owner_text,
    owner_down,
    w_query,
    m_query,
    v_query,
    w_up,
    m_up,
    v_up,
    w_outs,
    m_outs,
    v_outs,
    w_text,
    m_text,
    v_text,
    w_down,
    m_down,
    v_down,
    norm_weight,
    m_norm,
    v_norm,
):
    n_dp = lax.axis_size("dp")
    n_z = lax.axis_size("fsdp")
    width = tokens_in.shape[1]
    own_rows = w_query.shape[0]
    chunk = own_rows // n_dp
    cap_big = w_query.shape[1] // BLK
    cap_out = w_outs.shape[1] // BLK
    heads_z = HEADS // n_z
    share = width // n_z
    owner_query, owner_up, owner_outs, owner_text, owner_down = (
        owner[:, 0] for owner in (owner_query, owner_up, owner_outs, owner_text, owner_down)
    )
    split_places = [split_place(b, heads_z, n_z) for b in range(owner_query.shape[0])]
    big_places = [flat_place(b) for b in range(owner_down.shape[0])]
    out_places = [flat_place(b) for b in range(owner_outs.shape[0])]
    owners = (owner_query, owner_outs, owner_text, owner_up, owner_down)
    places = (split_places, out_places, split_places, split_places, big_places)
    capacities = (cap_big, cap_out, cap_big, cap_big, cap_big)
    firsts = [sum(len(one) for one in places[:index]) for index in range(5)]
    slot_firsts = [sum(capacities[:index]) * n_dp for index in range(5)]
    slots = block_slots(owners)
    contents = slot_contents(owners, slots, places, capacities, firsts, n_dp)

    def spread(rows):
        return lax.all_gather(rows.reshape(-1, rows.shape[-1]), "dp", axis=0, tiled=True)

    def gather_sum(piece, parts):
        summed = lax.psum_scatter(piece, "dp", scatter_dimension=0, tiled=True)
        return summed.reshape(parts, chunk, -1)

    token_count = tokens_in.shape[0]
    marks = jnp.concatenate([seg_ids, capt_ids], axis=1)
    marks = jnp.pad(marks, ((0, 7), (0, 256 - marks.shape[1])))
    norms = jnp.pad(norm_weight, ((0, 2), (0, 0)))
    half = token_count // 2
    query_rows, grad_low, marks, norm_full = enter_call(
        "enter_query",
        0,
        slots,
        [(w_query, split_places, True, firsts[0])],
        [(grad_out[:half], False), (marks, False)],
        norms,
        True,
        False,
        n_z,
        n_dp,
        width,
    )
    outs_rows, hidden1, text_all, grad_high = enter_call(
        "enter_outs",
        6,
        slots,
        [(w_outs, out_places, False, firsts[1])],
        [(tokens_in, True), (text_in, True), (grad_out[half:], False)],
        norm_full[0:2],
        False,
        True,
        n_z,
        n_dp,
        width,
    )
    query_z, outs_z = spread(query_rows), spread(outs_rows)
    grad_all = jnp.concatenate([grad_low, grad_high], axis=1).reshape(-1, width)
    hidden1 = hidden1.reshape(-1, width)
    text_all = text_all.reshape(-1, text_in.shape[1])
    segment = marks[:, 0, :token_count]
    caption = marks[:, 0, token_count : token_count + capt_ids.shape[1]]
    self_mask = (segment[:, :, None] == segment[:, None, :]).astype(jnp.int32)
    text_row = lax.broadcasted_iota(jnp.int32, caption.shape, 0).reshape(1, 1, -1)
    packed_row = lax.broadcasted_iota(jnp.int32, (n_z, 1, 1), 0)
    cross_mask = jnp.logical_and(
        segment[:, :, None] == caption.reshape(1, 1, -1), packed_row == text_row
    ).astype(jnp.int32)

    projected, attended1, shares1 = self_forward(hidden1, query_z, self_mask)
    text_rows, up_rows = enter_call(
        "enter_text",
        7,
        after(slots, attended1),
        [
            (w_text, split_places, True, firsts[2]),
            (w_up, split_places, True, firsts[3]),
        ],
        [],
        None,
        False,
        False,
        n_z,
        n_dp,
        width,
    )
    down_rows, middle1, hidden2, cross_query = enter_call(
        "forward0",
        1,
        slots,
        [(w_down, big_places, False, firsts[4])],
        [],
        None,
        False,
        False,
        n_z,
        n_dp,
        width,
        forward_parts(
            attended1,
            outs_z,
            0,
            tokens_in,
            after(norm_full[2:4], up_rows),
            query_z,
            n_z,
            n_dp,
            False,
        ),
    )
    hidden2 = hidden2.reshape(-1, width)
    text_z, up_z, down_z = spread(text_rows), spread(up_rows), spread(down_rows)
    text_pairs, attended2, shares2 = cross_forward(cross_query, text_all, text_z, cross_mask)
    middle2, hidden3 = forward_call(
        attended2, outs_z, 1, middle1, norm_full[4:6], None, n_z, n_dp, 2
    )
    hidden3 = hidden3.reshape(-1, width)
    activated, slope, down_part = ffn(hidden3, up_z, grad_all)
    down_sum = gather_sum(down_part, 1)
    back_up, branch3, up_part = ffn_back(hidden3, down_z, grad_all, activated, slope)
    branch3 = branch3.reshape(n_z, token_count, width)
    up_sum = gather_sum(up_part, n_z)
    at_middle2, carry2, back_att2, term3 = back_call(
        back_up, up_z, 0, grad_out, middle2, norm_full[4:6], outs_z, 1, n_z, n_dp, 3
    )
    carry2 = carry2.reshape(-1, width)
    back_cross, text_part = cross_back(
        back_att2, cross_query, text_pairs, shares2, text_all, token_count
    )
    text_sum = gather_sum(text_part, n_z)
    at_middle1, carry1, back_att1, term2 = back_call(
        back_cross, query_z, 3, at_middle2, middle1, norm_full[2:4], outs_z, 0, n_z, n_dp, 4
    )
    carry1 = carry1.reshape(-1, width)
    back_projected, query_part = self_back(
        back_att1, projected, shares1, hidden1, hidden2, back_cross, token_count
    )
    query_sum = gather_sum(query_part, n_z)
    outs_sum = gather_sum(outs_grad(after(attended1, query_part), carry1, attended2, carry2), 1)
    down_grad, up_grad, grad_in, result, term1 = leave_call(
        "leave_up",
        8,
        contents,
        [
            (down_sum, False, cap_big, slot_firsts[4]),
            (up_sum, True, cap_big, slot_firsts[3]),
        ],
        None,
        n_z,
        n_dp,
        last_parts(
            back_projected,
            query_z,
            at_middle1,
            tokens_in,
            norm_full[0:2],
            branch3,
            middle2,
            n_z,
            n_dp,
        ),
    )
    (text_grad,) = leave_call(
        "leave_text",
        5,
        after(contents, term1),
        [(text_sum, True, cap_big, slot_firsts[2])],
        None,
        n_z,
        n_dp,
    )
    text_grad, up_grad, down_grad = (
        grad.reshape(own_rows, -1).astype(f32) for grad in (text_grad, up_grad, down_grad)
    )
    up_new = adamw_update(w_up, m_up, v_up, up_grad, rate_up, decay_rate)
    text_new = adamw_update(w_text, m_text, v_text, text_grad, rate_text, decay_rate)
    down_new = adamw_update(w_down, m_down, v_down, down_grad, rate_down, decay_rate)
    norm_term = jnp.concatenate([term1[:2], term2[:2], term3[:4]], axis=0)
    query_grad, norm_grad = leave_call(
        "leave_query",
        9,
        after(contents, (up_new, down_new, text_new)),
        [(query_sum, True, cap_big, slot_firsts[0])],
        norm_term,
        n_z,
        n_dp,
    )
    (outs_slots,) = leave_call(
        "leave_outs",
        10,
        after(contents, query_grad),
        [(outs_sum, False, cap_out, slot_firsts[1])],
        None,
        n_z,
        n_dp,
    )
    norm_grad = norm_grad[:6]
    query_grad, outs_slots = (
        grad.reshape(own_rows, -1).astype(f32) for grad in (query_grad, outs_slots)
    )
    query_new = adamw_update(w_query, m_query, v_query, query_grad, rate_query, decay_rate)
    outs_new = adamw_update(w_outs, m_outs, v_outs, outs_slots, rate_outs, decay_rate)
    norm_new = adamw_update(norm_weight, m_norm, v_norm, norm_grad, rate_norm, 0.0)
    return (
        result,
        grad_in,
        *query_new,
        *up_new,
        *outs_new,
        *text_new,
        *down_new,
        *norm_new,
    )


def solution(mesh):
    rows = P(("dp", "fsdp"), None)
    slots = P("fsdp", "dp")
    norms = P(None, "dp")
    in_specs = (rows,) * 5 + (P(),) * 5 + (slots,) * 15 + (norms,) * 3
    out_specs = (rows,) * 2 + (slots,) * 15 + (norms,) * 3
    return jax.shard_map(body, mesh=mesh, in_specs=in_specs, out_specs=out_specs, check_vma=False)
```

```python
import functools

import jax
import jax.numpy as jnp
from jax import lax
from jax.experimental import pallas as pl
from jax.experimental.pallas import tpu as pltpu
from jax.sharding import PartitionSpec as P

HEADS = 16
HEAD = 128
STEP = 10
BLK = 128


beta_first = 0.9
beta_second = 0.999
adam_eps = 1e-08
decay_rate = 0.01
rate_query = 0.04
rate_up = 0.04
rate_outs = 0.12
rate_text = 0.03
rate_down = 0.03
rate_norm = 0.5
norm_eps = 1e-05
score_floor = -1e30
bf16 = jnp.bfloat16
f32 = jnp.float32


def normalize(values):
    centered = values - jnp.mean(values, axis=-1, keepdims=True)
    inverse_std = lax.rsqrt(jnp.mean(centered * centered, axis=-1, keepdims=True) + norm_eps)
    return (centered * inverse_std, inverse_std)


def norm_back(back_hidden, normed, inverse_std, gain_row):
    back_normed = back_hidden * gain_row
    return inverse_std * (
        back_normed
        - jnp.mean(back_normed, axis=-1, keepdims=True)
        - normed * jnp.mean(back_normed * normed, axis=-1, keepdims=True)
    )


def adamw_update(weight, first, second, gradient, rate, decay):
    first_new = beta_first * first + (1.0 - beta_first) * gradient
    second_new = beta_second * second + (1.0 - beta_second) * gradient * gradient
    first_hat = first_new / (1.0 - beta_first**STEP)
    second_hat = second_new / (1.0 - beta_second**STEP)
    weight_new = weight - rate * (first_hat / (jnp.sqrt(second_hat) + adam_eps) + decay * weight)
    return (first_new, second_new, weight_new)


def dot(left, right):
    return jnp.dot(left, right, preferred_element_type=f32)


def dot_nt(left, right):
    return lax.dot_general(left, right, (((1,), (1,)), ((), ())), preferred_element_type=f32)


def dot_tn(left, right):
    return lax.dot_general(left, right, (((0,), (0,)), ((), ())), preferred_element_type=f32)


def split_place(block, per_part, parts):
    group, rest = divmod(block, per_part * parts)
    part, inner = divmod(rest, per_part)
    return part, group * per_part + inner


def flat_place(block):
    return 0, block


MESH = pl.DeviceIdType.MESH


SUBS = 4


class Line:
    def __init__(self, n, rows, step):
        self.n, self.rows, self.step = n, rows, step
        self.at = lax.axis_index("fsdp")

    def has(self, way):
        return self.at < self.n - 1 if way == 0 else self.at > 0

    def peer(self, way):
        index = jnp.clip(self.at + (1 if way == 0 else -1), 0, self.n - 1)
        return {"fsdp": index}

    def greet(self, others=0):
        barrier = pltpu.get_barrier_semaphore()
        for way in (0, 1):

            @pl.when(self.has(way))
            def _():
                pl.semaphore_signal(
                    barrier, inc=1, device_id=self.peer(way), device_id_type=pl.DeviceIdType.MESH
                )

        pl.semaphore_wait(
            barrier, others + self.has(0).astype(jnp.int32) + self.has(1).astype(jnp.int32)
        )

    def copy(self, source, target, send, recv, way):
        return pltpu.make_async_remote_copy(
            src_ref=source,
            dst_ref=target,
            send_sem=send,
            recv_sem=recv,
            device_id=self.peer(way),
            device_id_type=pl.DeviceIdType.MESH,
        )

    def part(self, sub):
        return pl.ds(sub * self.step, self.step)


class Sums:
    def __init__(self, line, part, held, send, recv):
        self.line, self.part, self.held, self.send, self.recv = line, part, held, send, recv

    def move(self, way, target, sub, source):
        line = self.line
        rows = line.part(sub)
        return line.copy(
            source,
            self.held.at[way, target, rows],
            self.send.at[way, target, sub],
            self.recv.at[way, target, sub],
            way,
        )

    def target(self, way, time):
        n, at = self.line.n, self.line.at
        return n - 1 - (time - at) if way == 0 else time - (n - 1 - at)

    def passes(self, way, target):
        n, at = self.line.n, self.line.at
        if way == 0:
            return jnp.logical_and(target > at, target < n)
        return jnp.logical_and(target < at, target >= 0)

    def forward(self, sub, time):
        line = self.line
        rows = line.part(sub)
        for way in (0, 1):
            target = self.target(way, time)
            passes = self.passes(way, target)
            inner = jnp.logical_and(passes, line.has(1 - way))
            outer = jnp.logical_and(passes, jnp.logical_not(line.has(1 - way)))

            @pl.when(outer)
            def _():
                self.move(way, target, sub, self.part.at[target, rows]).start()

            @pl.when(inner)
            def _():
                held = self.held.at[way, target, rows]
                self.move(way, target, sub, held).wait_recv()
                total = held[...].astype(f32) + self.part[target, rows].astype(f32)
                held[...] = total.astype(bf16)
                self.move(way, target, sub, held).start()

    def total(self, sub, sum_ref):
        line = self.line
        rows = line.part(sub)
        sum_ref[...] = self.part[line.at, rows].astype(f32)
        for way in (0, 1):

            @pl.when(line.has(1 - way))
            def _():
                held = self.held.at[way, line.at, rows]
                self.move(way, line.at, sub, held).wait_recv()
                sum_ref[...] += held[...].astype(f32)

    def finish(self):
        line = self.line
        for way in (0, 1):
            for time in range(line.n - 1):
                target = self.target(way, time)

                @pl.when(self.passes(way, target))
                def _():
                    for sub in range(line.rows // line.step):
                        held = self.held.at[way, target, line.part(sub)]
                        self.move(way, target, sub, held).wait_send()


def relay(n, sums, blocks, settle, hook=None):
    for slot in range((SUBS + 2) * (n - 1)):
        sub, time = divmod(slot, n - 1)
        if hook is not None and slot == SUBS * (n - 1):
            hook()
        if sub < SUBS:
            for one in sums:
                one.forward(sub, time)
        if time == 0 and 0 <= sub - 1 < SUBS:
            settle(sub - 1)
        if blocks is not None:
            if time == n - 2 and 0 <= sub - 1 < SUBS:
                blocks.forward(sub - 1, 1)
            if time < n - 2 and 0 <= sub - 2 < SUBS:
                blocks.forward(sub - 2, time + 2)
    for one in sums:
        one.finish()
    if blocks is not None:
        blocks.finish()


class Blocks:
    def __init__(self, line, full, send, recv):
        self.line, self.full, self.send, self.recv = line, full, send, recv

    def move(self, way, source, sub):
        line = self.line
        held = self.full.at[source, line.part(sub)]
        return line.copy(
            held, held, self.send.at[way, source, sub], self.recv.at[way, source, sub], way
        )

    def behind(self, way, source):
        return self.line.at > source if way == 0 else self.line.at < source

    def start(self, sub):
        for way in (0, 1):

            @pl.when(self.line.has(way))
            def _():
                self.move(way, self.line.at, sub).start()

    def forward(self, sub, step):
        line = self.line
        for way in (0, 1):
            source = line.at - step if way == 0 else line.at + step

            @pl.when(jnp.logical_and(source >= 0, source < line.n))
            def _():
                self.move(way, source, sub).wait_recv()

                @pl.when(line.has(way))
                def _():
                    self.move(way, source, sub).start()

    def finish(self):
        line = self.line
        for way in (0, 1):
            for source in range(line.n):
                ours = jnp.logical_or(self.behind(way, source), line.at == source)

                @pl.when(jnp.logical_and(ours, line.has(way)))
                def _():
                    for sub in range(line.rows // line.step):
                        self.move(way, source, sub).wait_send()


def lane_moves(width, order):
    moves = []
    piece = width // len(order)
    for group in range(width // BLK):
        parts = []
        for offset in range(0, BLK, piece):
            start = order[(group * BLK + offset) // piece] * piece
            parts.append((offset, start // BLK, start % BLK))
        moves.append(parts)
    return piece, moves


def reorder(load, store, rows, width, order):
    piece, moves = lane_moves(width, order)
    lane = lax.broadcasted_iota(jnp.int32, (rows, BLK), 1)
    for group, parts in enumerate(moves):
        value = None
        for offset, source, start in parts:
            block = load(source)
            if start != offset:
                block = pltpu.roll(block, (offset - start) % BLK, 1)
            value = block if value is None else jnp.where(lane >= offset, block, value)
        store(group, value)


def shuffle_order(n_z, n_dp):
    return [z * n_dp + i for i in range(n_dp) for z in range(n_z)]


def unshuffle_order(n_z, n_dp):
    return [i * n_z + z for z in range(n_z) for i in range(n_dp)]


def by_tiles(columns, tile, run):
    def one(index, carry):
        run(pl.ds(pl.multiple_of(index * tile, tile), tile))
        return carry

    lax.fori_loop(0, columns // tile, one, 0)


class Swap:
    def __init__(self, axis, source, target, send, recv):
        self.axis, self.source, self.target = axis, source, target
        self.send, self.recv = send, recv
        self.n = lax.axis_size(axis)
        self.me = lax.axis_index(axis)

    def copy(self, jump, arrival=False):
        peer = lax.rem(self.me + jump, self.n)
        slot = peer if arrival else self.me
        return pltpu.make_async_remote_copy(
            src_ref=self.source.at[peer],
            dst_ref=self.target.at[slot],
            send_sem=self.send.at[jump],
            recv_sem=self.recv.at[slot],
            device_id={self.axis: peer},
            device_id_type=MESH,
        )

    def start(self):
        for jump in range(1, self.n):
            self.copy(jump).start()

    def keep(self):
        self.target[self.me] = self.source[self.me]

    def wait(self):
        for jump in range(1, self.n):
            self.copy(jump, True).wait_recv()

    def finish(self):
        for jump in range(1, self.n):
            self.copy(jump).wait_send()


def greet_all():
    barrier = pltpu.get_barrier_semaphore()
    count = 0
    for axis in ("dp", "fsdp"):
        n, me = lax.axis_size(axis), lax.axis_index(axis)
        count += n - 1
        for jump in range(1, n):
            pl.semaphore_signal(
                barrier, inc=1, device_id={axis: lax.rem(me + jump, n)}, device_id_type=MESH
            )
    pl.semaphore_wait(barrier, count)


class Refs:
    def __init__(self, refs):
        self.refs = list(refs)

    def take(self, count=None):
        taken = self.refs[: 1 if count is None else count]
        self.refs = self.refs[len(taken) :]
        return taken[0] if count is None else taken


def enter_kernel(weights, gathers, order, normed, hidden, inner, inner_counts, *refs):
    refs = Refs(refs)
    n_dp, n_z = lax.axis_size("dp"), lax.axis_size("fsdp")
    slots_ref = refs.take()
    w_refs = refs.take(len(weights))
    in_refs = refs.take(len(gathers))
    norm_in = refs.take() if normed or hidden else None
    inner_refs = refs.take(inner_counts[0])
    row_refs = refs.take(len(weights))
    full_refs = refs.take(len(gathers))
    norm_out = refs.take() if normed else None
    inner_refs += refs.take(inner_counts[1])
    inner_refs += refs.take(inner_counts[2])
    loads = []
    for w_ref in w_refs:
        stage, sem = refs.take(2)
        load = pltpu.make_async_copy(w_ref, stage, sem)
        load.start()
        loads.append((stage, load))
    greet_all()
    if normed:
        parts, *sems = refs.take(3)
        norm_swap = Spread("dp", norm_in, parts, *sems)
        norm_swap.start()
    lines = []
    for in_ref, full_ref in zip(in_refs, full_refs):
        rows = in_ref.shape[0]
        step = rows // pieces_of(rows)
        lines.append(Blocks(Line(n_z, rows, step), full_ref, *refs.take(2)))
    swaps = []
    for (stage, load), (places, split, _) in zip(loads, weights):
        source, target, *sems = refs.take(4)
        swap = Swap("dp", source, target, *sems)
        load.wait()
        chunk = source.shape[2]
        for jump in range(n_dp):
            peer = lax.rem(swap.me + jump, n_dp)
            into = source if jump else target
            for slot in range(source.shape[1]):
                here = pl.ds(pl.multiple_of(peer * chunk, chunk), chunk)
                piece = stage[here, slot * BLK : (slot + 1) * BLK]
                into[peer, slot] = piece.astype(bf16)
            if jump:
                swap.copy(jump).start()
        swaps.append(swap)
    if hidden:
        work = refs.take()
    for index, (in_ref, full_ref, blocks) in enumerate(zip(in_refs, full_refs, lines)):
        line = blocks.line
        if hidden and index == 0:
            for sub in range(line.rows // line.step):
                here = line.part(sub)
                values, _ = normalize(in_ref[here].astype(f32))
                work[...] = values * norm_in[0:1] + norm_in[1:2]
                store_shuffled(work, full_ref, line, here, order)
                blocks.start(sub)
        elif in_ref.dtype == bf16 and gathers[index]:
            work2 = refs.take()
            work2[...] = in_ref[...].astype(f32)
            store_shuffled(work2, full_ref, line, line.part(0), order)
            blocks.start(0)
        else:
            for sub in range(line.rows // line.step):
                here = line.part(sub)
                full_ref[line.at, here] = in_ref[here]
                blocks.start(sub)
    if normed:
        parts[norm_swap.me] = norm_in[...]
        norm_swap.wait()
        share = norm_in.shape[1]
        for index in range(n_dp):
            norm_out[:, index * share : (index + 1) * share] = parts[index]
    shares = []

    def compact(index):
        swap, row_ref, (places, split, first) = swaps[index], row_refs[index], weights[index]
        swap.wait()
        if split:
            cut, *sems = refs.take(3)
            share = Swap("fsdp", cut, row_ref, *sems)
            shares.append(share)
        else:
            cut = row_ref
        for block, (part, column) in enumerate(places):
            owner, slot = slots_ref[0, first + block], slots_ref[1, first + block]
            cut[part, :, column * BLK : (column + 1) * BLK] = swap.target[owner, slot]
        if split:
            share.start()
            share.keep()

    ahead = 0
    if inner is not None:
        ahead = 1
        inner(*inner_refs, hook=lambda: compact(0))
    for step in range(1, n_z):
        for blocks in lines:
            for sub in range(blocks.line.rows // blocks.line.step):
                blocks.forward(sub, step)
    for index in range(ahead, len(weights)):
        compact(index)
    for share in shares:
        share.wait()
    for one in [*swaps, *shares, *lines]:
        one.finish()
    if normed:
        norm_swap.finish()


class Spread(Swap):
    def copy(self, jump, arrival=False):
        peer = lax.rem(self.me + jump, self.n)
        slot = peer if arrival else self.me
        return pltpu.make_async_remote_copy(
            src_ref=self.source,
            dst_ref=self.target.at[slot],
            send_sem=self.send.at[jump],
            recv_sem=self.recv.at[slot],
            device_id={self.axis: peer},
            device_id_type=MESH,
        )


def store_shuffled(work, full_ref, line, here, order):
    rows, width = work.shape
    folds = width // order.width
    pieces = len(order.pieces)
    orders = [fold * pieces + piece for fold in range(folds) for piece in order.pieces]

    def load(group):
        return work[:, group * BLK : (group + 1) * BLK]

    def store(group, value):
        full_ref[line.at, here, group * BLK : (group + 1) * BLK] = value.astype(bf16)

    reorder(load, store, rows, width, orders)


def expand_slots(slots_ref, rows, cut, blocks, capacity, first):
    columns = rows.shape[2] // BLK
    for part in range(rows.shape[0]):
        for column in range(columns):
            blocks[part * columns + column] = rows[part, :, column * BLK : (column + 1) * BLK]
    for owner in range(cut.shape[0]):
        for position in range(capacity):
            slot = first + owner * capacity + position
            value = blocks[slots_ref[0, slot]].astype(f32)
            live = slots_ref[1, slot].astype(f32)
            cut[owner, :, position * BLK : (position + 1) * BLK] = (value * live).astype(bf16)


def expand_call(slots, rows, capacity, first, n_dp):
    chunk = rows.shape[1]
    blocks = rows.shape[0] * rows.shape[2] // BLK

    def kernel(slots_ref, row_ref, cut, blocks):
        expand_slots(slots_ref, row_ref, cut, blocks, capacity, first)

    return pl.pallas_call(
        kernel,
        name="expand",
        out_shape=shape((n_dp, chunk, capacity * BLK), bf16),
        in_specs=[pl.BlockSpec(memory_space=pltpu.SMEM), whole_vmem()],
        out_specs=whole_vmem(),
        scratch_shapes=[pltpu.VMEM((blocks, chunk, BLK), bf16)],
        compiler_params=pltpu.CompilerParams(vmem_limit_bytes=VMEM_CAP),
        cost_estimate=pl.CostEstimate(flops=0, bytes_accessed=1_000_000, transcendentals=0),
    )(slots, rows)


def leave_kernel(weights, summed, inner, inner_counts, *refs):
    refs = Refs(refs)
    n_dp = lax.axis_size("dp")
    slots_ref = refs.take()
    row_refs = refs.take(len(weights))
    term_ref = refs.take() if summed else None
    inner_refs = refs.take(inner_counts[0])
    out_refs = refs.take(len(weights))
    sum_ref = refs.take() if summed else None
    inner_refs += refs.take(inner_counts[1])
    inner_refs += refs.take(inner_counts[2])
    greet_all()
    if summed:
        cut, parts, send, recv, total, others, send2, recv2 = refs.take(8)
        share = cut.shape[2]
        for index in range(n_dp):
            cut[index] = term_ref[:, index * share : (index + 1) * share]
        term_swap = Swap("dp", cut, parts, send, recv)
        term_swap.start()
        term_swap.keep()
    shares = []
    for row_ref, (split, _, _, _) in zip(row_refs, weights):
        if split:
            held, *sems = refs.take(3)
            share = Swap("fsdp", row_ref, held, *sems)
            share.start()
            share.keep()
            shares.append(share)
        else:
            shares.append(None)
    if summed:
        term_swap.wait()
        total[...] = jnp.sum(parts[...], axis=0)
        total_spread = Spread("fsdp", total, others, send2, recv2)
        total_spread.start()
        others[total_spread.me] = total[...]
    swaps = []
    for row_ref, out_ref, share, (split, capacity, first, whole) in zip(
        row_refs, out_refs, shares, weights
    ):
        if split:
            share.wait()
        rows = share.target if split else row_ref
        if not whole:
            expand_slots(slots_ref, rows, out_ref, refs.take(), capacity, first)
            continue
        cut, *sems, blocks = refs.take(4)
        expand_slots(slots_ref, rows, cut, blocks, capacity, first)
        swap = Swap("dp", cut, out_ref, *sems)
        swap.start()
        swap.keep()
        swaps.append(swap)
    if inner is not None:
        inner(*inner_refs)
    if summed:
        total_spread.wait()
        sum_ref[...] = jnp.sum(others[...], axis=0)
    for swap in swaps:
        swap.wait()
    for one in [*swaps, *shares]:
        if one is not None:
            one.finish()
    if summed:
        term_swap.finish()
        total_spread.finish()


def fetch_columns(source, index, target, sem):
    columns = target.shape[1]
    return pltpu.make_async_copy(source.at[:, pl.ds(index * columns, columns)], target, sem)


def forward_kernel(
    n, order, half, wide, alone, att_ref, outs_hbm, base_ref, norm_ref, *rest, hook=None
):
    if wide:
        next_hbm, middle_ref, full_ref, result_ref = rest[:4]
        *rest, next_ref, next_sem = rest[4:]
    else:
        middle_ref, full_ref = rest[:2]
        rest = rest[2:]
    part, held, work, s_send, s_recv, b_send, b_recv, outs_ref, outs_sem = rest
    rows, width = base_ref.shape
    step = rows // SUBS
    load_outs = fetch_columns(outs_hbm, half, outs_ref, outs_sem)
    load_outs.start()
    if wide:
        load_next = fetch_columns(next_hbm, 3, next_ref, next_sem)
        load_next.start()
    line = Line(n, rows, step)
    if alone:
        line.greet()
    load_outs.wait()
    sums = Sums(line, part, held, s_send, s_recv)
    blocks = Blocks(line, full_ref, b_send, b_recv)

    def multiply(columns):
        product = dot(att_ref[...], outs_ref[:, columns]).astype(bf16)
        part[:, :, columns] = product.reshape(n, rows, -1)

    by_tiles(width, 256, multiply)

    def settle(sub):
        here = line.part(sub)
        sums.total(sub, work)
        middle = base_ref[here].astype(f32) + work[...]
        middle_ref[here] = middle
        normed, _ = normalize(middle)
        work[...] = normed * norm_ref[0:1] + norm_ref[1:2]

        def load(group):
            return work[:, group * BLK : (group + 1) * BLK]

        def store(group, value):
            full_ref[line.at, here, group * BLK : (group + 1) * BLK] = value.astype(bf16)

        reorder(load, store, step, width, order)
        blocks.start(sub)

    relay(n, [sums], blocks, settle, hook)
    if wide:
        load_next.wait()

        def multiply_next(columns):
            whole = full_ref[...].reshape(n * rows, width)
            result_ref[:, columns] = dot(whole, next_ref[:, columns]).astype(bf16)

        by_tiles(result_ref.shape[1], 256, multiply_next)


def carry_back(work, plain, order, step, width, middle, base, gain, term_ref, first):
    def load(group):
        return work[:, group * BLK : (group + 1) * BLK]

    def store(group, value):
        plain[:, group * BLK : (group + 1) * BLK] = value

    reorder(load, store, step, width, order)
    back_hidden = plain[...]
    normed, inverse = normalize(middle)
    gain_term = jnp.sum(back_hidden * normed, axis=0, keepdims=True)
    bias_term = jnp.sum(back_hidden, axis=0, keepdims=True)
    if first:
        term_ref[...] = jnp.zeros_like(term_ref)
        term_ref[0:1] = gain_term
        term_ref[1:2] = bias_term
    else:
        term_ref[0:1] += gain_term
        term_ref[1:2] += bias_term
    return base + norm_back(back_hidden, normed, inverse, gain)


def back_kernel(
    n, order, column, half, alone, dy_ref, w_hbm, base_ref, middle_ref, norm_ref, outs_hbm, *rest
):
    carry_ref, full_ref, att_ref, term_ref = rest[:4]
    part, held, work, plain, s_send, s_recv, b_send, b_recv = rest[4:12]
    w_ref, w_sem, outs_ref, outs_sem = rest[12:]
    rows, width = base_ref.shape
    step = rows // SUBS
    load_w = fetch_columns(w_hbm, column, w_ref, w_sem)
    load_w.start()
    load_outs = fetch_columns(outs_hbm, half, outs_ref, outs_sem)
    load_outs.start()
    line = Line(n, rows, step)
    if alone:
        line.greet()
    load_w.wait()
    sums = Sums(line, part, held, s_send, s_recv)
    blocks = Blocks(line, full_ref, b_send, b_recv)

    def multiply(columns):
        product = dot_nt(dy_ref[...], w_ref[columns]).astype(bf16)
        part[:, :, columns] = product.reshape(n, rows, -1)

    by_tiles(width, 256, multiply)

    def settle(sub):
        here = line.part(sub)
        sums.total(sub, work)
        carry = carry_back(
            work,
            plain,
            order,
            step,
            width,
            middle_ref[here].astype(f32),
            base_ref[here].astype(f32),
            norm_ref[0:1],
            term_ref,
            sub == 0,
        )
        carry_ref[here] = carry
        full_ref[line.at, here] = carry.astype(bf16)
        blocks.start(sub)

    relay(n, [sums], blocks, settle)
    load_outs.wait()

    def multiply_next(columns):
        whole = full_ref[...].reshape(n * rows, width)
        att_ref[:, columns] = dot_nt(whole, outs_ref[columns]).astype(bf16)

    by_tiles(att_ref.shape[1], 256, multiply_next)


def last_kernel(n, order, dy_ref, w_hbm, base_ref, tokens, norm_ref, branch, middle, *rest):
    grad_ref, result_ref, term_ref = rest[:3]
    part, held, held2, work, plain, s_send, s_recv, r_send, r_recv, w_ref, w_sem = rest[3:]
    rows, width = base_ref.shape
    step = rows // SUBS
    load_w = fetch_columns(w_hbm, 0, w_ref, w_sem)
    load_w.start()
    line = Line(n, rows, step)
    load_w.wait()
    sums = Sums(line, part, held, s_send, s_recv)
    results = Sums(line, branch, held2, r_send, r_recv)

    def multiply(columns):
        product = dot_nt(dy_ref[...], w_ref[columns]).astype(bf16)
        part[:, :, columns] = product.reshape(n, rows, -1)

    by_tiles(width, 256, multiply)

    def settle(sub):
        here = line.part(sub)
        sums.total(sub, work)
        carry = carry_back(
            work,
            plain,
            order,
            step,
            width,
            tokens[here].astype(f32),
            base_ref[here],
            norm_ref[0:1],
            term_ref,
            sub == 0,
        )
        grad_ref[here] = carry.astype(bf16)
        results.total(sub, work)
        result_ref[here] = (middle[here] + work[...]).astype(bf16)

    relay(n, [sums, results], None, settle)


VMEM_CAP = 52 * 1024 * 1024


def in_place():
    return pl.BlockSpec(memory_space=pl.ANY)


def whole_vmem():
    return pl.BlockSpec(memory_space=pltpu.VMEM)


def sem_pair(n, subs):
    return [pltpu.SemaphoreType.DMA((2, n, subs)), pltpu.SemaphoreType.DMA((2, n, subs))]


def line_call(kernel, name, ident, outs, specs, scratch, flops, moved):
    return pl.pallas_call(
        kernel,
        name=name,
        out_shape=outs,
        in_specs=specs,
        out_specs=jax.tree.map(lambda _: whole_vmem(), outs),
        scratch_shapes=scratch,
        compiler_params=pltpu.CompilerParams(
            collective_id=ident, has_side_effects=True, vmem_limit_bytes=VMEM_CAP
        ),
        cost_estimate=pl.CostEstimate(flops=flops, bytes_accessed=moved, transcendentals=0),
    )


def shape(dims, kind):
    return jax.ShapeDtypeStruct(dims, kind)


LINK_COST = 4_000_000


def pieces_of(rows):
    return max(1, rows * SUBS // 128)


class Order:
    def __init__(self, pieces, width):
        self.pieces, self.width = pieces, width


def swap_sems(n):
    return [pltpu.SemaphoreType.DMA((n,)), pltpu.SemaphoreType.DMA((n,))]


def enter_call(
    name, ident, slots, weights, gathers, norms, normed, hidden, n, n_dp, width, inner=None
):
    chunk = weights[0][0].shape[0] // n_dp
    run, inner_args, inner_specs, inner_outs, scratch = inner or (None, [], [], [], [])
    counts = (len(inner_args), len(inner_outs), len(scratch))
    outs, scratch = [], list(scratch)
    for array, places, split, _ in weights:
        parts = n if split else 1
        outs.append(shape((parts, chunk, len(places) // parts * BLK), bf16))
        scratch += [pltpu.VMEM(array.shape, f32), pltpu.SemaphoreType.DMA]
    if normed:
        scratch += [pltpu.VMEM((n_dp, *norms.shape), f32), *swap_sems(n_dp)]
    for array, _ in gathers:
        rows = array.shape[0]
        outs.append(shape((n, *array.shape), array.dtype))
        scratch += sem_pair(n, pieces_of(rows))
    if normed:
        outs.append(shape((norms.shape[0], n_dp * norms.shape[1]), f32))
    for array, _, _, _ in weights:
        slots_shape = (n_dp, array.shape[1] // BLK, chunk, BLK)
        scratch += [pltpu.VMEM(slots_shape, bf16)] * 2 + swap_sems(n_dp)
    if hidden:
        scratch.append(pltpu.VMEM((gathers[0][0].shape[0] // SUBS, width), f32))
    for array, moved in gathers[1 if hidden else 0 :]:
        if moved:
            scratch.append(pltpu.VMEM(array.shape, f32))
    for index, (_, places, split, _) in enumerate(weights):
        if split:
            scratch += [pltpu.VMEM(outs[index].shape, bf16), *swap_sems(n)]
    args = [slots, *(weight[0] for weight in weights), *(gather[0] for gather in gathers)]
    specs = [pl.BlockSpec(memory_space=pltpu.SMEM)] + [in_place()] * len(weights)
    specs += [whole_vmem()] * len(gathers)
    if normed or hidden:
        args.append(norms)
        specs.append(whole_vmem())
    args += inner_args
    specs += inner_specs
    outs += inner_outs
    kernel = functools.partial(
        enter_kernel,
        [weight[1:] for weight in weights],
        [gather[1] for gather in gathers],
        Order(shuffle_order(n, n_dp), width),
        normed,
        hidden,
        run,
        counts,
    )
    return line_call(kernel, name, ident, outs, specs, scratch, 0, LINK_COST)(*args)


def leave_call(name, ident, slots, weights, term, n, n_dp, inner=None):
    outs, scratch = [], []
    specs = [pl.BlockSpec(memory_space=pltpu.SMEM)] + [whole_vmem()] * len(weights)
    args = [slots, *(weight[0] for weight in weights)]
    chunk = weights[0][0].shape[1]
    if term is not None:
        args.append(term)
        specs.append(whole_vmem())
        block = (term.shape[0], term.shape[1] // n_dp)
    counts = (0, 0, 0)
    run = None
    if inner is not None:
        run, inner_args, inner_specs, inner_outs, inner_scratch = inner
        counts = (len(inner_args), len(inner_outs), len(inner_scratch))
        args += inner_args
        specs += inner_specs
        scratch += inner_scratch
    if term is not None:
        scratch += [pltpu.VMEM((n_dp, *block), f32)] * 2 + swap_sems(n_dp)
        scratch += [pltpu.VMEM(block, f32), pltpu.VMEM((n, *block), f32), *swap_sems(n)]
    for rows, split, _, _, _ in weights:
        if split:
            scratch += [pltpu.VMEM(rows.shape, bf16), *swap_sems(n)]
    for rows, _, capacity, _, whole in weights:
        slots_shape = (n_dp, chunk, capacity * BLK)
        outs.append(shape(slots_shape, bf16))
        if whole:
            scratch += [pltpu.VMEM(slots_shape, bf16), *swap_sems(n_dp)]
        blocks = rows.shape[0] * rows.shape[2] // BLK
        scratch.append(pltpu.VMEM((blocks, chunk, BLK), bf16))
    if term is not None:
        outs.append(shape(block, f32))
    if inner is not None:
        outs += inner_outs
    kernel = functools.partial(
        leave_kernel, [weight[1:] for weight in weights], term is not None, run, counts
    )
    return line_call(kernel, name, ident, outs, specs, scratch, 0, LINK_COST)(*args)


def forward_parts(attended, outs_z, half, base, norm_rows, after, n, n_dp, alone):
    rows, width = base.shape
    share = outs_z.shape[0]
    outs = [shape((rows, width), f32), shape((n, rows, width), bf16)]
    specs = [whole_vmem(), in_place(), whole_vmem(), whole_vmem()]
    args = [attended, outs_z, base, norm_rows]
    scratch = [
        pltpu.VMEM((n, rows, width), bf16),
        pltpu.VMEM((2, n, rows, width), bf16),
        pltpu.VMEM((rows // SUBS, width), f32),
        *sem_pair(n, SUBS),
        *sem_pair(n, SUBS),
        pltpu.VMEM((share, width), bf16),
        pltpu.SemaphoreType.DMA,
    ]
    if after is not None:
        outs.append(shape((n * rows, share), bf16))
        specs.append(in_place())
        args.append(after)
        scratch += [pltpu.VMEM((width, share), bf16), pltpu.SemaphoreType.DMA]
    kernel = functools.partial(
        forward_kernel, n, shuffle_order(n, n_dp), half, after is not None, alone
    )
    return kernel, args, specs, outs, scratch


def forward_call(attended, outs_z, half, base, norm_rows, after, n, n_dp, ident):
    kernel, args, specs, outs, scratch = forward_parts(
        attended, outs_z, half, base, norm_rows, after, n, n_dp, True
    )
    call = line_call(kernel, f"forward{half}", ident, outs, specs, scratch, 0, LINK_COST)
    return call(*args)


def back_parts(dy, weight, column, base, middle, norm_rows, outs_z, half, n, n_dp, alone):
    rows, width = base.shape
    share = outs_z.shape[0]
    outs = [
        shape((rows, width), f32),
        shape((n, rows, width), bf16),
        shape((n * rows, share), bf16),
        shape((8, width), f32),
    ]
    specs = [
        whole_vmem(),
        in_place(),
        whole_vmem(),
        whole_vmem(),
        whole_vmem(),
        in_place(),
    ]
    scratch = [
        pltpu.VMEM((n, rows, width), bf16),
        pltpu.VMEM((2, n, rows, width), bf16),
        pltpu.VMEM((rows // SUBS, width), f32),
        pltpu.VMEM((rows // SUBS, width), f32),
        *sem_pair(n, SUBS),
        *sem_pair(n, SUBS),
        pltpu.VMEM((width, dy.shape[1]), bf16),
        pltpu.SemaphoreType.DMA,
        pltpu.VMEM((share, width), bf16),
        pltpu.SemaphoreType.DMA,
    ]
    kernel = functools.partial(back_kernel, n, unshuffle_order(n, n_dp), column, half, alone)
    return kernel, [dy, weight, base, middle, norm_rows, outs_z], specs, outs, scratch


def back_call(dy, weight, column, base, middle, norm_rows, outs_z, half, n, n_dp, ident):
    kernel, args, specs, outs, scratch = back_parts(
        dy, weight, column, base, middle, norm_rows, outs_z, half, n, n_dp, True
    )
    call = line_call(kernel, f"back{half}", ident, outs, specs, scratch, 0, LINK_COST)
    return call(*args)


def last_parts(dy, weight, base, tokens, norm_rows, branch, middle, n, n_dp):
    rows, width = base.shape
    outs = [
        shape((rows, width), bf16),
        shape((rows, width), bf16),
        shape((8, width), f32),
    ]
    specs = [whole_vmem(), in_place()] + [whole_vmem()] * 5
    scratch = [
        pltpu.VMEM((n, rows, width), bf16),
        pltpu.VMEM((2, n, rows, width), bf16),
        pltpu.VMEM((2, n, rows, width), bf16),
        pltpu.VMEM((rows // SUBS, width), f32),
        pltpu.VMEM((rows // SUBS, width), f32),
        *sem_pair(n, SUBS),
        *sem_pair(n, SUBS),
        pltpu.VMEM((width, dy.shape[1]), bf16),
        pltpu.SemaphoreType.DMA,
    ]
    kernel = functools.partial(last_kernel, n, unshuffle_order(n, n_dp))
    return kernel, [dy, weight, base, tokens, norm_rows, branch, middle], specs, outs, scratch


def attend_forward(query, keys, values, mask_ref, keyed, att_ref, share_ref):
    packed, rows, _ = mask_ref.shape
    heads = att_ref.shape[1] // HEAD
    for p in range(packed):
        here = slice(p * rows, (p + 1) * rows)
        there = here if keyed else slice(None)
        for h in range(heads):
            columns = slice(h * HEAD, (h + 1) * HEAD)
            scores = dot_nt(query[here, columns], keys[there, columns]) * HEAD ** (-0.5)
            scores = jnp.where(mask_ref[p] > 0, scores, score_floor)
            powers = jnp.exp(scores - jnp.max(scores, axis=-1, keepdims=True))
            shares = powers / jnp.sum(powers, axis=-1, keepdims=True)
            share_ref[p * heads + h] = shares
            att_ref[here, columns] = dot(shares.astype(bf16), values[there, columns]).astype(bf16)


def attend_backward(query, keys, values, share_ref, back_ref, rows, keyed, put_query, put_pair):
    heads = back_ref.shape[1] // HEAD
    packed = back_ref.shape[0] // rows
    score_scale = HEAD ** (-0.5)
    for h in range(heads):
        columns = slice(h * HEAD, (h + 1) * HEAD)
        key_grad = value_grad = None
        for p in range(packed):
            here = slice(p * rows, (p + 1) * rows)
            there = here if keyed else slice(None)
            shares = share_ref[p * heads + h]
            back = back_ref[here, columns]
            back_shares = dot_nt(back, values[there, columns])
            inner_sum = jnp.sum(shares * back_shares, axis=-1, keepdims=True)
            back_scores = (shares * (back_shares - inner_sum)).astype(bf16)
            put_query(here, columns, dot(back_scores, keys[there, columns]) * score_scale)
            key_term = dot_tn(back_scores, query[here, columns]) * score_scale
            value_term = dot_tn(shares.astype(bf16), back)
            if keyed:
                put_pair(there, columns, key_term, value_term)
            else:
                key_grad = key_term if key_grad is None else key_grad + key_term
                value_grad = value_term if value_grad is None else value_grad + value_term
        if not keyed:
            put_pair(slice(None), columns, key_grad, value_grad)


def self_forward_kernel(h_ref, w_ref, mask_ref, proj_ref, att_ref, share_ref):
    tile = pl.program_id(0)
    proj_ref[tile] = dot(h_ref[...], w_ref[...]).astype(bf16)

    @pl.when(tile == 2)
    def _():
        attend_forward(
            proj_ref.at[0], proj_ref.at[1], proj_ref.at[2], mask_ref, True, att_ref, share_ref
        )


def cross_forward_kernel(cq_ref, text_ref, w_ref, mask_ref, kv_ref, att_ref, share_ref, total):
    tile = pl.program_id(0)
    product = dot(text_ref[...], w_ref[...])

    @pl.when(tile < 2)
    def _():
        total[tile] = product

    @pl.when(tile >= 2)
    def _():
        kv_ref[tile - 2] = (total[tile - 2] + product).astype(bf16)

    @pl.when(tile == 3)
    def _():
        attend_forward(cq_ref, kv_ref.at[0], kv_ref.at[1], mask_ref, False, att_ref, share_ref)


def ffn_kernel(h_ref, up_ref, grad_ref, act_ref, slope_ref, gdown_ref):
    up_values = dot(h_ref[...], up_ref[...])
    chance = 0.5 * (1.0 + lax.erf(up_values * 0.5**0.5))
    density = jnp.exp(-0.5 * up_values * up_values) * 0.3989422804014327
    activated = (up_values * chance).astype(bf16)
    act_ref[...] = activated
    slope_ref[...] = chance + up_values * density
    gdown_ref[...] = dot_tn(activated, grad_ref[...]).astype(bf16)


def ffn_back_kernel(
    h_ref, down_ref, grad_ref, act_ref, slope_ref, du_ref, branch_ref, gup_ref, total
):
    tile = pl.program_id(0)
    back_act = dot_nt(grad_ref[...], down_ref[...])
    back_up = (back_act * slope_ref[...]).astype(bf16)
    du_ref[...] = back_up
    gup_ref[...] = dot_tn(h_ref[...], back_up).astype(bf16)

    @pl.when(tile == 0)
    def _():
        total[...] = dot(act_ref[...], down_ref[...])

    @pl.when(tile > 0)
    def _():
        total[...] += dot(act_ref[...], down_ref[...])

    @pl.when(tile == 3)
    def _():
        branch_ref[...] = total[...].astype(bf16)


def cross_back_kernel(
    rows, back_ref, cq_ref, kv_ref, share_ref, text_ref, dcq_ref, grad_ref, pairs
):
    share = cq_ref.shape[1]

    @pl.when(pl.program_id(0) == 0)
    def _():
        def put_query(here, columns, value):
            dcq_ref[here, columns] = value.astype(bf16)

        def put_pair(there, columns, key_grad, value_grad):
            pairs[there, columns] = key_grad.astype(bf16)
            after_keys = slice(share + columns.start, share + columns.stop)
            pairs[there, after_keys] = value_grad.astype(bf16)

        attend_backward(
            cq_ref, kv_ref.at[0], kv_ref.at[1], share_ref, back_ref, rows, False, put_query, put_pair
        )

    grad_ref[...] = dot_tn(text_ref[...], pairs[...]).astype(bf16)


def outs_grad_kernel(att1_ref, carry1_ref, att2_ref, carry2_ref, grad_ref):
    tile = pl.program_id(0)

    @pl.when(tile == 0)
    def _():
        grad_ref[...] = dot_tn(att1_ref[...], carry1_ref[...]).astype(bf16)

    @pl.when(tile == 1)
    def _():
        grad_ref[...] = dot_tn(att2_ref[...], carry2_ref[...]).astype(bf16)


def self_back_kernel(
    rows, back_ref, proj_ref, share_ref, h1_ref, h2_ref, dcq_ref, dproj_ref, grad_ref, parts
):
    tile = pl.program_id(0)
    share = dcq_ref.shape[1]

    @pl.when(tile == 0)
    def _():
        def put(part, here, columns, value):
            value = value.astype(bf16)
            parts[part, here, columns] = value
            dproj_ref[here, part * share + columns.start : part * share + columns.stop] = value

        def put_query(here, columns, value):
            put(0, here, columns, value)

        def put_pair(there, columns, key_grad, value_grad):
            put(1, there, columns, key_grad)
            put(2, there, columns, value_grad)

        attend_backward(
            proj_ref.at[0],
            proj_ref.at[1],
            proj_ref.at[2],
            share_ref,
            back_ref,
            rows,
            True,
            put_query,
            put_pair,
        )

    @pl.when(tile < 3)
    def _():
        grad_ref[...] = dot_tn(h1_ref[...], parts[tile]).astype(bf16)

    @pl.when(tile == 3)
    def _():
        grad_ref[...] = dot_tn(h2_ref[...], dcq_ref[...]).astype(bf16)


def fixed(dims):
    return pl.BlockSpec(dims, lambda t: (0,) * len(dims))


def moving(dims, index):
    return pl.BlockSpec(dims, lambda t: (0, index(t)))


def local_call(kernel, name, tiles, outs, specs, out_specs, scratch, flops, moved):
    return pl.pallas_call(
        kernel,
        name=name,
        grid=(tiles,),
        out_shape=outs,
        in_specs=specs,
        out_specs=out_specs,
        scratch_shapes=scratch,
        compiler_params=pltpu.CompilerParams(vmem_limit_bytes=VMEM_CAP),
        cost_estimate=pl.CostEstimate(
            flops=flops // 8, bytes_accessed=moved // 8, transcendentals=0
        ),
    )


def self_forward(hidden, query_z, mask):
    tokens, width = hidden.shape
    share = query_z.shape[1] // 4
    packed, rows, _ = mask.shape
    pairs = (packed * share // HEAD, rows, rows)
    return local_call(
        self_forward_kernel,
        "self_forward",
        3,
        (shape((3, tokens, share), bf16), shape((tokens, share), bf16), shape(pairs, f32)),
        [fixed(hidden.shape), moving((width, share), lambda t: t), fixed(mask.shape)],
        (fixed((3, tokens, share)), fixed((tokens, share)), fixed(pairs)),
        [],
        6 * tokens * width * share,
        20_000_000,
    )(hidden, query_z, mask)


def cross_forward(cross_query, text_all, text_z, mask):
    tokens, share = cross_query.shape
    texts = text_all.shape[0]
    width = text_z.shape[0]
    packed, rows, _ = mask.shape
    pairs = (packed * share // HEAD, rows, texts)
    return local_call(
        cross_forward_kernel,
        "cross_forward",
        4,
        (shape((2, texts, share), bf16), shape((tokens, share), bf16), shape(pairs, f32)),
        [
            fixed(cross_query.shape),
            moving((texts, width), lambda t: t // 2),
            moving((width, share), lambda t: t),
            fixed(mask.shape),
        ],
        (fixed((2, texts, share)), fixed((tokens, share)), fixed(pairs)),
        [pltpu.VMEM((2, texts, share), f32)],
        8 * texts * width * share,
        20_000_000,
    )(cross_query, text_all, text_z, mask)


def ffn(hidden, up_z, grad_all):
    tokens, width = hidden.shape
    share = up_z.shape[1] // 4
    return local_call(
        ffn_kernel,
        "ffn",
        4,
        (
            shape((tokens, 4 * share), bf16),
            shape((tokens, 4 * share), f32),
            shape((share, 4 * width), bf16),
        ),
        [fixed(hidden.shape), moving((width, share), lambda t: t), fixed(grad_all.shape)],
        (
            moving((tokens, share), lambda t: t),
            moving((tokens, share), lambda t: t),
            moving((share, width), lambda t: t),
        ),
        [],
        16 * tokens * width * share,
        30_000_000,
    )(hidden, up_z, grad_all)


def ffn_back(hidden, down_z, grad_all, activated, slope):
    tokens, width = hidden.shape
    share = down_z.shape[0]
    return local_call(
        ffn_back_kernel,
        "ffn_back",
        4,
        (
            shape((tokens, 4 * share), bf16),
            shape((tokens, width), bf16),
            shape((width, 4 * share), bf16),
        ),
        [
            fixed(hidden.shape),
            moving((share, width), lambda t: t),
            fixed(grad_all.shape),
            moving((tokens, share), lambda t: t),
            moving((tokens, share), lambda t: t),
        ],
        (
            moving((tokens, share), lambda t: t),
            fixed((tokens, width)),
            moving((width, share), lambda t: t),
        ),
        [pltpu.VMEM((tokens, width), f32)],
        24 * tokens * width * share,
        40_000_000,
    )(hidden, down_z, grad_all, activated, slope)


def cross_back(back_attended, cross_query, text_pairs, shares, text_all, rows):
    tokens, share = cross_query.shape
    texts = text_all.shape[0]
    width = text_all.shape[1] // 2
    return local_call(
        functools.partial(cross_back_kernel, rows),
        "cross_back",
        2,
        (shape((tokens, share), bf16), shape((width, 4 * share), bf16)),
        [
            fixed(back_attended.shape),
            fixed(cross_query.shape),
            fixed(text_pairs.shape),
            fixed(shares.shape),
            moving((texts, width), lambda t: t),
        ],
        (fixed((tokens, share)), moving((width, 2 * share), lambda t: t)),
        [pltpu.VMEM((texts, 2 * share), bf16)],
        8 * texts * width * share,
        20_000_000,
    )(back_attended, cross_query, text_pairs, shares, text_all)


def outs_grad(attended1, carry1, attended2, carry2):
    tokens, share = attended1.shape
    width = carry1.shape[1]
    return local_call(
        outs_grad_kernel,
        "outs_grad",
        2,
        shape((share, 2 * width), bf16),
        [fixed((tokens, share)), fixed((tokens, width))] * 2,
        moving((share, width), lambda t: t),
        [],
        4 * tokens * width * share,
        10_000_000,
    )(attended1, carry1, attended2, carry2)


def self_back(back_attended, projected, shares, hidden1, hidden2, back_cross, rows):
    tokens, width = hidden1.shape
    share = back_cross.shape[1]
    return local_call(
        functools.partial(self_back_kernel, rows),
        "self_back",
        4,
        (shape((tokens, 3 * share), bf16), shape((width, 4 * share), bf16)),
        [
            fixed(back_attended.shape),
            fixed(projected.shape),
            fixed(shares.shape),
            fixed(hidden1.shape),
            fixed(hidden2.shape),
            fixed(back_cross.shape),
        ],
        (fixed((tokens, 3 * share)), moving((width, share), lambda t: t)),
        [pltpu.VMEM((3, tokens, share), bf16)],
        8 * tokens * width * share,
        25_000_000,
    )(back_attended, projected, shares, hidden1, hidden2, back_cross)


def block_slots(owners):
    owner = jnp.concatenate(owners)
    weight = jnp.concatenate([jnp.full(one.shape, at, jnp.int32) for at, one in enumerate(owners)])
    mark = owner + weight * 1024
    count = mark.shape[0]
    earlier = lax.broadcasted_iota(jnp.int32, (count, count), 1) < lax.broadcasted_iota(
        jnp.int32, (count, count), 0
    )
    same = jnp.logical_and(mark[:, None] == mark[None, :], earlier)
    return jnp.stack([owner, jnp.sum(same.astype(jnp.int32), axis=1)])


def slot_contents(owners, slots, places, capacities, firsts, n_dp):
    rows = []
    for owner, place, capacity, first in zip(owners, places, capacities, firsts):
        count = owner.shape[0]
        at = owner * capacity + slots[1, first : first + count]
        hit = at[None, :] == lax.broadcasted_iota(jnp.int32, (n_dp * capacity, count), 0)
        block = lax.broadcasted_iota(jnp.int32, (n_dp * capacity, count), 1)
        per_group, per_part, split = place_rule(place)
        part = block % per_group // per_part if split else block * 0
        column = block // per_group * per_part + block % per_part if split else block
        index = part * (count // (per_group // per_part)) + column if split else column
        rows.append(
            jnp.stack([jnp.sum(jnp.where(hit, value, 0), axis=1) for value in (index, block * 0 + 1)])
        )
    return jnp.concatenate(rows, axis=1)


def place_rule(place):
    parts = 1 + max(part for part, _ in place)
    if parts == 1:
        return 0, 0, False
    per_part = sum(1 for part, _ in place[:HEADS] if part == 0)
    return per_part * parts, per_part, True


def after(small, first):
    return lax.optimization_barrier((small, first))[0]


def body(
    tokens_in,
    text_in,
    seg_ids,
    capt_ids,
    grad_out,
    owner_query,
    owner_up,
    owner_outs,
    owner_text,
    owner_down,
    w_query,
    m_query,
    v_query,
    w_up,
    m_up,
    v_up,
    w_outs,
    m_outs,
    v_outs,
    w_text,
    m_text,
    v_text,
    w_down,
    m_down,
    v_down,
    norm_weight,
    m_norm,
    v_norm,
):
    n_dp = lax.axis_size("dp")
    n_z = lax.axis_size("fsdp")
    width = tokens_in.shape[1]
    own_rows = w_query.shape[0]
    chunk = own_rows // n_dp
    cap_big = w_query.shape[1] // BLK
    cap_out = w_outs.shape[1] // BLK
    heads_z = HEADS // n_z
    share = width // n_z
    owner_query, owner_up, owner_outs, owner_text, owner_down = (
        owner[:, 0] for owner in (owner_query, owner_up, owner_outs, owner_text, owner_down)
    )
    split_places = [split_place(b, heads_z, n_z) for b in range(owner_query.shape[0])]
    big_places = [flat_place(b) for b in range(owner_down.shape[0])]
    out_places = [flat_place(b) for b in range(owner_outs.shape[0])]
    owners = (owner_query, owner_outs, owner_text, owner_up, owner_down)
    places = (split_places, out_places, split_places, split_places, big_places)
    capacities = (cap_big, cap_out, cap_big, cap_big, cap_big)
    firsts = [sum(len(one) for one in places[:index]) for index in range(5)]
    slot_firsts = [sum(capacities[:index]) * n_dp for index in range(5)]
    slots = block_slots(owners)
    contents = slot_contents(owners, slots, places, capacities, firsts, n_dp)

    def spread(rows):
        return lax.all_gather(rows.reshape(-1, rows.shape[-1]), "dp", axis=0, tiled=True)

    def gather_sum(piece, parts):
        summed = lax.psum_scatter(piece, "dp", scatter_dimension=0, tiled=True)
        return summed.reshape(parts, chunk, -1)

    token_count = tokens_in.shape[0]
    marks = jnp.concatenate([seg_ids, capt_ids], axis=1)
    marks = jnp.pad(marks, ((0, 7), (0, 256 - marks.shape[1])))
    norms = jnp.pad(norm_weight, ((0, 2), (0, 0)))
    half = token_count // 2
    query_rows, grad_low, marks, norm_full = enter_call(
        "enter_query",
        0,
        slots,
        [(w_query, split_places, True, firsts[0])],
        [(grad_out[:half], False), (marks, False)],
        norms,
        True,
        False,
        n_z,
        n_dp,
        width,
    )
    outs_rows, hidden1, text_all, grad_high = enter_call(
        "enter_outs",
        6,
        slots,
        [(w_outs, out_places, False, firsts[1])],
        [(tokens_in, True), (text_in, True), (grad_out[half:], False)],
        norm_full[0:2],
        False,
        True,
        n_z,
        n_dp,
        width,
    )
    query_z, outs_z = spread(query_rows), spread(outs_rows)
    grad_all = jnp.concatenate([grad_low, grad_high], axis=1).reshape(-1, width)
    hidden1 = hidden1.reshape(-1, width)
    text_all = text_all.reshape(-1, text_in.shape[1])
    segment = marks[:, 0, :token_count]
    caption = marks[:, 0, token_count : token_count + capt_ids.shape[1]]
    self_mask = (segment[:, :, None] == segment[:, None, :]).astype(jnp.int32)
    text_row = lax.broadcasted_iota(jnp.int32, caption.shape, 0).reshape(1, 1, -1)
    packed_row = lax.broadcasted_iota(jnp.int32, (n_z, 1, 1), 0)
    cross_mask = jnp.logical_and(
        segment[:, :, None] == caption.reshape(1, 1, -1), packed_row == text_row
    ).astype(jnp.int32)

    projected, attended1, shares1 = self_forward(hidden1, query_z, self_mask)
    (text_rows,) = enter_call(
        "enter_text",
        7,
        after(slots, attended1),
        [(w_text, split_places, True, firsts[2])],
        [],
        None,
        False,
        False,
        n_z,
        n_dp,
        width,
    )
    up_rows, down_rows, middle1, hidden2, cross_query = enter_call(
        "forward0",
        1,
        slots,
        [(w_up, split_places, True, firsts[3]), (w_down, big_places, False, firsts[4])],
        [],
        None,
        False,
        False,
        n_z,
        n_dp,
        width,
        forward_parts(
            attended1,
            outs_z,
            0,
            tokens_in,
            after(norm_full[2:4], text_rows),
            query_z,
            n_z,
            n_dp,
            False,
        ),
    )
    hidden2 = hidden2.reshape(-1, width)
    text_z, up_z, down_z = spread(text_rows), spread(up_rows), spread(down_rows)
    text_pairs, attended2, shares2 = cross_forward(cross_query, text_all, text_z, cross_mask)
    middle2, hidden3 = forward_call(
        attended2, outs_z, 1, middle1, norm_full[4:6], None, n_z, n_dp, 2
    )
    hidden3 = hidden3.reshape(-1, width)
    activated, slope, down_part = ffn(hidden3, up_z, grad_all)
    down_sum = gather_sum(down_part, 1)
    back_up, branch3, up_part = ffn_back(hidden3, down_z, grad_all, activated, slope)
    branch3 = branch3.reshape(n_z, token_count, width)
    up_sum = gather_sum(up_part, n_z)
    at_middle2, carry2, back_att2, term3 = back_call(
        back_up, up_z, 0, grad_out, middle2, norm_full[4:6], outs_z, 1, n_z, n_dp, 3
    )
    carry2 = carry2.reshape(-1, width)
    back_cross, text_part = cross_back(
        back_att2, cross_query, text_pairs, shares2, text_all, token_count
    )
    text_sum = gather_sum(text_part, n_z)
    down_grad, at_middle1, carry1, back_att1, term2 = leave_call(
        "back0",
        4,
        contents,
        [(down_sum, False, cap_big, slot_firsts[4], True)],
        None,
        n_z,
        n_dp,
        back_parts(
            back_cross,
            query_z,
            3,
            at_middle2,
            middle1,
            after(norm_full[2:4], back_cross),
            outs_z,
            0,
            n_z,
            n_dp,
            False,
        ),
    )
    carry1 = carry1.reshape(-1, width)
    back_projected, query_part = self_back(
        back_att1, projected, shares1, hidden1, hidden2, back_cross, token_count
    )
    query_sum = gather_sum(query_part, n_z)
    outs_sum = gather_sum(outs_grad(after(attended1, query_part), carry1, attended2, carry2), 1)
    up_grad, grad_in, result, term1 = leave_call(
        "leave_up",
        8,
        contents,
        [(up_sum, True, cap_big, slot_firsts[3], True)],
        None,
        n_z,
        n_dp,
        last_parts(
            back_projected,
            query_z,
            at_middle1,
            tokens_in,
            norm_full[0:2],
            branch3,
            middle2,
            n_z,
            n_dp,
        ),
    )
    norm_term = jnp.concatenate([term1[:2], term2[:2], term3[:4]], axis=0)
    text_grad, query_slots, norm_grad = leave_call(
        "leave_query",
        9,
        contents,
        [
            (text_sum, True, cap_big, slot_firsts[2], True),
            (query_sum, True, cap_big, slot_firsts[0], False),
        ],
        norm_term,
        n_z,
        n_dp,
    )
    query_grad = lax.all_to_all(query_slots, "dp", 0, 0, tiled=True)
    outs_slots = expand_call(after(contents, query_slots), outs_sum, cap_out, slot_firsts[1], n_dp)
    outs_slots = lax.all_to_all(outs_slots, "dp", 0, 0, tiled=True)
    norm_grad = norm_grad[:6]
    query_grad, outs_slots = (
        grad.reshape(own_rows, -1).astype(f32) for grad in (query_grad, outs_slots)
    )
    text_grad, up_grad, down_grad = (
        grad.reshape(own_rows, -1).astype(f32) for grad in (text_grad, up_grad, down_grad)
    )
    up_new = adamw_update(w_up, m_up, v_up, up_grad, rate_up, decay_rate)
    text_new = adamw_update(w_text, m_text, v_text, text_grad, rate_text, decay_rate)
    down_new = adamw_update(w_down, m_down, v_down, down_grad, rate_down, decay_rate)
    query_new = adamw_update(w_query, m_query, v_query, query_grad, rate_query, decay_rate)
    outs_new = adamw_update(w_outs, m_outs, v_outs, outs_slots, rate_outs, decay_rate)
    norm_new = adamw_update(norm_weight, m_norm, v_norm, norm_grad, rate_norm, 0.0)
    return (
        result,
        grad_in,
        *query_new,
        *up_new,
        *outs_new,
        *text_new,
        *down_new,
        *norm_new,
    )


def solution(mesh):
    rows = P(("dp", "fsdp"), None)
    slots = P("fsdp", "dp")
    norms = P(None, "dp")
    in_specs = (rows,) * 5 + (P(),) * 5 + (slots,) * 15 + (norms,) * 3
    out_specs = (rows,) * 2 + (slots,) * 15 + (norms,) * 3
    return jax.shard_map(body, mesh=mesh, in_specs=in_specs, out_specs=out_specs, check_vma=False)
```

```python
import functools

import jax
import jax.numpy as jnp
from jax import lax
from jax.experimental import pallas as pl
from jax.experimental.pallas import tpu as pltpu
from jax.sharding import PartitionSpec as P

HEADS = 16
HEAD = 128
STEP = 10
BLK = 128


beta_first = 0.9
beta_second = 0.999
adam_eps = 1e-08
decay_rate = 0.01
rate_query = 0.04
rate_up = 0.04
rate_outs = 0.12
rate_text = 0.03
rate_down = 0.03
rate_norm = 0.5
norm_eps = 1e-05
score_floor = -1e30
bf16 = jnp.bfloat16
f32 = jnp.float32


def normalize(values):
    centered = values - jnp.mean(values, axis=-1, keepdims=True)
    inverse_std = lax.rsqrt(jnp.mean(centered * centered, axis=-1, keepdims=True) + norm_eps)
    return (centered * inverse_std, inverse_std)


def norm_back(back_hidden, normed, inverse_std, gain_row):
    back_normed = back_hidden * gain_row
    return inverse_std * (
        back_normed
        - jnp.mean(back_normed, axis=-1, keepdims=True)
        - normed * jnp.mean(back_normed * normed, axis=-1, keepdims=True)
    )


def adamw_update(weight, first, second, gradient, rate, decay):
    first_new = beta_first * first + (1.0 - beta_first) * gradient
    second_new = beta_second * second + (1.0 - beta_second) * gradient * gradient
    first_hat = first_new / (1.0 - beta_first**STEP)
    second_hat = second_new / (1.0 - beta_second**STEP)
    weight_new = weight - rate * (first_hat / (jnp.sqrt(second_hat) + adam_eps) + decay * weight)
    return (first_new, second_new, weight_new)


def dot(left, right):
    return jnp.dot(left, right, preferred_element_type=f32)


def dot_nt(left, right):
    return lax.dot_general(left, right, (((1,), (1,)), ((), ())), preferred_element_type=f32)


def dot_tn(left, right):
    return lax.dot_general(left, right, (((0,), (0,)), ((), ())), preferred_element_type=f32)


def split_place(block, per_part, parts):
    group, rest = divmod(block, per_part * parts)
    part, inner = divmod(rest, per_part)
    return part, group * per_part + inner


def flat_place(block):
    return 0, block


MESH = pl.DeviceIdType.MESH


SUBS = 4


class Line:
    def __init__(self, n, rows, step):
        self.n, self.rows, self.step = n, rows, step
        self.at = lax.axis_index("fsdp")

    def has(self, way):
        return self.at < self.n - 1 if way == 0 else self.at > 0

    def peer(self, way):
        index = jnp.clip(self.at + (1 if way == 0 else -1), 0, self.n - 1)
        return {"fsdp": index}

    def greet(self, others=0):
        barrier = pltpu.get_barrier_semaphore()
        for way in (0, 1):

            @pl.when(self.has(way))
            def _():
                pl.semaphore_signal(
                    barrier, inc=1, device_id=self.peer(way), device_id_type=pl.DeviceIdType.MESH
                )

        pl.semaphore_wait(
            barrier, others + self.has(0).astype(jnp.int32) + self.has(1).astype(jnp.int32)
        )

    def copy(self, source, target, send, recv, way):
        return pltpu.make_async_remote_copy(
            src_ref=source,
            dst_ref=target,
            send_sem=send,
            recv_sem=recv,
            device_id=self.peer(way),
            device_id_type=pl.DeviceIdType.MESH,
        )

    def part(self, sub):
        return pl.ds(sub * self.step, self.step)


class Sums:
    def __init__(self, line, part, held, send, recv):
        self.line, self.part, self.held, self.send, self.recv = line, part, held, send, recv

    def move(self, way, target, sub, source):
        line = self.line
        rows = line.part(sub)
        return line.copy(
            source,
            self.held.at[way, target, rows],
            self.send.at[way, target, sub],
            self.recv.at[way, target, sub],
            way,
        )

    def target(self, way, time):
        n, at = self.line.n, self.line.at
        return n - 1 - (time - at) if way == 0 else time - (n - 1 - at)

    def passes(self, way, target):
        n, at = self.line.n, self.line.at
        if way == 0:
            return jnp.logical_and(target > at, target < n)
        return jnp.logical_and(target < at, target >= 0)

    def forward(self, sub, time):
        line = self.line
        rows = line.part(sub)
        for way in (0, 1):
            target = self.target(way, time)
            passes = self.passes(way, target)
            inner = jnp.logical_and(passes, line.has(1 - way))
            outer = jnp.logical_and(passes, jnp.logical_not(line.has(1 - way)))

            @pl.when(outer)
            def _():
                self.move(way, target, sub, self.part.at[target, rows]).start()

            @pl.when(inner)
            def _():
                held = self.held.at[way, target, rows]
                self.move(way, target, sub, held).wait_recv()
                total = held[...].astype(f32) + self.part[target, rows].astype(f32)
                held[...] = total.astype(bf16)
                self.move(way, target, sub, held).start()

    def total(self, sub, sum_ref):
        line = self.line
        rows = line.part(sub)
        sum_ref[...] = self.part[line.at, rows].astype(f32)
        for way in (0, 1):

            @pl.when(line.has(1 - way))
            def _():
                held = self.held.at[way, line.at, rows]
                self.move(way, line.at, sub, held).wait_recv()
                sum_ref[...] += held[...].astype(f32)

    def finish(self):
        line = self.line
        for way in (0, 1):
            for time in range(line.n - 1):
                target = self.target(way, time)

                @pl.when(self.passes(way, target))
                def _():
                    for sub in range(line.rows // line.step):
                        held = self.held.at[way, target, line.part(sub)]
                        self.move(way, target, sub, held).wait_send()


def relay(n, sums, blocks, settle, hook=None):
    for slot in range((SUBS + 2) * (n - 1)):
        sub, time = divmod(slot, n - 1)
        if hook is not None and slot == SUBS * (n - 1):
            hook()
        if sub < SUBS:
            for one in sums:
                one.forward(sub, time)
        if time == 0 and 0 <= sub - 1 < SUBS:
            settle(sub - 1)
        if blocks is not None:
            if time == n - 2 and 0 <= sub - 1 < SUBS:
                blocks.forward(sub - 1, 1)
            if time < n - 2 and 0 <= sub - 2 < SUBS:
                blocks.forward(sub - 2, time + 2)
    for one in sums:
        one.finish()
    if blocks is not None:
        blocks.finish()


class Blocks:
    def __init__(self, line, full, send, recv):
        self.line, self.full, self.send, self.recv = line, full, send, recv

    def move(self, way, source, sub):
        line = self.line
        held = self.full.at[source, line.part(sub)]
        return line.copy(
            held, held, self.send.at[way, source, sub], self.recv.at[way, source, sub], way
        )

    def behind(self, way, source):
        return self.line.at > source if way == 0 else self.line.at < source

    def start(self, sub):
        for way in (0, 1):

            @pl.when(self.line.has(way))
            def _():
                self.move(way, self.line.at, sub).start()

    def forward(self, sub, step):
        line = self.line
        for way in (0, 1):
            source = line.at - step if way == 0 else line.at + step

            @pl.when(jnp.logical_and(source >= 0, source < line.n))
            def _():
                self.move(way, source, sub).wait_recv()

                @pl.when(line.has(way))
                def _():
                    self.move(way, source, sub).start()

    def finish(self):
        line = self.line
        for way in (0, 1):
            for source in range(line.n):
                ours = jnp.logical_or(self.behind(way, source), line.at == source)

                @pl.when(jnp.logical_and(ours, line.has(way)))
                def _():
                    for sub in range(line.rows // line.step):
                        self.move(way, source, sub).wait_send()


def lane_moves(width, order):
    moves = []
    piece = width // len(order)
    for group in range(width // BLK):
        parts = []
        for offset in range(0, BLK, piece):
            start = order[(group * BLK + offset) // piece] * piece
            parts.append((offset, start // BLK, start % BLK))
        moves.append(parts)
    return piece, moves


def reorder(load, store, rows, width, order):
    piece, moves = lane_moves(width, order)
    lane = lax.broadcasted_iota(jnp.int32, (rows, BLK), 1)
    for group, parts in enumerate(moves):
        value = None
        for offset, source, start in parts:
            block = load(source)
            if start != offset:
                block = pltpu.roll(block, (offset - start) % BLK, 1)
            value = block if value is None else jnp.where(lane >= offset, block, value)
        store(group, value)


def shuffle_order(n_z, n_dp):
    return [z * n_dp + i for i in range(n_dp) for z in range(n_z)]


def unshuffle_order(n_z, n_dp):
    return [i * n_z + z for z in range(n_z) for i in range(n_dp)]


def by_tiles(columns, tile, run):
    def one(index, carry):
        run(pl.ds(pl.multiple_of(index * tile, tile), tile))
        return carry

    lax.fori_loop(0, columns // tile, one, 0)


class Swap:
    def __init__(self, axis, source, target, send, recv):
        self.axis, self.source, self.target = axis, source, target
        self.send, self.recv = send, recv
        self.n = lax.axis_size(axis)
        self.me = lax.axis_index(axis)

    def copy(self, jump, arrival=False):
        peer = lax.rem(self.me + jump, self.n)
        slot = peer if arrival else self.me
        return pltpu.make_async_remote_copy(
            src_ref=self.source.at[peer],
            dst_ref=self.target.at[slot],
            send_sem=self.send.at[jump],
            recv_sem=self.recv.at[slot],
            device_id={self.axis: peer},
            device_id_type=MESH,
        )

    def start(self):
        for jump in range(1, self.n):
            self.copy(jump).start()

    def keep(self):
        self.target[self.me] = self.source[self.me]

    def wait(self):
        for jump in range(1, self.n):
            self.copy(jump, True).wait_recv()

    def finish(self):
        for jump in range(1, self.n):
            self.copy(jump).wait_send()


def greet_all():
    barrier = pltpu.get_barrier_semaphore()
    count = 0
    for axis in ("dp", "fsdp"):
        n, me = lax.axis_size(axis), lax.axis_index(axis)
        count += n - 1
        for jump in range(1, n):
            pl.semaphore_signal(
                barrier, inc=1, device_id={axis: lax.rem(me + jump, n)}, device_id_type=MESH
            )
    pl.semaphore_wait(barrier, count)


class Refs:
    def __init__(self, refs):
        self.refs = list(refs)

    def take(self, count=None):
        taken = self.refs[: 1 if count is None else count]
        self.refs = self.refs[len(taken) :]
        return taken[0] if count is None else taken


def enter_kernel(weights, gathers, order, normed, hidden, inner, inner_counts, *refs):
    refs = Refs(refs)
    n_dp, n_z = lax.axis_size("dp"), lax.axis_size("fsdp")
    slots_ref = refs.take()
    w_refs = refs.take(len(weights))
    in_refs = refs.take(len(gathers))
    norm_in = refs.take() if normed or hidden else None
    inner_refs = refs.take(inner_counts[0])
    row_refs = refs.take(len(weights))
    full_refs = refs.take(len(gathers))
    norm_out = refs.take() if normed else None
    inner_refs += refs.take(inner_counts[1])
    inner_refs += refs.take(inner_counts[2])
    loads = []
    for w_ref in w_refs:
        stage, sem = refs.take(2)
        load = pltpu.make_async_copy(w_ref, stage, sem)
        load.start()
        loads.append((stage, load))
    greet_all()
    if normed:
        parts, *sems = refs.take(3)
        norm_swap = Spread("dp", norm_in, parts, *sems)
        norm_swap.start()
    lines = []
    for in_ref, full_ref in zip(in_refs, full_refs):
        rows = in_ref.shape[0]
        step = rows // pieces_of(rows)
        lines.append(Blocks(Line(n_z, rows, step), full_ref, *refs.take(2)))
    swaps = []
    for (stage, load), (places, split, _) in zip(loads, weights):
        source, target, *sems = refs.take(4)
        swap = Swap("dp", source, target, *sems)
        load.wait()
        chunk = source.shape[2]
        for jump in range(n_dp):
            peer = lax.rem(swap.me + jump, n_dp)
            into = source if jump else target
            for slot in range(source.shape[1]):
                here = pl.ds(pl.multiple_of(peer * chunk, chunk), chunk)
                piece = stage[here, slot * BLK : (slot + 1) * BLK]
                into[peer, slot] = piece.astype(bf16)
            if jump:
                swap.copy(jump).start()
        swaps.append(swap)
    if hidden:
        work = refs.take()
    for index, (in_ref, full_ref, blocks) in enumerate(zip(in_refs, full_refs, lines)):
        line = blocks.line
        if hidden and index == 0:
            for sub in range(line.rows // line.step):
                here = line.part(sub)
                values, _ = normalize(in_ref[here].astype(f32))
                work[...] = values * norm_in[0:1] + norm_in[1:2]
                store_shuffled(work, full_ref, line, here, order)
                blocks.start(sub)
        elif in_ref.dtype == bf16 and gathers[index]:
            work2 = refs.take()
            work2[...] = in_ref[...].astype(f32)
            store_shuffled(work2, full_ref, line, line.part(0), order)
            blocks.start(0)
        else:
            for sub in range(line.rows // line.step):
                here = line.part(sub)
                full_ref[line.at, here] = in_ref[here]
                blocks.start(sub)
    if normed:
        parts[norm_swap.me] = norm_in[...]
        norm_swap.wait()
        share = norm_in.shape[1]
        for index in range(n_dp):
            norm_out[:, index * share : (index + 1) * share] = parts[index]
    shares = []

    def compact(index):
        swap, row_ref, (places, split, first) = swaps[index], row_refs[index], weights[index]
        swap.wait()
        if split:
            cut, *sems = refs.take(3)
            share = Swap("fsdp", cut, row_ref, *sems)
            shares.append(share)
        else:
            cut = row_ref
        for block, (part, column) in enumerate(places):
            owner, slot = slots_ref[0, first + block], slots_ref[1, first + block]
            cut[part, :, column * BLK : (column + 1) * BLK] = swap.target[owner, slot]
        if split:
            share.start()
            share.keep()

    ahead = 0
    if inner is not None:
        ahead = 1
        inner(*inner_refs, hook=lambda: compact(0))
    for step in range(1, n_z):
        for blocks in lines:
            for sub in range(blocks.line.rows // blocks.line.step):
                blocks.forward(sub, step)
    for index in range(ahead, len(weights)):
        compact(index)
    for share in shares:
        share.wait()
    for one in [*swaps, *shares, *lines]:
        one.finish()
    if normed:
        norm_swap.finish()


class Spread(Swap):
    def copy(self, jump, arrival=False):
        peer = lax.rem(self.me + jump, self.n)
        slot = peer if arrival else self.me
        return pltpu.make_async_remote_copy(
            src_ref=self.source,
            dst_ref=self.target.at[slot],
            send_sem=self.send.at[jump],
            recv_sem=self.recv.at[slot],
            device_id={self.axis: peer},
            device_id_type=MESH,
        )


def store_shuffled(work, full_ref, line, here, order):
    rows, width = work.shape
    folds = width // order.width
    pieces = len(order.pieces)
    orders = [fold * pieces + piece for fold in range(folds) for piece in order.pieces]

    def load(group):
        return work[:, group * BLK : (group + 1) * BLK]

    def store(group, value):
        full_ref[line.at, here, group * BLK : (group + 1) * BLK] = value.astype(bf16)

    reorder(load, store, rows, width, orders)


def expand_slots(slots_ref, rows, cut, blocks, capacity, first, offset):
    columns = rows.shape[2] // BLK
    for part in range(rows.shape[0]):
        for column in range(columns):
            blocks[part * columns + column] = rows[part, :, column * BLK : (column + 1) * BLK]
    for owner in range(cut.shape[0]):
        for position in range(capacity):
            slot = first + owner * capacity + position
            value = blocks[slots_ref[0, slot]].astype(f32)
            live = slots_ref[1, slot].astype(f32)
            start = offset + position * BLK
            cut[owner, :, start : start + BLK] = (value * live).astype(bf16)


def leave_kernel(weights, summed, inner, inner_counts, *refs):
    refs = Refs(refs)
    n_dp = lax.axis_size("dp")
    slots_ref = refs.take()
    row_refs = refs.take(len(weights))
    term_ref = refs.take() if summed else None
    inner_refs = refs.take(inner_counts[0])
    gone = sum(1 for weight in weights if weight[3])
    out_refs = refs.take(gone)
    loose_ref = refs.take() if gone < len(weights) else None
    sum_ref = refs.take() if summed else None
    inner_refs += refs.take(inner_counts[1])
    inner_refs += refs.take(inner_counts[2])
    greet_all()
    if summed:
        cut, parts, send, recv, total, others, send2, recv2 = refs.take(8)
        share = cut.shape[2]
        for index in range(n_dp):
            cut[index] = term_ref[:, index * share : (index + 1) * share]
        term_swap = Swap("dp", cut, parts, send, recv)
        term_swap.start()
        term_swap.keep()
    shares = []
    for row_ref, (split, _, _, _) in zip(row_refs, weights):
        if split:
            held, *sems = refs.take(3)
            share = Swap("fsdp", row_ref, held, *sems)
            share.start()
            share.keep()
            shares.append(share)
        else:
            shares.append(None)
    if summed:
        term_swap.wait()
        total[...] = jnp.sum(parts[...], axis=0)
        total_spread = Spread("fsdp", total, others, send2, recv2)
        total_spread.start()
        others[total_spread.me] = total[...]
    swaps = []
    offset = 0
    for row_ref, share, (split, capacity, first, whole) in zip(row_refs, shares, weights):
        if split:
            share.wait()
        rows = share.target if split else row_ref
        if not whole:
            expand_slots(slots_ref, rows, loose_ref, refs.take(), capacity, first, offset)
            offset += capacity * BLK
            continue
        out_ref = out_refs.pop(0)
        cut, *sems, blocks = refs.take(4)
        expand_slots(slots_ref, rows, cut, blocks, capacity, first, 0)
        swap = Swap("dp", cut, out_ref, *sems)
        swap.start()
        swap.keep()
        swaps.append(swap)
    if inner is not None:
        inner(*inner_refs)
    if summed:
        total_spread.wait()
        sum_ref[...] = jnp.sum(others[...], axis=0)
    for swap in swaps:
        swap.wait()
    for one in [*swaps, *shares]:
        if one is not None:
            one.finish()
    if summed:
        term_swap.finish()
        total_spread.finish()


def fetch_columns(source, index, target, sem):
    columns = target.shape[1]
    return pltpu.make_async_copy(source.at[:, pl.ds(index * columns, columns)], target, sem)


def forward_kernel(
    n, order, half, wide, alone, att_ref, outs_hbm, base_ref, norm_ref, *rest, hook=None
):
    if wide:
        next_hbm, middle_ref, full_ref, result_ref = rest[:4]
        *rest, next_ref, next_sem = rest[4:]
    else:
        middle_ref, full_ref = rest[:2]
        rest = rest[2:]
    part, held, work, s_send, s_recv, b_send, b_recv, outs_ref, outs_sem = rest
    rows, width = base_ref.shape
    step = rows // SUBS
    load_outs = fetch_columns(outs_hbm, half, outs_ref, outs_sem)
    load_outs.start()
    if wide:
        load_next = fetch_columns(next_hbm, 3, next_ref, next_sem)
        load_next.start()
    line = Line(n, rows, step)
    if alone:
        line.greet()
    load_outs.wait()
    sums = Sums(line, part, held, s_send, s_recv)
    blocks = Blocks(line, full_ref, b_send, b_recv)

    def multiply(columns):
        product = dot(att_ref[...], outs_ref[:, columns]).astype(bf16)
        part[:, :, columns] = product.reshape(n, rows, -1)

    by_tiles(width, 256, multiply)

    def settle(sub):
        here = line.part(sub)
        sums.total(sub, work)
        middle = base_ref[here].astype(f32) + work[...]
        middle_ref[here] = middle
        normed, _ = normalize(middle)
        work[...] = normed * norm_ref[0:1] + norm_ref[1:2]

        def load(group):
            return work[:, group * BLK : (group + 1) * BLK]

        def store(group, value):
            full_ref[line.at, here, group * BLK : (group + 1) * BLK] = value.astype(bf16)

        reorder(load, store, step, width, order)
        blocks.start(sub)

    relay(n, [sums], blocks, settle, hook)
    if wide:
        load_next.wait()

        def multiply_next(columns):
            whole = full_ref[...].reshape(n * rows, width)
            result_ref[:, columns] = dot(whole, next_ref[:, columns]).astype(bf16)

        by_tiles(result_ref.shape[1], 256, multiply_next)


def carry_back(work, plain, order, step, width, middle, base, gain, term_ref, first):
    def load(group):
        return work[:, group * BLK : (group + 1) * BLK]

    def store(group, value):
        plain[:, group * BLK : (group + 1) * BLK] = value

    reorder(load, store, step, width, order)
    back_hidden = plain[...]
    normed, inverse = normalize(middle)
    gain_term = jnp.sum(back_hidden * normed, axis=0, keepdims=True)
    bias_term = jnp.sum(back_hidden, axis=0, keepdims=True)
    if first:
        term_ref[...] = jnp.zeros_like(term_ref)
        term_ref[0:1] = gain_term
        term_ref[1:2] = bias_term
    else:
        term_ref[0:1] += gain_term
        term_ref[1:2] += bias_term
    return base + norm_back(back_hidden, normed, inverse, gain)


def back_kernel(
    n, order, column, half, alone, dy_ref, w_hbm, base_ref, middle_ref, norm_ref, outs_hbm, *rest
):
    carry_ref, full_ref, att_ref, term_ref = rest[:4]
    held, work, plain, s_send, s_recv, b_send, b_recv, outs_ref, outs_sem = rest[4:13]
    rows, width = base_ref.shape
    step = rows // SUBS
    if column is not None:
        part, w_ref, w_sem = rest[13:]
        load_w = fetch_columns(w_hbm, column, w_ref, w_sem)
        load_w.start()
    else:
        part = dy_ref
    load_outs = fetch_columns(outs_hbm, half, outs_ref, outs_sem)
    load_outs.start()
    line = Line(n, rows, step)
    if alone:
        line.greet()
    sums = Sums(line, part, held, s_send, s_recv)
    blocks = Blocks(line, full_ref, b_send, b_recv)
    if column is not None:
        load_w.wait()

        def multiply(columns):
            product = dot_nt(dy_ref[...], w_ref[columns]).astype(bf16)
            part[:, :, columns] = product.reshape(n, rows, -1)

        by_tiles(width, 256, multiply)

    def settle(sub):
        here = line.part(sub)
        sums.total(sub, work)
        carry = carry_back(
            work,
            plain,
            order,
            step,
            width,
            middle_ref[here].astype(f32),
            base_ref[here].astype(f32),
            norm_ref[0:1],
            term_ref,
            sub == 0,
        )
        carry_ref[here] = carry
        full_ref[line.at, here] = carry.astype(bf16)
        blocks.start(sub)

    relay(n, [sums], blocks, settle)
    load_outs.wait()

    def multiply_next(columns):
        whole = full_ref[...].reshape(n * rows, width)
        att_ref[:, columns] = dot_nt(whole, outs_ref[columns]).astype(bf16)

    by_tiles(att_ref.shape[1], 256, multiply_next)


def last_kernel(n, order, dy_ref, w_hbm, base_ref, tokens, norm_ref, branch, middle, *rest):
    grad_ref, result_ref, term_ref = rest[:3]
    part, held, held2, work, plain, s_send, s_recv, r_send, r_recv, w_ref, w_sem = rest[3:]
    rows, width = base_ref.shape
    step = rows // SUBS
    load_w = fetch_columns(w_hbm, 0, w_ref, w_sem)
    load_w.start()
    line = Line(n, rows, step)
    load_w.wait()
    sums = Sums(line, part, held, s_send, s_recv)
    results = Sums(line, branch, held2, r_send, r_recv)

    def multiply(columns):
        product = dot_nt(dy_ref[...], w_ref[columns]).astype(bf16)
        part[:, :, columns] = product.reshape(n, rows, -1)

    by_tiles(width, 256, multiply)

    def settle(sub):
        here = line.part(sub)
        sums.total(sub, work)
        carry = carry_back(
            work,
            plain,
            order,
            step,
            width,
            tokens[here].astype(f32),
            base_ref[here],
            norm_ref[0:1],
            term_ref,
            sub == 0,
        )
        grad_ref[here] = carry.astype(bf16)
        results.total(sub, work)
        result_ref[here] = (middle[here] + work[...]).astype(bf16)

    relay(n, [sums, results], None, settle)


VMEM_CAP = 52 * 1024 * 1024


def in_place():
    return pl.BlockSpec(memory_space=pl.ANY)


def whole_vmem():
    return pl.BlockSpec(memory_space=pltpu.VMEM)


def sem_pair(n, subs):
    return [pltpu.SemaphoreType.DMA((2, n, subs)), pltpu.SemaphoreType.DMA((2, n, subs))]


def line_call(kernel, name, ident, outs, specs, scratch, flops, moved):
    return pl.pallas_call(
        kernel,
        name=name,
        out_shape=outs,
        in_specs=specs,
        out_specs=jax.tree.map(lambda _: whole_vmem(), outs),
        scratch_shapes=scratch,
        compiler_params=pltpu.CompilerParams(
            collective_id=ident, has_side_effects=True, vmem_limit_bytes=VMEM_CAP
        ),
        cost_estimate=pl.CostEstimate(flops=flops, bytes_accessed=moved, transcendentals=0),
    )


def shape(dims, kind):
    return jax.ShapeDtypeStruct(dims, kind)


LINK_COST = 4_000_000


def pieces_of(rows):
    return max(1, rows * SUBS // 128)


class Order:
    def __init__(self, pieces, width):
        self.pieces, self.width = pieces, width


def swap_sems(n):
    return [pltpu.SemaphoreType.DMA((n,)), pltpu.SemaphoreType.DMA((n,))]


def enter_call(
    name, ident, slots, weights, gathers, norms, normed, hidden, n, n_dp, width, inner=None
):
    chunk = weights[0][0].shape[0] // n_dp
    run, inner_args, inner_specs, inner_outs, scratch = inner or (None, [], [], [], [])
    counts = (len(inner_args), len(inner_outs), len(scratch))
    outs, scratch = [], list(scratch)
    for array, places, split, _ in weights:
        parts = n if split else 1
        outs.append(shape((parts, chunk, len(places) // parts * BLK), bf16))
        scratch += [pltpu.VMEM(array.shape, f32), pltpu.SemaphoreType.DMA]
    if normed:
        scratch += [pltpu.VMEM((n_dp, *norms.shape), f32), *swap_sems(n_dp)]
    for array, _ in gathers:
        rows = array.shape[0]
        outs.append(shape((n, *array.shape), array.dtype))
        scratch += sem_pair(n, pieces_of(rows))
    if normed:
        outs.append(shape((norms.shape[0], n_dp * norms.shape[1]), f32))
    for array, _, _, _ in weights:
        slots_shape = (n_dp, array.shape[1] // BLK, chunk, BLK)
        scratch += [pltpu.VMEM(slots_shape, bf16)] * 2 + swap_sems(n_dp)
    if hidden:
        scratch.append(pltpu.VMEM((gathers[0][0].shape[0] // SUBS, width), f32))
    for array, moved in gathers[1 if hidden else 0 :]:
        if moved:
            scratch.append(pltpu.VMEM(array.shape, f32))
    for index, (_, places, split, _) in enumerate(weights):
        if split:
            scratch += [pltpu.VMEM(outs[index].shape, bf16), *swap_sems(n)]
    args = [slots, *(weight[0] for weight in weights), *(gather[0] for gather in gathers)]
    specs = [pl.BlockSpec(memory_space=pltpu.SMEM)] + [in_place()] * len(weights)
    specs += [whole_vmem()] * len(gathers)
    if normed or hidden:
        args.append(norms)
        specs.append(whole_vmem())
    args += inner_args
    specs += inner_specs
    outs += inner_outs
    kernel = functools.partial(
        enter_kernel,
        [weight[1:] for weight in weights],
        [gather[1] for gather in gathers],
        Order(shuffle_order(n, n_dp), width),
        normed,
        hidden,
        run,
        counts,
    )
    return line_call(kernel, name, ident, outs, specs, scratch, 0, LINK_COST)(*args)


def leave_call(name, ident, slots, weights, term, n, n_dp, inner=None):
    outs, scratch = [], []
    specs = [pl.BlockSpec(memory_space=pltpu.SMEM)] + [whole_vmem()] * len(weights)
    args = [slots, *(weight[0] for weight in weights)]
    chunk = weights[0][0].shape[1]
    if term is not None:
        args.append(term)
        specs.append(whole_vmem())
        block = (term.shape[0], term.shape[1] // n_dp)
    counts = (0, 0, 0)
    run = None
    if inner is not None:
        run, inner_args, inner_specs, inner_outs, inner_scratch = inner
        counts = (len(inner_args), len(inner_outs), len(inner_scratch))
        args += inner_args
        specs += inner_specs
        scratch += inner_scratch
    if term is not None:
        scratch += [pltpu.VMEM((n_dp, *block), f32)] * 2 + swap_sems(n_dp)
        scratch += [pltpu.VMEM(block, f32), pltpu.VMEM((n, *block), f32), *swap_sems(n)]
    for rows, split, _, _, _ in weights:
        if split:
            scratch += [pltpu.VMEM(rows.shape, bf16), *swap_sems(n)]
    for rows, _, capacity, _, whole in weights:
        slots_shape = (n_dp, chunk, capacity * BLK)
        if whole:
            outs.append(shape(slots_shape, bf16))
            scratch += [pltpu.VMEM(slots_shape, bf16), *swap_sems(n_dp)]
        blocks = rows.shape[0] * rows.shape[2] // BLK
        scratch.append(pltpu.VMEM((blocks, chunk, BLK), bf16))
    loose = sum(capacity * BLK for _, _, capacity, _, whole in weights if not whole)
    if loose:
        outs.append(shape((n_dp, chunk, loose), bf16))
    if term is not None:
        outs.append(shape(block, f32))
    if inner is not None:
        outs += inner_outs
    kernel = functools.partial(
        leave_kernel, [weight[1:] for weight in weights], term is not None, run, counts
    )
    return line_call(kernel, name, ident, outs, specs, scratch, 0, LINK_COST)(*args)


def forward_parts(attended, outs_z, half, base, norm_rows, after, n, n_dp, alone):
    rows, width = base.shape
    share = outs_z.shape[0]
    outs = [shape((rows, width), f32), shape((n, rows, width), bf16)]
    specs = [whole_vmem(), in_place(), whole_vmem(), whole_vmem()]
    args = [attended, outs_z, base, norm_rows]
    scratch = [
        pltpu.VMEM((n, rows, width), bf16),
        pltpu.VMEM((2, n, rows, width), bf16),
        pltpu.VMEM((rows // SUBS, width), f32),
        *sem_pair(n, SUBS),
        *sem_pair(n, SUBS),
        pltpu.VMEM((share, width), bf16),
        pltpu.SemaphoreType.DMA,
    ]
    if after is not None:
        outs.append(shape((n * rows, share), bf16))
        specs.append(in_place())
        args.append(after)
        scratch += [pltpu.VMEM((width, share), bf16), pltpu.SemaphoreType.DMA]
    kernel = functools.partial(
        forward_kernel, n, shuffle_order(n, n_dp), half, after is not None, alone
    )
    return kernel, args, specs, outs, scratch


def forward_call(attended, outs_z, half, base, norm_rows, after, n, n_dp, ident):
    kernel, args, specs, outs, scratch = forward_parts(
        attended, outs_z, half, base, norm_rows, after, n, n_dp, True
    )
    call = line_call(kernel, f"forward{half}", ident, outs, specs, scratch, 0, LINK_COST)
    return call(*args)


def back_parts(dy, weight, column, base, middle, norm_rows, outs_z, half, n, n_dp, alone):
    rows, width = base.shape
    share = outs_z.shape[0]
    outs = [
        shape((rows, width), f32),
        shape((n, rows, width), bf16),
        shape((n * rows, share), bf16),
        shape((8, width), f32),
    ]
    specs = [
        whole_vmem(),
        in_place(),
        whole_vmem(),
        whole_vmem(),
        whole_vmem(),
        in_place(),
    ]
    scratch = [
        pltpu.VMEM((2, n, rows, width), bf16),
        pltpu.VMEM((rows // SUBS, width), f32),
        pltpu.VMEM((rows // SUBS, width), f32),
        *sem_pair(n, SUBS),
        *sem_pair(n, SUBS),
        pltpu.VMEM((share, width), bf16),
        pltpu.SemaphoreType.DMA,
    ]
    if column is not None:
        scratch += [
            pltpu.VMEM((n, rows, width), bf16),
            pltpu.VMEM((width, dy.shape[1]), bf16),
            pltpu.SemaphoreType.DMA,
        ]
    kernel = functools.partial(back_kernel, n, unshuffle_order(n, n_dp), column, half, alone)
    return kernel, [dy, weight, base, middle, norm_rows, outs_z], specs, outs, scratch


def back_call(dy, weight, column, base, middle, norm_rows, outs_z, half, n, n_dp, ident):
    kernel, args, specs, outs, scratch = back_parts(
        dy, weight, column, base, middle, norm_rows, outs_z, half, n, n_dp, True
    )
    call = line_call(kernel, f"back{half}", ident, outs, specs, scratch, 0, LINK_COST)
    return call(*args)


def last_parts(dy, weight, base, tokens, norm_rows, branch, middle, n, n_dp):
    rows, width = base.shape
    outs = [
        shape((rows, width), bf16),
        shape((rows, width), bf16),
        shape((8, width), f32),
    ]
    specs = [whole_vmem(), in_place()] + [whole_vmem()] * 5
    scratch = [
        pltpu.VMEM((n, rows, width), bf16),
        pltpu.VMEM((2, n, rows, width), bf16),
        pltpu.VMEM((2, n, rows, width), bf16),
        pltpu.VMEM((rows // SUBS, width), f32),
        pltpu.VMEM((rows // SUBS, width), f32),
        *sem_pair(n, SUBS),
        *sem_pair(n, SUBS),
        pltpu.VMEM((width, dy.shape[1]), bf16),
        pltpu.SemaphoreType.DMA,
    ]
    kernel = functools.partial(last_kernel, n, unshuffle_order(n, n_dp))
    return kernel, [dy, weight, base, tokens, norm_rows, branch, middle], specs, outs, scratch


def attend_forward(query, keys, values, mask_ref, keyed, att_ref, share_ref):
    packed, rows, _ = mask_ref.shape
    heads = att_ref.shape[1] // HEAD
    for p in range(packed):
        here = slice(p * rows, (p + 1) * rows)
        there = here if keyed else slice(None)
        for h in range(heads):
            columns = slice(h * HEAD, (h + 1) * HEAD)
            scores = dot_nt(query[here, columns], keys[there, columns]) * HEAD ** (-0.5)
            scores = jnp.where(mask_ref[p] > 0, scores, score_floor)
            powers = jnp.exp(scores - jnp.max(scores, axis=-1, keepdims=True))
            shares = powers / jnp.sum(powers, axis=-1, keepdims=True)
            share_ref[p * heads + h] = shares
            att_ref[here, columns] = dot(shares.astype(bf16), values[there, columns]).astype(bf16)


def attend_backward(query, keys, values, share_ref, back_ref, rows, keyed, put_query, put_pair):
    heads = back_ref.shape[1] // HEAD
    packed = back_ref.shape[0] // rows
    score_scale = HEAD ** (-0.5)
    for h in range(heads):
        columns = slice(h * HEAD, (h + 1) * HEAD)
        key_grad = value_grad = None
        for p in range(packed):
            here = slice(p * rows, (p + 1) * rows)
            there = here if keyed else slice(None)
            shares = share_ref[p * heads + h]
            back = back_ref[here, columns]
            back_shares = dot_nt(back, values[there, columns])
            inner_sum = jnp.sum(shares * back_shares, axis=-1, keepdims=True)
            back_scores = (shares * (back_shares - inner_sum)).astype(bf16)
            put_query(here, columns, dot(back_scores, keys[there, columns]) * score_scale)
            key_term = dot_tn(back_scores, query[here, columns]) * score_scale
            value_term = dot_tn(shares.astype(bf16), back)
            if keyed:
                put_pair(there, columns, key_term, value_term)
            else:
                key_grad = key_term if key_grad is None else key_grad + key_term
                value_grad = value_term if value_grad is None else value_grad + value_term
        if not keyed:
            put_pair(slice(None), columns, key_grad, value_grad)


def self_forward_kernel(h_ref, w_ref, mask_ref, proj_ref, att_ref, share_ref):
    tile = pl.program_id(0)
    proj_ref[tile] = dot(h_ref[...], w_ref[...]).astype(bf16)

    @pl.when(tile == 2)
    def _():
        attend_forward(
            proj_ref.at[0], proj_ref.at[1], proj_ref.at[2], mask_ref, True, att_ref, share_ref
        )


def cross_forward_kernel(cq_ref, text_ref, w_ref, mask_ref, kv_ref, att_ref, share_ref, total):
    tile = pl.program_id(0)
    product = dot(text_ref[...], w_ref[...])

    @pl.when(tile < 2)
    def _():
        total[tile] = product

    @pl.when(tile >= 2)
    def _():
        kv_ref[tile - 2] = (total[tile - 2] + product).astype(bf16)

    @pl.when(tile == 3)
    def _():
        attend_forward(cq_ref, kv_ref.at[0], kv_ref.at[1], mask_ref, False, att_ref, share_ref)


def ffn_kernel(h_ref, up_ref, grad_ref, act_ref, slope_ref, gdown_ref):
    up_values = dot(h_ref[...], up_ref[...])
    chance = 0.5 * (1.0 + lax.erf(up_values * 0.5**0.5))
    density = jnp.exp(-0.5 * up_values * up_values) * 0.3989422804014327
    activated = (up_values * chance).astype(bf16)
    act_ref[...] = activated
    slope_ref[...] = chance + up_values * density
    gradient = dot_tn(activated, grad_ref[...]).astype(bf16)
    n_dp, rows, columns = gdown_ref.shape
    chunk = gradient.shape[0] // n_dp
    for piece in range(rows // chunk):
        cut = gradient[:, piece * columns : (piece + 1) * columns]
        gdown_ref[:, piece * chunk : (piece + 1) * chunk] = cut.reshape(n_dp, chunk, columns)


def ffn_back_kernel(
    h_ref,
    down_ref,
    up_ref,
    grad_ref,
    act_ref,
    slope_ref,
    both_ref,
    branch_ref,
    part_ref,
    gup_ref,
    total,
    part,
):
    del both_ref
    tile = pl.program_id(0)
    back_act = dot_nt(grad_ref[...], down_ref[...])
    back_up = (back_act * slope_ref[...]).astype(bf16)
    gup_ref[...] = dot_tn(h_ref[...], back_up).astype(bf16).reshape(gup_ref.shape)

    @pl.when(tile == 0)
    def _():
        total[...] = dot(act_ref[...], down_ref[...])
        part[...] = dot_nt(back_up, up_ref[...])

    @pl.when(tile > 0)
    def _():
        total[...] += dot(act_ref[...], down_ref[...])
        part[...] += dot_nt(back_up, up_ref[...])

    @pl.when(tile == 3)
    def _():
        branch_ref[...] = total[...].astype(bf16)
        part_ref[...] = part[...].astype(bf16)


def cross_back_kernel(
    rows, back_ref, cq_ref, kv_ref, share_ref, text_ref, dcq_ref, grad_ref, pairs
):
    share = cq_ref.shape[1]

    @pl.when(pl.program_id(0) == 0)
    def _():
        def put_query(here, columns, value):
            dcq_ref[here, columns] = value.astype(bf16)

        def put_pair(there, columns, key_grad, value_grad):
            pairs[there, columns] = key_grad.astype(bf16)
            after_keys = slice(share + columns.start, share + columns.stop)
            pairs[there, after_keys] = value_grad.astype(bf16)

        attend_backward(
            cq_ref, kv_ref.at[0], kv_ref.at[1], share_ref, back_ref, rows, False, put_query, put_pair
        )

    grad_ref[...] = dot_tn(text_ref[...], pairs[...]).astype(bf16)


def outs_grad_kernel(att1_ref, carry1_ref, att2_ref, carry2_ref, grad_ref):
    tile = pl.program_id(0)

    @pl.when(tile == 0)
    def _():
        grad_ref[...] = dot_tn(att1_ref[...], carry1_ref[...]).astype(bf16)

    @pl.when(tile == 1)
    def _():
        grad_ref[...] = dot_tn(att2_ref[...], carry2_ref[...]).astype(bf16)


def self_back_kernel(
    rows, back_ref, proj_ref, share_ref, h1_ref, h2_ref, dcq_ref, dproj_ref, grad_ref, parts
):
    tile = pl.program_id(0)
    share = dcq_ref.shape[1]

    @pl.when(tile == 0)
    def _():
        def put(part, here, columns, value):
            value = value.astype(bf16)
            parts[part, here, columns] = value
            dproj_ref[here, part * share + columns.start : part * share + columns.stop] = value

        def put_query(here, columns, value):
            put(0, here, columns, value)

        def put_pair(there, columns, key_grad, value_grad):
            put(1, there, columns, key_grad)
            put(2, there, columns, value_grad)

        attend_backward(
            proj_ref.at[0],
            proj_ref.at[1],
            proj_ref.at[2],
            share_ref,
            back_ref,
            rows,
            True,
            put_query,
            put_pair,
        )

    @pl.when(tile < 3)
    def _():
        grad_ref[...] = dot_tn(h1_ref[...], parts[tile]).astype(bf16)

    @pl.when(tile == 3)
    def _():
        grad_ref[...] = dot_tn(h2_ref[...], dcq_ref[...]).astype(bf16)


def fixed(dims):
    return pl.BlockSpec(dims, lambda t: (0,) * len(dims))


def moving(dims, index):
    return pl.BlockSpec(dims, lambda t: (0, index(t)))


def local_call(
    kernel, name, tiles, outs, specs, out_specs, scratch, flops, moved, aliases=None
):
    return pl.pallas_call(
        kernel,
        name=name,
        grid=(tiles,),
        input_output_aliases=aliases or {},
        out_shape=outs,
        in_specs=specs,
        out_specs=out_specs,
        scratch_shapes=scratch,
        compiler_params=pltpu.CompilerParams(vmem_limit_bytes=VMEM_CAP),
        cost_estimate=pl.CostEstimate(
            flops=flops // 8, bytes_accessed=moved // 8, transcendentals=0
        ),
    )


def self_forward(hidden, query_z, mask):
    tokens, width = hidden.shape
    share = query_z.shape[1] // 4
    packed, rows, _ = mask.shape
    pairs = (packed * share // HEAD, rows, rows)
    return local_call(
        self_forward_kernel,
        "self_forward",
        3,
        (shape((3, tokens, share), bf16), shape((tokens, share), bf16), shape(pairs, f32)),
        [fixed(hidden.shape), moving((width, share), lambda t: t), fixed(mask.shape)],
        (fixed((3, tokens, share)), fixed((tokens, share)), fixed(pairs)),
        [],
        6 * tokens * width * share,
        20_000_000,
    )(hidden, query_z, mask)


def cross_forward(cross_query, text_all, text_z, mask):
    tokens, share = cross_query.shape
    texts = text_all.shape[0]
    width = text_z.shape[0]
    packed, rows, _ = mask.shape
    pairs = (packed * share // HEAD, rows, texts)
    return local_call(
        cross_forward_kernel,
        "cross_forward",
        4,
        (shape((2, texts, share), bf16), shape((tokens, share), bf16), shape(pairs, f32)),
        [
            fixed(cross_query.shape),
            moving((texts, width), lambda t: t // 2),
            moving((width, share), lambda t: t),
            fixed(mask.shape),
        ],
        (fixed((2, texts, share)), fixed((tokens, share)), fixed(pairs)),
        [pltpu.VMEM((2, texts, share), f32)],
        8 * texts * width * share,
        20_000_000,
    )(cross_query, text_all, text_z, mask)


def ffn(hidden, up_z, grad_all, n, n_dp):
    tokens, width = hidden.shape
    share = up_z.shape[1] // 4
    chunk = share // n_dp
    return local_call(
        ffn_kernel,
        "ffn",
        4,
        (
            shape((tokens, 4 * share), bf16),
            shape((tokens, 4 * share), f32),
            shape((n_dp, 2 * n * chunk, 4 * share), bf16),
        ),
        [fixed(hidden.shape), moving((width, share), lambda t: t), fixed(grad_all.shape)],
        (
            moving((tokens, share), lambda t: t),
            moving((tokens, share), lambda t: t),
            pl.BlockSpec((n_dp, n * chunk // 4, 4 * share), lambda t: (0, 4 + t, 0)),
        ),
        [],
        16 * tokens * width * share,
        30_000_000,
    )(hidden, up_z, grad_all)


def ffn_back(hidden, down_z, up_z, grad_all, activated, slope, both):
    tokens, width = hidden.shape
    share = down_z.shape[0]
    return local_call(
        ffn_back_kernel,
        "ffn_back",
        4,
        (shape((tokens, width), bf16), shape((tokens, width), bf16), shape(both.shape, bf16)),
        [
            fixed(hidden.shape),
            moving((share, width), lambda t: t),
            moving((width, share), lambda t: t),
            fixed(grad_all.shape),
            moving((tokens, share), lambda t: t),
            moving((tokens, share), lambda t: t),
            in_place(),
        ],
        (
            fixed((tokens, width)),
            fixed((tokens, width)),
            pl.BlockSpec((both.shape[0], both.shape[1] // 2, share), lambda t: (0, 0, t)),
        ),
        [pltpu.VMEM((tokens, width), f32)] * 2,
        32 * tokens * width * share,
        50_000_000,
        {6: 2},
    )(hidden, down_z, up_z, grad_all, activated, slope, both)


def cross_back(back_attended, cross_query, text_pairs, shares, text_all, rows):
    tokens, share = cross_query.shape
    texts = text_all.shape[0]
    width = text_all.shape[1] // 2
    return local_call(
        functools.partial(cross_back_kernel, rows),
        "cross_back",
        2,
        (shape((tokens, share), bf16), shape((width, 4 * share), bf16)),
        [
            fixed(back_attended.shape),
            fixed(cross_query.shape),
            fixed(text_pairs.shape),
            fixed(shares.shape),
            moving((texts, width), lambda t: t),
        ],
        (fixed((tokens, share)), moving((width, 2 * share), lambda t: t)),
        [pltpu.VMEM((texts, 2 * share), bf16)],
        8 * texts * width * share,
        20_000_000,
    )(back_attended, cross_query, text_pairs, shares, text_all)


def outs_grad(attended1, carry1, attended2, carry2):
    tokens, share = attended1.shape
    width = carry1.shape[1]
    return local_call(
        outs_grad_kernel,
        "outs_grad",
        2,
        shape((share, 2 * width), bf16),
        [fixed((tokens, share)), fixed((tokens, width))] * 2,
        moving((share, width), lambda t: t),
        [],
        4 * tokens * width * share,
        10_000_000,
    )(attended1, carry1, attended2, carry2)


def self_back(back_attended, projected, shares, hidden1, hidden2, back_cross, rows):
    tokens, width = hidden1.shape
    share = back_cross.shape[1]
    return local_call(
        functools.partial(self_back_kernel, rows),
        "self_back",
        4,
        (shape((tokens, 3 * share), bf16), shape((width, 4 * share), bf16)),
        [
            fixed(back_attended.shape),
            fixed(projected.shape),
            fixed(shares.shape),
            fixed(hidden1.shape),
            fixed(hidden2.shape),
            fixed(back_cross.shape),
        ],
        (fixed((tokens, 3 * share)), moving((width, share), lambda t: t)),
        [pltpu.VMEM((3, tokens, share), bf16)],
        8 * tokens * width * share,
        25_000_000,
    )(back_attended, projected, shares, hidden1, hidden2, back_cross)


def block_slots(owners):
    owner = jnp.concatenate(owners)
    weight = jnp.concatenate([jnp.full(one.shape, at, jnp.int32) for at, one in enumerate(owners)])
    mark = owner + weight * 1024
    count = mark.shape[0]
    earlier = lax.broadcasted_iota(jnp.int32, (count, count), 1) < lax.broadcasted_iota(
        jnp.int32, (count, count), 0
    )
    same = jnp.logical_and(mark[:, None] == mark[None, :], earlier)
    return jnp.stack([owner, jnp.sum(same.astype(jnp.int32), axis=1)])


def slot_contents(owners, slots, places, capacities, firsts, n_dp):
    rows = []
    for owner, place, capacity, first in zip(owners, places, capacities, firsts):
        count = owner.shape[0]
        at = owner * capacity + slots[1, first : first + count]
        hit = at[None, :] == lax.broadcasted_iota(jnp.int32, (n_dp * capacity, count), 0)
        block = lax.broadcasted_iota(jnp.int32, (n_dp * capacity, count), 1)
        per_group, per_part, split = place_rule(place)
        part = block % per_group // per_part if split else block * 0
        column = block // per_group * per_part + block % per_part if split else block
        index = part * (count // (per_group // per_part)) + column if split else column
        rows.append(
            jnp.stack([jnp.sum(jnp.where(hit, value, 0), axis=1) for value in (index, block * 0 + 1)])
        )
    return jnp.concatenate(rows, axis=1)


def place_rule(place):
    parts = 1 + max(part for part, _ in place)
    if parts == 1:
        return 0, 0, False
    per_part = sum(1 for part, _ in place[:HEADS] if part == 0)
    return per_part * parts, per_part, True


def after(small, first):
    return lax.optimization_barrier((small, first))[0]


def body(
    tokens_in,
    text_in,
    seg_ids,
    capt_ids,
    grad_out,
    owner_query,
    owner_up,
    owner_outs,
    owner_text,
    owner_down,
    w_query,
    m_query,
    v_query,
    w_up,
    m_up,
    v_up,
    w_outs,
    m_outs,
    v_outs,
    w_text,
    m_text,
    v_text,
    w_down,
    m_down,
    v_down,
    norm_weight,
    m_norm,
    v_norm,
):
    n_dp = lax.axis_size("dp")
    n_z = lax.axis_size("fsdp")
    width = tokens_in.shape[1]
    own_rows = w_query.shape[0]
    chunk = own_rows // n_dp
    cap_big = w_query.shape[1] // BLK
    cap_out = w_outs.shape[1] // BLK
    heads_z = HEADS // n_z
    share = width // n_z
    owner_query, owner_up, owner_outs, owner_text, owner_down = (
        owner[:, 0] for owner in (owner_query, owner_up, owner_outs, owner_text, owner_down)
    )
    split_places = [split_place(b, heads_z, n_z) for b in range(owner_query.shape[0])]
    big_places = [flat_place(b) for b in range(owner_down.shape[0])]
    out_places = [flat_place(b) for b in range(owner_outs.shape[0])]
    owners = (owner_query, owner_outs, owner_text, owner_up, owner_down)
    places = (split_places, out_places, split_places, split_places, big_places)
    capacities = (cap_big, cap_out, cap_big, cap_big, cap_big)
    firsts = [sum(len(one) for one in places[:index]) for index in range(5)]
    slot_firsts = [sum(capacities[:index]) * n_dp for index in range(5)]
    slots = block_slots(owners)
    contents = slot_contents(owners, slots, places, capacities, firsts, n_dp)

    def spread(rows):
        return lax.all_gather(rows.reshape(-1, rows.shape[-1]), "dp", axis=0, tiled=True)

    def gather_sum(piece, parts):
        summed = lax.psum_scatter(piece, "dp", scatter_dimension=0, tiled=True)
        return summed.reshape(parts, chunk, -1)

    token_count = tokens_in.shape[0]
    marks = jnp.concatenate([seg_ids, capt_ids], axis=1)
    marks = jnp.pad(marks, ((0, 7), (0, 256 - marks.shape[1])))
    norms = jnp.pad(norm_weight, ((0, 2), (0, 0)))
    half = token_count // 2
    query_rows, grad_low, marks, norm_full = enter_call(
        "enter_query",
        0,
        slots,
        [(w_query, split_places, True, firsts[0])],
        [(grad_out[:half], False), (marks, False)],
        norms,
        True,
        False,
        n_z,
        n_dp,
        width,
    )
    outs_rows, hidden1, text_all = enter_call(
        "enter_outs",
        6,
        slots,
        [(w_outs, out_places, False, firsts[1])],
        [(tokens_in, True), (text_in, True)],
        norm_full[0:2],
        False,
        True,
        n_z,
        n_dp,
        width,
    )
    query_z, outs_z = spread(query_rows), spread(outs_rows)
    hidden1 = hidden1.reshape(-1, width)
    text_all = text_all.reshape(-1, text_in.shape[1])
    segment = marks[:, 0, :token_count]
    caption = marks[:, 0, token_count : token_count + capt_ids.shape[1]]
    self_mask = (segment[:, :, None] == segment[:, None, :]).astype(jnp.int32)
    text_row = lax.broadcasted_iota(jnp.int32, caption.shape, 0).reshape(1, 1, -1)
    packed_row = lax.broadcasted_iota(jnp.int32, (n_z, 1, 1), 0)
    cross_mask = jnp.logical_and(
        segment[:, :, None] == caption.reshape(1, 1, -1), packed_row == text_row
    ).astype(jnp.int32)

    projected, attended1, shares1 = self_forward(hidden1, query_z, self_mask)
    text_rows, grad_high = enter_call(
        "enter_text",
        7,
        after(slots, attended1),
        [(w_text, split_places, True, firsts[2])],
        [(grad_out[half:], False)],
        None,
        False,
        False,
        n_z,
        n_dp,
        width,
    )
    grad_all = jnp.concatenate([grad_low, grad_high], axis=1).reshape(-1, width)
    up_rows, down_rows, middle1, hidden2, cross_query = enter_call(
        "forward0",
        1,
        slots,
        [(w_up, split_places, True, firsts[3]), (w_down, big_places, False, firsts[4])],
        [],
        None,
        False,
        False,
        n_z,
        n_dp,
        width,
        forward_parts(
            attended1,
            outs_z,
            0,
            tokens_in,
            after(norm_full[2:4], text_rows),
            query_z,
            n_z,
            n_dp,
            False,
        ),
    )
    hidden2 = hidden2.reshape(-1, width)
    text_z, up_z, down_z = spread(text_rows), spread(up_rows), spread(down_rows)
    text_pairs, attended2, shares2 = cross_forward(cross_query, text_all, text_z, cross_mask)
    middle2, hidden3 = forward_call(
        attended2, outs_z, 1, middle1, norm_full[4:6], None, n_z, n_dp, 2
    )
    hidden3 = hidden3.reshape(-1, width)
    activated, slope, both = ffn(hidden3, up_z, grad_all, n_z, n_dp)
    branch3, part3, both = ffn_back(hidden3, down_z, up_z, grad_all, activated, slope, both)
    branch3 = branch3.reshape(n_z, token_count, width)
    part3 = part3.reshape(n_z, token_count, width)
    up_down_sum = gather_sum(both.reshape(-1, 4 * share), 2 * n_z)
    up_sum, down_sum = up_down_sum[:n_z], up_down_sum[n_z:]
    at_middle2, carry2, back_att2, term3 = back_call(
        part3, after(slots, part3), None, grad_out, middle2, norm_full[4:6], outs_z, 1, n_z, n_dp, 3
    )
    carry2 = carry2.reshape(-1, width)
    back_cross, text_part = cross_back(
        back_att2, cross_query, text_pairs, shares2, text_all, token_count
    )
    text_sum = gather_sum(text_part, n_z)
    at_middle1, carry1, back_att1, term2 = back_call(
        back_cross, query_z, 3, at_middle2, middle1, norm_full[2:4], outs_z, 0, n_z, n_dp, 4
    )
    carry1 = carry1.reshape(-1, width)
    back_projected, query_part = self_back(
        back_att1, projected, shares1, hidden1, hidden2, back_cross, token_count
    )
    query_sum = gather_sum(query_part, n_z)
    outs_sum = gather_sum(outs_grad(after(attended1, query_part), carry1, attended2, carry2), 1)
    down_grad, up_grad, text_grad, grad_in, result, term1 = leave_call(
        "leave_up",
        8,
        contents,
        [
            (down_sum, False, cap_big, slot_firsts[4], True),
            (up_sum, True, cap_big, slot_firsts[3], True),
            (text_sum, True, cap_big, slot_firsts[2], True),
        ],
        None,
        n_z,
        n_dp,
        last_parts(
            back_projected,
            query_z,
            at_middle1,
            tokens_in,
            norm_full[0:2],
            branch3,
            middle2,
            n_z,
            n_dp,
        ),
    )
    norm_term = jnp.concatenate([term1[:2], term2[:2], term3[:4]], axis=0)
    loose, norm_grad = leave_call(
        "leave_query",
        9,
        contents,
        [
            (outs_sum, False, cap_out, slot_firsts[1], False),
            (query_sum, True, cap_big, slot_firsts[0], False),
        ],
        norm_term,
        n_z,
        n_dp,
    )
    loose = lax.all_to_all(loose, "dp", 0, 0, tiled=True).reshape(own_rows, -1)
    outs_slots = loose[:, : cap_out * BLK].astype(f32)
    query_grad = loose[:, cap_out * BLK :].astype(f32)
    norm_grad = norm_grad[:6]
    text_grad, up_grad, down_grad = (
        grad.reshape(own_rows, -1).astype(f32) for grad in (text_grad, up_grad, down_grad)
    )
    up_new = adamw_update(w_up, m_up, v_up, up_grad, rate_up, decay_rate)
    text_new = adamw_update(w_text, m_text, v_text, text_grad, rate_text, decay_rate)
    down_new = adamw_update(w_down, m_down, v_down, down_grad, rate_down, decay_rate)
    query_new = adamw_update(w_query, m_query, v_query, query_grad, rate_query, decay_rate)
    outs_new = adamw_update(w_outs, m_outs, v_outs, outs_slots, rate_outs, decay_rate)
    norm_new = adamw_update(norm_weight, m_norm, v_norm, norm_grad, rate_norm, 0.0)
    return (
        result,
        grad_in,
        *query_new,
        *up_new,
        *outs_new,
        *text_new,
        *down_new,
        *norm_new,
    )


def solution(mesh):
    rows = P(("dp", "fsdp"), None)
    slots = P("fsdp", "dp")
    norms = P(None, "dp")
    in_specs = (rows,) * 5 + (P(),) * 5 + (slots,) * 15 + (norms,) * 3
    out_specs = (rows,) * 2 + (slots,) * 15 + (norms,) * 3
    return jax.shard_map(body, mesh=mesh, in_specs=in_specs, out_specs=out_specs, check_vma=False)
```

```python
import functools

import jax
import jax.numpy as jnp
from jax import lax
from jax.experimental import pallas as pl
from jax.experimental.pallas import tpu as pltpu
from jax.sharding import PartitionSpec as P

HEADS = 16
HEAD = 128
STEP = 10
BLK = 128


beta_first = 0.9
beta_second = 0.999
adam_eps = 1e-08
decay_rate = 0.01
rate_query = 0.04
rate_up = 0.04
rate_outs = 0.12
rate_text = 0.03
rate_down = 0.03
rate_norm = 0.5
norm_eps = 1e-05
score_floor = -1e30
bf16 = jnp.bfloat16
f32 = jnp.float32


def normalize(values):
    centered = values - jnp.mean(values, axis=-1, keepdims=True)
    inverse_std = lax.rsqrt(jnp.mean(centered * centered, axis=-1, keepdims=True) + norm_eps)
    return (centered * inverse_std, inverse_std)


def norm_back(back_hidden, normed, inverse_std, gain_row):
    back_normed = back_hidden * gain_row
    return inverse_std * (
        back_normed
        - jnp.mean(back_normed, axis=-1, keepdims=True)
        - normed * jnp.mean(back_normed * normed, axis=-1, keepdims=True)
    )


def adamw_update(weight, first, second, gradient, rate, decay):
    first_new = beta_first * first + (1.0 - beta_first) * gradient
    second_new = beta_second * second + (1.0 - beta_second) * gradient * gradient
    first_hat = first_new / (1.0 - beta_first**STEP)
    second_hat = second_new / (1.0 - beta_second**STEP)
    weight_new = weight - rate * (first_hat / (jnp.sqrt(second_hat) + adam_eps) + decay * weight)
    return (first_new, second_new, weight_new)


def dot(left, right):
    return jnp.dot(left, right, preferred_element_type=f32)


def dot_nt(left, right):
    return lax.dot_general(left, right, (((1,), (1,)), ((), ())), preferred_element_type=f32)


def dot_tn(left, right):
    return lax.dot_general(left, right, (((0,), (0,)), ((), ())), preferred_element_type=f32)


def split_place(block, per_part, parts):
    group, rest = divmod(block, per_part * parts)
    part, inner = divmod(rest, per_part)
    return part, group * per_part + inner


def flat_place(block):
    return 0, block


MESH = pl.DeviceIdType.MESH


SUBS = 4


class Line:
    def __init__(self, n, rows, step):
        self.n, self.rows, self.step = n, rows, step
        self.at = lax.axis_index("fsdp")

    def has(self, way):
        return self.at < self.n - 1 if way == 0 else self.at > 0

    def peer(self, way):
        index = jnp.clip(self.at + (1 if way == 0 else -1), 0, self.n - 1)
        return {"fsdp": index}

    def greet(self, others=0):
        barrier = pltpu.get_barrier_semaphore()
        for way in (0, 1):

            @pl.when(self.has(way))
            def _():
                pl.semaphore_signal(
                    barrier, inc=1, device_id=self.peer(way), device_id_type=pl.DeviceIdType.MESH
                )

        pl.semaphore_wait(
            barrier, others + self.has(0).astype(jnp.int32) + self.has(1).astype(jnp.int32)
        )

    def copy(self, source, target, send, recv, way):
        return pltpu.make_async_remote_copy(
            src_ref=source,
            dst_ref=target,
            send_sem=send,
            recv_sem=recv,
            device_id=self.peer(way),
            device_id_type=pl.DeviceIdType.MESH,
        )

    def part(self, sub):
        return pl.ds(sub * self.step, self.step)


class Sums:
    def __init__(self, line, part, held, send, recv):
        self.line, self.part, self.held, self.send, self.recv = line, part, held, send, recv

    def move(self, way, target, sub, source):
        line = self.line
        rows = line.part(sub)
        return line.copy(
            source,
            self.held.at[way, target, rows],
            self.send.at[way, target, sub],
            self.recv.at[way, target, sub],
            way,
        )

    def target(self, way, time):
        n, at = self.line.n, self.line.at
        return n - 1 - (time - at) if way == 0 else time - (n - 1 - at)

    def passes(self, way, target):
        n, at = self.line.n, self.line.at
        if way == 0:
            return jnp.logical_and(target > at, target < n)
        return jnp.logical_and(target < at, target >= 0)

    def forward(self, sub, time):
        line = self.line
        rows = line.part(sub)
        for way in (0, 1):
            target = self.target(way, time)
            passes = self.passes(way, target)
            inner = jnp.logical_and(passes, line.has(1 - way))
            outer = jnp.logical_and(passes, jnp.logical_not(line.has(1 - way)))

            @pl.when(outer)
            def _():
                self.move(way, target, sub, self.part.at[target, rows]).start()

            @pl.when(inner)
            def _():
                held = self.held.at[way, target, rows]
                self.move(way, target, sub, held).wait_recv()
                total = held[...].astype(f32) + self.part[target, rows].astype(f32)
                held[...] = total.astype(bf16)
                self.move(way, target, sub, held).start()

    def total(self, sub, sum_ref):
        line = self.line
        rows = line.part(sub)
        sum_ref[...] = self.part[line.at, rows].astype(f32)
        for way in (0, 1):

            @pl.when(line.has(1 - way))
            def _():
                held = self.held.at[way, line.at, rows]
                self.move(way, line.at, sub, held).wait_recv()
                sum_ref[...] += held[...].astype(f32)

    def finish(self):
        line = self.line
        for way in (0, 1):
            for time in range(line.n - 1):
                target = self.target(way, time)

                @pl.when(self.passes(way, target))
                def _():
                    for sub in range(line.rows // line.step):
                        held = self.held.at[way, target, line.part(sub)]
                        self.move(way, target, sub, held).wait_send()


def relay(n, sums, blocks, settle, hook=None, later=None):
    lag = 2 * (n - 1)
    for slot in range((SUBS + 2) * (n - 1)):
        sub, time = divmod(slot, n - 1)
        if later is not None and slot >= lag:
            later.forward(*divmod(slot - lag, n - 1))
        if hook is not None and slot == SUBS * (n - 1):
            hook()
        if sub < SUBS:
            for one in sums:
                one.forward(sub, time)
        if time == 0 and 0 <= sub - 1 < SUBS:
            settle(sub - 1)
        if blocks is not None:
            if time == n - 2 and 0 <= sub - 1 < SUBS:
                blocks.forward(sub - 1, 1)
            if time < n - 2 and 0 <= sub - 2 < SUBS:
                blocks.forward(sub - 2, time + 2)
    for one in sums:
        one.finish()
    if blocks is not None:
        blocks.finish()


class Blocks:
    def __init__(self, line, full, send, recv):
        self.line, self.full, self.send, self.recv = line, full, send, recv

    def move(self, way, source, sub):
        line = self.line
        held = self.full.at[source, line.part(sub)]
        return line.copy(
            held, held, self.send.at[way, source, sub], self.recv.at[way, source, sub], way
        )

    def behind(self, way, source):
        return self.line.at > source if way == 0 else self.line.at < source

    def start(self, sub):
        for way in (0, 1):

            @pl.when(self.line.has(way))
            def _():
                self.move(way, self.line.at, sub).start()

    def forward(self, sub, step):
        line = self.line
        for way in (0, 1):
            source = line.at - step if way == 0 else line.at + step

            @pl.when(jnp.logical_and(source >= 0, source < line.n))
            def _():
                self.move(way, source, sub).wait_recv()

                @pl.when(line.has(way))
                def _():
                    self.move(way, source, sub).start()

    def finish(self):
        line = self.line
        for way in (0, 1):
            for source in range(line.n):
                ours = jnp.logical_or(self.behind(way, source), line.at == source)

                @pl.when(jnp.logical_and(ours, line.has(way)))
                def _():
                    for sub in range(line.rows // line.step):
                        self.move(way, source, sub).wait_send()


def lane_moves(width, order):
    moves = []
    piece = width // len(order)
    for group in range(width // BLK):
        parts = []
        for offset in range(0, BLK, piece):
            start = order[(group * BLK + offset) // piece] * piece
            parts.append((offset, start // BLK, start % BLK))
        moves.append(parts)
    return piece, moves


def reorder(load, store, rows, width, order):
    piece, moves = lane_moves(width, order)
    lane = lax.broadcasted_iota(jnp.int32, (rows, BLK), 1)
    for group, parts in enumerate(moves):
        value = None
        for offset, source, start in parts:
            block = load(source)
            if start != offset:
                block = pltpu.roll(block, (offset - start) % BLK, 1)
            value = block if value is None else jnp.where(lane >= offset, block, value)
        store(group, value)


def shuffle_order(n_z, n_dp):
    return [z * n_dp + i for i in range(n_dp) for z in range(n_z)]


def unshuffle_order(n_z, n_dp):
    return [i * n_z + z for z in range(n_z) for i in range(n_dp)]


def by_tiles(columns, tile, run):
    def one(index, carry):
        run(pl.ds(pl.multiple_of(index * tile, tile), tile))
        return carry

    lax.fori_loop(0, columns // tile, one, 0)


class Swap:
    def __init__(self, axis, source, target, send, recv):
        self.axis, self.source, self.target = axis, source, target
        self.send, self.recv = send, recv
        self.n = lax.axis_size(axis)
        self.me = lax.axis_index(axis)

    def copy(self, jump, arrival=False):
        peer = lax.rem(self.me + jump, self.n)
        slot = peer if arrival else self.me
        return pltpu.make_async_remote_copy(
            src_ref=self.source.at[peer],
            dst_ref=self.target.at[slot],
            send_sem=self.send.at[jump],
            recv_sem=self.recv.at[slot],
            device_id={self.axis: peer},
            device_id_type=MESH,
        )

    def start(self):
        for jump in range(1, self.n):
            self.copy(jump).start()

    def keep(self):
        self.target[self.me] = self.source[self.me]

    def wait(self):
        for jump in range(1, self.n):
            self.copy(jump, True).wait_recv()

    def finish(self):
        for jump in range(1, self.n):
            self.copy(jump).wait_send()


def greet_all():
    barrier = pltpu.get_barrier_semaphore()
    count = 0
    for axis in ("dp", "fsdp"):
        n, me = lax.axis_size(axis), lax.axis_index(axis)
        count += n - 1
        for jump in range(1, n):
            pl.semaphore_signal(
                barrier, inc=1, device_id={axis: lax.rem(me + jump, n)}, device_id_type=MESH
            )
    pl.semaphore_wait(barrier, count)


class Refs:
    def __init__(self, refs):
        self.refs = list(refs)

    def take(self, count=None):
        taken = self.refs[: 1 if count is None else count]
        self.refs = self.refs[len(taken) :]
        return taken[0] if count is None else taken


def enter_kernel(weights, gathers, order, normed, hidden, inner, inner_counts, *refs):
    refs = Refs(refs)
    n_dp, n_z = lax.axis_size("dp"), lax.axis_size("fsdp")
    slots_ref = refs.take()
    w_refs = refs.take(len(weights))
    in_refs = refs.take(len(gathers))
    norm_in = refs.take() if normed or hidden else None
    inner_refs = refs.take(inner_counts[0])
    row_refs = refs.take(len(weights))
    full_refs = refs.take(len(gathers))
    norm_out = refs.take() if normed else None
    inner_refs += refs.take(inner_counts[1])
    inner_refs += refs.take(inner_counts[2])
    loads = []
    for w_ref in w_refs:
        stage, sem = refs.take(2)
        load = pltpu.make_async_copy(w_ref, stage, sem)
        load.start()
        loads.append((stage, load))
    greet_all()
    if normed:
        parts, *sems = refs.take(3)
        norm_swap = Spread("dp", norm_in, parts, *sems)
        norm_swap.start()
    lines = []
    for in_ref, full_ref in zip(in_refs, full_refs):
        rows = in_ref.shape[0]
        step = rows // pieces_of(rows)
        lines.append(Blocks(Line(n_z, rows, step), full_ref, *refs.take(2)))
    swaps = []
    for (stage, load), (places, split, _) in zip(loads, weights):
        source, target, *sems = refs.take(4)
        swap = Swap("dp", source, target, *sems)
        load.wait()
        chunk = source.shape[2]
        for jump in range(n_dp):
            peer = lax.rem(swap.me + jump, n_dp)
            into = source if jump else target
            for slot in range(source.shape[1]):
                here = pl.ds(pl.multiple_of(peer * chunk, chunk), chunk)
                piece = stage[here, slot * BLK : (slot + 1) * BLK]
                into[peer, slot] = piece.astype(bf16)
            if jump:
                swap.copy(jump).start()
        swaps.append(swap)
    if hidden:
        work = refs.take()
    for index, (in_ref, full_ref, blocks) in enumerate(zip(in_refs, full_refs, lines)):
        line = blocks.line
        if hidden and index == 0:
            for sub in range(line.rows // line.step):
                here = line.part(sub)
                values, _ = normalize(in_ref[here].astype(f32))
                work[...] = values * norm_in[0:1] + norm_in[1:2]
                store_shuffled(work, full_ref, line, here, order)
                blocks.start(sub)
        elif in_ref.dtype == bf16 and gathers[index]:
            work2 = refs.take()
            work2[...] = in_ref[...].astype(f32)
            store_shuffled(work2, full_ref, line, line.part(0), order)
            blocks.start(0)
        else:
            for sub in range(line.rows // line.step):
                here = line.part(sub)
                full_ref[line.at, here] = in_ref[here]
                blocks.start(sub)
    if normed:
        parts[norm_swap.me] = norm_in[...]
        norm_swap.wait()
        share = norm_in.shape[1]
        for index in range(n_dp):
            norm_out[:, index * share : (index + 1) * share] = parts[index]
    shares = []

    def compact(index):
        swap, row_ref, (places, split, first) = swaps[index], row_refs[index], weights[index]
        swap.wait()
        if split:
            cut, *sems = refs.take(3)
            share = Swap("fsdp", cut, row_ref, *sems)
            shares.append(share)
        else:
            cut = row_ref
        for block, (part, column) in enumerate(places):
            owner, slot = slots_ref[0, first + block], slots_ref[1, first + block]
            cut[part, :, column * BLK : (column + 1) * BLK] = swap.target[owner, slot]
        if split:
            share.start()
            share.keep()

    ahead = 0
    if inner is not None:
        ahead = 1
        inner(*inner_refs, hook=lambda: compact(0))
    for step in range(1, n_z):
        for blocks in lines:
            for sub in range(blocks.line.rows // blocks.line.step):
                blocks.forward(sub, step)
    for index in range(ahead, len(weights)):
        compact(index)
    for share in shares:
        share.wait()
    for one in [*swaps, *shares, *lines]:
        one.finish()
    if normed:
        norm_swap.finish()


class Spread(Swap):
    def copy(self, jump, arrival=False):
        peer = lax.rem(self.me + jump, self.n)
        slot = peer if arrival else self.me
        return pltpu.make_async_remote_copy(
            src_ref=self.source,
            dst_ref=self.target.at[slot],
            send_sem=self.send.at[jump],
            recv_sem=self.recv.at[slot],
            device_id={self.axis: peer},
            device_id_type=MESH,
        )


def store_shuffled(work, full_ref, line, here, order):
    rows, width = work.shape
    folds = width // order.width
    pieces = len(order.pieces)
    orders = [fold * pieces + piece for fold in range(folds) for piece in order.pieces]

    def load(group):
        return work[:, group * BLK : (group + 1) * BLK]

    def store(group, value):
        full_ref[line.at, here, group * BLK : (group + 1) * BLK] = value.astype(bf16)

    reorder(load, store, rows, width, orders)


def expand_slots(slots_ref, rows, cut, blocks, capacity, first, offset):
    columns = rows.shape[2] // BLK
    for part in range(rows.shape[0]):
        for column in range(columns):
            blocks[part * columns + column] = rows[part, :, column * BLK : (column + 1) * BLK]
    for owner in range(cut.shape[0]):
        for position in range(capacity):
            slot = first + owner * capacity + position
            value = blocks[slots_ref[0, slot]].astype(f32)
            live = slots_ref[1, slot].astype(f32)
            start = offset + position * BLK
            cut[owner, :, start : start + BLK] = (value * live).astype(bf16)


def leave_kernel(weights, summed, inner, inner_counts, *refs):
    refs = Refs(refs)
    n_dp = lax.axis_size("dp")
    slots_ref = refs.take()
    row_refs = refs.take(len(weights))
    term_ref = refs.take() if summed else None
    inner_refs = refs.take(inner_counts[0])
    gone = sum(1 for weight in weights if weight[3])
    out_refs = refs.take(gone)
    loose_ref = refs.take() if gone < len(weights) else None
    sum_ref = refs.take() if summed else None
    inner_refs += refs.take(inner_counts[1])
    inner_refs += refs.take(inner_counts[2])
    greet_all()
    if summed:
        cut, parts, send, recv, total, others, send2, recv2 = refs.take(8)
        share = cut.shape[2]
        for index in range(n_dp):
            cut[index] = term_ref[:, index * share : (index + 1) * share]
        term_swap = Swap("dp", cut, parts, send, recv)
        term_swap.start()
        term_swap.keep()
    shares = []
    for row_ref, (split, _, _, _) in zip(row_refs, weights):
        if split:
            held, *sems = refs.take(3)
            share = Swap("fsdp", row_ref, held, *sems)
            share.start()
            share.keep()
            shares.append(share)
        else:
            shares.append(None)
    if summed:
        term_swap.wait()
        total[...] = jnp.sum(parts[...], axis=0)
        total_spread = Spread("fsdp", total, others, send2, recv2)
        total_spread.start()
        others[total_spread.me] = total[...]
    swaps = []
    offset = 0
    for row_ref, share, (split, capacity, first, whole) in zip(row_refs, shares, weights):
        if split:
            share.wait()
        rows = share.target if split else row_ref
        if not whole:
            expand_slots(slots_ref, rows, loose_ref, refs.take(), capacity, first, offset)
            offset += capacity * BLK
            continue
        out_ref = out_refs.pop(0)
        cut, *sems, blocks = refs.take(4)
        expand_slots(slots_ref, rows, cut, blocks, capacity, first, 0)
        swap = Swap("dp", cut, out_ref, *sems)
        swap.start()
        swap.keep()
        swaps.append(swap)
    if inner is not None:
        inner(*inner_refs)
    if summed:
        total_spread.wait()
        sum_ref[...] = jnp.sum(others[...], axis=0)
    for swap in swaps:
        swap.wait()
    for one in [*swaps, *shares]:
        if one is not None:
            one.finish()
    if summed:
        term_swap.finish()
        total_spread.finish()


def fetch_columns(source, index, target, sem):
    columns = target.shape[1]
    return pltpu.make_async_copy(source.at[:, pl.ds(index * columns, columns)], target, sem)


def forward_kernel(
    n, order, half, wide, alone, att_ref, outs_hbm, base_ref, norm_ref, *rest, hook=None
):
    if wide:
        next_hbm, middle_ref, full_ref, result_ref = rest[:4]
        *rest, next_ref, next_sem = rest[4:]
    else:
        middle_ref, full_ref = rest[:2]
        rest = rest[2:]
    part, held, work, s_send, s_recv, b_send, b_recv, outs_ref, outs_sem = rest
    rows, width = base_ref.shape
    step = rows // SUBS
    load_outs = fetch_columns(outs_hbm, half, outs_ref, outs_sem)
    load_outs.start()
    if wide:
        load_next = fetch_columns(next_hbm, 3, next_ref, next_sem)
        load_next.start()
    line = Line(n, rows, step)
    if alone:
        line.greet()
    load_outs.wait()
    sums = Sums(line, part, held, s_send, s_recv)
    blocks = Blocks(line, full_ref, b_send, b_recv)

    def multiply(columns):
        product = dot(att_ref[...], outs_ref[:, columns]).astype(bf16)
        part[:, :, columns] = product.reshape(n, rows, -1)

    by_tiles(width, 256, multiply)

    def settle(sub):
        here = line.part(sub)
        sums.total(sub, work)
        middle = base_ref[here].astype(f32) + work[...]
        middle_ref[here] = middle
        normed, _ = normalize(middle)
        work[...] = normed * norm_ref[0:1] + norm_ref[1:2]

        def load(group):
            return work[:, group * BLK : (group + 1) * BLK]

        def store(group, value):
            full_ref[line.at, here, group * BLK : (group + 1) * BLK] = value.astype(bf16)

        reorder(load, store, step, width, order)
        blocks.start(sub)

    relay(n, [sums], blocks, settle, hook)
    if wide:
        load_next.wait()

        def multiply_next(columns):
            whole = full_ref[...].reshape(n * rows, width)
            result_ref[:, columns] = dot(whole, next_ref[:, columns]).astype(bf16)

        by_tiles(result_ref.shape[1], 256, multiply_next)


def carry_back(work, plain, order, step, width, middle, base, gain, term_ref, first):
    def load(group):
        return work[:, group * BLK : (group + 1) * BLK]

    def store(group, value):
        plain[:, group * BLK : (group + 1) * BLK] = value

    reorder(load, store, step, width, order)
    back_hidden = plain[...]
    normed, inverse = normalize(middle)
    gain_term = jnp.sum(back_hidden * normed, axis=0, keepdims=True)
    bias_term = jnp.sum(back_hidden, axis=0, keepdims=True)
    if first:
        term_ref[...] = jnp.zeros_like(term_ref)
        term_ref[0:1] = gain_term
        term_ref[1:2] = bias_term
    else:
        term_ref[0:1] += gain_term
        term_ref[1:2] += bias_term
    return base + norm_back(back_hidden, normed, inverse, gain)


def back_kernel(
    n, order, column, half, alone, dy_ref, w_hbm, base_ref, middle_ref, norm_ref, outs_hbm, *rest
):
    if column is None:
        branch, *rest = rest
    carry_ref, full_ref, att_ref, term_ref, *rest = rest
    if column is None:
        result_ref, *rest = rest
    held, work, plain, s_send, s_recv, b_send, b_recv, outs_ref, outs_sem = rest[:9]
    rows, width = base_ref.shape
    step = rows // SUBS
    if column is not None:
        part, w_ref, w_sem = rest[9:]
        load_w = fetch_columns(w_hbm, column, w_ref, w_sem)
        load_w.start()
    else:
        part = dy_ref
        held2, r_send, r_recv = rest[9:]
    load_outs = fetch_columns(outs_hbm, half, outs_ref, outs_sem)
    load_outs.start()
    line = Line(n, rows, step)
    if alone:
        line.greet()
    sums = Sums(line, part, held, s_send, s_recv)
    blocks = Blocks(line, full_ref, b_send, b_recv)
    results = None
    if column is None:
        results = Sums(line, branch, held2, r_send, r_recv)
    if column is not None:
        load_w.wait()

        def multiply(columns):
            product = dot_nt(dy_ref[...], w_ref[columns]).astype(bf16)
            part[:, :, columns] = product.reshape(n, rows, -1)

        by_tiles(width, 256, multiply)

    def settle(sub):
        here = line.part(sub)
        sums.total(sub, work)
        carry = carry_back(
            work,
            plain,
            order,
            step,
            width,
            middle_ref[here].astype(f32),
            base_ref[here].astype(f32),
            norm_ref[0:1],
            term_ref,
            sub == 0,
        )
        carry_ref[here] = carry
        full_ref[line.at, here] = carry.astype(bf16)
        blocks.start(sub)

    relay(n, [sums], blocks, settle, None, results)
    if results is not None:
        for sub in range(SUBS):
            here = line.part(sub)
            results.total(sub, work)
            result_ref[here] = (middle_ref[here] + work[...]).astype(bf16)
        results.finish()
    load_outs.wait()

    def multiply_next(columns):
        whole = full_ref[...].reshape(n * rows, width)
        att_ref[:, columns] = dot_nt(whole, outs_ref[columns]).astype(bf16)

    by_tiles(att_ref.shape[1], 256, multiply_next)


def last_kernel(n, order, dy_ref, w_hbm, base_ref, tokens, norm_ref, *rest):
    grad_ref, term_ref = rest[:2]
    part, held, work, plain, s_send, s_recv, w_ref, w_sem = rest[2:]
    rows, width = base_ref.shape
    step = rows // SUBS
    load_w = fetch_columns(w_hbm, 0, w_ref, w_sem)
    load_w.start()
    line = Line(n, rows, step)
    load_w.wait()
    sums = Sums(line, part, held, s_send, s_recv)

    def multiply(columns):
        product = dot_nt(dy_ref[...], w_ref[columns]).astype(bf16)
        part[:, :, columns] = product.reshape(n, rows, -1)

    by_tiles(width, 256, multiply)

    def settle(sub):
        here = line.part(sub)
        sums.total(sub, work)
        carry = carry_back(
            work,
            plain,
            order,
            step,
            width,
            tokens[here].astype(f32),
            base_ref[here],
            norm_ref[0:1],
            term_ref,
            sub == 0,
        )
        grad_ref[here] = carry.astype(bf16)

    relay(n, [sums], None, settle)


VMEM_CAP = 52 * 1024 * 1024


def in_place():
    return pl.BlockSpec(memory_space=pl.ANY)


def whole_vmem():
    return pl.BlockSpec(memory_space=pltpu.VMEM)


def sem_pair(n, subs):
    return [pltpu.SemaphoreType.DMA((2, n, subs)), pltpu.SemaphoreType.DMA((2, n, subs))]


def line_call(kernel, name, ident, outs, specs, scratch, flops, moved):
    return pl.pallas_call(
        kernel,
        name=name,
        out_shape=outs,
        in_specs=specs,
        out_specs=jax.tree.map(lambda _: whole_vmem(), outs),
        scratch_shapes=scratch,
        compiler_params=pltpu.CompilerParams(
            collective_id=ident, has_side_effects=True, vmem_limit_bytes=VMEM_CAP
        ),
        cost_estimate=pl.CostEstimate(flops=flops, bytes_accessed=moved, transcendentals=0),
    )


def shape(dims, kind):
    return jax.ShapeDtypeStruct(dims, kind)


LINK_COST = 4_000_000


def pieces_of(rows):
    return max(1, rows * SUBS // 128)


class Order:
    def __init__(self, pieces, width):
        self.pieces, self.width = pieces, width


def swap_sems(n):
    return [pltpu.SemaphoreType.DMA((n,)), pltpu.SemaphoreType.DMA((n,))]


def enter_call(
    name, ident, slots, weights, gathers, norms, normed, hidden, n, n_dp, width, inner=None
):
    chunk = weights[0][0].shape[0] // n_dp
    run, inner_args, inner_specs, inner_outs, scratch = inner or (None, [], [], [], [])
    counts = (len(inner_args), len(inner_outs), len(scratch))
    outs, scratch = [], list(scratch)
    for array, places, split, _ in weights:
        parts = n if split else 1
        outs.append(shape((parts, chunk, len(places) // parts * BLK), bf16))
        scratch += [pltpu.VMEM(array.shape, f32), pltpu.SemaphoreType.DMA]
    if normed:
        scratch += [pltpu.VMEM((n_dp, *norms.shape), f32), *swap_sems(n_dp)]
    for array, _ in gathers:
        rows = array.shape[0]
        outs.append(shape((n, *array.shape), array.dtype))
        scratch += sem_pair(n, pieces_of(rows))
    if normed:
        outs.append(shape((norms.shape[0], n_dp * norms.shape[1]), f32))
    for array, _, _, _ in weights:
        slots_shape = (n_dp, array.shape[1] // BLK, chunk, BLK)
        scratch += [pltpu.VMEM(slots_shape, bf16)] * 2 + swap_sems(n_dp)
    if hidden:
        scratch.append(pltpu.VMEM((gathers[0][0].shape[0] // SUBS, width), f32))
    for array, moved in gathers[1 if hidden else 0 :]:
        if moved:
            scratch.append(pltpu.VMEM(array.shape, f32))
    for index, (_, places, split, _) in enumerate(weights):
        if split:
            scratch += [pltpu.VMEM(outs[index].shape, bf16), *swap_sems(n)]
    args = [slots, *(weight[0] for weight in weights), *(gather[0] for gather in gathers)]
    specs = [pl.BlockSpec(memory_space=pltpu.SMEM)] + [in_place()] * len(weights)
    specs += [whole_vmem()] * len(gathers)
    if normed or hidden:
        args.append(norms)
        specs.append(whole_vmem())
    args += inner_args
    specs += inner_specs
    outs += inner_outs
    kernel = functools.partial(
        enter_kernel,
        [weight[1:] for weight in weights],
        [gather[1] for gather in gathers],
        Order(shuffle_order(n, n_dp), width),
        normed,
        hidden,
        run,
        counts,
    )
    return line_call(kernel, name, ident, outs, specs, scratch, 0, LINK_COST)(*args)


def leave_call(name, ident, slots, weights, term, n, n_dp, inner=None):
    outs, scratch = [], []
    specs = [pl.BlockSpec(memory_space=pltpu.SMEM)] + [whole_vmem()] * len(weights)
    args = [slots, *(weight[0] for weight in weights)]
    chunk = weights[0][0].shape[1]
    if term is not None:
        args.append(term)
        specs.append(whole_vmem())
        block = (term.shape[0], term.shape[1] // n_dp)
    counts = (0, 0, 0)
    run = None
    if inner is not None:
        run, inner_args, inner_specs, inner_outs, inner_scratch = inner
        counts = (len(inner_args), len(inner_outs), len(inner_scratch))
        args += inner_args
        specs += inner_specs
        scratch += inner_scratch
    if term is not None:
        scratch += [pltpu.VMEM((n_dp, *block), f32)] * 2 + swap_sems(n_dp)
        scratch += [pltpu.VMEM(block, f32), pltpu.VMEM((n, *block), f32), *swap_sems(n)]
    for rows, split, _, _, _ in weights:
        if split:
            scratch += [pltpu.VMEM(rows.shape, bf16), *swap_sems(n)]
    for rows, _, capacity, _, whole in weights:
        slots_shape = (n_dp, chunk, capacity * BLK)
        if whole:
            outs.append(shape(slots_shape, bf16))
            scratch += [pltpu.VMEM(slots_shape, bf16), *swap_sems(n_dp)]
        blocks = rows.shape[0] * rows.shape[2] // BLK
        scratch.append(pltpu.VMEM((blocks, chunk, BLK), bf16))
    loose = sum(capacity * BLK for _, _, capacity, _, whole in weights if not whole)
    if loose:
        outs.append(shape((n_dp, chunk, loose), bf16))
    if term is not None:
        outs.append(shape(block, f32))
    if inner is not None:
        outs += inner_outs
    kernel = functools.partial(
        leave_kernel, [weight[1:] for weight in weights], term is not None, run, counts
    )
    return line_call(kernel, name, ident, outs, specs, scratch, 0, LINK_COST)(*args)


def forward_parts(attended, outs_z, half, base, norm_rows, after, n, n_dp, alone):
    rows, width = base.shape
    share = outs_z.shape[0]
    outs = [shape((rows, width), f32), shape((n, rows, width), bf16)]
    specs = [whole_vmem(), in_place(), whole_vmem(), whole_vmem()]
    args = [attended, outs_z, base, norm_rows]
    scratch = [
        pltpu.VMEM((n, rows, width), bf16),
        pltpu.VMEM((2, n, rows, width), bf16),
        pltpu.VMEM((rows // SUBS, width), f32),
        *sem_pair(n, SUBS),
        *sem_pair(n, SUBS),
        pltpu.VMEM((share, width), bf16),
        pltpu.SemaphoreType.DMA,
    ]
    if after is not None:
        outs.append(shape((n * rows, share), bf16))
        specs.append(in_place())
        args.append(after)
        scratch += [pltpu.VMEM((width, share), bf16), pltpu.SemaphoreType.DMA]
    kernel = functools.partial(
        forward_kernel, n, shuffle_order(n, n_dp), half, after is not None, alone
    )
    return kernel, args, specs, outs, scratch


def forward_call(attended, outs_z, half, base, norm_rows, after, n, n_dp, ident):
    kernel, args, specs, outs, scratch = forward_parts(
        attended, outs_z, half, base, norm_rows, after, n, n_dp, True
    )
    call = line_call(kernel, f"forward{half}", ident, outs, specs, scratch, 0, LINK_COST)
    return call(*args)


def back_parts(dy, weight, column, base, middle, norm_rows, outs_z, half, branch, n, n_dp, alone):
    rows, width = base.shape
    share = outs_z.shape[0]
    outs = [
        shape((rows, width), f32),
        shape((n, rows, width), bf16),
        shape((n * rows, share), bf16),
        shape((8, width), f32),
    ]
    specs = [
        whole_vmem(),
        in_place(),
        whole_vmem(),
        whole_vmem(),
        whole_vmem(),
        in_place(),
    ]
    scratch = [
        pltpu.VMEM((2, n, rows, width), bf16),
        pltpu.VMEM((rows // SUBS, width), f32),
        pltpu.VMEM((rows // SUBS, width), f32),
        *sem_pair(n, SUBS),
        *sem_pair(n, SUBS),
        pltpu.VMEM((share, width), bf16),
        pltpu.SemaphoreType.DMA,
    ]
    if column is not None:
        scratch += [
            pltpu.VMEM((n, rows, width), bf16),
            pltpu.VMEM((width, dy.shape[1]), bf16),
            pltpu.SemaphoreType.DMA,
        ]
    args = [dy, weight, base, middle, norm_rows, outs_z]
    if branch is not None:
        args.append(branch)
        specs.append(whole_vmem())
        outs.append(shape((rows, width), bf16))
        scratch += [pltpu.VMEM((2, n, rows, width), bf16), *sem_pair(n, SUBS)]
    kernel = functools.partial(back_kernel, n, unshuffle_order(n, n_dp), column, half, alone)
    return kernel, args, specs, outs, scratch


def back_call(dy, weight, column, base, middle, norm_rows, outs_z, half, branch, n, n_dp, ident):
    kernel, args, specs, outs, scratch = back_parts(
        dy, weight, column, base, middle, norm_rows, outs_z, half, branch, n, n_dp, True
    )
    call = line_call(kernel, f"back{half}", ident, outs, specs, scratch, 0, LINK_COST)
    return call(*args)


def last_parts(dy, weight, base, tokens, norm_rows, n, n_dp):
    rows, width = base.shape
    outs = [
        shape((rows, width), bf16),
        shape((8, width), f32),
    ]
    specs = [whole_vmem(), in_place()] + [whole_vmem()] * 3
    scratch = [
        pltpu.VMEM((n, rows, width), bf16),
        pltpu.VMEM((2, n, rows, width), bf16),
        pltpu.VMEM((rows // SUBS, width), f32),
        pltpu.VMEM((rows // SUBS, width), f32),
        *sem_pair(n, SUBS),
        pltpu.VMEM((width, dy.shape[1]), bf16),
        pltpu.SemaphoreType.DMA,
    ]
    kernel = functools.partial(last_kernel, n, unshuffle_order(n, n_dp))
    return kernel, [dy, weight, base, tokens, norm_rows], specs, outs, scratch


def attend_forward(query, keys, values, mask_ref, keyed, att_ref, share_ref):
    packed, rows, _ = mask_ref.shape
    heads = att_ref.shape[1] // HEAD
    for p in range(packed):
        here = slice(p * rows, (p + 1) * rows)
        there = here if keyed else slice(None)
        for h in range(heads):
            columns = slice(h * HEAD, (h + 1) * HEAD)
            scores = dot_nt(query[here, columns], keys[there, columns]) * HEAD ** (-0.5)
            scores = jnp.where(mask_ref[p] > 0, scores, score_floor)
            powers = jnp.exp(scores - jnp.max(scores, axis=-1, keepdims=True))
            shares = powers / jnp.sum(powers, axis=-1, keepdims=True)
            share_ref[p * heads + h] = shares
            att_ref[here, columns] = dot(shares.astype(bf16), values[there, columns]).astype(bf16)


def attend_backward(query, keys, values, share_ref, back_ref, rows, keyed, put_query, put_pair):
    heads = back_ref.shape[1] // HEAD
    packed = back_ref.shape[0] // rows
    score_scale = HEAD ** (-0.5)
    for h in range(heads):
        columns = slice(h * HEAD, (h + 1) * HEAD)
        key_grad = value_grad = None
        for p in range(packed):
            here = slice(p * rows, (p + 1) * rows)
            there = here if keyed else slice(None)
            shares = share_ref[p * heads + h]
            back = back_ref[here, columns]
            back_shares = dot_nt(back, values[there, columns])
            inner_sum = jnp.sum(shares * back_shares, axis=-1, keepdims=True)
            back_scores = (shares * (back_shares - inner_sum)).astype(bf16)
            put_query(here, columns, dot(back_scores, keys[there, columns]) * score_scale)
            key_term = dot_tn(back_scores, query[here, columns]) * score_scale
            value_term = dot_tn(shares.astype(bf16), back)
            if keyed:
                put_pair(there, columns, key_term, value_term)
            else:
                key_grad = key_term if key_grad is None else key_grad + key_term
                value_grad = value_term if value_grad is None else value_grad + value_term
        if not keyed:
            put_pair(slice(None), columns, key_grad, value_grad)


def self_forward_kernel(h_ref, w_ref, mask_ref, proj_ref, att_ref, share_ref):
    tile = pl.program_id(0)
    proj_ref[tile] = dot(h_ref[...], w_ref[...]).astype(bf16)

    @pl.when(tile == 2)
    def _():
        attend_forward(
            proj_ref.at[0], proj_ref.at[1], proj_ref.at[2], mask_ref, True, att_ref, share_ref
        )


def cross_forward_kernel(cq_ref, text_ref, w_ref, mask_ref, kv_ref, att_ref, share_ref, total):
    tile = pl.program_id(0)
    product = dot(text_ref[...], w_ref[...])

    @pl.when(tile < 2)
    def _():
        total[tile] = product

    @pl.when(tile >= 2)
    def _():
        kv_ref[tile - 2] = (total[tile - 2] + product).astype(bf16)

    @pl.when(tile == 3)
    def _():
        attend_forward(cq_ref, kv_ref.at[0], kv_ref.at[1], mask_ref, False, att_ref, share_ref)


def ffn_kernel(h_ref, up_ref, grad_ref, act_ref, slope_ref, gdown_ref):
    up_values = dot(h_ref[...], up_ref[...])
    chance = 0.5 * (1.0 + lax.erf(up_values * 0.5**0.5))
    density = jnp.exp(-0.5 * up_values * up_values) * 0.3989422804014327
    activated = (up_values * chance).astype(bf16)
    act_ref[...] = activated
    slope_ref[...] = chance + up_values * density
    store_pieces(dot_tn(activated, grad_ref[...]), gdown_ref)


def ffn_back_kernel(
    h_ref,
    down_ref,
    up_ref,
    grad_ref,
    act_ref,
    slope_ref,
    both_ref,
    branch_ref,
    part_ref,
    gup_ref,
    total,
    part,
):
    del both_ref
    tile = pl.program_id(0)
    back_act = dot_nt(grad_ref[...], down_ref[...])
    back_up = (back_act * slope_ref[...]).astype(bf16)
    gup_ref[...] = dot_tn(h_ref[...], back_up).astype(bf16).reshape(gup_ref.shape)

    @pl.when(tile == 0)
    def _():
        total[...] = dot(act_ref[...], down_ref[...])
        part[...] = dot_nt(back_up, up_ref[...])

    @pl.when(tile > 0)
    def _():
        total[...] += dot(act_ref[...], down_ref[...])
        part[...] += dot_nt(back_up, up_ref[...])

    @pl.when(tile == 3)
    def _():
        branch_ref[...] = total[...].astype(bf16)
        part_ref[...] = part[...].astype(bf16)


def cross_back_kernel(
    rows, back_ref, cq_ref, kv_ref, share_ref, text_ref, dcq_ref, grad_ref, pairs
):
    share = cq_ref.shape[1]

    @pl.when(pl.program_id(0) == 0)
    def _():
        def put_query(here, columns, value):
            dcq_ref[here, columns] = value.astype(bf16)

        def put_pair(there, columns, key_grad, value_grad):
            pairs[there, columns] = key_grad.astype(bf16)
            after_keys = slice(share + columns.start, share + columns.stop)
            pairs[there, after_keys] = value_grad.astype(bf16)

        attend_backward(
            cq_ref, kv_ref.at[0], kv_ref.at[1], share_ref, back_ref, rows, False, put_query, put_pair
        )

    grad_ref[...] = dot_tn(text_ref[...], pairs[...]).astype(bf16)


def outs_grad_kernel(att1_ref, carry1_ref, att2_ref, carry2_ref, grad_ref):
    tile = pl.program_id(0)

    @pl.when(tile == 0)
    def _():
        store_pieces(dot_tn(att1_ref[...], carry1_ref[...]), grad_ref)

    @pl.when(tile == 1)
    def _():
        store_pieces(dot_tn(att2_ref[...], carry2_ref[...]), grad_ref)


def store_pieces(gradient, target):
    n_dp, rows, columns = target.shape
    gradient = gradient.astype(bf16)
    chunk = gradient.shape[0] // n_dp
    for piece in range(rows // chunk):
        cut = gradient[:, piece * columns : (piece + 1) * columns]
        target[:, piece * chunk : (piece + 1) * chunk] = cut.reshape(n_dp, chunk, columns)


def self_back_kernel(
    rows,
    back_ref,
    proj_ref,
    share_ref,
    h1_ref,
    h2_ref,
    dcq_ref,
    both_ref,
    dproj_ref,
    grad_ref,
    parts,
):
    del both_ref
    tile = pl.program_id(0)
    share = dcq_ref.shape[1]

    @pl.when(tile == 0)
    def _():
        def put(part, here, columns, value):
            value = value.astype(bf16)
            parts[part, here, columns] = value
            dproj_ref[here, part * share + columns.start : part * share + columns.stop] = value

        def put_query(here, columns, value):
            put(0, here, columns, value)

        def put_pair(there, columns, key_grad, value_grad):
            put(1, there, columns, key_grad)
            put(2, there, columns, value_grad)

        attend_backward(
            proj_ref.at[0],
            proj_ref.at[1],
            proj_ref.at[2],
            share_ref,
            back_ref,
            rows,
            True,
            put_query,
            put_pair,
        )

    @pl.when(tile < 3)
    def _():
        grad_ref[...] = dot_tn(h1_ref[...], parts[tile]).astype(bf16).reshape(grad_ref.shape)

    @pl.when(tile == 3)
    def _():
        grad_ref[...] = dot_tn(h2_ref[...], dcq_ref[...]).astype(bf16).reshape(grad_ref.shape)


def fixed(dims):
    return pl.BlockSpec(dims, lambda t: (0,) * len(dims))


def moving(dims, index):
    return pl.BlockSpec(dims, lambda t: (0, index(t)))


def local_call(
    kernel, name, tiles, outs, specs, out_specs, scratch, flops, moved, aliases=None
):
    return pl.pallas_call(
        kernel,
        name=name,
        grid=(tiles,),
        input_output_aliases=aliases or {},
        out_shape=outs,
        in_specs=specs,
        out_specs=out_specs,
        scratch_shapes=scratch,
        compiler_params=pltpu.CompilerParams(vmem_limit_bytes=VMEM_CAP),
        cost_estimate=pl.CostEstimate(
            flops=flops // 8, bytes_accessed=moved // 8, transcendentals=0
        ),
    )


def self_forward(hidden, query_z, mask):
    tokens, width = hidden.shape
    share = query_z.shape[1] // 4
    packed, rows, _ = mask.shape
    pairs = (packed * share // HEAD, rows, rows)
    return local_call(
        self_forward_kernel,
        "self_forward",
        3,
        (shape((3, tokens, share), bf16), shape((tokens, share), bf16), shape(pairs, f32)),
        [fixed(hidden.shape), moving((width, share), lambda t: t), fixed(mask.shape)],
        (fixed((3, tokens, share)), fixed((tokens, share)), fixed(pairs)),
        [],
        6 * tokens * width * share,
        20_000_000,
    )(hidden, query_z, mask)


def cross_forward(cross_query, text_all, text_z, mask):
    tokens, share = cross_query.shape
    texts = text_all.shape[0]
    width = text_z.shape[0]
    packed, rows, _ = mask.shape
    pairs = (packed * share // HEAD, rows, texts)
    return local_call(
        cross_forward_kernel,
        "cross_forward",
        4,
        (shape((2, texts, share), bf16), shape((tokens, share), bf16), shape(pairs, f32)),
        [
            fixed(cross_query.shape),
            moving((texts, width), lambda t: t // 2),
            moving((width, share), lambda t: t),
            fixed(mask.shape),
        ],
        (fixed((2, texts, share)), fixed((tokens, share)), fixed(pairs)),
        [pltpu.VMEM((2, texts, share), f32)],
        8 * texts * width * share,
        20_000_000,
    )(cross_query, text_all, text_z, mask)


def ffn(hidden, up_z, grad_all, n, n_dp):
    tokens, width = hidden.shape
    share = up_z.shape[1] // 4
    chunk = share // n_dp
    return local_call(
        ffn_kernel,
        "ffn",
        4,
        (
            shape((tokens, 4 * share), bf16),
            shape((tokens, 4 * share), f32),
            shape((n_dp, 2 * n * chunk, 4 * share), bf16),
        ),
        [fixed(hidden.shape), moving((width, share), lambda t: t), fixed(grad_all.shape)],
        (
            moving((tokens, share), lambda t: t),
            moving((tokens, share), lambda t: t),
            pl.BlockSpec((n_dp, n * chunk // 4, 4 * share), lambda t: (0, 4 + t, 0)),
        ),
        [],
        16 * tokens * width * share,
        30_000_000,
    )(hidden, up_z, grad_all)


def ffn_back(hidden, down_z, up_z, grad_all, activated, slope, both):
    tokens, width = hidden.shape
    share = down_z.shape[0]
    return local_call(
        ffn_back_kernel,
        "ffn_back",
        4,
        (shape((tokens, width), bf16), shape((tokens, width), bf16), shape(both.shape, bf16)),
        [
            fixed(hidden.shape),
            moving((share, width), lambda t: t),
            moving((width, share), lambda t: t),
            fixed(grad_all.shape),
            moving((tokens, share), lambda t: t),
            moving((tokens, share), lambda t: t),
            in_place(),
        ],
        (
            fixed((tokens, width)),
            fixed((tokens, width)),
            pl.BlockSpec((both.shape[0], both.shape[1] // 2, share), lambda t: (0, 0, t)),
        ),
        [pltpu.VMEM((tokens, width), f32)] * 2,
        32 * tokens * width * share,
        50_000_000,
        {6: 2},
    )(hidden, down_z, up_z, grad_all, activated, slope, both)


def cross_back(back_attended, cross_query, text_pairs, shares, text_all, rows):
    tokens, share = cross_query.shape
    texts = text_all.shape[0]
    width = text_all.shape[1] // 2
    return local_call(
        functools.partial(cross_back_kernel, rows),
        "cross_back",
        2,
        (shape((tokens, share), bf16), shape((width, 4 * share), bf16)),
        [
            fixed(back_attended.shape),
            fixed(cross_query.shape),
            fixed(text_pairs.shape),
            fixed(shares.shape),
            moving((texts, width), lambda t: t),
        ],
        (fixed((tokens, share)), moving((width, 2 * share), lambda t: t)),
        [pltpu.VMEM((texts, 2 * share), bf16)],
        8 * texts * width * share,
        20_000_000,
    )(back_attended, cross_query, text_pairs, shares, text_all)


def outs_grad(attended1, carry1, attended2, carry2, n, n_dp):
    tokens, share = attended1.shape
    width = carry1.shape[1]
    chunk = share // n_dp
    return local_call(
        outs_grad_kernel,
        "outs_grad",
        2,
        shape((n_dp, n * chunk * 3 // 2, 4 * share), bf16),
        [fixed((tokens, share)), fixed((tokens, width))] * 2,
        pl.BlockSpec((n_dp, n * chunk // 4, 4 * share), lambda t: (0, 4 + t, 0)),
        [],
        4 * tokens * width * share,
        10_000_000,
    )(attended1, carry1, attended2, carry2)


def self_back(back_attended, projected, shares, hidden1, hidden2, back_cross, both, rows):
    tokens, width = hidden1.shape
    share = back_cross.shape[1]
    return local_call(
        functools.partial(self_back_kernel, rows),
        "self_back",
        4,
        (shape((tokens, 3 * share), bf16), shape(both.shape, bf16)),
        [
            fixed(back_attended.shape),
            fixed(projected.shape),
            fixed(shares.shape),
            fixed(hidden1.shape),
            fixed(hidden2.shape),
            fixed(back_cross.shape),
            in_place(),
        ],
        (
            fixed((tokens, 3 * share)),
            pl.BlockSpec((both.shape[0], both.shape[1] * 2 // 3, share), lambda t: (0, 0, t)),
        ),
        [pltpu.VMEM((3, tokens, share), bf16)],
        8 * tokens * width * share,
        25_000_000,
        {6: 1},
    )(back_attended, projected, shares, hidden1, hidden2, back_cross, both)


def block_slots(owners):
    owner = jnp.concatenate(owners)
    weight = jnp.concatenate([jnp.full(one.shape, at, jnp.int32) for at, one in enumerate(owners)])
    mark = owner + weight * 1024
    count = mark.shape[0]
    earlier = lax.broadcasted_iota(jnp.int32, (count, count), 1) < lax.broadcasted_iota(
        jnp.int32, (count, count), 0
    )
    same = jnp.logical_and(mark[:, None] == mark[None, :], earlier)
    return jnp.stack([owner, jnp.sum(same.astype(jnp.int32), axis=1)])


def slot_contents(owners, slots, places, capacities, firsts, n_dp):
    rows = []
    for owner, place, capacity, first in zip(owners, places, capacities, firsts):
        count = owner.shape[0]
        at = owner * capacity + slots[1, first : first + count]
        hit = at[None, :] == lax.broadcasted_iota(jnp.int32, (n_dp * capacity, count), 0)
        block = lax.broadcasted_iota(jnp.int32, (n_dp * capacity, count), 1)
        per_group, per_part, split = place_rule(place)
        part = block % per_group // per_part if split else block * 0
        column = block // per_group * per_part + block % per_part if split else block
        index = part * (count // (per_group // per_part)) + column if split else column
        rows.append(
            jnp.stack([jnp.sum(jnp.where(hit, value, 0), axis=1) for value in (index, block * 0 + 1)])
        )
    return jnp.concatenate(rows, axis=1)


def place_rule(place):
    parts = 1 + max(part for part, _ in place)
    if parts == 1:
        return 0, 0, False
    per_part = sum(1 for part, _ in place[:HEADS] if part == 0)
    return per_part * parts, per_part, True


def after(small, first):
    return lax.optimization_barrier((small, first))[0]


def body(
    tokens_in,
    text_in,
    seg_ids,
    capt_ids,
    grad_out,
    owner_query,
    owner_up,
    owner_outs,
    owner_text,
    owner_down,
    w_query,
    m_query,
    v_query,
    w_up,
    m_up,
    v_up,
    w_outs,
    m_outs,
    v_outs,
    w_text,
    m_text,
    v_text,
    w_down,
    m_down,
    v_down,
    norm_weight,
    m_norm,
    v_norm,
):
    n_dp = lax.axis_size("dp")
    n_z = lax.axis_size("fsdp")
    width = tokens_in.shape[1]
    own_rows = w_query.shape[0]
    chunk = own_rows // n_dp
    cap_big = w_query.shape[1] // BLK
    cap_out = w_outs.shape[1] // BLK
    heads_z = HEADS // n_z
    share = width // n_z
    owner_query, owner_up, owner_outs, owner_text, owner_down = (
        owner[:, 0] for owner in (owner_query, owner_up, owner_outs, owner_text, owner_down)
    )
    split_places = [split_place(b, heads_z, n_z) for b in range(owner_query.shape[0])]
    big_places = [flat_place(b) for b in range(owner_down.shape[0])]
    out_places = [flat_place(b) for b in range(owner_outs.shape[0])]
    owners = (owner_query, owner_outs, owner_text, owner_up, owner_down)
    places = (split_places, out_places, split_places, split_places, big_places)
    capacities = (cap_big, cap_out, cap_big, cap_big, cap_big)
    firsts = [sum(len(one) for one in places[:index]) for index in range(5)]
    slot_firsts = [sum(capacities[:index]) * n_dp for index in range(5)]
    slots = block_slots(owners)
    contents = slot_contents(owners, slots, places, capacities, firsts, n_dp)

    def spread(rows):
        return lax.all_gather(rows.reshape(-1, rows.shape[-1]), "dp", axis=0, tiled=True)

    def gather_sum(piece, parts):
        summed = lax.psum_scatter(piece, "dp", scatter_dimension=0, tiled=True)
        return summed.reshape(parts, chunk, -1)

    token_count = tokens_in.shape[0]
    marks = jnp.concatenate([seg_ids, capt_ids], axis=1)
    marks = jnp.pad(marks, ((0, 7), (0, 256 - marks.shape[1])))
    norms = jnp.pad(norm_weight, ((0, 2), (0, 0)))
    half = token_count // 2
    query_rows, grad_low, marks, norm_full = enter_call(
        "enter_query",
        0,
        slots,
        [(w_query, split_places, True, firsts[0])],
        [(grad_out[:half], False), (marks, False)],
        norms,
        True,
        False,
        n_z,
        n_dp,
        width,
    )
    outs_rows, hidden1, text_all = enter_call(
        "enter_outs",
        6,
        slots,
        [(w_outs, out_places, False, firsts[1])],
        [(tokens_in, True), (text_in, True)],
        norm_full[0:2],
        False,
        True,
        n_z,
        n_dp,
        width,
    )
    query_z, outs_z = spread(query_rows), spread(outs_rows)
    hidden1 = hidden1.reshape(-1, width)
    text_all = text_all.reshape(-1, text_in.shape[1])
    segment = marks[:, 0, :token_count]
    caption = marks[:, 0, token_count : token_count + capt_ids.shape[1]]
    self_mask = (segment[:, :, None] == segment[:, None, :]).astype(jnp.int32)
    text_row = lax.broadcasted_iota(jnp.int32, caption.shape, 0).reshape(1, 1, -1)
    packed_row = lax.broadcasted_iota(jnp.int32, (n_z, 1, 1), 0)
    cross_mask = jnp.logical_and(
        segment[:, :, None] == caption.reshape(1, 1, -1), packed_row == text_row
    ).astype(jnp.int32)

    projected, attended1, shares1 = self_forward(hidden1, query_z, self_mask)
    text_rows, grad_high = enter_call(
        "enter_text",
        7,
        after(slots, attended1),
        [(w_text, split_places, True, firsts[2])],
        [(grad_out[half:], False)],
        None,
        False,
        False,
        n_z,
        n_dp,
        width,
    )
    grad_all = jnp.concatenate([grad_low, grad_high], axis=1).reshape(-1, width)
    up_rows, down_rows, middle1, hidden2, cross_query = enter_call(
        "forward0",
        1,
        slots,
        [(w_up, split_places, True, firsts[3]), (w_down, big_places, False, firsts[4])],
        [],
        None,
        False,
        False,
        n_z,
        n_dp,
        width,
        forward_parts(
            attended1,
            outs_z,
            0,
            tokens_in,
            after(norm_full[2:4], text_rows),
            query_z,
            n_z,
            n_dp,
            False,
        ),
    )
    hidden2 = hidden2.reshape(-1, width)
    text_z, up_z, down_z = spread(text_rows), spread(up_rows), spread(down_rows)
    text_pairs, attended2, shares2 = cross_forward(cross_query, text_all, text_z, cross_mask)
    middle2, hidden3 = forward_call(
        attended2, outs_z, 1, middle1, norm_full[4:6], None, n_z, n_dp, 2
    )
    hidden3 = hidden3.reshape(-1, width)
    activated, slope, both = ffn(hidden3, up_z, grad_all, n_z, n_dp)
    branch3, part3, both = ffn_back(hidden3, down_z, up_z, grad_all, activated, slope, both)
    branch3 = branch3.reshape(n_z, token_count, width)
    part3 = part3.reshape(n_z, token_count, width)
    up_down_sum = gather_sum(both.reshape(-1, 4 * share), 2 * n_z)
    up_sum, down_sum = up_down_sum[:n_z], up_down_sum[n_z:]
    at_middle2, carry2, back_att2, term3, result = back_call(
        part3, after(slots, part3), None, grad_out, middle2, norm_full[4:6], outs_z, 1, branch3, n_z, n_dp, 3
    )
    carry2 = carry2.reshape(-1, width)
    back_cross, text_part = cross_back(
        back_att2, cross_query, text_pairs, shares2, text_all, token_count
    )
    text_sum = gather_sum(text_part, n_z)
    at_middle1, carry1, back_att1, term2 = back_call(
        back_cross, query_z, 3, at_middle2, middle1, norm_full[2:4], outs_z, 0, None, n_z, n_dp, 4
    )
    carry1 = carry1.reshape(-1, width)
    both = outs_grad(after(attended1, up_down_sum), carry1, attended2, carry2, n_z, n_dp)
    back_projected, both = self_back(
        back_att1, projected, shares1, hidden1, hidden2, back_cross, both, token_count
    )
    query_outs_sum = gather_sum(both.reshape(-1, 4 * share), 3 * n_z // 2)
    down_grad, up_grad, text_grad, grad_in, term1 = leave_call(
        "leave_up",
        8,
        contents,
        [
            (down_sum, False, cap_big, slot_firsts[4], True),
            (up_sum, True, cap_big, slot_firsts[3], True),
            (text_sum, True, cap_big, slot_firsts[2], True),
        ],
        None,
        n_z,
        n_dp,
        last_parts(
            back_projected,
            query_z,
            at_middle1,
            tokens_in,
            norm_full[0:2],
            n_z,
            n_dp,
        ),
    )
    query_outs_sum = after(query_outs_sum, term1)
    query_sum, outs_sum = query_outs_sum[:n_z], query_outs_sum[n_z:]
    norm_term = jnp.concatenate([term1[:2], term2[:2], term3[:4]], axis=0)
    loose, norm_grad = leave_call(
        "leave_query",
        9,
        contents,
        [
            (outs_sum, False, cap_out, slot_firsts[1], False),
            (query_sum, True, cap_big, slot_firsts[0], False),
        ],
        norm_term,
        n_z,
        n_dp,
    )
    loose = lax.all_to_all(loose, "dp", 0, 0, tiled=True).reshape(own_rows, -1)
    outs_slots = loose[:, : cap_out * BLK].astype(f32)
    query_grad = loose[:, cap_out * BLK :].astype(f32)
    norm_grad = norm_grad[:6]
    text_grad, up_grad, down_grad = (
        grad.reshape(own_rows, -1).astype(f32) for grad in (text_grad, up_grad, down_grad)
    )
    up_new = adamw_update(w_up, m_up, v_up, up_grad, rate_up, decay_rate)
    text_new = adamw_update(w_text, m_text, v_text, text_grad, rate_text, decay_rate)
    down_new = adamw_update(w_down, m_down, v_down, down_grad, rate_down, decay_rate)
    query_new = adamw_update(w_query, m_query, v_query, query_grad, rate_query, decay_rate)
    outs_new = adamw_update(w_outs, m_outs, v_outs, outs_slots, rate_outs, decay_rate)
    norm_new = adamw_update(norm_weight, m_norm, v_norm, norm_grad, rate_norm, 0.0)
    return (
        result,
        grad_in,
        *query_new,
        *up_new,
        *outs_new,
        *text_new,
        *down_new,
        *norm_new,
    )


def solution(mesh):
    rows = P(("dp", "fsdp"), None)
    slots = P("fsdp", "dp")
    norms = P(None, "dp")
    in_specs = (rows,) * 5 + (P(),) * 5 + (slots,) * 15 + (norms,) * 3
    out_specs = (rows,) * 2 + (slots,) * 15 + (norms,) * 3
    return jax.shard_map(body, mesh=mesh, in_specs=in_specs, out_specs=out_specs, check_vma=False)
```

```python
import functools

import jax
import jax.numpy as jnp
from jax import lax
from jax.experimental import pallas as pl
from jax.experimental.pallas import tpu as pltpu
from jax.sharding import PartitionSpec as P

HEADS = 16
HEAD = 128
STEP = 10
BLK = 128


beta_first = 0.9
beta_second = 0.999
adam_eps = 1e-08
decay_rate = 0.01
rate_query = 0.04
rate_up = 0.04
rate_outs = 0.12
rate_text = 0.03
rate_down = 0.03
rate_norm = 0.5
norm_eps = 1e-05
score_floor = -1e30
bf16 = jnp.bfloat16
f32 = jnp.float32


def normalize(values):
    centered = values - jnp.mean(values, axis=-1, keepdims=True)
    inverse_std = lax.rsqrt(jnp.mean(centered * centered, axis=-1, keepdims=True) + norm_eps)
    return (centered * inverse_std, inverse_std)


def norm_back(back_hidden, normed, inverse_std, gain_row):
    back_normed = back_hidden * gain_row
    return inverse_std * (
        back_normed
        - jnp.mean(back_normed, axis=-1, keepdims=True)
        - normed * jnp.mean(back_normed * normed, axis=-1, keepdims=True)
    )


def adamw_update(weight, first, second, gradient, rate, decay):
    first_new = beta_first * first + (1.0 - beta_first) * gradient
    second_new = beta_second * second + (1.0 - beta_second) * gradient * gradient
    first_hat = first_new / (1.0 - beta_first**STEP)
    second_hat = second_new / (1.0 - beta_second**STEP)
    weight_new = weight - rate * (first_hat / (jnp.sqrt(second_hat) + adam_eps) + decay * weight)
    return (first_new, second_new, weight_new)


def dot(left, right):
    return jnp.dot(left, right, preferred_element_type=f32)


def dot_nt(left, right):
    return lax.dot_general(left, right, (((1,), (1,)), ((), ())), preferred_element_type=f32)


def dot_tn(left, right):
    return lax.dot_general(left, right, (((0,), (0,)), ((), ())), preferred_element_type=f32)


def split_place(block, per_part, parts):
    group, rest = divmod(block, per_part * parts)
    part, inner = divmod(rest, per_part)
    return part, group * per_part + inner


def flat_place(block):
    return 0, block


MESH = pl.DeviceIdType.MESH


SUBS = 4


class Line:
    def __init__(self, n, rows, step):
        self.n, self.rows, self.step = n, rows, step
        self.at = lax.axis_index("fsdp")

    def has(self, way):
        return self.at < self.n - 1 if way == 0 else self.at > 0

    def peer(self, way):
        index = jnp.clip(self.at + (1 if way == 0 else -1), 0, self.n - 1)
        return {"fsdp": index}

    def greet(self, others=0):
        barrier = pltpu.get_barrier_semaphore()
        for way in (0, 1):

            @pl.when(self.has(way))
            def _():
                pl.semaphore_signal(
                    barrier, inc=1, device_id=self.peer(way), device_id_type=pl.DeviceIdType.MESH
                )

        pl.semaphore_wait(
            barrier, others + self.has(0).astype(jnp.int32) + self.has(1).astype(jnp.int32)
        )

    def copy(self, source, target, send, recv, way):
        return pltpu.make_async_remote_copy(
            src_ref=source,
            dst_ref=target,
            send_sem=send,
            recv_sem=recv,
            device_id=self.peer(way),
            device_id_type=pl.DeviceIdType.MESH,
        )

    def part(self, sub):
        return pl.ds(sub * self.step, self.step)


class Sums:
    def __init__(self, line, part, held, send, recv):
        self.line, self.part, self.held, self.send, self.recv = line, part, held, send, recv

    def move(self, way, target, sub, source):
        line = self.line
        rows = line.part(sub)
        return line.copy(
            source,
            self.held.at[way, target, rows],
            self.send.at[way, target, sub],
            self.recv.at[way, target, sub],
            way,
        )

    def target(self, way, time):
        n, at = self.line.n, self.line.at
        return n - 1 - (time - at) if way == 0 else time - (n - 1 - at)

    def passes(self, way, target):
        n, at = self.line.n, self.line.at
        if way == 0:
            return jnp.logical_and(target > at, target < n)
        return jnp.logical_and(target < at, target >= 0)

    def forward(self, sub, time):
        line = self.line
        rows = line.part(sub)
        for way in (0, 1):
            target = self.target(way, time)
            passes = self.passes(way, target)
            inner = jnp.logical_and(passes, line.has(1 - way))
            outer = jnp.logical_and(passes, jnp.logical_not(line.has(1 - way)))

            @pl.when(outer)
            def _():
                self.move(way, target, sub, self.part.at[target, rows]).start()

            @pl.when(inner)
            def _():
                held = self.held.at[way, target, rows]
                self.move(way, target, sub, held).wait_recv()
                total = held[...].astype(f32) + self.part[target, rows].astype(f32)
                held[...] = total.astype(bf16)
                self.move(way, target, sub, held).start()

    def total(self, sub, sum_ref):
        line = self.line
        rows = line.part(sub)
        sum_ref[...] = self.part[line.at, rows].astype(f32)
        for way in (0, 1):

            @pl.when(line.has(1 - way))
            def _():
                held = self.held.at[way, line.at, rows]
                self.move(way, line.at, sub, held).wait_recv()
                sum_ref[...] += held[...].astype(f32)

    def finish(self):
        line = self.line
        for way in (0, 1):
            for time in range(line.n - 1):
                target = self.target(way, time)

                @pl.when(self.passes(way, target))
                def _():
                    for sub in range(line.rows // line.step):
                        held = self.held.at[way, target, line.part(sub)]
                        self.move(way, target, sub, held).wait_send()


def relay(n, sums, blocks, settle, hook=None, later=None):
    lag = 2 * (n - 1)
    for slot in range((SUBS + 2) * (n - 1)):
        sub, time = divmod(slot, n - 1)
        if later is not None and slot >= lag:
            later.forward(*divmod(slot - lag, n - 1))
        if hook is not None and slot == SUBS * (n - 1):
            hook()
        if sub < SUBS:
            for one in sums:
                one.forward(sub, time)
        if time == 0 and 0 <= sub - 1 < SUBS:
            settle(sub - 1)
        if blocks is not None:
            if time == n - 2 and 0 <= sub - 1 < SUBS:
                blocks.forward(sub - 1, 1)
            if time < n - 2 and 0 <= sub - 2 < SUBS:
                blocks.forward(sub - 2, time + 2)
    for one in sums:
        one.finish()
    if blocks is not None:
        blocks.finish()


class Blocks:
    def __init__(self, line, full, send, recv):
        self.line, self.full, self.send, self.recv = line, full, send, recv

    def move(self, way, source, sub):
        line = self.line
        held = self.full.at[source, line.part(sub)]
        return line.copy(
            held, held, self.send.at[way, source, sub], self.recv.at[way, source, sub], way
        )

    def behind(self, way, source):
        return self.line.at > source if way == 0 else self.line.at < source

    def start(self, sub):
        for way in (0, 1):

            @pl.when(self.line.has(way))
            def _():
                self.move(way, self.line.at, sub).start()

    def forward(self, sub, step):
        line = self.line
        for way in (0, 1):
            source = line.at - step if way == 0 else line.at + step

            @pl.when(jnp.logical_and(source >= 0, source < line.n))
            def _():
                self.move(way, source, sub).wait_recv()

                @pl.when(line.has(way))
                def _():
                    self.move(way, source, sub).start()

    def finish(self):
        line = self.line
        for way in (0, 1):
            for source in range(line.n):
                ours = jnp.logical_or(self.behind(way, source), line.at == source)

                @pl.when(jnp.logical_and(ours, line.has(way)))
                def _():
                    for sub in range(line.rows // line.step):
                        self.move(way, source, sub).wait_send()


def lane_moves(width, order):
    moves = []
    piece = width // len(order)
    for group in range(width // BLK):
        parts = []
        for offset in range(0, BLK, piece):
            start = order[(group * BLK + offset) // piece] * piece
            parts.append((offset, start // BLK, start % BLK))
        moves.append(parts)
    return piece, moves


def reorder(load, store, rows, width, order):
    piece, moves = lane_moves(width, order)
    lane = lax.broadcasted_iota(jnp.int32, (rows, BLK), 1)
    for group, parts in enumerate(moves):
        value = None
        for offset, source, start in parts:
            block = load(source)
            if start != offset:
                block = pltpu.roll(block, (offset - start) % BLK, 1)
            value = block if value is None else jnp.where(lane >= offset, block, value)
        store(group, value)


def shuffle_order(n_z, n_dp):
    return [z * n_dp + i for i in range(n_dp) for z in range(n_z)]


def unshuffle_order(n_z, n_dp):
    return [i * n_z + z for z in range(n_z) for i in range(n_dp)]


def by_tiles(columns, tile, run):
    def one(index, carry):
        run(pl.ds(pl.multiple_of(index * tile, tile), tile))
        return carry

    lax.fori_loop(0, columns // tile, one, 0)


class Swap:
    def __init__(self, axis, source, target, send, recv):
        self.axis, self.source, self.target = axis, source, target
        self.send, self.recv = send, recv
        self.n = lax.axis_size(axis)
        self.me = lax.axis_index(axis)

    def copy(self, jump, arrival=False):
        peer = lax.rem(self.me + jump, self.n)
        slot = peer if arrival else self.me
        return pltpu.make_async_remote_copy(
            src_ref=self.source.at[peer],
            dst_ref=self.target.at[slot],
            send_sem=self.send.at[jump],
            recv_sem=self.recv.at[slot],
            device_id={self.axis: peer},
            device_id_type=MESH,
        )

    def start(self):
        for jump in range(1, self.n):
            self.copy(jump).start()

    def keep(self):
        self.target[self.me] = self.source[self.me]

    def wait(self):
        for jump in range(1, self.n):
            self.copy(jump, True).wait_recv()

    def finish(self):
        for jump in range(1, self.n):
            self.copy(jump).wait_send()


def greet_all():
    barrier = pltpu.get_barrier_semaphore()
    count = 0
    for axis in ("dp", "fsdp"):
        n, me = lax.axis_size(axis), lax.axis_index(axis)
        count += n - 1
        for jump in range(1, n):
            pl.semaphore_signal(
                barrier, inc=1, device_id={axis: lax.rem(me + jump, n)}, device_id_type=MESH
            )
    pl.semaphore_wait(barrier, count)


class Refs:
    def __init__(self, refs):
        self.refs = list(refs)

    def take(self, count=None):
        taken = self.refs[: 1 if count is None else count]
        self.refs = self.refs[len(taken) :]
        return taken[0] if count is None else taken


def enter_kernel(weights, gathers, order, normed, hidden, inner, inner_counts, *refs):
    refs = Refs(refs)
    n_dp, n_z = lax.axis_size("dp"), lax.axis_size("fsdp")
    slots_ref = refs.take()
    w_refs = refs.take(len(weights))
    in_refs = refs.take(len(gathers))
    norm_in = refs.take() if normed or hidden else None
    inner_refs = refs.take(inner_counts[0])
    row_refs = refs.take(len(weights))
    full_refs = refs.take(len(gathers))
    norm_out = refs.take() if normed else None
    inner_refs += refs.take(inner_counts[1])
    inner_refs += refs.take(inner_counts[2])
    loads = []
    for w_ref in w_refs:
        stage, sem = refs.take(2)
        load = pltpu.make_async_copy(w_ref, stage, sem)
        load.start()
        loads.append((stage, load))
    greet_all()
    if normed:
        parts, *sems = refs.take(3)
        norm_swap = Spread("dp", norm_in, parts, *sems)
        norm_swap.start()
    lines = []
    for in_ref, full_ref in zip(in_refs, full_refs):
        rows = in_ref.shape[0]
        step = rows // pieces_of(rows)
        lines.append(Blocks(Line(n_z, rows, step), full_ref, *refs.take(2)))
    swaps = []
    for (stage, load), (places, split, _) in zip(loads, weights):
        source, target, *sems = refs.take(4)
        swap = Swap("dp", source, target, *sems)
        load.wait()
        chunk = source.shape[2]
        for jump in range(n_dp):
            peer = lax.rem(swap.me + jump, n_dp)
            into = source if jump else target
            for slot in range(source.shape[1]):
                here = pl.ds(pl.multiple_of(peer * chunk, chunk), chunk)
                piece = stage[here, slot * BLK : (slot + 1) * BLK]
                into[peer, slot] = piece.astype(bf16)
            if jump:
                swap.copy(jump).start()
        swaps.append(swap)
    if hidden:
        work = refs.take()
    for index, (in_ref, full_ref, blocks) in enumerate(zip(in_refs, full_refs, lines)):
        line = blocks.line
        if hidden and index == 0:
            for sub in range(line.rows // line.step):
                here = line.part(sub)
                values, _ = normalize(in_ref[here].astype(f32))
                work[...] = values * norm_in[0:1] + norm_in[1:2]
                store_shuffled(work, full_ref, line, here, order)
                blocks.start(sub)
        elif in_ref.dtype == bf16 and gathers[index]:
            work2 = refs.take()
            work2[...] = in_ref[...].astype(f32)
            store_shuffled(work2, full_ref, line, line.part(0), order)
            blocks.start(0)
        else:
            for sub in range(line.rows // line.step):
                here = line.part(sub)
                full_ref[line.at, here] = in_ref[here]
                blocks.start(sub)
    if normed:
        parts[norm_swap.me] = norm_in[...]
        norm_swap.wait()
        share = norm_in.shape[1]
        for index in range(n_dp):
            norm_out[:, index * share : (index + 1) * share] = parts[index]
    shares = []

    def compact(index):
        swap, row_ref, (places, split, first) = swaps[index], row_refs[index], weights[index]
        swap.wait()
        if split:
            cut, *sems = refs.take(3)
            share = Swap("fsdp", cut, row_ref, *sems)
            shares.append(share)
        else:
            cut = row_ref
        for block, (part, column) in enumerate(places):
            owner, slot = slots_ref[0, first + block], slots_ref[1, first + block]
            cut[part, :, column * BLK : (column + 1) * BLK] = swap.target[owner, slot]
        if split:
            share.start()
            share.keep()

    ahead = 0
    if inner is not None:
        ahead = 1
        inner(*inner_refs, hook=lambda: compact(0))
    for step in range(1, n_z):
        for blocks in lines:
            for sub in range(blocks.line.rows // blocks.line.step):
                blocks.forward(sub, step)
    for index in range(ahead, len(weights)):
        compact(index)
    for share in shares:
        share.wait()
    for one in [*swaps, *shares, *lines]:
        one.finish()
    if normed:
        norm_swap.finish()


class Spread(Swap):
    def copy(self, jump, arrival=False):
        peer = lax.rem(self.me + jump, self.n)
        slot = peer if arrival else self.me
        return pltpu.make_async_remote_copy(
            src_ref=self.source,
            dst_ref=self.target.at[slot],
            send_sem=self.send.at[jump],
            recv_sem=self.recv.at[slot],
            device_id={self.axis: peer},
            device_id_type=MESH,
        )


def store_shuffled(work, full_ref, line, here, order):
    rows, width = work.shape
    folds = width // order.width
    pieces = len(order.pieces)
    orders = [fold * pieces + piece for fold in range(folds) for piece in order.pieces]

    def load(group):
        return work[:, group * BLK : (group + 1) * BLK]

    def store(group, value):
        full_ref[line.at, here, group * BLK : (group + 1) * BLK] = value.astype(bf16)

    reorder(load, store, rows, width, orders)


def expand_slots(slots_ref, rows, cut, blocks, capacity, first, offset):
    columns = rows.shape[2] // BLK
    for part in range(rows.shape[0]):
        for column in range(columns):
            blocks[part * columns + column] = rows[part, :, column * BLK : (column + 1) * BLK]
    for owner in range(cut.shape[0]):
        for position in range(capacity):
            slot = first + owner * capacity + position
            value = blocks[slots_ref[0, slot]].astype(f32)
            live = slots_ref[1, slot].astype(f32)
            start = offset + position * BLK
            cut[owner, :, start : start + BLK] = (value * live).astype(bf16)


def leave_kernel(weights, summed, inner, inner_counts, *refs):
    refs = Refs(refs)
    n_dp = lax.axis_size("dp")
    slots_ref = refs.take()
    row_refs = refs.take(len(weights))
    term_ref = refs.take() if summed else None
    inner_refs = refs.take(inner_counts[0])
    gone = sum(1 for weight in weights if weight[3])
    out_refs = refs.take(gone)
    loose_ref = refs.take() if gone < len(weights) else None
    sum_ref = refs.take() if summed else None
    inner_refs += refs.take(inner_counts[1])
    inner_refs += refs.take(inner_counts[2])
    greet_all()
    if summed:
        cut, parts, send, recv, total, others, send2, recv2 = refs.take(8)
        share = cut.shape[2]
        for index in range(n_dp):
            cut[index] = term_ref[:, index * share : (index + 1) * share]
        term_swap = Swap("dp", cut, parts, send, recv)
        term_swap.start()
        term_swap.keep()
    shares = []
    for row_ref, (split, _, _, _) in zip(row_refs, weights):
        if split:
            held, *sems = refs.take(3)
            share = Swap("fsdp", row_ref, held, *sems)
            share.start()
            share.keep()
            shares.append(share)
        else:
            shares.append(None)
    if summed:
        term_swap.wait()
        total[...] = jnp.sum(parts[...], axis=0)
        total_spread = Spread("fsdp", total, others, send2, recv2)
        total_spread.start()
        others[total_spread.me] = total[...]
    swaps = []
    offset = 0
    for row_ref, share, (split, capacity, first, whole) in zip(row_refs, shares, weights):
        if split:
            share.wait()
        rows = share.target if split else row_ref
        if not whole:
            expand_slots(slots_ref, rows, loose_ref, refs.take(), capacity, first, offset)
            offset += capacity * BLK
            continue
        out_ref = out_refs.pop(0)
        cut, *sems, blocks = refs.take(4)
        expand_slots(slots_ref, rows, cut, blocks, capacity, first, 0)
        swap = Swap("dp", cut, out_ref, *sems)
        swap.start()
        swap.keep()
        swaps.append(swap)
    if inner is not None:
        inner(*inner_refs)
    if summed:
        total_spread.wait()
        sum_ref[...] = jnp.sum(others[...], axis=0)
    for swap in swaps:
        swap.wait()
    for one in [*swaps, *shares]:
        if one is not None:
            one.finish()
    if summed:
        term_swap.finish()
        total_spread.finish()


def fetch_columns(source, index, target, sem):
    columns = target.shape[1]
    return pltpu.make_async_copy(source.at[:, pl.ds(index * columns, columns)], target, sem)


def forward_kernel(
    n, order, half, wide, alone, att_ref, outs_hbm, base_ref, norm_ref, *rest, hook=None
):
    if wide:
        next_hbm, middle_ref, full_ref, result_ref = rest[:4]
        *rest, next_ref, next_sem = rest[4:]
    else:
        middle_ref, full_ref = rest[:2]
        rest = rest[2:]
    part, held, work, s_send, s_recv, b_send, b_recv, outs_ref, outs_sem = rest
    rows, width = base_ref.shape
    step = rows // SUBS
    load_outs = fetch_columns(outs_hbm, half, outs_ref, outs_sem)
    load_outs.start()
    if wide:
        load_next = fetch_columns(next_hbm, 3, next_ref, next_sem)
        load_next.start()
    line = Line(n, rows, step)
    if alone:
        line.greet()
    load_outs.wait()
    sums = Sums(line, part, held, s_send, s_recv)
    blocks = Blocks(line, full_ref, b_send, b_recv)

    def multiply(columns):
        product = dot(att_ref[...], outs_ref[:, columns]).astype(bf16)
        part[:, :, columns] = product.reshape(n, rows, -1)

    by_tiles(width, 256, multiply)

    def settle(sub):
        here = line.part(sub)
        sums.total(sub, work)
        middle = base_ref[here].astype(f32) + work[...]
        middle_ref[here] = middle
        normed, _ = normalize(middle)
        work[...] = normed * norm_ref[0:1] + norm_ref[1:2]

        def load(group):
            return work[:, group * BLK : (group + 1) * BLK]

        def store(group, value):
            full_ref[line.at, here, group * BLK : (group + 1) * BLK] = value.astype(bf16)

        reorder(load, store, step, width, order)
        blocks.start(sub)

    relay(n, [sums], blocks, settle, hook)
    if wide:
        load_next.wait()

        def multiply_next(columns):
            whole = full_ref[...].reshape(n * rows, width)
            result_ref[:, columns] = dot(whole, next_ref[:, columns]).astype(bf16)

        by_tiles(result_ref.shape[1], 256, multiply_next)


def carry_back(work, plain, order, step, width, middle, base, gain, term_ref, first):
    def load(group):
        return work[:, group * BLK : (group + 1) * BLK]

    def store(group, value):
        plain[:, group * BLK : (group + 1) * BLK] = value

    reorder(load, store, step, width, order)
    back_hidden = plain[...]
    normed, inverse = normalize(middle)
    gain_term = jnp.sum(back_hidden * normed, axis=0, keepdims=True)
    bias_term = jnp.sum(back_hidden, axis=0, keepdims=True)
    if first:
        term_ref[...] = jnp.zeros_like(term_ref)
        term_ref[0:1] = gain_term
        term_ref[1:2] = bias_term
    else:
        term_ref[0:1] += gain_term
        term_ref[1:2] += bias_term
    return base + norm_back(back_hidden, normed, inverse, gain)


def back_kernel(
    n, order, column, half, alone, dy_ref, w_hbm, base_ref, middle_ref, norm_ref, outs_hbm, *rest
):
    if column is None:
        branch, *rest = rest
    carry_ref, full_ref, att_ref, term_ref, *rest = rest
    if column is None:
        result_ref, *rest = rest
    held, work, plain, s_send, s_recv, b_send, b_recv, outs_ref, outs_sem = rest[:9]
    rows, width = base_ref.shape
    step = rows // SUBS
    if column is not None:
        part, w_ref, w_sem = rest[9:]
        load_w = fetch_columns(w_hbm, column, w_ref, w_sem)
        load_w.start()
    else:
        part = dy_ref
        held2, r_send, r_recv = rest[9:]
    load_outs = fetch_columns(outs_hbm, half, outs_ref, outs_sem)
    load_outs.start()
    line = Line(n, rows, step)
    if alone:
        line.greet()
    sums = Sums(line, part, held, s_send, s_recv)
    blocks = Blocks(line, full_ref, b_send, b_recv)
    results = None
    if column is None:
        results = Sums(line, branch, held2, r_send, r_recv)
    if column is not None:
        load_w.wait()

        def multiply(columns):
            product = dot_nt(dy_ref[...], w_ref[columns]).astype(bf16)
            part[:, :, columns] = product.reshape(n, rows, -1)

        by_tiles(width, 256, multiply)

    def settle(sub):
        here = line.part(sub)
        sums.total(sub, work)
        carry = carry_back(
            work,
            plain,
            order,
            step,
            width,
            middle_ref[here].astype(f32),
            base_ref[here].astype(f32),
            norm_ref[0:1],
            term_ref,
            sub == 0,
        )
        carry_ref[here] = carry
        full_ref[line.at, here] = carry.astype(bf16)
        blocks.start(sub)

    relay(n, [sums], blocks, settle, None, results)
    if results is not None:
        for sub in range(SUBS):
            here = line.part(sub)
            results.total(sub, work)
            result_ref[here] = (middle_ref[here] + work[...]).astype(bf16)
        results.finish()
    load_outs.wait()

    def multiply_next(columns):
        whole = full_ref[...].reshape(n * rows, width)
        att_ref[:, columns] = dot_nt(whole, outs_ref[columns]).astype(bf16)

    by_tiles(att_ref.shape[1], 256, multiply_next)


def last_kernel(n, order, dy_ref, w_hbm, base_ref, tokens, norm_ref, *rest):
    grad_ref, term_ref = rest[:2]
    part, held, work, plain, s_send, s_recv, w_ref, w_sem = rest[2:]
    rows, width = base_ref.shape
    step = rows // SUBS
    load_w = fetch_columns(w_hbm, 0, w_ref, w_sem)
    load_w.start()
    line = Line(n, rows, step)
    load_w.wait()
    sums = Sums(line, part, held, s_send, s_recv)

    def multiply(columns):
        product = dot_nt(dy_ref[...], w_ref[columns]).astype(bf16)
        part[:, :, columns] = product.reshape(n, rows, -1)

    by_tiles(width, 256, multiply)

    def settle(sub):
        here = line.part(sub)
        sums.total(sub, work)
        carry = carry_back(
            work,
            plain,
            order,
            step,
            width,
            tokens[here].astype(f32),
            base_ref[here],
            norm_ref[0:1],
            term_ref,
            sub == 0,
        )
        grad_ref[here] = carry.astype(bf16)

    relay(n, [sums], None, settle)


VMEM_CAP = 52 * 1024 * 1024


def in_place():
    return pl.BlockSpec(memory_space=pl.ANY)


def whole_vmem():
    return pl.BlockSpec(memory_space=pltpu.VMEM)


def sem_pair(n, subs):
    return [pltpu.SemaphoreType.DMA((2, n, subs)), pltpu.SemaphoreType.DMA((2, n, subs))]


def line_call(kernel, name, ident, outs, specs, scratch, flops, moved):
    return pl.pallas_call(
        kernel,
        name=name,
        out_shape=outs,
        in_specs=specs,
        out_specs=jax.tree.map(lambda _: whole_vmem(), outs),
        scratch_shapes=scratch,
        compiler_params=pltpu.CompilerParams(
            collective_id=ident, has_side_effects=True, vmem_limit_bytes=VMEM_CAP
        ),
        cost_estimate=pl.CostEstimate(flops=flops, bytes_accessed=moved, transcendentals=0),
    )


def shape(dims, kind):
    return jax.ShapeDtypeStruct(dims, kind)


LINK_COST = 4_000_000


def pieces_of(rows):
    return max(1, rows * SUBS // 128)


class Order:
    def __init__(self, pieces, width):
        self.pieces, self.width = pieces, width


def swap_sems(n):
    return [pltpu.SemaphoreType.DMA((n,)), pltpu.SemaphoreType.DMA((n,))]


def enter_call(
    name, ident, slots, weights, gathers, norms, normed, hidden, n, n_dp, width, inner=None
):
    chunk = weights[0][0].shape[0] // n_dp
    run, inner_args, inner_specs, inner_outs, scratch = inner or (None, [], [], [], [])
    counts = (len(inner_args), len(inner_outs), len(scratch))
    outs, scratch = [], list(scratch)
    for array, places, split, _ in weights:
        parts = n if split else 1
        outs.append(shape((parts, chunk, len(places) // parts * BLK), bf16))
        scratch += [pltpu.VMEM(array.shape, f32), pltpu.SemaphoreType.DMA]
    if normed:
        scratch += [pltpu.VMEM((n_dp, *norms.shape), f32), *swap_sems(n_dp)]
    for array, _ in gathers:
        rows = array.shape[0]
        outs.append(shape((n, *array.shape), array.dtype))
        scratch += sem_pair(n, pieces_of(rows))
    if normed:
        outs.append(shape((norms.shape[0], n_dp * norms.shape[1]), f32))
    for array, _, _, _ in weights:
        slots_shape = (n_dp, array.shape[1] // BLK, chunk, BLK)
        scratch += [pltpu.VMEM(slots_shape, bf16)] * 2 + swap_sems(n_dp)
    if hidden:
        scratch.append(pltpu.VMEM((gathers[0][0].shape[0] // SUBS, width), f32))
    for array, moved in gathers[1 if hidden else 0 :]:
        if moved:
            scratch.append(pltpu.VMEM(array.shape, f32))
    for index, (_, places, split, _) in enumerate(weights):
        if split:
            scratch += [pltpu.VMEM(outs[index].shape, bf16), *swap_sems(n)]
    args = [slots, *(weight[0] for weight in weights), *(gather[0] for gather in gathers)]
    specs = [pl.BlockSpec(memory_space=pltpu.SMEM)] + [in_place()] * len(weights)
    specs += [whole_vmem()] * len(gathers)
    if normed or hidden:
        args.append(norms)
        specs.append(whole_vmem())
    args += inner_args
    specs += inner_specs
    outs += inner_outs
    kernel = functools.partial(
        enter_kernel,
        [weight[1:] for weight in weights],
        [gather[1] for gather in gathers],
        Order(shuffle_order(n, n_dp), width),
        normed,
        hidden,
        run,
        counts,
    )
    return line_call(kernel, name, ident, outs, specs, scratch, 0, LINK_COST)(*args)


def leave_call(name, ident, slots, weights, term, n, n_dp, inner=None):
    outs, scratch = [], []
    specs = [pl.BlockSpec(memory_space=pltpu.SMEM)] + [whole_vmem()] * len(weights)
    args = [slots, *(weight[0] for weight in weights)]
    chunk = weights[0][0].shape[1]
    if term is not None:
        args.append(term)
        specs.append(whole_vmem())
        block = (term.shape[0], term.shape[1] // n_dp)
    counts = (0, 0, 0)
    run = None
    if inner is not None:
        run, inner_args, inner_specs, inner_outs, inner_scratch = inner
        counts = (len(inner_args), len(inner_outs), len(inner_scratch))
        args += inner_args
        specs += inner_specs
        scratch += inner_scratch
    if term is not None:
        scratch += [pltpu.VMEM((n_dp, *block), f32)] * 2 + swap_sems(n_dp)
        scratch += [pltpu.VMEM(block, f32), pltpu.VMEM((n, *block), f32), *swap_sems(n)]
    for rows, split, _, _, _ in weights:
        if split:
            scratch += [pltpu.VMEM(rows.shape, bf16), *swap_sems(n)]
    for rows, _, capacity, _, whole in weights:
        slots_shape = (n_dp, chunk, capacity * BLK)
        if whole:
            outs.append(shape(slots_shape, bf16))
            scratch += [pltpu.VMEM(slots_shape, bf16), *swap_sems(n_dp)]
        blocks = rows.shape[0] * rows.shape[2] // BLK
        scratch.append(pltpu.VMEM((blocks, chunk, BLK), bf16))
    loose = sum(capacity * BLK for _, _, capacity, _, whole in weights if not whole)
    if loose:
        outs.append(shape((n_dp, chunk, loose), bf16))
    if term is not None:
        outs.append(shape(block, f32))
    if inner is not None:
        outs += inner_outs
    kernel = functools.partial(
        leave_kernel, [weight[1:] for weight in weights], term is not None, run, counts
    )
    return line_call(kernel, name, ident, outs, specs, scratch, 0, LINK_COST)(*args)


def forward_parts(attended, outs_z, half, base, norm_rows, after, n, n_dp, alone):
    rows, width = base.shape
    share = outs_z.shape[0]
    outs = [shape((rows, width), f32), shape((n, rows, width), bf16)]
    specs = [whole_vmem(), in_place(), whole_vmem(), whole_vmem()]
    args = [attended, outs_z, base, norm_rows]
    scratch = [
        pltpu.VMEM((n, rows, width), bf16),
        pltpu.VMEM((2, n, rows, width), bf16),
        pltpu.VMEM((rows // SUBS, width), f32),
        *sem_pair(n, SUBS),
        *sem_pair(n, SUBS),
        pltpu.VMEM((share, width), bf16),
        pltpu.SemaphoreType.DMA,
    ]
    if after is not None:
        outs.append(shape((n * rows, share), bf16))
        specs.append(in_place())
        args.append(after)
        scratch += [pltpu.VMEM((width, share), bf16), pltpu.SemaphoreType.DMA]
    kernel = functools.partial(
        forward_kernel, n, shuffle_order(n, n_dp), half, after is not None, alone
    )
    return kernel, args, specs, outs, scratch


def forward_call(attended, outs_z, half, base, norm_rows, after, n, n_dp, ident):
    kernel, args, specs, outs, scratch = forward_parts(
        attended, outs_z, half, base, norm_rows, after, n, n_dp, True
    )
    call = line_call(kernel, f"forward{half}", ident, outs, specs, scratch, 0, LINK_COST)
    return call(*args)


def back_parts(dy, weight, column, base, middle, norm_rows, outs_z, half, branch, n, n_dp, alone):
    rows, width = base.shape
    share = outs_z.shape[0]
    outs = [
        shape((rows, width), f32),
        shape((n, rows, width), bf16),
        shape((n * rows, share), bf16),
        shape((8, width), f32),
    ]
    specs = [
        whole_vmem(),
        in_place(),
        whole_vmem(),
        whole_vmem(),
        whole_vmem(),
        in_place(),
    ]
    scratch = [
        pltpu.VMEM((2, n, rows, width), bf16),
        pltpu.VMEM((rows // SUBS, width), f32),
        pltpu.VMEM((rows // SUBS, width), f32),
        *sem_pair(n, SUBS),
        *sem_pair(n, SUBS),
        pltpu.VMEM((share, width), bf16),
        pltpu.SemaphoreType.DMA,
    ]
    if column is not None:
        scratch += [
            pltpu.VMEM((n, rows, width), bf16),
            pltpu.VMEM((width, dy.shape[1]), bf16),
            pltpu.SemaphoreType.DMA,
        ]
    args = [dy, weight, base, middle, norm_rows, outs_z]
    if branch is not None:
        args.append(branch)
        specs.append(whole_vmem())
        outs.append(shape((rows, width), bf16))
        scratch += [pltpu.VMEM((2, n, rows, width), bf16), *sem_pair(n, SUBS)]
    kernel = functools.partial(back_kernel, n, unshuffle_order(n, n_dp), column, half, alone)
    return kernel, args, specs, outs, scratch


def back_call(dy, weight, column, base, middle, norm_rows, outs_z, half, branch, n, n_dp, ident):
    kernel, args, specs, outs, scratch = back_parts(
        dy, weight, column, base, middle, norm_rows, outs_z, half, branch, n, n_dp, True
    )
    call = line_call(kernel, f"back{half}", ident, outs, specs, scratch, 0, LINK_COST)
    return call(*args)


def last_parts(dy, weight, base, tokens, norm_rows, n, n_dp):
    rows, width = base.shape
    outs = [
        shape((rows, width), bf16),
        shape((8, width), f32),
    ]
    specs = [whole_vmem(), in_place()] + [whole_vmem()] * 3
    scratch = [
        pltpu.VMEM((n, rows, width), bf16),
        pltpu.VMEM((2, n, rows, width), bf16),
        pltpu.VMEM((rows // SUBS, width), f32),
        pltpu.VMEM((rows // SUBS, width), f32),
        *sem_pair(n, SUBS),
        pltpu.VMEM((width, dy.shape[1]), bf16),
        pltpu.SemaphoreType.DMA,
    ]
    kernel = functools.partial(last_kernel, n, unshuffle_order(n, n_dp))
    return kernel, [dy, weight, base, tokens, norm_rows], specs, outs, scratch


def attend_forward(query, keys, values, mask_ref, keyed, att_ref, share_ref):
    packed, rows, _ = mask_ref.shape
    heads = att_ref.shape[1] // HEAD
    for p in range(packed):
        here = slice(p * rows, (p + 1) * rows)
        there = here if keyed else slice(None)
        for h in range(heads):
            columns = slice(h * HEAD, (h + 1) * HEAD)
            scores = dot_nt(query[here, columns], keys[there, columns]) * HEAD ** (-0.5)
            scores = jnp.where(mask_ref[p] > 0, scores, score_floor)
            powers = jnp.exp(scores - jnp.max(scores, axis=-1, keepdims=True))
            shares = powers / jnp.sum(powers, axis=-1, keepdims=True)
            share_ref[p * heads + h] = shares
            att_ref[here, columns] = dot(shares.astype(bf16), values[there, columns]).astype(bf16)


def attend_backward(query, keys, values, share_ref, back_ref, rows, keyed, put_query, put_pair):
    heads = back_ref.shape[1] // HEAD
    packed = back_ref.shape[0] // rows
    score_scale = HEAD ** (-0.5)
    for h in range(heads):
        columns = slice(h * HEAD, (h + 1) * HEAD)
        key_grad = value_grad = None
        for p in range(packed):
            here = slice(p * rows, (p + 1) * rows)
            there = here if keyed else slice(None)
            shares = share_ref[p * heads + h]
            back = back_ref[here, columns]
            back_shares = dot_nt(back, values[there, columns])
            inner_sum = jnp.sum(shares * back_shares, axis=-1, keepdims=True)
            back_scores = (shares * (back_shares - inner_sum)).astype(bf16)
            put_query(here, columns, dot(back_scores, keys[there, columns]) * score_scale)
            key_term = dot_tn(back_scores, query[here, columns]) * score_scale
            value_term = dot_tn(shares.astype(bf16), back)
            if keyed:
                put_pair(there, columns, key_term, value_term)
            else:
                key_grad = key_term if key_grad is None else key_grad + key_term
                value_grad = value_term if value_grad is None else value_grad + value_term
        if not keyed:
            put_pair(slice(None), columns, key_grad, value_grad)


def self_forward_kernel(h_ref, w_ref, mask_ref, proj_ref, att_ref, share_ref):
    tile = pl.program_id(0)
    proj_ref[tile] = dot(h_ref[...], w_ref[...]).astype(bf16)

    @pl.when(tile == 2)
    def _():
        attend_forward(
            proj_ref.at[0], proj_ref.at[1], proj_ref.at[2], mask_ref, True, att_ref, share_ref
        )


def cross_forward_kernel(cq_ref, text_ref, w_ref, mask_ref, kv_ref, att_ref, share_ref, total):
    tile = pl.program_id(0)
    product = dot(text_ref[...], w_ref[...])

    @pl.when(tile < 2)
    def _():
        total[tile] = product

    @pl.when(tile >= 2)
    def _():
        kv_ref[tile - 2] = (total[tile - 2] + product).astype(bf16)

    @pl.when(tile == 3)
    def _():
        attend_forward(cq_ref, kv_ref.at[0], kv_ref.at[1], mask_ref, False, att_ref, share_ref)


def ffn_kernel(h_ref, up_ref, grad_ref, act_ref, slope_ref, gdown_ref):
    up_values = dot(h_ref[...], up_ref[...])
    chance = 0.5 * (1.0 + lax.erf(up_values * 0.5**0.5))
    density = jnp.exp(-0.5 * up_values * up_values) * 0.3989422804014327
    activated = (up_values * chance).astype(bf16)
    act_ref[...] = activated
    slope_ref[...] = chance + up_values * density
    store_pieces(dot_tn(activated, grad_ref[...]), gdown_ref)


def ffn_back_kernel(
    h_ref,
    down_ref,
    up_ref,
    grad_ref,
    act_ref,
    slope_ref,
    branch_ref,
    part_ref,
    gup_ref,
    total,
    part,
):
    tile = pl.program_id(0)
    back_act = dot_nt(grad_ref[...], down_ref[...])
    back_up = (back_act * slope_ref[...]).astype(bf16)
    gup_ref[...] = dot_tn(h_ref[...], back_up).astype(bf16).reshape(gup_ref.shape)

    @pl.when(tile == 0)
    def _():
        total[...] = dot(act_ref[...], down_ref[...])
        part[...] = dot_nt(back_up, up_ref[...])

    @pl.when(tile > 0)
    def _():
        total[...] += dot(act_ref[...], down_ref[...])
        part[...] += dot_nt(back_up, up_ref[...])

    @pl.when(tile == 3)
    def _():
        branch_ref[...] = total[...].astype(bf16)
        part_ref[...] = part[...].astype(bf16)


def cross_back_kernel(
    rows, back_ref, cq_ref, kv_ref, share_ref, text_ref, dcq_ref, grad_ref, pairs
):
    share = cq_ref.shape[1]

    @pl.when(pl.program_id(0) == 0)
    def _():
        def put_query(here, columns, value):
            dcq_ref[here, columns] = value.astype(bf16)

        def put_pair(there, columns, key_grad, value_grad):
            pairs[there, columns] = key_grad.astype(bf16)
            after_keys = slice(share + columns.start, share + columns.stop)
            pairs[there, after_keys] = value_grad.astype(bf16)

        attend_backward(
            cq_ref, kv_ref.at[0], kv_ref.at[1], share_ref, back_ref, rows, False, put_query, put_pair
        )

    grad_ref[...] = dot_tn(text_ref[...], pairs[...]).astype(bf16)


def outs_grad_kernel(att1_ref, carry1_ref, att2_ref, carry2_ref, grad_ref):
    tile = pl.program_id(0)

    @pl.when(tile == 0)
    def _():
        store_pieces(dot_tn(att1_ref[...], carry1_ref[...]), grad_ref)

    @pl.when(tile == 1)
    def _():
        store_pieces(dot_tn(att2_ref[...], carry2_ref[...]), grad_ref)


def store_pieces(gradient, target):
    n_dp, rows, columns = target.shape
    gradient = gradient.astype(bf16)
    chunk = gradient.shape[0] // n_dp
    for piece in range(rows // chunk):
        cut = gradient[:, piece * columns : (piece + 1) * columns]
        target[:, piece * chunk : (piece + 1) * chunk] = cut.reshape(n_dp, chunk, columns)


def self_back_kernel(
    rows,
    back_ref,
    proj_ref,
    share_ref,
    h1_ref,
    h2_ref,
    dcq_ref,
    both_ref,
    dproj_ref,
    grad_ref,
    parts,
):
    del both_ref
    tile = pl.program_id(0)
    share = dcq_ref.shape[1]

    @pl.when(tile == 0)
    def _():
        def put(part, here, columns, value):
            value = value.astype(bf16)
            parts[part, here, columns] = value
            dproj_ref[here, part * share + columns.start : part * share + columns.stop] = value

        def put_query(here, columns, value):
            put(0, here, columns, value)

        def put_pair(there, columns, key_grad, value_grad):
            put(1, there, columns, key_grad)
            put(2, there, columns, value_grad)

        attend_backward(
            proj_ref.at[0],
            proj_ref.at[1],
            proj_ref.at[2],
            share_ref,
            back_ref,
            rows,
            True,
            put_query,
            put_pair,
        )

    @pl.when(tile < 3)
    def _():
        grad_ref[...] = dot_tn(h1_ref[...], parts[tile]).astype(bf16).reshape(grad_ref.shape)

    @pl.when(tile == 3)
    def _():
        grad_ref[...] = dot_tn(h2_ref[...], dcq_ref[...]).astype(bf16).reshape(grad_ref.shape)


def fixed(dims):
    return pl.BlockSpec(dims, lambda t: (0,) * len(dims))


def moving(dims, index):
    return pl.BlockSpec(dims, lambda t: (0, index(t)))


def local_call(
    kernel, name, tiles, outs, specs, out_specs, scratch, flops, moved, aliases=None
):
    return pl.pallas_call(
        kernel,
        name=name,
        grid=(tiles,),
        input_output_aliases=aliases or {},
        out_shape=outs,
        in_specs=specs,
        out_specs=out_specs,
        scratch_shapes=scratch,
        compiler_params=pltpu.CompilerParams(vmem_limit_bytes=VMEM_CAP),
        cost_estimate=pl.CostEstimate(
            flops=flops // 8, bytes_accessed=moved // 8, transcendentals=0
        ),
    )


def self_forward(hidden, query_z, mask):
    tokens, width = hidden.shape
    share = query_z.shape[1] // 4
    packed, rows, _ = mask.shape
    pairs = (packed * share // HEAD, rows, rows)
    return local_call(
        self_forward_kernel,
        "self_forward",
        3,
        (shape((3, tokens, share), bf16), shape((tokens, share), bf16), shape(pairs, f32)),
        [fixed(hidden.shape), moving((width, share), lambda t: t), fixed(mask.shape)],
        (fixed((3, tokens, share)), fixed((tokens, share)), fixed(pairs)),
        [],
        6 * tokens * width * share,
        20_000_000,
    )(hidden, query_z, mask)


def cross_forward(cross_query, text_all, text_z, mask):
    tokens, share = cross_query.shape
    texts = text_all.shape[0]
    width = text_z.shape[0]
    packed, rows, _ = mask.shape
    pairs = (packed * share // HEAD, rows, texts)
    return local_call(
        cross_forward_kernel,
        "cross_forward",
        4,
        (shape((2, texts, share), bf16), shape((tokens, share), bf16), shape(pairs, f32)),
        [
            fixed(cross_query.shape),
            moving((texts, width), lambda t: t // 2),
            moving((width, share), lambda t: t),
            fixed(mask.shape),
        ],
        (fixed((2, texts, share)), fixed((tokens, share)), fixed(pairs)),
        [pltpu.VMEM((2, texts, share), f32)],
        8 * texts * width * share,
        20_000_000,
    )(cross_query, text_all, text_z, mask)


def ffn(hidden, up_z, grad_all, n, n_dp):
    tokens, width = hidden.shape
    share = up_z.shape[1] // 4
    chunk = share // n_dp
    return local_call(
        ffn_kernel,
        "ffn",
        4,
        (
            shape((tokens, 4 * share), bf16),
            shape((tokens, 4 * share), f32),
            shape((n_dp, n * chunk, 4 * share), bf16),
        ),
        [fixed(hidden.shape), moving((width, share), lambda t: t), fixed(grad_all.shape)],
        (
            moving((tokens, share), lambda t: t),
            moving((tokens, share), lambda t: t),
            pl.BlockSpec((n_dp, n * chunk // 4, 4 * share), lambda t: (0, t, 0)),
        ),
        [],
        16 * tokens * width * share,
        30_000_000,
    )(hidden, up_z, grad_all)


def ffn_back(hidden, down_z, up_z, grad_all, activated, slope, n_dp):
    tokens, width = hidden.shape
    share = down_z.shape[0]
    return local_call(
        ffn_back_kernel,
        "ffn_back",
        4,
        (
            shape((tokens, width), bf16),
            shape((tokens, width), bf16),
            shape((n_dp, width // n_dp, 4 * share), bf16),
        ),
        [
            fixed(hidden.shape),
            moving((share, width), lambda t: t),
            moving((width, share), lambda t: t),
            fixed(grad_all.shape),
            moving((tokens, share), lambda t: t),
            moving((tokens, share), lambda t: t),
        ],
        (
            fixed((tokens, width)),
            fixed((tokens, width)),
            pl.BlockSpec((n_dp, width // n_dp, share), lambda t: (0, 0, t)),
        ),
        [pltpu.VMEM((tokens, width), f32)] * 2,
        32 * tokens * width * share,
        50_000_000,
    )(hidden, down_z, up_z, grad_all, activated, slope)


def cross_back(back_attended, cross_query, text_pairs, shares, text_all, rows):
    tokens, share = cross_query.shape
    texts = text_all.shape[0]
    width = text_all.shape[1] // 2
    return local_call(
        functools.partial(cross_back_kernel, rows),
        "cross_back",
        2,
        (shape((tokens, share), bf16), shape((width, 4 * share), bf16)),
        [
            fixed(back_attended.shape),
            fixed(cross_query.shape),
            fixed(text_pairs.shape),
            fixed(shares.shape),
            moving((texts, width), lambda t: t),
        ],
        (fixed((tokens, share)), moving((width, 2 * share), lambda t: t)),
        [pltpu.VMEM((texts, 2 * share), bf16)],
        8 * texts * width * share,
        20_000_000,
    )(back_attended, cross_query, text_pairs, shares, text_all)


def outs_grad(attended1, carry1, attended2, carry2, n, n_dp):
    tokens, share = attended1.shape
    width = carry1.shape[1]
    chunk = share // n_dp
    return local_call(
        outs_grad_kernel,
        "outs_grad",
        2,
        shape((n_dp, n * chunk * 3 // 2, 4 * share), bf16),
        [fixed((tokens, share)), fixed((tokens, width))] * 2,
        pl.BlockSpec((n_dp, n * chunk // 4, 4 * share), lambda t: (0, 4 + t, 0)),
        [],
        4 * tokens * width * share,
        10_000_000,
    )(attended1, carry1, attended2, carry2)


def self_back(back_attended, projected, shares, hidden1, hidden2, back_cross, both, rows):
    tokens, width = hidden1.shape
    share = back_cross.shape[1]
    return local_call(
        functools.partial(self_back_kernel, rows),
        "self_back",
        4,
        (shape((tokens, 3 * share), bf16), shape(both.shape, bf16)),
        [
            fixed(back_attended.shape),
            fixed(projected.shape),
            fixed(shares.shape),
            fixed(hidden1.shape),
            fixed(hidden2.shape),
            fixed(back_cross.shape),
            in_place(),
        ],
        (
            fixed((tokens, 3 * share)),
            pl.BlockSpec((both.shape[0], both.shape[1] * 2 // 3, share), lambda t: (0, 0, t)),
        ),
        [pltpu.VMEM((3, tokens, share), bf16)],
        8 * tokens * width * share,
        25_000_000,
        {6: 1},
    )(back_attended, projected, shares, hidden1, hidden2, back_cross, both)


def block_slots(owners):
    owner = jnp.concatenate(owners)
    weight = jnp.concatenate([jnp.full(one.shape, at, jnp.int32) for at, one in enumerate(owners)])
    mark = owner + weight * 1024
    count = mark.shape[0]
    earlier = lax.broadcasted_iota(jnp.int32, (count, count), 1) < lax.broadcasted_iota(
        jnp.int32, (count, count), 0
    )
    same = jnp.logical_and(mark[:, None] == mark[None, :], earlier)
    return jnp.stack([owner, jnp.sum(same.astype(jnp.int32), axis=1)])


def slot_contents(owners, slots, places, capacities, firsts, n_dp):
    rows = []
    for owner, place, capacity, first in zip(owners, places, capacities, firsts):
        count = owner.shape[0]
        at = owner * capacity + slots[1, first : first + count]
        hit = at[None, :] == lax.broadcasted_iota(jnp.int32, (n_dp * capacity, count), 0)
        block = lax.broadcasted_iota(jnp.int32, (n_dp * capacity, count), 1)
        per_group, per_part, split = place_rule(place)
        part = block % per_group // per_part if split else block * 0
        column = block // per_group * per_part + block % per_part if split else block
        index = part * (count // (per_group // per_part)) + column if split else column
        rows.append(
            jnp.stack([jnp.sum(jnp.where(hit, value, 0), axis=1) for value in (index, block * 0 + 1)])
        )
    return jnp.concatenate(rows, axis=1)


def place_rule(place):
    parts = 1 + max(part for part, _ in place)
    if parts == 1:
        return 0, 0, False
    per_part = sum(1 for part, _ in place[:HEADS] if part == 0)
    return per_part * parts, per_part, True


def after(small, first):
    return lax.optimization_barrier((small, first))[0]


def body(
    tokens_in,
    text_in,
    seg_ids,
    capt_ids,
    grad_out,
    owner_query,
    owner_up,
    owner_outs,
    owner_text,
    owner_down,
    w_query,
    m_query,
    v_query,
    w_up,
    m_up,
    v_up,
    w_outs,
    m_outs,
    v_outs,
    w_text,
    m_text,
    v_text,
    w_down,
    m_down,
    v_down,
    norm_weight,
    m_norm,
    v_norm,
):
    n_dp = lax.axis_size("dp")
    n_z = lax.axis_size("fsdp")
    width = tokens_in.shape[1]
    own_rows = w_query.shape[0]
    chunk = own_rows // n_dp
    cap_big = w_query.shape[1] // BLK
    cap_out = w_outs.shape[1] // BLK
    heads_z = HEADS // n_z
    share = width // n_z
    owner_query, owner_up, owner_outs, owner_text, owner_down = (
        owner[:, 0] for owner in (owner_query, owner_up, owner_outs, owner_text, owner_down)
    )
    split_places = [split_place(b, heads_z, n_z) for b in range(owner_query.shape[0])]
    big_places = [flat_place(b) for b in range(owner_down.shape[0])]
    out_places = [flat_place(b) for b in range(owner_outs.shape[0])]
    owners = (owner_query, owner_outs, owner_text, owner_up, owner_down)
    places = (split_places, out_places, split_places, split_places, big_places)
    capacities = (cap_big, cap_out, cap_big, cap_big, cap_big)
    firsts = [sum(len(one) for one in places[:index]) for index in range(5)]
    slot_firsts = [sum(capacities[:index]) * n_dp for index in range(5)]
    slots = block_slots(owners)
    contents = slot_contents(owners, slots, places, capacities, firsts, n_dp)

    def spread(rows):
        return lax.all_gather(rows.reshape(-1, rows.shape[-1]), "dp", axis=0, tiled=True)

    def gather_sum(piece, parts):
        summed = lax.psum_scatter(piece, "dp", scatter_dimension=0, tiled=True)
        return summed.reshape(parts, chunk, -1)

    token_count = tokens_in.shape[0]
    marks = jnp.concatenate([seg_ids, capt_ids], axis=1)
    marks = jnp.pad(marks, ((0, 7), (0, 256 - marks.shape[1])))
    norms = jnp.pad(norm_weight, ((0, 2), (0, 0)))
    half = token_count // 2
    query_rows, grad_low, marks, norm_full = enter_call(
        "enter_query",
        0,
        slots,
        [(w_query, split_places, True, firsts[0])],
        [(grad_out[:half], False), (marks, False)],
        norms,
        True,
        False,
        n_z,
        n_dp,
        width,
    )
    outs_rows, hidden1, text_all = enter_call(
        "enter_outs",
        6,
        slots,
        [(w_outs, out_places, False, firsts[1])],
        [(tokens_in, True), (text_in, True)],
        norm_full[0:2],
        False,
        True,
        n_z,
        n_dp,
        width,
    )
    query_z, outs_z = spread(query_rows), spread(outs_rows)
    hidden1 = hidden1.reshape(-1, width)
    text_all = text_all.reshape(-1, text_in.shape[1])
    segment = marks[:, 0, :token_count]
    caption = marks[:, 0, token_count : token_count + capt_ids.shape[1]]
    self_mask = (segment[:, :, None] == segment[:, None, :]).astype(jnp.int32)
    text_row = lax.broadcasted_iota(jnp.int32, caption.shape, 0).reshape(1, 1, -1)
    packed_row = lax.broadcasted_iota(jnp.int32, (n_z, 1, 1), 0)
    cross_mask = jnp.logical_and(
        segment[:, :, None] == caption.reshape(1, 1, -1), packed_row == text_row
    ).astype(jnp.int32)

    projected, attended1, shares1 = self_forward(hidden1, query_z, self_mask)
    text_rows, grad_high = enter_call(
        "enter_text",
        7,
        after(slots, attended1),
        [(w_text, split_places, True, firsts[2])],
        [(grad_out[half:], False)],
        None,
        False,
        False,
        n_z,
        n_dp,
        width,
    )
    grad_all = jnp.concatenate([grad_low, grad_high], axis=1).reshape(-1, width)
    up_rows, down_rows, middle1, hidden2, cross_query = enter_call(
        "forward0",
        1,
        slots,
        [(w_up, split_places, True, firsts[3]), (w_down, big_places, False, firsts[4])],
        [],
        None,
        False,
        False,
        n_z,
        n_dp,
        width,
        forward_parts(
            attended1,
            outs_z,
            0,
            tokens_in,
            after(norm_full[2:4], text_rows),
            query_z,
            n_z,
            n_dp,
            False,
        ),
    )
    hidden2 = hidden2.reshape(-1, width)
    text_z, up_z, down_z = spread(text_rows), spread(up_rows), spread(down_rows)
    text_pairs, attended2, shares2 = cross_forward(cross_query, text_all, text_z, cross_mask)
    middle2, hidden3 = forward_call(
        attended2, outs_z, 1, middle1, norm_full[4:6], None, n_z, n_dp, 2
    )
    hidden3 = hidden3.reshape(-1, width)
    activated, slope, down_part = ffn(hidden3, up_z, grad_all, n_z, n_dp)
    down_sum = gather_sum(down_part.reshape(-1, 4 * share), n_z)
    branch3, part3, up_part = ffn_back(hidden3, down_z, up_z, grad_all, activated, slope, n_dp)
    branch3 = branch3.reshape(n_z, token_count, width)
    part3 = part3.reshape(n_z, token_count, width)
    up_sum = gather_sum(up_part.reshape(-1, 4 * share), n_z)
    at_middle2, carry2, back_att2, term3, result = back_call(
        part3, after(slots, part3), None, grad_out, middle2, norm_full[4:6], outs_z, 1, branch3, n_z, n_dp, 3
    )
    carry2 = carry2.reshape(-1, width)
    back_cross, text_part = cross_back(
        back_att2, cross_query, text_pairs, shares2, text_all, token_count
    )
    text_sum = gather_sum(text_part, n_z)
    down_grad, at_middle1, carry1, back_att1, term2 = leave_call(
        "back0",
        4,
        contents,
        [(down_sum, False, cap_big, slot_firsts[4], True)],
        None,
        n_z,
        n_dp,
        back_parts(
            back_cross,
            query_z,
            3,
            at_middle2,
            middle1,
            norm_full[2:4],
            outs_z,
            0,
            None,
            n_z,
            n_dp,
            False,
        ),
    )
    carry1 = carry1.reshape(-1, width)
    both = outs_grad(attended1, after(carry1, up_sum), attended2, carry2, n_z, n_dp)
    back_projected, both = self_back(
        back_att1, projected, shares1, hidden1, hidden2, back_cross, both, token_count
    )
    query_outs_sum = gather_sum(both.reshape(-1, 4 * share), 3 * n_z // 2)
    up_grad, text_grad, grad_in, term1 = leave_call(
        "leave_up",
        8,
        contents,
        [
            (up_sum, True, cap_big, slot_firsts[3], True),
            (text_sum, True, cap_big, slot_firsts[2], True),
        ],
        None,
        n_z,
        n_dp,
        last_parts(
            back_projected,
            query_z,
            at_middle1,
            tokens_in,
            norm_full[0:2],
            n_z,
            n_dp,
        ),
    )
    query_outs_sum = after(query_outs_sum, term1)
    query_sum, outs_sum = query_outs_sum[:n_z], query_outs_sum[n_z:]
    norm_term = jnp.concatenate([term1[:2], term2[:2], term3[:4]], axis=0)
    loose, norm_grad = leave_call(
        "leave_query",
        9,
        contents,
        [
            (outs_sum, False, cap_out, slot_firsts[1], False),
            (query_sum, True, cap_big, slot_firsts[0], False),
        ],
        norm_term,
        n_z,
        n_dp,
    )
    loose = lax.all_to_all(loose, "dp", 0, 0, tiled=True).reshape(own_rows, -1)
    outs_slots = loose[:, : cap_out * BLK].astype(f32)
    query_grad = loose[:, cap_out * BLK :].astype(f32)
    norm_grad = norm_grad[:6]
    text_grad, up_grad, down_grad = (
        grad.reshape(own_rows, -1).astype(f32) for grad in (text_grad, up_grad, down_grad)
    )
    up_new = adamw_update(w_up, m_up, v_up, up_grad, rate_up, decay_rate)
    text_new = adamw_update(w_text, m_text, v_text, text_grad, rate_text, decay_rate)
    down_new = adamw_update(w_down, m_down, v_down, down_grad, rate_down, decay_rate)
    query_new = adamw_update(w_query, m_query, v_query, query_grad, rate_query, decay_rate)
    outs_new = adamw_update(w_outs, m_outs, v_outs, outs_slots, rate_outs, decay_rate)
    norm_new = adamw_update(norm_weight, m_norm, v_norm, norm_grad, rate_norm, 0.0)
    return (
        result,
        grad_in,
        *query_new,
        *up_new,
        *outs_new,
        *text_new,
        *down_new,
        *norm_new,
    )


def solution(mesh):
    rows = P(("dp", "fsdp"), None)
    slots = P("fsdp", "dp")
    norms = P(None, "dp")
    in_specs = (rows,) * 5 + (P(),) * 5 + (slots,) * 15 + (norms,) * 3
    out_specs = (rows,) * 2 + (slots,) * 15 + (norms,) * 3
    return jax.shard_map(body, mesh=mesh, in_specs=in_specs, out_specs=out_specs, check_vma=False)
```

```python
import functools

import jax
import jax.numpy as jnp
from jax import lax
from jax.experimental import pallas as pl
from jax.experimental.pallas import tpu as pltpu
from jax.sharding import PartitionSpec as P

HEADS = 16
HEAD = 128
STEP = 10
BLK = 128


beta_first = 0.9
beta_second = 0.999
adam_eps = 1e-08
decay_rate = 0.01
rate_query = 0.04
rate_up = 0.04
rate_outs = 0.12
rate_text = 0.03
rate_down = 0.03
rate_norm = 0.5
norm_eps = 1e-05
score_floor = -1e30
bf16 = jnp.bfloat16
f32 = jnp.float32


def normalize(values):
    centered = values - jnp.mean(values, axis=-1, keepdims=True)
    inverse_std = lax.rsqrt(jnp.mean(centered * centered, axis=-1, keepdims=True) + norm_eps)
    return (centered * inverse_std, inverse_std)


def norm_back(back_hidden, normed, inverse_std, gain_row):
    back_normed = back_hidden * gain_row
    return inverse_std * (
        back_normed
        - jnp.mean(back_normed, axis=-1, keepdims=True)
        - normed * jnp.mean(back_normed * normed, axis=-1, keepdims=True)
    )


def adamw_update(weight, first, second, gradient, rate, decay):
    first_new = beta_first * first + (1.0 - beta_first) * gradient
    second_new = beta_second * second + (1.0 - beta_second) * gradient * gradient
    first_hat = first_new / (1.0 - beta_first**STEP)
    second_hat = second_new / (1.0 - beta_second**STEP)
    weight_new = weight - rate * (first_hat / (jnp.sqrt(second_hat) + adam_eps) + decay * weight)
    return (first_new, second_new, weight_new)


def dot(left, right):
    return jnp.dot(left, right, preferred_element_type=f32)


def dot_nt(left, right):
    return lax.dot_general(left, right, (((1,), (1,)), ((), ())), preferred_element_type=f32)


def dot_tn(left, right):
    return lax.dot_general(left, right, (((0,), (0,)), ((), ())), preferred_element_type=f32)


def split_place(block, per_part, parts):
    group, rest = divmod(block, per_part * parts)
    part, inner = divmod(rest, per_part)
    return part, group * per_part + inner


def flat_place(block):
    return 0, block


MESH = pl.DeviceIdType.MESH


SUBS = 4


class Line:
    def __init__(self, n, rows, step):
        self.n, self.rows, self.step = n, rows, step
        self.at = lax.axis_index("fsdp")

    def has(self, way):
        return self.at < self.n - 1 if way == 0 else self.at > 0

    def peer(self, way):
        index = jnp.clip(self.at + (1 if way == 0 else -1), 0, self.n - 1)
        return {"fsdp": index}

    def greet(self, others=0):
        barrier = pltpu.get_barrier_semaphore()
        for way in (0, 1):

            @pl.when(self.has(way))
            def _():
                pl.semaphore_signal(
                    barrier, inc=1, device_id=self.peer(way), device_id_type=pl.DeviceIdType.MESH
                )

        pl.semaphore_wait(
            barrier, others + self.has(0).astype(jnp.int32) + self.has(1).astype(jnp.int32)
        )

    def copy(self, source, target, send, recv, way):
        return pltpu.make_async_remote_copy(
            src_ref=source,
            dst_ref=target,
            send_sem=send,
            recv_sem=recv,
            device_id=self.peer(way),
            device_id_type=pl.DeviceIdType.MESH,
        )

    def part(self, sub):
        return pl.ds(sub * self.step, self.step)


class Sums:
    def __init__(self, line, part, held, send, recv):
        self.line, self.part, self.held, self.send, self.recv = line, part, held, send, recv

    def move(self, way, target, sub, source):
        line = self.line
        rows = line.part(sub)
        return line.copy(
            source,
            self.held.at[way, target, rows],
            self.send.at[way, target, sub],
            self.recv.at[way, target, sub],
            way,
        )

    def target(self, way, time):
        n, at = self.line.n, self.line.at
        return n - 1 - (time - at) if way == 0 else time - (n - 1 - at)

    def passes(self, way, target):
        n, at = self.line.n, self.line.at
        if way == 0:
            return jnp.logical_and(target > at, target < n)
        return jnp.logical_and(target < at, target >= 0)

    def forward(self, sub, time):
        line = self.line
        rows = line.part(sub)
        for way in (0, 1):
            target = self.target(way, time)
            passes = self.passes(way, target)
            inner = jnp.logical_and(passes, line.has(1 - way))
            outer = jnp.logical_and(passes, jnp.logical_not(line.has(1 - way)))

            @pl.when(outer)
            def _():
                self.move(way, target, sub, self.part.at[target, rows]).start()

            @pl.when(inner)
            def _():
                held = self.held.at[way, target, rows]
                self.move(way, target, sub, held).wait_recv()
                total = held[...].astype(f32) + self.part[target, rows].astype(f32)
                held[...] = total.astype(bf16)
                self.move(way, target, sub, held).start()

    def total(self, sub, sum_ref):
        line = self.line
        rows = line.part(sub)
        sum_ref[...] = self.part[line.at, rows].astype(f32)
        for way in (0, 1):

            @pl.when(line.has(1 - way))
            def _():
                held = self.held.at[way, line.at, rows]
                self.move(way, line.at, sub, held).wait_recv()
                sum_ref[...] += held[...].astype(f32)

    def finish(self):
        line = self.line
        for way in (0, 1):
            for time in range(line.n - 1):
                target = self.target(way, time)

                @pl.when(self.passes(way, target))
                def _():
                    for sub in range(line.rows // line.step):
                        held = self.held.at[way, target, line.part(sub)]
                        self.move(way, target, sub, held).wait_send()


def relay(n, sums, blocks, settle, hook=None):
    for slot in range((SUBS + 2) * (n - 1)):
        sub, time = divmod(slot, n - 1)
        if hook is not None and slot == SUBS * (n - 1):
            hook()
        if sub < SUBS:
            for one in sums:
                one.forward(sub, time)
        if time == 0 and 0 <= sub - 1 < SUBS:
            settle(sub - 1)
        if blocks is not None:
            if time == n - 2 and 0 <= sub - 1 < SUBS:
                blocks.forward(sub - 1, 1)
            if time < n - 2 and 0 <= sub - 2 < SUBS:
                blocks.forward(sub - 2, time + 2)
    for one in sums:
        one.finish()
    if blocks is not None:
        blocks.finish()


class Blocks:
    def __init__(self, line, full, send, recv):
        self.line, self.full, self.send, self.recv = line, full, send, recv

    def move(self, way, source, sub):
        line = self.line
        held = self.full.at[source, line.part(sub)]
        return line.copy(
            held, held, self.send.at[way, source, sub], self.recv.at[way, source, sub], way
        )

    def behind(self, way, source):
        return self.line.at > source if way == 0 else self.line.at < source

    def start(self, sub):
        for way in (0, 1):

            @pl.when(self.line.has(way))
            def _():
                self.move(way, self.line.at, sub).start()

    def forward(self, sub, step):
        line = self.line
        for way in (0, 1):
            source = line.at - step if way == 0 else line.at + step

            @pl.when(jnp.logical_and(source >= 0, source < line.n))
            def _():
                self.move(way, source, sub).wait_recv()

                @pl.when(line.has(way))
                def _():
                    self.move(way, source, sub).start()

    def finish(self):
        line = self.line
        for way in (0, 1):
            for source in range(line.n):
                ours = jnp.logical_or(self.behind(way, source), line.at == source)

                @pl.when(jnp.logical_and(ours, line.has(way)))
                def _():
                    for sub in range(line.rows // line.step):
                        self.move(way, source, sub).wait_send()


def lane_moves(width, order):
    moves = []
    piece = width // len(order)
    for group in range(width // BLK):
        parts = []
        for offset in range(0, BLK, piece):
            start = order[(group * BLK + offset) // piece] * piece
            parts.append((offset, start // BLK, start % BLK))
        moves.append(parts)
    return piece, moves


def reorder(load, store, rows, width, order):
    piece, moves = lane_moves(width, order)
    lane = lax.broadcasted_iota(jnp.int32, (rows, BLK), 1)
    for group, parts in enumerate(moves):
        value = None
        for offset, source, start in parts:
            block = load(source)
            if start != offset:
                block = pltpu.roll(block, (offset - start) % BLK, 1)
            value = block if value is None else jnp.where(lane >= offset, block, value)
        store(group, value)


def shuffle_order(n_z, n_dp):
    return [z * n_dp + i for i in range(n_dp) for z in range(n_z)]


def unshuffle_order(n_z, n_dp):
    return [i * n_z + z for z in range(n_z) for i in range(n_dp)]


def by_tiles(columns, tile, run):
    def one(index, carry):
        run(pl.ds(pl.multiple_of(index * tile, tile), tile))
        return carry

    lax.fori_loop(0, columns // tile, one, 0)


class Swap:
    def __init__(self, axis, source, target, send, recv):
        self.axis, self.source, self.target = axis, source, target
        self.send, self.recv = send, recv
        self.n = lax.axis_size(axis)
        self.me = lax.axis_index(axis)

    def copy(self, jump, arrival=False):
        peer = lax.rem(self.me + jump, self.n)
        slot = peer if arrival else self.me
        return pltpu.make_async_remote_copy(
            src_ref=self.source.at[peer],
            dst_ref=self.target.at[slot],
            send_sem=self.send.at[jump],
            recv_sem=self.recv.at[slot],
            device_id={self.axis: peer},
            device_id_type=MESH,
        )

    def start(self):
        for jump in range(1, self.n):
            self.copy(jump).start()

    def keep(self):
        self.target[self.me] = self.source[self.me]

    def wait(self):
        for jump in range(1, self.n):
            self.copy(jump, True).wait_recv()

    def finish(self):
        for jump in range(1, self.n):
            self.copy(jump).wait_send()


def greet_all():
    barrier = pltpu.get_barrier_semaphore()
    count = 0
    for axis in ("dp", "fsdp"):
        n, me = lax.axis_size(axis), lax.axis_index(axis)
        count += n - 1
        for jump in range(1, n):
            pl.semaphore_signal(
                barrier, inc=1, device_id={axis: lax.rem(me + jump, n)}, device_id_type=MESH
            )
    pl.semaphore_wait(barrier, count)


class Refs:
    def __init__(self, refs):
        self.refs = list(refs)

    def take(self, count=None):
        taken = self.refs[: 1 if count is None else count]
        self.refs = self.refs[len(taken) :]
        return taken[0] if count is None else taken


def enter_kernel(weights, gathers, order, normed, hidden, inner, inner_counts, *refs):
    refs = Refs(refs)
    n_dp, n_z = lax.axis_size("dp"), lax.axis_size("fsdp")
    slots_ref = refs.take()
    w_refs = refs.take(len(weights))
    in_refs = refs.take(len(gathers))
    norm_in = refs.take() if normed or hidden else None
    inner_refs = refs.take(inner_counts[0])
    row_refs = refs.take(len(weights))
    full_refs = refs.take(len(gathers))
    norm_out = refs.take() if normed else None
    inner_refs += refs.take(inner_counts[1])
    inner_refs += refs.take(inner_counts[2])
    loads = []
    for w_ref in w_refs:
        stage, sem = refs.take(2)
        load = pltpu.make_async_copy(w_ref, stage, sem)
        load.start()
        loads.append((stage, load))
    greet_all()
    if normed:
        parts, *sems = refs.take(3)
        norm_swap = Spread("dp", norm_in, parts, *sems)
        norm_swap.start()
    lines = []
    for in_ref, full_ref in zip(in_refs, full_refs):
        rows = in_ref.shape[0]
        step = rows // pieces_of(rows)
        lines.append(Blocks(Line(n_z, rows, step), full_ref, *refs.take(2)))
    swaps = []
    for (stage, load), (places, split, _) in zip(loads, weights):
        source, target, *sems = refs.take(4)
        swap = Swap("dp", source, target, *sems)
        load.wait()
        chunk = source.shape[2]
        for jump in range(n_dp):
            peer = lax.rem(swap.me + jump, n_dp)
            into = source if jump else target
            for slot in range(source.shape[1]):
                here = pl.ds(pl.multiple_of(peer * chunk, chunk), chunk)
                piece = stage[here, slot * BLK : (slot + 1) * BLK]
                into[peer, slot] = piece.astype(bf16)
            if jump:
                swap.copy(jump).start()
        swaps.append(swap)
    if hidden:
        work = refs.take()
    for index, (in_ref, full_ref, blocks) in enumerate(zip(in_refs, full_refs, lines)):
        line = blocks.line
        if hidden and index == 0:
            for sub in range(line.rows // line.step):
                here = line.part(sub)
                values, _ = normalize(in_ref[here].astype(f32))
                work[...] = values * norm_in[0:1] + norm_in[1:2]
                store_shuffled(work, full_ref, line, here, order)
                blocks.start(sub)
        elif in_ref.dtype == bf16 and gathers[index]:
            work2 = refs.take()
            work2[...] = in_ref[...].astype(f32)
            store_shuffled(work2, full_ref, line, line.part(0), order)
            blocks.start(0)
        else:
            for sub in range(line.rows // line.step):
                here = line.part(sub)
                full_ref[line.at, here] = in_ref[here]
                blocks.start(sub)
    if normed:
        parts[norm_swap.me] = norm_in[...]
        norm_swap.wait()
        share = norm_in.shape[1]
        for index in range(n_dp):
            norm_out[:, index * share : (index + 1) * share] = parts[index]
    shares = []

    def compact(index):
        swap, row_ref, (places, split, first) = swaps[index], row_refs[index], weights[index]
        swap.wait()
        if split:
            cut, *sems = refs.take(3)
            share = Swap("fsdp", cut, row_ref, *sems)
            shares.append(share)
        else:
            cut = row_ref
        for block, (part, column) in enumerate(places):
            owner, slot = slots_ref[0, first + block], slots_ref[1, first + block]
            cut[part, :, column * BLK : (column + 1) * BLK] = swap.target[owner, slot]
        if split:
            share.start()
            share.keep()

    ahead = 0
    if inner is not None:
        ahead = 1
        inner(*inner_refs, hook=lambda: compact(0))
    for step in range(1, n_z):
        for blocks in lines:
            for sub in range(blocks.line.rows // blocks.line.step):
                blocks.forward(sub, step)
    for index in range(ahead, len(weights)):
        compact(index)
    for share in shares:
        share.wait()
    for one in [*swaps, *shares, *lines]:
        one.finish()
    if normed:
        norm_swap.finish()


class Spread(Swap):
    def copy(self, jump, arrival=False):
        peer = lax.rem(self.me + jump, self.n)
        slot = peer if arrival else self.me
        return pltpu.make_async_remote_copy(
            src_ref=self.source,
            dst_ref=self.target.at[slot],
            send_sem=self.send.at[jump],
            recv_sem=self.recv.at[slot],
            device_id={self.axis: peer},
            device_id_type=MESH,
        )


def store_shuffled(work, full_ref, line, here, order):
    rows, width = work.shape
    folds = width // order.width
    pieces = len(order.pieces)
    orders = [fold * pieces + piece for fold in range(folds) for piece in order.pieces]

    def load(group):
        return work[:, group * BLK : (group + 1) * BLK]

    def store(group, value):
        full_ref[line.at, here, group * BLK : (group + 1) * BLK] = value.astype(bf16)

    reorder(load, store, rows, width, orders)


def expand_slots(slots_ref, rows, cut, blocks, capacity, first, offset):
    columns = rows.shape[2] // BLK
    for part in range(rows.shape[0]):
        for column in range(columns):
            blocks[part * columns + column] = rows[part, :, column * BLK : (column + 1) * BLK]
    for owner in range(cut.shape[0]):
        for position in range(capacity):
            slot = first + owner * capacity + position
            value = blocks[slots_ref[0, slot]].astype(f32)
            live = slots_ref[1, slot].astype(f32)
            start = offset + position * BLK
            cut[owner, :, start : start + BLK] = (value * live).astype(bf16)


def leave_kernel(weights, summed, inner, inner_counts, *refs):
    refs = Refs(refs)
    n_dp = lax.axis_size("dp")
    slots_ref = refs.take()
    row_refs = refs.take(len(weights))
    term_ref = refs.take() if summed else None
    inner_refs = refs.take(inner_counts[0])
    gone = sum(1 for weight in weights if weight[3])
    out_refs = refs.take(gone)
    loose_ref = refs.take() if gone < len(weights) else None
    sum_ref = refs.take() if summed else None
    inner_refs += refs.take(inner_counts[1])
    inner_refs += refs.take(inner_counts[2])
    greet_all()
    if summed:
        cut, parts, send, recv, total, others, send2, recv2 = refs.take(8)
        share = cut.shape[2]
        for index in range(n_dp):
            cut[index] = term_ref[:, index * share : (index + 1) * share]
        term_swap = Swap("dp", cut, parts, send, recv)
        term_swap.start()
        term_swap.keep()
    shares = []
    for row_ref, (split, _, _, _) in zip(row_refs, weights):
        if split:
            held, *sems = refs.take(3)
            share = Swap("fsdp", row_ref, held, *sems)
            share.start()
            share.keep()
            shares.append(share)
        else:
            shares.append(None)
    if summed:
        term_swap.wait()
        total[...] = jnp.sum(parts[...], axis=0)
        total_spread = Spread("fsdp", total, others, send2, recv2)
        total_spread.start()
        others[total_spread.me] = total[...]
    swaps = []
    offset = 0
    for row_ref, share, (split, capacity, first, whole) in zip(row_refs, shares, weights):
        if split:
            share.wait()
        rows = share.target if split else row_ref
        if not whole:
            expand_slots(slots_ref, rows, loose_ref, refs.take(), capacity, first, offset)
            offset += capacity * BLK
            continue
        out_ref = out_refs.pop(0)
        cut, *sems, blocks = refs.take(4)
        expand_slots(slots_ref, rows, cut, blocks, capacity, first, 0)
        swap = Swap("dp", cut, out_ref, *sems)
        swap.start()
        swap.keep()
        swaps.append(swap)
    if inner is not None:
        inner(*inner_refs)
    if summed:
        total_spread.wait()
        sum_ref[...] = jnp.sum(others[...], axis=0)
    for swap in swaps:
        swap.wait()
    for one in [*swaps, *shares]:
        if one is not None:
            one.finish()
    if summed:
        term_swap.finish()
        total_spread.finish()


def fetch_columns(source, index, target, sem):
    columns = target.shape[1]
    return pltpu.make_async_copy(source.at[:, pl.ds(index * columns, columns)], target, sem)


def forward_kernel(
    n, order, half, wide, alone, att_ref, outs_hbm, base_ref, norm_ref, *rest, hook=None
):
    if wide:
        next_hbm, middle_ref, full_ref, result_ref = rest[:4]
        *rest, next_ref, next_sem = rest[4:]
    else:
        middle_ref, full_ref = rest[:2]
        rest = rest[2:]
    part, held, work, s_send, s_recv, b_send, b_recv, outs_ref, outs_sem = rest
    rows, width = base_ref.shape
    step = rows // SUBS
    load_outs = fetch_columns(outs_hbm, half, outs_ref, outs_sem)
    load_outs.start()
    if wide:
        load_next = fetch_columns(next_hbm, 3, next_ref, next_sem)
        load_next.start()
    line = Line(n, rows, step)
    if alone:
        line.greet()
    load_outs.wait()
    sums = Sums(line, part, held, s_send, s_recv)
    blocks = Blocks(line, full_ref, b_send, b_recv)

    def multiply(columns):
        product = dot(att_ref[...], outs_ref[:, columns]).astype(bf16)
        part[:, :, columns] = product.reshape(n, rows, -1)

    by_tiles(width, 256, multiply)

    def settle(sub):
        here = line.part(sub)
        sums.total(sub, work)
        middle = base_ref[here].astype(f32) + work[...]
        middle_ref[here] = middle
        normed, _ = normalize(middle)
        work[...] = normed * norm_ref[0:1] + norm_ref[1:2]

        def load(group):
            return work[:, group * BLK : (group + 1) * BLK]

        def store(group, value):
            full_ref[line.at, here, group * BLK : (group + 1) * BLK] = value.astype(bf16)

        reorder(load, store, step, width, order)
        blocks.start(sub)

    relay(n, [sums], blocks, settle, hook)
    if wide:
        load_next.wait()

        def multiply_next(columns):
            whole = full_ref[...].reshape(n * rows, width)
            result_ref[:, columns] = dot(whole, next_ref[:, columns]).astype(bf16)

        by_tiles(result_ref.shape[1], 256, multiply_next)


def carry_back(work, plain, order, step, width, middle, base, gain, term_ref, first):
    def load(group):
        return work[:, group * BLK : (group + 1) * BLK]

    def store(group, value):
        plain[:, group * BLK : (group + 1) * BLK] = value

    reorder(load, store, step, width, order)
    back_hidden = plain[...]
    normed, inverse = normalize(middle)
    gain_term = jnp.sum(back_hidden * normed, axis=0, keepdims=True)
    bias_term = jnp.sum(back_hidden, axis=0, keepdims=True)
    if first:
        term_ref[...] = jnp.zeros_like(term_ref)
        term_ref[0:1] = gain_term
        term_ref[1:2] = bias_term
    else:
        term_ref[0:1] += gain_term
        term_ref[1:2] += bias_term
    return base + norm_back(back_hidden, normed, inverse, gain)


def back_kernel(
    n, order, column, half, alone, dy_ref, w_hbm, base_ref, middle_ref, norm_ref, outs_hbm, *rest
):
    carry_ref, full_ref, att_ref, term_ref = rest[:4]
    held, work, plain, s_send, s_recv, b_send, b_recv, outs_ref, outs_sem = rest[4:13]
    rows, width = base_ref.shape
    step = rows // SUBS
    if column is not None:
        part, w_ref, w_sem = rest[13:]
        load_w = fetch_columns(w_hbm, column, w_ref, w_sem)
        load_w.start()
    else:
        part = dy_ref
    load_outs = fetch_columns(outs_hbm, half, outs_ref, outs_sem)
    load_outs.start()
    line = Line(n, rows, step)
    if alone:
        line.greet()
    sums = Sums(line, part, held, s_send, s_recv)
    blocks = Blocks(line, full_ref, b_send, b_recv)
    if column is not None:
        load_w.wait()

        def multiply(columns):
            product = dot_nt(dy_ref[...], w_ref[columns]).astype(bf16)
            part[:, :, columns] = product.reshape(n, rows, -1)

        by_tiles(width, 256, multiply)

    def settle(sub):
        here = line.part(sub)
        sums.total(sub, work)
        carry = carry_back(
            work,
            plain,
            order,
            step,
            width,
            middle_ref[here].astype(f32),
            base_ref[here].astype(f32),
            norm_ref[0:1],
            term_ref,
            sub == 0,
        )
        carry_ref[here] = carry
        full_ref[line.at, here] = carry.astype(bf16)
        blocks.start(sub)

    relay(n, [sums], blocks, settle)
    load_outs.wait()

    def multiply_next(columns):
        whole = full_ref[...].reshape(n * rows, width)
        att_ref[:, columns] = dot_nt(whole, outs_ref[columns]).astype(bf16)

    by_tiles(att_ref.shape[1], 256, multiply_next)


def last_kernel(n, order, dy_ref, w_hbm, base_ref, tokens, norm_ref, branch, middle, *rest):
    grad_ref, result_ref, term_ref = rest[:3]
    part, held, held2, work, plain, s_send, s_recv, r_send, r_recv, w_ref, w_sem = rest[3:]
    rows, width = base_ref.shape
    step = rows // SUBS
    load_w = fetch_columns(w_hbm, 0, w_ref, w_sem)
    load_w.start()
    line = Line(n, rows, step)
    load_w.wait()
    sums = Sums(line, part, held, s_send, s_recv)
    results = Sums(line, branch, held2, r_send, r_recv)

    def multiply(columns):
        product = dot_nt(dy_ref[...], w_ref[columns]).astype(bf16)
        part[:, :, columns] = product.reshape(n, rows, -1)

    by_tiles(width, 256, multiply)

    def settle(sub):
        here = line.part(sub)
        sums.total(sub, work)
        carry = carry_back(
            work,
            plain,
            order,
            step,
            width,
            tokens[here].astype(f32),
            base_ref[here],
            norm_ref[0:1],
            term_ref,
            sub == 0,
        )
        grad_ref[here] = carry.astype(bf16)
        results.total(sub, work)
        result_ref[here] = (middle[here] + work[...]).astype(bf16)

    relay(n, [sums, results], None, settle)


VMEM_CAP = 52 * 1024 * 1024


def in_place():
    return pl.BlockSpec(memory_space=pl.ANY)


def whole_vmem():
    return pl.BlockSpec(memory_space=pltpu.VMEM)


def sem_pair(n, subs):
    return [pltpu.SemaphoreType.DMA((2, n, subs)), pltpu.SemaphoreType.DMA((2, n, subs))]


def line_call(kernel, name, ident, outs, specs, scratch, flops, moved):
    return pl.pallas_call(
        kernel,
        name=name,
        out_shape=outs,
        in_specs=specs,
        out_specs=jax.tree.map(lambda _: whole_vmem(), outs),
        scratch_shapes=scratch,
        compiler_params=pltpu.CompilerParams(
            collective_id=ident, has_side_effects=True, vmem_limit_bytes=VMEM_CAP
        ),
        cost_estimate=pl.CostEstimate(flops=flops, bytes_accessed=moved, transcendentals=0),
    )


def shape(dims, kind):
    return jax.ShapeDtypeStruct(dims, kind)


LINK_COST = 4_000_000


def pieces_of(rows):
    return max(1, rows * SUBS // 128)


class Order:
    def __init__(self, pieces, width):
        self.pieces, self.width = pieces, width


def swap_sems(n):
    return [pltpu.SemaphoreType.DMA((n,)), pltpu.SemaphoreType.DMA((n,))]


def enter_call(
    name, ident, slots, weights, gathers, norms, normed, hidden, n, n_dp, width, inner=None
):
    chunk = weights[0][0].shape[0] // n_dp
    run, inner_args, inner_specs, inner_outs, scratch = inner or (None, [], [], [], [])
    counts = (len(inner_args), len(inner_outs), len(scratch))
    outs, scratch = [], list(scratch)
    for array, places, split, _ in weights:
        parts = n if split else 1
        outs.append(shape((parts, chunk, len(places) // parts * BLK), bf16))
        scratch += [pltpu.VMEM(array.shape, f32), pltpu.SemaphoreType.DMA]
    if normed:
        scratch += [pltpu.VMEM((n_dp, *norms.shape), f32), *swap_sems(n_dp)]
    for array, _ in gathers:
        rows = array.shape[0]
        outs.append(shape((n, *array.shape), array.dtype))
        scratch += sem_pair(n, pieces_of(rows))
    if normed:
        outs.append(shape((norms.shape[0], n_dp * norms.shape[1]), f32))
    for array, _, _, _ in weights:
        slots_shape = (n_dp, array.shape[1] // BLK, chunk, BLK)
        scratch += [pltpu.VMEM(slots_shape, bf16)] * 2 + swap_sems(n_dp)
    if hidden:
        scratch.append(pltpu.VMEM((gathers[0][0].shape[0] // SUBS, width), f32))
    for array, moved in gathers[1 if hidden else 0 :]:
        if moved:
            scratch.append(pltpu.VMEM(array.shape, f32))
    for index, (_, places, split, _) in enumerate(weights):
        if split:
            scratch += [pltpu.VMEM(outs[index].shape, bf16), *swap_sems(n)]
    args = [slots, *(weight[0] for weight in weights), *(gather[0] for gather in gathers)]
    specs = [pl.BlockSpec(memory_space=pltpu.SMEM)] + [in_place()] * len(weights)
    specs += [whole_vmem()] * len(gathers)
    if normed or hidden:
        args.append(norms)
        specs.append(whole_vmem())
    args += inner_args
    specs += inner_specs
    outs += inner_outs
    kernel = functools.partial(
        enter_kernel,
        [weight[1:] for weight in weights],
        [gather[1] for gather in gathers],
        Order(shuffle_order(n, n_dp), width),
        normed,
        hidden,
        run,
        counts,
    )
    return line_call(kernel, name, ident, outs, specs, scratch, 0, LINK_COST)(*args)


def leave_call(name, ident, slots, weights, term, n, n_dp, inner=None):
    outs, scratch = [], []
    specs = [pl.BlockSpec(memory_space=pltpu.SMEM)] + [whole_vmem()] * len(weights)
    args = [slots, *(weight[0] for weight in weights)]
    chunk = weights[0][0].shape[1]
    if term is not None:
        args.append(term)
        specs.append(whole_vmem())
        block = (term.shape[0], term.shape[1] // n_dp)
    counts = (0, 0, 0)
    run = None
    if inner is not None:
        run, inner_args, inner_specs, inner_outs, inner_scratch = inner
        counts = (len(inner_args), len(inner_outs), len(inner_scratch))
        args += inner_args
        specs += inner_specs
        scratch += inner_scratch
    if term is not None:
        scratch += [pltpu.VMEM((n_dp, *block), f32)] * 2 + swap_sems(n_dp)
        scratch += [pltpu.VMEM(block, f32), pltpu.VMEM((n, *block), f32), *swap_sems(n)]
    for rows, split, _, _, _ in weights:
        if split:
            scratch += [pltpu.VMEM(rows.shape, bf16), *swap_sems(n)]
    for rows, _, capacity, _, whole in weights:
        slots_shape = (n_dp, chunk, capacity * BLK)
        if whole:
            outs.append(shape(slots_shape, bf16))
            scratch += [pltpu.VMEM(slots_shape, bf16), *swap_sems(n_dp)]
        blocks = rows.shape[0] * rows.shape[2] // BLK
        scratch.append(pltpu.VMEM((blocks, chunk, BLK), bf16))
    loose = sum(capacity * BLK for _, _, capacity, _, whole in weights if not whole)
    if loose:
        outs.append(shape((n_dp, chunk, loose), bf16))
    if term is not None:
        outs.append(shape(block, f32))
    if inner is not None:
        outs += inner_outs
    kernel = functools.partial(
        leave_kernel, [weight[1:] for weight in weights], term is not None, run, counts
    )
    return line_call(kernel, name, ident, outs, specs, scratch, 0, LINK_COST)(*args)


def forward_parts(attended, outs_z, half, base, norm_rows, after, n, n_dp, alone):
    rows, width = base.shape
    share = outs_z.shape[0]
    outs = [shape((rows, width), f32), shape((n, rows, width), bf16)]
    specs = [whole_vmem(), in_place(), whole_vmem(), whole_vmem()]
    args = [attended, outs_z, base, norm_rows]
    scratch = [
        pltpu.VMEM((n, rows, width), bf16),
        pltpu.VMEM((2, n, rows, width), bf16),
        pltpu.VMEM((rows // SUBS, width), f32),
        *sem_pair(n, SUBS),
        *sem_pair(n, SUBS),
        pltpu.VMEM((share, width), bf16),
        pltpu.SemaphoreType.DMA,
    ]
    if after is not None:
        outs.append(shape((n * rows, share), bf16))
        specs.append(in_place())
        args.append(after)
        scratch += [pltpu.VMEM((width, share), bf16), pltpu.SemaphoreType.DMA]
    kernel = functools.partial(
        forward_kernel, n, shuffle_order(n, n_dp), half, after is not None, alone
    )
    return kernel, args, specs, outs, scratch


def forward_call(attended, outs_z, half, base, norm_rows, after, n, n_dp, ident):
    kernel, args, specs, outs, scratch = forward_parts(
        attended, outs_z, half, base, norm_rows, after, n, n_dp, True
    )
    call = line_call(kernel, f"forward{half}", ident, outs, specs, scratch, 0, LINK_COST)
    return call(*args)


def back_parts(dy, weight, column, base, middle, norm_rows, outs_z, half, n, n_dp, alone):
    rows, width = base.shape
    share = outs_z.shape[0]
    outs = [
        shape((rows, width), f32),
        shape((n, rows, width), bf16),
        shape((n * rows, share), bf16),
        shape((8, width), f32),
    ]
    specs = [
        whole_vmem(),
        in_place(),
        whole_vmem(),
        whole_vmem(),
        whole_vmem(),
        in_place(),
    ]
    scratch = [
        pltpu.VMEM((2, n, rows, width), bf16),
        pltpu.VMEM((rows // SUBS, width), f32),
        pltpu.VMEM((rows // SUBS, width), f32),
        *sem_pair(n, SUBS),
        *sem_pair(n, SUBS),
        pltpu.VMEM((share, width), bf16),
        pltpu.SemaphoreType.DMA,
    ]
    if column is not None:
        scratch += [
            pltpu.VMEM((n, rows, width), bf16),
            pltpu.VMEM((width, dy.shape[1]), bf16),
            pltpu.SemaphoreType.DMA,
        ]
    kernel = functools.partial(back_kernel, n, unshuffle_order(n, n_dp), column, half, alone)
    return kernel, [dy, weight, base, middle, norm_rows, outs_z], specs, outs, scratch


def back_call(dy, weight, column, base, middle, norm_rows, outs_z, half, n, n_dp, ident):
    kernel, args, specs, outs, scratch = back_parts(
        dy, weight, column, base, middle, norm_rows, outs_z, half, n, n_dp, True
    )
    call = line_call(kernel, f"back{half}", ident, outs, specs, scratch, 0, LINK_COST)
    return call(*args)


def last_parts(dy, weight, base, tokens, norm_rows, branch, middle, n, n_dp):
    rows, width = base.shape
    outs = [
        shape((rows, width), bf16),
        shape((rows, width), bf16),
        shape((8, width), f32),
    ]
    specs = [whole_vmem(), in_place()] + [whole_vmem()] * 5
    scratch = [
        pltpu.VMEM((n, rows, width), bf16),
        pltpu.VMEM((2, n, rows, width), bf16),
        pltpu.VMEM((2, n, rows, width), bf16),
        pltpu.VMEM((rows // SUBS, width), f32),
        pltpu.VMEM((rows // SUBS, width), f32),
        *sem_pair(n, SUBS),
        *sem_pair(n, SUBS),
        pltpu.VMEM((width, dy.shape[1]), bf16),
        pltpu.SemaphoreType.DMA,
    ]
    kernel = functools.partial(last_kernel, n, unshuffle_order(n, n_dp))
    return kernel, [dy, weight, base, tokens, norm_rows, branch, middle], specs, outs, scratch


def attend_forward(query, keys, values, mask_ref, keyed, att_ref, share_ref):
    packed, rows, _ = mask_ref.shape
    heads = att_ref.shape[1] // HEAD
    for p in range(packed):
        here = slice(p * rows, (p + 1) * rows)
        there = here if keyed else slice(None)
        for h in range(heads):
            columns = slice(h * HEAD, (h + 1) * HEAD)
            scores = dot_nt(query[here, columns], keys[there, columns]) * HEAD ** (-0.5)
            scores = jnp.where(mask_ref[p] > 0, scores, score_floor)
            powers = jnp.exp(scores - jnp.max(scores, axis=-1, keepdims=True))
            shares = powers / jnp.sum(powers, axis=-1, keepdims=True)
            share_ref[p * heads + h] = shares
            att_ref[here, columns] = dot(shares.astype(bf16), values[there, columns]).astype(bf16)


def attend_backward(query, keys, values, share_ref, back_ref, rows, keyed, put_query, put_pair):
    heads = back_ref.shape[1] // HEAD
    packed = back_ref.shape[0] // rows
    score_scale = HEAD ** (-0.5)
    for h in range(heads):
        columns = slice(h * HEAD, (h + 1) * HEAD)
        key_grad = value_grad = None
        for p in range(packed):
            here = slice(p * rows, (p + 1) * rows)
            there = here if keyed else slice(None)
            shares = share_ref[p * heads + h]
            back = back_ref[here, columns]
            back_shares = dot_nt(back, values[there, columns])
            inner_sum = jnp.sum(shares * back_shares, axis=-1, keepdims=True)
            back_scores = (shares * (back_shares - inner_sum)).astype(bf16)
            put_query(here, columns, dot(back_scores, keys[there, columns]) * score_scale)
            key_term = dot_tn(back_scores, query[here, columns]) * score_scale
            value_term = dot_tn(shares.astype(bf16), back)
            if keyed:
                put_pair(there, columns, key_term, value_term)
            else:
                key_grad = key_term if key_grad is None else key_grad + key_term
                value_grad = value_term if value_grad is None else value_grad + value_term
        if not keyed:
            put_pair(slice(None), columns, key_grad, value_grad)


def self_forward_kernel(h_ref, w_ref, mask_ref, proj_ref, att_ref, share_ref):
    tile = pl.program_id(0)
    proj_ref[tile] = dot(h_ref[...], w_ref[...]).astype(bf16)

    @pl.when(tile == 2)
    def _():
        attend_forward(
            proj_ref.at[0], proj_ref.at[1], proj_ref.at[2], mask_ref, True, att_ref, share_ref
        )


def cross_forward_kernel(cq_ref, text_ref, w_ref, mask_ref, kv_ref, att_ref, share_ref, total):
    tile = pl.program_id(0)
    product = dot(text_ref[...], w_ref[...])

    @pl.when(tile < 2)
    def _():
        total[tile] = product

    @pl.when(tile >= 2)
    def _():
        kv_ref[tile - 2] = (total[tile - 2] + product).astype(bf16)

    @pl.when(tile == 3)
    def _():
        attend_forward(cq_ref, kv_ref.at[0], kv_ref.at[1], mask_ref, False, att_ref, share_ref)


def ffn_kernel(h_ref, up_ref, grad_ref, act_ref, slope_ref, gdown_ref):
    up_values = dot(h_ref[...], up_ref[...])
    chance = 0.5 * (1.0 + lax.erf(up_values * 0.5**0.5))
    density = jnp.exp(-0.5 * up_values * up_values) * 0.3989422804014327
    activated = (up_values * chance).astype(bf16)
    act_ref[...] = activated
    slope_ref[...] = chance + up_values * density
    store_pieces(dot_tn(activated, grad_ref[...]), gdown_ref)


def ffn_back_kernel(
    h_ref,
    down_ref,
    up_ref,
    grad_ref,
    act_ref,
    slope_ref,
    both_ref,
    branch_ref,
    part_ref,
    gup_ref,
    total,
    part,
):
    del both_ref
    tile = pl.program_id(0)
    back_act = dot_nt(grad_ref[...], down_ref[...])
    back_up = (back_act * slope_ref[...]).astype(bf16)
    gup_ref[...] = dot_tn(h_ref[...], back_up).astype(bf16).reshape(gup_ref.shape)

    @pl.when(tile == 0)
    def _():
        total[...] = dot(act_ref[...], down_ref[...])
        part[...] = dot_nt(back_up, up_ref[...])

    @pl.when(tile > 0)
    def _():
        total[...] += dot(act_ref[...], down_ref[...])
        part[...] += dot_nt(back_up, up_ref[...])

    @pl.when(tile == 3)
    def _():
        branch_ref[...] = total[...].astype(bf16)
        part_ref[...] = part[...].astype(bf16)


def cross_back_kernel(
    rows, back_ref, cq_ref, kv_ref, share_ref, text_ref, dcq_ref, grad_ref, pairs
):
    share = cq_ref.shape[1]

    @pl.when(pl.program_id(0) == 0)
    def _():
        def put_query(here, columns, value):
            dcq_ref[here, columns] = value.astype(bf16)

        def put_pair(there, columns, key_grad, value_grad):
            pairs[there, columns] = key_grad.astype(bf16)
            after_keys = slice(share + columns.start, share + columns.stop)
            pairs[there, after_keys] = value_grad.astype(bf16)

        attend_backward(
            cq_ref, kv_ref.at[0], kv_ref.at[1], share_ref, back_ref, rows, False, put_query, put_pair
        )

    grad_ref[...] = dot_tn(text_ref[...], pairs[...]).astype(bf16)


def outs_grad_kernel(att1_ref, carry1_ref, att2_ref, carry2_ref, grad_ref):
    tile = pl.program_id(0)

    @pl.when(tile == 0)
    def _():
        store_pieces(dot_tn(att1_ref[...], carry1_ref[...]), grad_ref)

    @pl.when(tile == 1)
    def _():
        store_pieces(dot_tn(att2_ref[...], carry2_ref[...]), grad_ref)


def store_pieces(gradient, target):
    n_dp, rows, columns = target.shape
    gradient = gradient.astype(bf16)
    chunk = gradient.shape[0] // n_dp
    for piece in range(rows // chunk):
        cut = gradient[:, piece * columns : (piece + 1) * columns]
        target[:, piece * chunk : (piece + 1) * chunk] = cut.reshape(n_dp, chunk, columns)


def self_back_kernel(
    rows,
    back_ref,
    proj_ref,
    share_ref,
    h1_ref,
    h2_ref,
    dcq_ref,
    both_ref,
    dproj_ref,
    grad_ref,
    parts,
):
    del both_ref
    tile = pl.program_id(0)
    share = dcq_ref.shape[1]

    @pl.when(tile == 0)
    def _():
        def put(part, here, columns, value):
            value = value.astype(bf16)
            parts[part, here, columns] = value
            dproj_ref[here, part * share + columns.start : part * share + columns.stop] = value

        def put_query(here, columns, value):
            put(0, here, columns, value)

        def put_pair(there, columns, key_grad, value_grad):
            put(1, there, columns, key_grad)
            put(2, there, columns, value_grad)

        attend_backward(
            proj_ref.at[0],
            proj_ref.at[1],
            proj_ref.at[2],
            share_ref,
            back_ref,
            rows,
            True,
            put_query,
            put_pair,
        )

    @pl.when(tile < 3)
    def _():
        grad_ref[...] = dot_tn(h1_ref[...], parts[tile]).astype(bf16).reshape(grad_ref.shape)

    @pl.when(tile == 3)
    def _():
        grad_ref[...] = dot_tn(h2_ref[...], dcq_ref[...]).astype(bf16).reshape(grad_ref.shape)


def fixed(dims):
    return pl.BlockSpec(dims, lambda t: (0,) * len(dims))


def moving(dims, index):
    return pl.BlockSpec(dims, lambda t: (0, index(t)))


def local_call(
    kernel, name, tiles, outs, specs, out_specs, scratch, flops, moved, aliases=None
):
    return pl.pallas_call(
        kernel,
        name=name,
        grid=(tiles,),
        input_output_aliases=aliases or {},
        out_shape=outs,
        in_specs=specs,
        out_specs=out_specs,
        scratch_shapes=scratch,
        compiler_params=pltpu.CompilerParams(vmem_limit_bytes=VMEM_CAP),
        cost_estimate=pl.CostEstimate(
            flops=flops // 8, bytes_accessed=moved // 8, transcendentals=0
        ),
    )


def self_forward(hidden, query_z, mask):
    tokens, width = hidden.shape
    share = query_z.shape[1] // 4
    packed, rows, _ = mask.shape
    pairs = (packed * share // HEAD, rows, rows)
    return local_call(
        self_forward_kernel,
        "self_forward",
        3,
        (shape((3, tokens, share), bf16), shape((tokens, share), bf16), shape(pairs, f32)),
        [fixed(hidden.shape), moving((width, share), lambda t: t), fixed(mask.shape)],
        (fixed((3, tokens, share)), fixed((tokens, share)), fixed(pairs)),
        [],
        6 * tokens * width * share,
        20_000_000,
    )(hidden, query_z, mask)


def cross_forward(cross_query, text_all, text_z, mask):
    tokens, share = cross_query.shape
    texts = text_all.shape[0]
    width = text_z.shape[0]
    packed, rows, _ = mask.shape
    pairs = (packed * share // HEAD, rows, texts)
    return local_call(
        cross_forward_kernel,
        "cross_forward",
        4,
        (shape((2, texts, share), bf16), shape((tokens, share), bf16), shape(pairs, f32)),
        [
            fixed(cross_query.shape),
            moving((texts, width), lambda t: t // 2),
            moving((width, share), lambda t: t),
            fixed(mask.shape),
        ],
        (fixed((2, texts, share)), fixed((tokens, share)), fixed(pairs)),
        [pltpu.VMEM((2, texts, share), f32)],
        8 * texts * width * share,
        20_000_000,
    )(cross_query, text_all, text_z, mask)


def ffn(hidden, up_z, grad_all, n, n_dp):
    tokens, width = hidden.shape
    share = up_z.shape[1] // 4
    chunk = share // n_dp
    return local_call(
        ffn_kernel,
        "ffn",
        4,
        (
            shape((tokens, 4 * share), bf16),
            shape((tokens, 4 * share), f32),
            shape((n_dp, 2 * n * chunk, 4 * share), bf16),
        ),
        [fixed(hidden.shape), moving((width, share), lambda t: t), fixed(grad_all.shape)],
        (
            moving((tokens, share), lambda t: t),
            moving((tokens, share), lambda t: t),
            pl.BlockSpec((n_dp, n * chunk // 4, 4 * share), lambda t: (0, 4 + t, 0)),
        ),
        [],
        16 * tokens * width * share,
        30_000_000,
    )(hidden, up_z, grad_all)


def ffn_back(hidden, down_z, up_z, grad_all, activated, slope, both):
    tokens, width = hidden.shape
    share = down_z.shape[0]
    return local_call(
        ffn_back_kernel,
        "ffn_back",
        4,
        (shape((tokens, width), bf16), shape((tokens, width), bf16), shape(both.shape, bf16)),
        [
            fixed(hidden.shape),
            moving((share, width), lambda t: t),
            moving((width, share), lambda t: t),
            fixed(grad_all.shape),
            moving((tokens, share), lambda t: t),
            moving((tokens, share), lambda t: t),
            in_place(),
        ],
        (
            fixed((tokens, width)),
            fixed((tokens, width)),
            pl.BlockSpec((both.shape[0], both.shape[1] // 2, share), lambda t: (0, 0, t)),
        ),
        [pltpu.VMEM((tokens, width), f32)] * 2,
        32 * tokens * width * share,
        50_000_000,
        {6: 2},
    )(hidden, down_z, up_z, grad_all, activated, slope, both)


def cross_back(back_attended, cross_query, text_pairs, shares, text_all, rows):
    tokens, share = cross_query.shape
    texts = text_all.shape[0]
    width = text_all.shape[1] // 2
    return local_call(
        functools.partial(cross_back_kernel, rows),
        "cross_back",
        2,
        (shape((tokens, share), bf16), shape((width, 4 * share), bf16)),
        [
            fixed(back_attended.shape),
            fixed(cross_query.shape),
            fixed(text_pairs.shape),
            fixed(shares.shape),
            moving((texts, width), lambda t: t),
        ],
        (fixed((tokens, share)), moving((width, 2 * share), lambda t: t)),
        [pltpu.VMEM((texts, 2 * share), bf16)],
        8 * texts * width * share,
        20_000_000,
    )(back_attended, cross_query, text_pairs, shares, text_all)


def outs_grad(attended1, carry1, attended2, carry2, n, n_dp):
    tokens, share = attended1.shape
    width = carry1.shape[1]
    chunk = share // n_dp
    return local_call(
        outs_grad_kernel,
        "outs_grad",
        2,
        shape((n_dp, n * chunk * 3 // 2, 4 * share), bf16),
        [fixed((tokens, share)), fixed((tokens, width))] * 2,
        pl.BlockSpec((n_dp, n * chunk // 4, 4 * share), lambda t: (0, 4 + t, 0)),
        [],
        4 * tokens * width * share,
        10_000_000,
    )(attended1, carry1, attended2, carry2)


def self_back(back_attended, projected, shares, hidden1, hidden2, back_cross, both, rows):
    tokens, width = hidden1.shape
    share = back_cross.shape[1]
    return local_call(
        functools.partial(self_back_kernel, rows),
        "self_back",
        4,
        (shape((tokens, 3 * share), bf16), shape(both.shape, bf16)),
        [
            fixed(back_attended.shape),
            fixed(projected.shape),
            fixed(shares.shape),
            fixed(hidden1.shape),
            fixed(hidden2.shape),
            fixed(back_cross.shape),
            in_place(),
        ],
        (
            fixed((tokens, 3 * share)),
            pl.BlockSpec((both.shape[0], both.shape[1] * 2 // 3, share), lambda t: (0, 0, t)),
        ),
        [pltpu.VMEM((3, tokens, share), bf16)],
        8 * tokens * width * share,
        25_000_000,
        {6: 1},
    )(back_attended, projected, shares, hidden1, hidden2, back_cross, both)


def block_slots(owners):
    owner = jnp.concatenate(owners)
    weight = jnp.concatenate([jnp.full(one.shape, at, jnp.int32) for at, one in enumerate(owners)])
    mark = owner + weight * 1024
    count = mark.shape[0]
    earlier = lax.broadcasted_iota(jnp.int32, (count, count), 1) < lax.broadcasted_iota(
        jnp.int32, (count, count), 0
    )
    same = jnp.logical_and(mark[:, None] == mark[None, :], earlier)
    return jnp.stack([owner, jnp.sum(same.astype(jnp.int32), axis=1)])


def slot_contents(owners, slots, places, capacities, firsts, n_dp):
    rows = []
    for owner, place, capacity, first in zip(owners, places, capacities, firsts):
        count = owner.shape[0]
        at = owner * capacity + slots[1, first : first + count]
        hit = at[None, :] == lax.broadcasted_iota(jnp.int32, (n_dp * capacity, count), 0)
        block = lax.broadcasted_iota(jnp.int32, (n_dp * capacity, count), 1)
        per_group, per_part, split = place_rule(place)
        part = block % per_group // per_part if split else block * 0
        column = block // per_group * per_part + block % per_part if split else block
        index = part * (count // (per_group // per_part)) + column if split else column
        rows.append(
            jnp.stack([jnp.sum(jnp.where(hit, value, 0), axis=1) for value in (index, block * 0 + 1)])
        )
    return jnp.concatenate(rows, axis=1)


def place_rule(place):
    parts = 1 + max(part for part, _ in place)
    if parts == 1:
        return 0, 0, False
    per_part = sum(1 for part, _ in place[:HEADS] if part == 0)
    return per_part * parts, per_part, True


def after(small, first):
    return lax.optimization_barrier((small, first))[0]


def body(
    tokens_in,
    text_in,
    seg_ids,
    capt_ids,
    grad_out,
    owner_query,
    owner_up,
    owner_outs,
    owner_text,
    owner_down,
    w_query,
    m_query,
    v_query,
    w_up,
    m_up,
    v_up,
    w_outs,
    m_outs,
    v_outs,
    w_text,
    m_text,
    v_text,
    w_down,
    m_down,
    v_down,
    norm_weight,
    m_norm,
    v_norm,
):
    n_dp = lax.axis_size("dp")
    n_z = lax.axis_size("fsdp")
    width = tokens_in.shape[1]
    own_rows = w_query.shape[0]
    chunk = own_rows // n_dp
    cap_big = w_query.shape[1] // BLK
    cap_out = w_outs.shape[1] // BLK
    heads_z = HEADS // n_z
    share = width // n_z
    owner_query, owner_up, owner_outs, owner_text, owner_down = (
        owner[:, 0] for owner in (owner_query, owner_up, owner_outs, owner_text, owner_down)
    )
    split_places = [split_place(b, heads_z, n_z) for b in range(owner_query.shape[0])]
    big_places = [flat_place(b) for b in range(owner_down.shape[0])]
    out_places = [flat_place(b) for b in range(owner_outs.shape[0])]
    owners = (owner_query, owner_outs, owner_text, owner_up, owner_down)
    places = (split_places, out_places, split_places, split_places, big_places)
    capacities = (cap_big, cap_out, cap_big, cap_big, cap_big)
    firsts = [sum(len(one) for one in places[:index]) for index in range(5)]
    slot_firsts = [sum(capacities[:index]) * n_dp for index in range(5)]
    slots = block_slots(owners)
    contents = slot_contents(owners, slots, places, capacities, firsts, n_dp)

    def spread(rows):
        return lax.all_gather(rows.reshape(-1, rows.shape[-1]), "dp", axis=0, tiled=True)

    def gather_sum(piece, parts):
        summed = lax.psum_scatter(piece, "dp", scatter_dimension=0, tiled=True)
        return summed.reshape(parts, chunk, -1)

    token_count = tokens_in.shape[0]
    marks = jnp.concatenate([seg_ids, capt_ids], axis=1)
    marks = jnp.pad(marks, ((0, 7), (0, 256 - marks.shape[1])))
    norms = jnp.pad(norm_weight, ((0, 2), (0, 0)))
    half = token_count // 2
    query_rows, grad_low, marks, norm_full = enter_call(
        "enter_query",
        0,
        slots,
        [(w_query, split_places, True, firsts[0])],
        [(grad_out[:half], False), (marks, False)],
        norms,
        True,
        False,
        n_z,
        n_dp,
        width,
    )
    outs_rows, hidden1, text_all = enter_call(
        "enter_outs",
        6,
        slots,
        [(w_outs, out_places, False, firsts[1])],
        [(tokens_in, True), (text_in, True)],
        norm_full[0:2],
        False,
        True,
        n_z,
        n_dp,
        width,
    )
    query_z, outs_z = spread(query_rows), spread(outs_rows)
    hidden1 = hidden1.reshape(-1, width)
    text_all = text_all.reshape(-1, text_in.shape[1])
    segment = marks[:, 0, :token_count]
    caption = marks[:, 0, token_count : token_count + capt_ids.shape[1]]
    self_mask = (segment[:, :, None] == segment[:, None, :]).astype(jnp.int32)
    text_row = lax.broadcasted_iota(jnp.int32, caption.shape, 0).reshape(1, 1, -1)
    packed_row = lax.broadcasted_iota(jnp.int32, (n_z, 1, 1), 0)
    cross_mask = jnp.logical_and(
        segment[:, :, None] == caption.reshape(1, 1, -1), packed_row == text_row
    ).astype(jnp.int32)

    projected, attended1, shares1 = self_forward(hidden1, query_z, self_mask)
    text_rows, grad_high = enter_call(
        "enter_text",
        7,
        after(slots, attended1),
        [(w_text, split_places, True, firsts[2])],
        [(grad_out[half:], False)],
        None,
        False,
        False,
        n_z,
        n_dp,
        width,
    )
    grad_all = jnp.concatenate([grad_low, grad_high], axis=1).reshape(-1, width)
    up_rows, down_rows, middle1, hidden2, cross_query = enter_call(
        "forward0",
        1,
        slots,
        [(w_up, split_places, True, firsts[3]), (w_down, big_places, False, firsts[4])],
        [],
        None,
        False,
        False,
        n_z,
        n_dp,
        width,
        forward_parts(
            attended1,
            outs_z,
            0,
            tokens_in,
            after(norm_full[2:4], text_rows),
            query_z,
            n_z,
            n_dp,
            False,
        ),
    )
    hidden2 = hidden2.reshape(-1, width)
    text_z, up_z, down_z = spread(text_rows), spread(up_rows), spread(down_rows)
    text_pairs, attended2, shares2 = cross_forward(cross_query, text_all, text_z, cross_mask)
    middle2, hidden3 = forward_call(
        attended2, outs_z, 1, middle1, norm_full[4:6], None, n_z, n_dp, 2
    )
    hidden3 = hidden3.reshape(-1, width)
    activated, slope, both = ffn(hidden3, up_z, grad_all, n_z, n_dp)
    branch3, part3, both = ffn_back(hidden3, down_z, up_z, grad_all, activated, slope, both)
    branch3 = branch3.reshape(n_z, token_count, width)
    part3 = part3.reshape(n_z, token_count, width)
    up_down_sum = gather_sum(both.reshape(-1, 4 * share), 2 * n_z)
    up_sum, down_sum = up_down_sum[:n_z], up_down_sum[n_z:]
    at_middle2, carry2, back_att2, term3 = back_call(
        part3, after(slots, part3), None, grad_out, middle2, norm_full[4:6], outs_z, 1, n_z, n_dp, 3
    )
    carry2 = carry2.reshape(-1, width)
    back_cross, text_part = cross_back(
        back_att2, cross_query, text_pairs, shares2, text_all, token_count
    )
    text_sum = gather_sum(text_part, n_z)
    at_middle1, carry1, back_att1, term2 = back_call(
        back_cross, query_z, 3, at_middle2, middle1, norm_full[2:4], outs_z, 0, n_z, n_dp, 4
    )
    carry1 = carry1.reshape(-1, width)
    both = outs_grad(attended1, after(carry1, up_down_sum), attended2, carry2, n_z, n_dp)
    back_projected, both = self_back(
        back_att1, projected, shares1, hidden1, hidden2, back_cross, both, token_count
    )
    query_outs_sum = gather_sum(both.reshape(-1, 4 * share), 3 * n_z // 2)
    down_grad, up_grad, text_grad, grad_in, result, term1 = leave_call(
        "leave_up",
        8,
        contents,
        [
            (down_sum, False, cap_big, slot_firsts[4], True),
            (up_sum, True, cap_big, slot_firsts[3], True),
            (text_sum, True, cap_big, slot_firsts[2], True),
        ],
        None,
        n_z,
        n_dp,
        last_parts(
            back_projected,
            query_z,
            at_middle1,
            tokens_in,
            norm_full[0:2],
            branch3,
            middle2,
            n_z,
            n_dp,
        ),
    )
    query_outs_sum = after(query_outs_sum, term1)
    query_sum, outs_sum = query_outs_sum[:n_z], query_outs_sum[n_z:]
    norm_term = jnp.concatenate([term1[:2], term2[:2], term3[:4]], axis=0)
    loose, norm_grad = leave_call(
        "leave_query",
        9,
        contents,
        [
            (outs_sum, False, cap_out, slot_firsts[1], False),
            (query_sum, True, cap_big, slot_firsts[0], False),
        ],
        norm_term,
        n_z,
        n_dp,
    )
    loose = lax.all_to_all(loose, "dp", 0, 0, tiled=True).reshape(own_rows, -1)
    outs_slots = loose[:, : cap_out * BLK].astype(f32)
    query_grad = loose[:, cap_out * BLK :].astype(f32)
    norm_grad = norm_grad[:6]
    text_grad, up_grad, down_grad = (
        grad.reshape(own_rows, -1).astype(f32) for grad in (text_grad, up_grad, down_grad)
    )
    up_new = adamw_update(w_up, m_up, v_up, up_grad, rate_up, decay_rate)
    text_new = adamw_update(w_text, m_text, v_text, text_grad, rate_text, decay_rate)
    down_new = adamw_update(w_down, m_down, v_down, down_grad, rate_down, decay_rate)
    query_new = adamw_update(w_query, m_query, v_query, query_grad, rate_query, decay_rate)
    outs_new = adamw_update(w_outs, m_outs, v_outs, outs_slots, rate_outs, decay_rate)
    norm_new = adamw_update(norm_weight, m_norm, v_norm, norm_grad, rate_norm, 0.0)
    return (
        result,
        grad_in,
        *query_new,
        *up_new,
        *outs_new,
        *text_new,
        *down_new,
        *norm_new,
    )


def solution(mesh):
    rows = P(("dp", "fsdp"), None)
    slots = P("fsdp", "dp")
    norms = P(None, "dp")
    in_specs = (rows,) * 5 + (P(),) * 5 + (slots,) * 15 + (norms,) * 3
    out_specs = (rows,) * 2 + (slots,) * 15 + (norms,) * 3
    return jax.shard_map(body, mesh=mesh, in_specs=in_specs, out_specs=out_specs, check_vma=False)
```

```python
import functools

import jax
import jax.numpy as jnp
from jax import lax
from jax.experimental import pallas as pl
from jax.experimental.pallas import tpu as pltpu
from jax.sharding import PartitionSpec as P

HEADS = 16
HEAD = 128
STEP = 10
BLK = 128


beta_first = 0.9
beta_second = 0.999
adam_eps = 1e-08
decay_rate = 0.01
rate_query = 0.04
rate_up = 0.04
rate_outs = 0.12
rate_text = 0.03
rate_down = 0.03
rate_norm = 0.5
norm_eps = 1e-05
score_floor = -1e30
bf16 = jnp.bfloat16
f32 = jnp.float32


def normalize(values):
    centered = values - jnp.mean(values, axis=-1, keepdims=True)
    inverse_std = lax.rsqrt(jnp.mean(centered * centered, axis=-1, keepdims=True) + norm_eps)
    return (centered * inverse_std, inverse_std)


def norm_back(back_hidden, normed, inverse_std, gain_row):
    back_normed = back_hidden * gain_row
    return inverse_std * (
        back_normed
        - jnp.mean(back_normed, axis=-1, keepdims=True)
        - normed * jnp.mean(back_normed * normed, axis=-1, keepdims=True)
    )


def adamw_update(weight, first, second, gradient, rate, decay):
    first_new = beta_first * first + (1.0 - beta_first) * gradient
    second_new = beta_second * second + (1.0 - beta_second) * gradient * gradient
    first_hat = first_new / (1.0 - beta_first**STEP)
    second_hat = second_new / (1.0 - beta_second**STEP)
    weight_new = weight - rate * (first_hat / (jnp.sqrt(second_hat) + adam_eps) + decay * weight)
    return (first_new, second_new, weight_new)


def dot(left, right):
    return jnp.dot(left, right, preferred_element_type=f32)


def dot_nt(left, right):
    return lax.dot_general(left, right, (((1,), (1,)), ((), ())), preferred_element_type=f32)


def dot_tn(left, right):
    return lax.dot_general(left, right, (((0,), (0,)), ((), ())), preferred_element_type=f32)


def split_place(block, per_part, parts):
    group, rest = divmod(block, per_part * parts)
    part, inner = divmod(rest, per_part)
    return part, group * per_part + inner


def flat_place(block):
    return 0, block


MESH = pl.DeviceIdType.MESH


SUBS = 4


class Line:
    def __init__(self, n, rows, step):
        self.n, self.rows, self.step = n, rows, step
        self.at = lax.axis_index("fsdp")

    def has(self, way):
        return self.at < self.n - 1 if way == 0 else self.at > 0

    def peer(self, way):
        index = jnp.clip(self.at + (1 if way == 0 else -1), 0, self.n - 1)
        return {"fsdp": index}

    def greet(self, others=0):
        barrier = pltpu.get_barrier_semaphore()
        for way in (0, 1):

            @pl.when(self.has(way))
            def _():
                pl.semaphore_signal(
                    barrier, inc=1, device_id=self.peer(way), device_id_type=pl.DeviceIdType.MESH
                )

        pl.semaphore_wait(
            barrier, others + self.has(0).astype(jnp.int32) + self.has(1).astype(jnp.int32)
        )

    def copy(self, source, target, send, recv, way):
        return pltpu.make_async_remote_copy(
            src_ref=source,
            dst_ref=target,
            send_sem=send,
            recv_sem=recv,
            device_id=self.peer(way),
            device_id_type=pl.DeviceIdType.MESH,
        )

    def part(self, sub):
        return pl.ds(sub * self.step, self.step)


class Sums:
    def __init__(self, line, part, held, send, recv):
        self.line, self.part, self.held, self.send, self.recv = line, part, held, send, recv

    def move(self, way, target, sub, source):
        line = self.line
        rows = line.part(sub)
        return line.copy(
            source,
            self.held.at[way, target, rows],
            self.send.at[way, target, sub],
            self.recv.at[way, target, sub],
            way,
        )

    def target(self, way, time):
        n, at = self.line.n, self.line.at
        return n - 1 - (time - at) if way == 0 else time - (n - 1 - at)

    def passes(self, way, target):
        n, at = self.line.n, self.line.at
        if way == 0:
            return jnp.logical_and(target > at, target < n)
        return jnp.logical_and(target < at, target >= 0)

    def forward(self, sub, time):
        line = self.line
        rows = line.part(sub)
        for way in (0, 1):
            target = self.target(way, time)
            passes = self.passes(way, target)
            inner = jnp.logical_and(passes, line.has(1 - way))
            outer = jnp.logical_and(passes, jnp.logical_not(line.has(1 - way)))

            @pl.when(outer)
            def _():
                self.move(way, target, sub, self.part.at[target, rows]).start()

            @pl.when(inner)
            def _():
                held = self.held.at[way, target, rows]
                self.move(way, target, sub, held).wait_recv()
                total = held[...].astype(f32) + self.part[target, rows].astype(f32)
                held[...] = total.astype(bf16)
                self.move(way, target, sub, held).start()

    def total(self, sub, sum_ref):
        line = self.line
        rows = line.part(sub)
        sum_ref[...] = self.part[line.at, rows].astype(f32)
        for way in (0, 1):

            @pl.when(line.has(1 - way))
            def _():
                held = self.held.at[way, line.at, rows]
                self.move(way, line.at, sub, held).wait_recv()
                sum_ref[...] += held[...].astype(f32)

    def finish(self):
        line = self.line
        for way in (0, 1):
            for time in range(line.n - 1):
                target = self.target(way, time)

                @pl.when(self.passes(way, target))
                def _():
                    for sub in range(line.rows // line.step):
                        held = self.held.at[way, target, line.part(sub)]
                        self.move(way, target, sub, held).wait_send()


def relay(n, sums, blocks, settle, hook=None):
    for slot in range((SUBS + 2) * (n - 1)):
        sub, time = divmod(slot, n - 1)
        if hook is not None and slot == SUBS * (n - 1):
            hook()
        if sub < SUBS:
            for one in sums:
                one.forward(sub, time)
        if time == 0 and 0 <= sub - 1 < SUBS:
            settle(sub - 1)
        if blocks is not None:
            if time == n - 2 and 0 <= sub - 1 < SUBS:
                blocks.forward(sub - 1, 1)
            if time < n - 2 and 0 <= sub - 2 < SUBS:
                blocks.forward(sub - 2, time + 2)
    for one in sums:
        one.finish()
    if blocks is not None:
        blocks.finish()


class Blocks:
    def __init__(self, line, full, send, recv):
        self.line, self.full, self.send, self.recv = line, full, send, recv

    def move(self, way, source, sub):
        line = self.line
        held = self.full.at[source, line.part(sub)]
        return line.copy(
            held, held, self.send.at[way, source, sub], self.recv.at[way, source, sub], way
        )

    def behind(self, way, source):
        return self.line.at > source if way == 0 else self.line.at < source

    def start(self, sub):
        for way in (0, 1):

            @pl.when(self.line.has(way))
            def _():
                self.move(way, self.line.at, sub).start()

    def forward(self, sub, step):
        line = self.line
        for way in (0, 1):
            source = line.at - step if way == 0 else line.at + step

            @pl.when(jnp.logical_and(source >= 0, source < line.n))
            def _():
                self.move(way, source, sub).wait_recv()

                @pl.when(line.has(way))
                def _():
                    self.move(way, source, sub).start()

    def finish(self):
        line = self.line
        for way in (0, 1):
            for source in range(line.n):
                ours = jnp.logical_or(self.behind(way, source), line.at == source)

                @pl.when(jnp.logical_and(ours, line.has(way)))
                def _():
                    for sub in range(line.rows // line.step):
                        self.move(way, source, sub).wait_send()


def lane_moves(width, order):
    moves = []
    piece = width // len(order)
    for group in range(width // BLK):
        parts = []
        for offset in range(0, BLK, piece):
            start = order[(group * BLK + offset) // piece] * piece
            parts.append((offset, start // BLK, start % BLK))
        moves.append(parts)
    return piece, moves


def reorder(load, store, rows, width, order):
    piece, moves = lane_moves(width, order)
    lane = lax.broadcasted_iota(jnp.int32, (rows, BLK), 1)
    for group, parts in enumerate(moves):
        value = None
        for offset, source, start in parts:
            block = load(source)
            if start != offset:
                block = pltpu.roll(block, (offset - start) % BLK, 1)
            value = block if value is None else jnp.where(lane >= offset, block, value)
        store(group, value)


def shuffle_order(n_z, n_dp):
    return [z * n_dp + i for i in range(n_dp) for z in range(n_z)]


def unshuffle_order(n_z, n_dp):
    return [i * n_z + z for z in range(n_z) for i in range(n_dp)]


def by_tiles(columns, tile, run):
    def one(index, carry):
        run(pl.ds(pl.multiple_of(index * tile, tile), tile))
        return carry

    lax.fori_loop(0, columns // tile, one, 0)


class Swap:
    def __init__(self, axis, source, target, send, recv):
        self.axis, self.source, self.target = axis, source, target
        self.send, self.recv = send, recv
        self.n = lax.axis_size(axis)
        self.me = lax.axis_index(axis)

    def copy(self, jump, arrival=False):
        peer = lax.rem(self.me + jump, self.n)
        slot = peer if arrival else self.me
        return pltpu.make_async_remote_copy(
            src_ref=self.source.at[peer],
            dst_ref=self.target.at[slot],
            send_sem=self.send.at[jump],
            recv_sem=self.recv.at[slot],
            device_id={self.axis: peer},
            device_id_type=MESH,
        )

    def start(self):
        for jump in range(1, self.n):
            self.copy(jump).start()

    def keep(self):
        self.target[self.me] = self.source[self.me]

    def wait(self):
        for jump in range(1, self.n):
            self.copy(jump, True).wait_recv()

    def finish(self):
        for jump in range(1, self.n):
            self.copy(jump).wait_send()


def greet_all():
    barrier = pltpu.get_barrier_semaphore()
    count = 0
    for axis in ("dp", "fsdp"):
        n, me = lax.axis_size(axis), lax.axis_index(axis)
        count += n - 1
        for jump in range(1, n):
            pl.semaphore_signal(
                barrier, inc=1, device_id={axis: lax.rem(me + jump, n)}, device_id_type=MESH
            )
    pl.semaphore_wait(barrier, count)


class Refs:
    def __init__(self, refs):
        self.refs = list(refs)

    def take(self, count=None):
        taken = self.refs[: 1 if count is None else count]
        self.refs = self.refs[len(taken) :]
        return taken[0] if count is None else taken


def enter_kernel(weights, gathers, order, normed, hidden, inner, inner_counts, *refs):
    refs = Refs(refs)
    n_dp, n_z = lax.axis_size("dp"), lax.axis_size("fsdp")
    slots_ref = refs.take()
    w_refs = refs.take(len(weights))
    in_refs = refs.take(len(gathers))
    norm_in = refs.take() if normed or hidden else None
    inner_refs = refs.take(inner_counts[0])
    row_refs = refs.take(len(weights))
    full_refs = refs.take(len(gathers))
    norm_out = refs.take() if normed else None
    inner_refs += refs.take(inner_counts[1])
    inner_refs += refs.take(inner_counts[2])
    loads = []
    for w_ref in w_refs:
        stage, sem = refs.take(2)
        load = pltpu.make_async_copy(w_ref, stage, sem)
        load.start()
        loads.append((stage, load))
    greet_all()
    if normed:
        parts, *sems = refs.take(3)
        norm_swap = Spread("dp", norm_in, parts, *sems)
        norm_swap.start()
    lines = []
    for in_ref, full_ref in zip(in_refs, full_refs):
        rows = in_ref.shape[0]
        step = rows // pieces_of(rows)
        lines.append(Blocks(Line(n_z, rows, step), full_ref, *refs.take(2)))
    swaps = []
    for (stage, load), (places, split, _) in zip(loads, weights):
        source, target, *sems = refs.take(4)
        swap = Swap("dp", source, target, *sems)
        load.wait()
        chunk = source.shape[2]
        for jump in range(n_dp):
            peer = lax.rem(swap.me + jump, n_dp)
            into = source if jump else target
            for slot in range(source.shape[1]):
                here = pl.ds(pl.multiple_of(peer * chunk, chunk), chunk)
                piece = stage[here, slot * BLK : (slot + 1) * BLK]
                into[peer, slot] = piece.astype(bf16)
            if jump:
                swap.copy(jump).start()
        swaps.append(swap)
    if hidden:
        work = refs.take()
    for index, (in_ref, full_ref, blocks) in enumerate(zip(in_refs, full_refs, lines)):
        line = blocks.line
        if hidden and index == 0:
            for sub in range(line.rows // line.step):
                here = line.part(sub)
                values, _ = normalize(in_ref[here].astype(f32))
                work[...] = values * norm_in[0:1] + norm_in[1:2]
                store_shuffled(work, full_ref, line, here, order)
                blocks.start(sub)
        elif in_ref.dtype == bf16 and gathers[index]:
            work2 = refs.take()
            work2[...] = in_ref[...].astype(f32)
            store_shuffled(work2, full_ref, line, line.part(0), order)
            blocks.start(0)
        else:
            for sub in range(line.rows // line.step):
                here = line.part(sub)
                full_ref[line.at, here] = in_ref[here]
                blocks.start(sub)
    if normed:
        parts[norm_swap.me] = norm_in[...]
        norm_swap.wait()
        share = norm_in.shape[1]
        for index in range(n_dp):
            norm_out[:, index * share : (index + 1) * share] = parts[index]
    shares = []

    def compact(index):
        swap, row_ref, (places, split, first) = swaps[index], row_refs[index], weights[index]
        swap.wait()
        if split:
            cut, *sems = refs.take(3)
            share = Swap("fsdp", cut, row_ref, *sems)
            shares.append(share)
        else:
            cut = row_ref
        for block, (part, column) in enumerate(places):
            owner, slot = slots_ref[0, first + block], slots_ref[1, first + block]
            cut[part, :, column * BLK : (column + 1) * BLK] = swap.target[owner, slot]
        if split:
            share.start()
            share.keep()

    ahead = 0
    if inner is not None:
        ahead = 1
        inner(*inner_refs, hook=lambda: compact(0))
    for step in range(1, n_z):
        for blocks in lines:
            for sub in range(blocks.line.rows // blocks.line.step):
                blocks.forward(sub, step)
    for index in range(ahead, len(weights)):
        compact(index)
    for share in shares:
        share.wait()
    for one in [*swaps, *shares, *lines]:
        one.finish()
    if normed:
        norm_swap.finish()


class Spread(Swap):
    def copy(self, jump, arrival=False):
        peer = lax.rem(self.me + jump, self.n)
        slot = peer if arrival else self.me
        return pltpu.make_async_remote_copy(
            src_ref=self.source,
            dst_ref=self.target.at[slot],
            send_sem=self.send.at[jump],
            recv_sem=self.recv.at[slot],
            device_id={self.axis: peer},
            device_id_type=MESH,
        )


def store_shuffled(work, full_ref, line, here, order):
    rows, width = work.shape
    folds = width // order.width
    pieces = len(order.pieces)
    orders = [fold * pieces + piece for fold in range(folds) for piece in order.pieces]

    def load(group):
        return work[:, group * BLK : (group + 1) * BLK]

    def store(group, value):
        full_ref[line.at, here, group * BLK : (group + 1) * BLK] = value.astype(bf16)

    reorder(load, store, rows, width, orders)


def expand_slots(slots_ref, rows, cut, blocks, capacity, first, offset):
    columns = rows.shape[2] // BLK
    for part in range(rows.shape[0]):
        for column in range(columns):
            blocks[part * columns + column] = rows[part, :, column * BLK : (column + 1) * BLK]
    for owner in range(cut.shape[0]):
        for position in range(capacity):
            slot = first + owner * capacity + position
            value = blocks[slots_ref[0, slot]].astype(f32)
            live = slots_ref[1, slot].astype(f32)
            start = offset + position * BLK
            cut[owner, :, start : start + BLK] = (value * live).astype(bf16)


def leave_kernel(weights, summed, inner, inner_counts, *refs):
    refs = Refs(refs)
    n_dp = lax.axis_size("dp")
    slots_ref = refs.take()
    row_refs = refs.take(len(weights))
    term_ref = refs.take() if summed else None
    inner_refs = refs.take(inner_counts[0])
    gone = sum(1 for weight in weights if weight[3])
    out_refs = refs.take(gone)
    loose_ref = refs.take() if gone < len(weights) else None
    sum_ref = refs.take() if summed else None
    inner_refs += refs.take(inner_counts[1])
    inner_refs += refs.take(inner_counts[2])
    greet_all()
    if summed:
        cut, parts, send, recv, total, others, send2, recv2 = refs.take(8)
        share = cut.shape[2]
        for index in range(n_dp):
            cut[index] = term_ref[:, index * share : (index + 1) * share]
        term_swap = Swap("dp", cut, parts, send, recv)
        term_swap.start()
        term_swap.keep()
    shares = []
    for row_ref, (split, _, _, _) in zip(row_refs, weights):
        if split:
            held, *sems = refs.take(3)
            share = Swap("fsdp", row_ref, held, *sems)
            share.start()
            share.keep()
            shares.append(share)
        else:
            shares.append(None)
    if summed:
        term_swap.wait()
        total[...] = jnp.sum(parts[...], axis=0)
        total_spread = Spread("fsdp", total, others, send2, recv2)
        total_spread.start()
        others[total_spread.me] = total[...]
    swaps = []
    offset = 0
    for row_ref, share, (split, capacity, first, whole) in zip(row_refs, shares, weights):
        if split:
            share.wait()
        rows = share.target if split else row_ref
        if not whole:
            expand_slots(slots_ref, rows, loose_ref, refs.take(), capacity, first, offset)
            offset += capacity * BLK
            continue
        out_ref = out_refs.pop(0)
        cut, *sems, blocks = refs.take(4)
        expand_slots(slots_ref, rows, cut, blocks, capacity, first, 0)
        swap = Swap("dp", cut, out_ref, *sems)
        swap.start()
        swap.keep()
        swaps.append(swap)
    if inner is not None:
        inner(*inner_refs)
    if summed:
        total_spread.wait()
        sum_ref[...] = jnp.sum(others[...], axis=0)
    for swap in swaps:
        swap.wait()
    for one in [*swaps, *shares]:
        if one is not None:
            one.finish()
    if summed:
        term_swap.finish()
        total_spread.finish()


def fetch_columns(source, index, target, sem):
    columns = target.shape[1]
    return pltpu.make_async_copy(source.at[:, pl.ds(index * columns, columns)], target, sem)


def forward_kernel(
    n, order, half, wide, alone, att_ref, outs_hbm, base_ref, norm_ref, *rest, hook=None
):
    if wide:
        next_hbm, middle_ref, full_ref, result_ref = rest[:4]
        *rest, next_ref, next_sem = rest[4:]
    else:
        middle_ref, full_ref = rest[:2]
        rest = rest[2:]
    part, held, work, s_send, s_recv, b_send, b_recv, outs_ref, outs_sem = rest
    rows, width = base_ref.shape
    step = rows // SUBS
    load_outs = fetch_columns(outs_hbm, half, outs_ref, outs_sem)
    load_outs.start()
    if wide:
        load_next = fetch_columns(next_hbm, 3, next_ref, next_sem)
        load_next.start()
    line = Line(n, rows, step)
    if alone:
        line.greet()
    load_outs.wait()
    sums = Sums(line, part, held, s_send, s_recv)
    blocks = Blocks(line, full_ref, b_send, b_recv)

    def multiply(columns):
        product = dot(att_ref[...], outs_ref[:, columns]).astype(bf16)
        part[:, :, columns] = product.reshape(n, rows, -1)

    by_tiles(width, 256, multiply)

    def settle(sub):
        here = line.part(sub)
        sums.total(sub, work)
        middle = base_ref[here].astype(f32) + work[...]
        middle_ref[here] = middle
        normed, _ = normalize(middle)
        work[...] = normed * norm_ref[0:1] + norm_ref[1:2]

        def load(group):
            return work[:, group * BLK : (group + 1) * BLK]

        def store(group, value):
            full_ref[line.at, here, group * BLK : (group + 1) * BLK] = value.astype(bf16)

        reorder(load, store, step, width, order)
        blocks.start(sub)

    relay(n, [sums], blocks, settle, hook)
    if wide:
        load_next.wait()

        def multiply_next(columns):
            whole = full_ref[...].reshape(n * rows, width)
            result_ref[:, columns] = dot(whole, next_ref[:, columns]).astype(bf16)

        by_tiles(result_ref.shape[1], 256, multiply_next)


def carry_back(work, plain, order, step, width, middle, base, gain, term_ref, first):
    def load(group):
        return work[:, group * BLK : (group + 1) * BLK]

    def store(group, value):
        plain[:, group * BLK : (group + 1) * BLK] = value

    reorder(load, store, step, width, order)
    back_hidden = plain[...]
    normed, inverse = normalize(middle)
    gain_term = jnp.sum(back_hidden * normed, axis=0, keepdims=True)
    bias_term = jnp.sum(back_hidden, axis=0, keepdims=True)
    if first:
        term_ref[...] = jnp.zeros_like(term_ref)
        term_ref[0:1] = gain_term
        term_ref[1:2] = bias_term
    else:
        term_ref[0:1] += gain_term
        term_ref[1:2] += bias_term
    return base + norm_back(back_hidden, normed, inverse, gain)


def back_kernel(
    n, order, column, half, alone, dy_ref, w_hbm, base_ref, middle_ref, norm_ref, outs_hbm, *rest
):
    carry_ref, full_ref, att_ref, term_ref = rest[:4]
    held, work, plain, s_send, s_recv, b_send, b_recv, outs_ref, outs_sem = rest[4:13]
    rows, width = base_ref.shape
    step = rows // SUBS
    if column is not None:
        part, w_ref, w_sem = rest[13:]
        load_w = fetch_columns(w_hbm, column, w_ref, w_sem)
        load_w.start()
    else:
        part = dy_ref
    load_outs = fetch_columns(outs_hbm, half, outs_ref, outs_sem)
    load_outs.start()
    line = Line(n, rows, step)
    if alone:
        line.greet()
    sums = Sums(line, part, held, s_send, s_recv)
    blocks = Blocks(line, full_ref, b_send, b_recv)
    if column is not None:
        load_w.wait()

        def multiply(columns):
            product = dot_nt(dy_ref[...], w_ref[columns]).astype(bf16)
            part[:, :, columns] = product.reshape(n, rows, -1)

        by_tiles(width, 256, multiply)

    def settle(sub):
        here = line.part(sub)
        sums.total(sub, work)
        carry = carry_back(
            work,
            plain,
            order,
            step,
            width,
            middle_ref[here].astype(f32),
            base_ref[here].astype(f32),
            norm_ref[0:1],
            term_ref,
            sub == 0,
        )
        carry_ref[here] = carry
        full_ref[line.at, here] = carry.astype(bf16)
        blocks.start(sub)

    relay(n, [sums], blocks, settle)
    load_outs.wait()

    def multiply_next(columns):
        whole = full_ref[...].reshape(n * rows, width)
        att_ref[:, columns] = dot_nt(whole, outs_ref[columns]).astype(bf16)

    by_tiles(att_ref.shape[1], 256, multiply_next)


def last_kernel(n, order, dy_ref, w_hbm, base_ref, tokens, norm_ref, branch, middle, *rest):
    grad_ref, result_ref, term_ref = rest[:3]
    part, held, held2, work, plain, s_send, s_recv, r_send, r_recv, w_ref, w_sem = rest[3:]
    rows, width = base_ref.shape
    step = rows // SUBS
    load_w = fetch_columns(w_hbm, 0, w_ref, w_sem)
    load_w.start()
    line = Line(n, rows, step)
    load_w.wait()
    sums = Sums(line, part, held, s_send, s_recv)
    results = Sums(line, branch, held2, r_send, r_recv)

    def multiply(columns):
        product = dot_nt(dy_ref[...], w_ref[columns]).astype(bf16)
        part[:, :, columns] = product.reshape(n, rows, -1)

    by_tiles(width, 256, multiply)

    def settle(sub):
        here = line.part(sub)
        sums.total(sub, work)
        carry = carry_back(
            work,
            plain,
            order,
            step,
            width,
            tokens[here].astype(f32),
            base_ref[here],
            norm_ref[0:1],
            term_ref,
            sub == 0,
        )
        grad_ref[here] = carry.astype(bf16)
        results.total(sub, work)
        result_ref[here] = (middle[here] + work[...]).astype(bf16)

    relay(n, [sums, results], None, settle)


VMEM_CAP = 52 * 1024 * 1024


def in_place():
    return pl.BlockSpec(memory_space=pl.ANY)


def whole_vmem():
    return pl.BlockSpec(memory_space=pltpu.VMEM)


def sem_pair(n, subs):
    return [pltpu.SemaphoreType.DMA((2, n, subs)), pltpu.SemaphoreType.DMA((2, n, subs))]


def line_call(kernel, name, ident, outs, specs, scratch, flops, moved):
    return pl.pallas_call(
        kernel,
        name=name,
        out_shape=outs,
        in_specs=specs,
        out_specs=jax.tree.map(lambda _: whole_vmem(), outs),
        scratch_shapes=scratch,
        compiler_params=pltpu.CompilerParams(
            collective_id=ident, has_side_effects=True, vmem_limit_bytes=VMEM_CAP
        ),
        cost_estimate=pl.CostEstimate(flops=flops, bytes_accessed=moved, transcendentals=0),
    )


def shape(dims, kind):
    return jax.ShapeDtypeStruct(dims, kind)


LINK_COST = 4_000_000


def pieces_of(rows):
    return max(1, rows * SUBS // 128)


class Order:
    def __init__(self, pieces, width):
        self.pieces, self.width = pieces, width


def swap_sems(n):
    return [pltpu.SemaphoreType.DMA((n,)), pltpu.SemaphoreType.DMA((n,))]


def enter_call(
    name, ident, slots, weights, gathers, norms, normed, hidden, n, n_dp, width, inner=None
):
    chunk = weights[0][0].shape[0] // n_dp
    run, inner_args, inner_specs, inner_outs, scratch = inner or (None, [], [], [], [])
    counts = (len(inner_args), len(inner_outs), len(scratch))
    outs, scratch = [], list(scratch)
    for array, places, split, _ in weights:
        parts = n if split else 1
        outs.append(shape((parts, chunk, len(places) // parts * BLK), bf16))
        scratch += [pltpu.VMEM(array.shape, f32), pltpu.SemaphoreType.DMA]
    if normed:
        scratch += [pltpu.VMEM((n_dp, *norms.shape), f32), *swap_sems(n_dp)]
    for array, _ in gathers:
        rows = array.shape[0]
        outs.append(shape((n, *array.shape), array.dtype))
        scratch += sem_pair(n, pieces_of(rows))
    if normed:
        outs.append(shape((norms.shape[0], n_dp * norms.shape[1]), f32))
    for array, _, _, _ in weights:
        slots_shape = (n_dp, array.shape[1] // BLK, chunk, BLK)
        scratch += [pltpu.VMEM(slots_shape, bf16)] * 2 + swap_sems(n_dp)
    if hidden:
        scratch.append(pltpu.VMEM((gathers[0][0].shape[0] // SUBS, width), f32))
    for array, moved in gathers[1 if hidden else 0 :]:
        if moved:
            scratch.append(pltpu.VMEM(array.shape, f32))
    for index, (_, places, split, _) in enumerate(weights):
        if split:
            scratch += [pltpu.VMEM(outs[index].shape, bf16), *swap_sems(n)]
    args = [slots, *(weight[0] for weight in weights), *(gather[0] for gather in gathers)]
    specs = [pl.BlockSpec(memory_space=pltpu.SMEM)] + [in_place()] * len(weights)
    specs += [whole_vmem()] * len(gathers)
    if normed or hidden:
        args.append(norms)
        specs.append(whole_vmem())
    args += inner_args
    specs += inner_specs
    outs += inner_outs
    kernel = functools.partial(
        enter_kernel,
        [weight[1:] for weight in weights],
        [gather[1] for gather in gathers],
        Order(shuffle_order(n, n_dp), width),
        normed,
        hidden,
        run,
        counts,
    )
    return line_call(kernel, name, ident, outs, specs, scratch, 0, LINK_COST)(*args)


def leave_call(name, ident, slots, weights, term, n, n_dp, inner=None):
    outs, scratch = [], []
    specs = [pl.BlockSpec(memory_space=pltpu.SMEM)] + [whole_vmem()] * len(weights)
    args = [slots, *(weight[0] for weight in weights)]
    chunk = weights[0][0].shape[1]
    if term is not None:
        args.append(term)
        specs.append(whole_vmem())
        block = (term.shape[0], term.shape[1] // n_dp)
    counts = (0, 0, 0)
    run = None
    if inner is not None:
        run, inner_args, inner_specs, inner_outs, inner_scratch = inner
        counts = (len(inner_args), len(inner_outs), len(inner_scratch))
        args += inner_args
        specs += inner_specs
        scratch += inner_scratch
    if term is not None:
        scratch += [pltpu.VMEM((n_dp, *block), f32)] * 2 + swap_sems(n_dp)
        scratch += [pltpu.VMEM(block, f32), pltpu.VMEM((n, *block), f32), *swap_sems(n)]
    for rows, split, _, _, _ in weights:
        if split:
            scratch += [pltpu.VMEM(rows.shape, bf16), *swap_sems(n)]
    for rows, _, capacity, _, whole in weights:
        slots_shape = (n_dp, chunk, capacity * BLK)
        if whole:
            outs.append(shape(slots_shape, bf16))
            scratch += [pltpu.VMEM(slots_shape, bf16), *swap_sems(n_dp)]
        blocks = rows.shape[0] * rows.shape[2] // BLK
        scratch.append(pltpu.VMEM((blocks, chunk, BLK), bf16))
    loose = sum(capacity * BLK for _, _, capacity, _, whole in weights if not whole)
    if loose:
        outs.append(shape((n_dp, chunk, loose), bf16))
    if term is not None:
        outs.append(shape(block, f32))
    if inner is not None:
        outs += inner_outs
    kernel = functools.partial(
        leave_kernel, [weight[1:] for weight in weights], term is not None, run, counts
    )
    return line_call(kernel, name, ident, outs, specs, scratch, 0, LINK_COST)(*args)


def forward_parts(attended, outs_z, half, base, norm_rows, after, n, n_dp, alone):
    rows, width = base.shape
    share = outs_z.shape[0]
    outs = [shape((rows, width), f32), shape((n, rows, width), bf16)]
    specs = [whole_vmem(), in_place(), whole_vmem(), whole_vmem()]
    args = [attended, outs_z, base, norm_rows]
    scratch = [
        pltpu.VMEM((n, rows, width), bf16),
        pltpu.VMEM((2, n, rows, width), bf16),
        pltpu.VMEM((rows // SUBS, width), f32),
        *sem_pair(n, SUBS),
        *sem_pair(n, SUBS),
        pltpu.VMEM((share, width), bf16),
        pltpu.SemaphoreType.DMA,
    ]
    if after is not None:
        outs.append(shape((n * rows, share), bf16))
        specs.append(in_place())
        args.append(after)
        scratch += [pltpu.VMEM((width, share), bf16), pltpu.SemaphoreType.DMA]
    kernel = functools.partial(
        forward_kernel, n, shuffle_order(n, n_dp), half, after is not None, alone
    )
    return kernel, args, specs, outs, scratch


def forward_call(attended, outs_z, half, base, norm_rows, after, n, n_dp, ident):
    kernel, args, specs, outs, scratch = forward_parts(
        attended, outs_z, half, base, norm_rows, after, n, n_dp, True
    )
    call = line_call(kernel, f"forward{half}", ident, outs, specs, scratch, 0, LINK_COST)
    return call(*args)


def back_parts(dy, weight, column, base, middle, norm_rows, outs_z, half, n, n_dp, alone):
    rows, width = base.shape
    share = outs_z.shape[0]
    outs = [
        shape((rows, width), f32),
        shape((n, rows, width), bf16),
        shape((n * rows, share), bf16),
        shape((8, width), f32),
    ]
    specs = [
        whole_vmem(),
        in_place(),
        whole_vmem(),
        whole_vmem(),
        whole_vmem(),
        in_place(),
    ]
    scratch = [
        pltpu.VMEM((2, n, rows, width), bf16),
        pltpu.VMEM((rows // SUBS, width), f32),
        pltpu.VMEM((rows // SUBS, width), f32),
        *sem_pair(n, SUBS),
        *sem_pair(n, SUBS),
        pltpu.VMEM((share, width), bf16),
        pltpu.SemaphoreType.DMA,
    ]
    if column is not None:
        scratch += [
            pltpu.VMEM((n, rows, width), bf16),
            pltpu.VMEM((width, dy.shape[1]), bf16),
            pltpu.SemaphoreType.DMA,
        ]
    kernel = functools.partial(back_kernel, n, unshuffle_order(n, n_dp), column, half, alone)
    return kernel, [dy, weight, base, middle, norm_rows, outs_z], specs, outs, scratch


def back_call(dy, weight, column, base, middle, norm_rows, outs_z, half, n, n_dp, ident):
    kernel, args, specs, outs, scratch = back_parts(
        dy, weight, column, base, middle, norm_rows, outs_z, half, n, n_dp, True
    )
    call = line_call(kernel, f"back{half}", ident, outs, specs, scratch, 0, LINK_COST)
    return call(*args)


def last_parts(dy, weight, base, tokens, norm_rows, branch, middle, n, n_dp):
    rows, width = base.shape
    outs = [
        shape((rows, width), bf16),
        shape((rows, width), bf16),
        shape((8, width), f32),
    ]
    specs = [whole_vmem(), in_place()] + [whole_vmem()] * 5
    scratch = [
        pltpu.VMEM((n, rows, width), bf16),
        pltpu.VMEM((2, n, rows, width), bf16),
        pltpu.VMEM((2, n, rows, width), bf16),
        pltpu.VMEM((rows // SUBS, width), f32),
        pltpu.VMEM((rows // SUBS, width), f32),
        *sem_pair(n, SUBS),
        *sem_pair(n, SUBS),
        pltpu.VMEM((width, dy.shape[1]), bf16),
        pltpu.SemaphoreType.DMA,
    ]
    kernel = functools.partial(last_kernel, n, unshuffle_order(n, n_dp))
    return kernel, [dy, weight, base, tokens, norm_rows, branch, middle], specs, outs, scratch


def attend_forward(query, keys, values, mask_ref, keyed, att_ref, share_ref):
    packed, rows, _ = mask_ref.shape
    heads = att_ref.shape[1] // HEAD
    for p in range(packed):
        here = slice(p * rows, (p + 1) * rows)
        there = here if keyed else slice(None)
        for h in range(heads):
            columns = slice(h * HEAD, (h + 1) * HEAD)
            scores = dot_nt(query[here, columns], keys[there, columns]) * HEAD ** (-0.5)
            scores = jnp.where(mask_ref[p] > 0, scores, score_floor)
            powers = jnp.exp(scores - jnp.max(scores, axis=-1, keepdims=True))
            shares = powers / jnp.sum(powers, axis=-1, keepdims=True)
            share_ref[p * heads + h] = shares
            att_ref[here, columns] = dot(shares.astype(bf16), values[there, columns]).astype(bf16)


def attend_backward(query, keys, values, share_ref, back_ref, rows, keyed, put_query, put_pair):
    heads = back_ref.shape[1] // HEAD
    packed = back_ref.shape[0] // rows
    score_scale = HEAD ** (-0.5)
    for h in range(heads):
        columns = slice(h * HEAD, (h + 1) * HEAD)
        key_grad = value_grad = None
        for p in range(packed):
            here = slice(p * rows, (p + 1) * rows)
            there = here if keyed else slice(None)
            shares = share_ref[p * heads + h]
            back = back_ref[here, columns]
            back_shares = dot_nt(back, values[there, columns])
            inner_sum = jnp.sum(shares * back_shares, axis=-1, keepdims=True)
            back_scores = (shares * (back_shares - inner_sum)).astype(bf16)
            put_query(here, columns, dot(back_scores, keys[there, columns]) * score_scale)
            key_term = dot_tn(back_scores, query[here, columns]) * score_scale
            value_term = dot_tn(shares.astype(bf16), back)
            if keyed:
                put_pair(there, columns, key_term, value_term)
            else:
                key_grad = key_term if key_grad is None else key_grad + key_term
                value_grad = value_term if value_grad is None else value_grad + value_term
        if not keyed:
            put_pair(slice(None), columns, key_grad, value_grad)


def self_forward_kernel(h_ref, w_ref, mask_ref, proj_ref, att_ref, share_ref):
    tile = pl.program_id(0)
    proj_ref[tile] = dot(h_ref[...], w_ref[...]).astype(bf16)

    @pl.when(tile == 2)
    def _():
        attend_forward(
            proj_ref.at[0], proj_ref.at[1], proj_ref.at[2], mask_ref, True, att_ref, share_ref
        )


def cross_forward_kernel(cq_ref, text_ref, w_ref, mask_ref, kv_ref, att_ref, share_ref, total):
    tile = pl.program_id(0)
    product = dot(text_ref[...], w_ref[...])

    @pl.when(tile < 2)
    def _():
        total[tile] = product

    @pl.when(tile >= 2)
    def _():
        kv_ref[tile - 2] = (total[tile - 2] + product).astype(bf16)

    @pl.when(tile == 3)
    def _():
        attend_forward(cq_ref, kv_ref.at[0], kv_ref.at[1], mask_ref, False, att_ref, share_ref)


def ffn_kernel(h_ref, up_ref, grad_ref, act_ref, slope_ref, gdown_ref):
    up_values = dot(h_ref[...], up_ref[...])
    chance = 0.5 * (1.0 + lax.erf(up_values * 0.5**0.5))
    density = jnp.exp(-0.5 * up_values * up_values) * 0.3989422804014327
    activated = (up_values * chance).astype(bf16)
    act_ref[...] = activated
    slope_ref[...] = chance + up_values * density
    store_pieces(dot_tn(activated, grad_ref[...]), gdown_ref)


def ffn_back_kernel(
    h_ref,
    down_ref,
    up_ref,
    grad_ref,
    act_ref,
    slope_ref,
    both_ref,
    branch_ref,
    part_ref,
    gup_ref,
    total,
    part,
):
    del both_ref
    tile = pl.program_id(0)
    back_act = dot_nt(grad_ref[...], down_ref[...])
    back_up = (back_act * slope_ref[...]).astype(bf16)
    gup_ref[...] = dot_tn(h_ref[...], back_up).astype(bf16).reshape(gup_ref.shape)

    @pl.when(tile == 0)
    def _():
        total[...] = dot(act_ref[...], down_ref[...])
        part[...] = dot_nt(back_up, up_ref[...])

    @pl.when(tile > 0)
    def _():
        total[...] += dot(act_ref[...], down_ref[...])
        part[...] += dot_nt(back_up, up_ref[...])

    @pl.when(tile == 3)
    def _():
        branch_ref[...] = total[...].astype(bf16)
        part_ref[...] = part[...].astype(bf16)


def cross_back_kernel(
    rows, back_ref, cq_ref, kv_ref, share_ref, text_ref, dcq_ref, grad_ref, pairs
):
    share = cq_ref.shape[1]

    @pl.when(pl.program_id(0) == 0)
    def _():
        def put_query(here, columns, value):
            dcq_ref[here, columns] = value.astype(bf16)

        def put_pair(there, columns, key_grad, value_grad):
            pairs[there, columns] = key_grad.astype(bf16)
            after_keys = slice(share + columns.start, share + columns.stop)
            pairs[there, after_keys] = value_grad.astype(bf16)

        attend_backward(
            cq_ref, kv_ref.at[0], kv_ref.at[1], share_ref, back_ref, rows, False, put_query, put_pair
        )

    grad_ref[...] = dot_tn(text_ref[...], pairs[...]).astype(bf16)


def outs_grad_kernel(att1_ref, carry1_ref, att2_ref, carry2_ref, grad_ref):
    tile = pl.program_id(0)

    @pl.when(tile == 0)
    def _():
        store_pieces(dot_tn(att1_ref[...], carry1_ref[...]), grad_ref)

    @pl.when(tile == 1)
    def _():
        store_pieces(dot_tn(att2_ref[...], carry2_ref[...]), grad_ref)


def store_pieces(gradient, target):
    n_dp, rows, columns = target.shape
    gradient = gradient.astype(bf16)
    chunk = gradient.shape[0] // n_dp
    for piece in range(rows // chunk):
        cut = gradient[:, piece * columns : (piece + 1) * columns]
        target[:, piece * chunk : (piece + 1) * chunk] = cut.reshape(n_dp, chunk, columns)


def self_back_kernel(
    rows,
    back_ref,
    proj_ref,
    share_ref,
    h1_ref,
    h2_ref,
    dcq_ref,
    both_ref,
    dproj_ref,
    grad_ref,
    parts,
):
    del both_ref
    tile = pl.program_id(0)
    share = dcq_ref.shape[1]

    @pl.when(tile == 0)
    def _():
        def put(part, here, columns, value):
            value = value.astype(bf16)
            parts[part, here, columns] = value
            dproj_ref[here, part * share + columns.start : part * share + columns.stop] = value

        def put_query(here, columns, value):
            put(0, here, columns, value)

        def put_pair(there, columns, key_grad, value_grad):
            put(1, there, columns, key_grad)
            put(2, there, columns, value_grad)

        attend_backward(
            proj_ref.at[0],
            proj_ref.at[1],
            proj_ref.at[2],
            share_ref,
            back_ref,
            rows,
            True,
            put_query,
            put_pair,
        )

    @pl.when(tile < 3)
    def _():
        grad_ref[...] = dot_tn(h1_ref[...], parts[tile]).astype(bf16).reshape(grad_ref.shape)

    @pl.when(tile == 3)
    def _():
        grad_ref[...] = dot_tn(h2_ref[...], dcq_ref[...]).astype(bf16).reshape(grad_ref.shape)


def fixed(dims):
    return pl.BlockSpec(dims, lambda t: (0,) * len(dims))


def moving(dims, index):
    return pl.BlockSpec(dims, lambda t: (0, index(t)))


def local_call(
    kernel, name, tiles, outs, specs, out_specs, scratch, flops, moved, aliases=None
):
    return pl.pallas_call(
        kernel,
        name=name,
        grid=(tiles,),
        input_output_aliases=aliases or {},
        out_shape=outs,
        in_specs=specs,
        out_specs=out_specs,
        scratch_shapes=scratch,
        compiler_params=pltpu.CompilerParams(vmem_limit_bytes=VMEM_CAP),
        cost_estimate=pl.CostEstimate(
            flops=flops // 8, bytes_accessed=moved // 8, transcendentals=0
        ),
    )


def self_forward(hidden, query_z, mask):
    tokens, width = hidden.shape
    share = query_z.shape[1] // 4
    packed, rows, _ = mask.shape
    pairs = (packed * share // HEAD, rows, rows)
    return local_call(
        self_forward_kernel,
        "self_forward",
        3,
        (shape((3, tokens, share), bf16), shape((tokens, share), bf16), shape(pairs, f32)),
        [fixed(hidden.shape), moving((width, share), lambda t: t), fixed(mask.shape)],
        (fixed((3, tokens, share)), fixed((tokens, share)), fixed(pairs)),
        [],
        6 * tokens * width * share,
        20_000_000,
    )(hidden, query_z, mask)


def cross_forward(cross_query, text_all, text_z, mask):
    tokens, share = cross_query.shape
    texts = text_all.shape[0]
    width = text_z.shape[0]
    packed, rows, _ = mask.shape
    pairs = (packed * share // HEAD, rows, texts)
    return local_call(
        cross_forward_kernel,
        "cross_forward",
        4,
        (shape((2, texts, share), bf16), shape((tokens, share), bf16), shape(pairs, f32)),
        [
            fixed(cross_query.shape),
            moving((texts, width), lambda t: t // 2),
            moving((width, share), lambda t: t),
            fixed(mask.shape),
        ],
        (fixed((2, texts, share)), fixed((tokens, share)), fixed(pairs)),
        [pltpu.VMEM((2, texts, share), f32)],
        8 * texts * width * share,
        20_000_000,
    )(cross_query, text_all, text_z, mask)


def ffn(hidden, up_z, grad_all, n, n_dp):
    tokens, width = hidden.shape
    share = up_z.shape[1] // 4
    chunk = share // n_dp
    return local_call(
        ffn_kernel,
        "ffn",
        4,
        (
            shape((tokens, 4 * share), bf16),
            shape((tokens, 4 * share), f32),
            shape((n_dp, 2 * n * chunk, 4 * share), bf16),
        ),
        [fixed(hidden.shape), moving((width, share), lambda t: t), fixed(grad_all.shape)],
        (
            moving((tokens, share), lambda t: t),
            moving((tokens, share), lambda t: t),
            pl.BlockSpec((n_dp, n * chunk // 4, 4 * share), lambda t: (0, 4 + t, 0)),
        ),
        [],
        16 * tokens * width * share,
        30_000_000,
    )(hidden, up_z, grad_all)


def ffn_back(hidden, down_z, up_z, grad_all, activated, slope, both):
    tokens, width = hidden.shape
    share = down_z.shape[0]
    return local_call(
        ffn_back_kernel,
        "ffn_back",
        4,
        (shape((tokens, width), bf16), shape((tokens, width), bf16), shape(both.shape, bf16)),
        [
            fixed(hidden.shape),
            moving((share, width), lambda t: t),
            moving((width, share), lambda t: t),
            fixed(grad_all.shape),
            moving((tokens, share), lambda t: t),
            moving((tokens, share), lambda t: t),
            in_place(),
        ],
        (
            fixed((tokens, width)),
            fixed((tokens, width)),
            pl.BlockSpec((both.shape[0], both.shape[1] // 2, share), lambda t: (0, 0, t)),
        ),
        [pltpu.VMEM((tokens, width), f32)] * 2,
        32 * tokens * width * share,
        50_000_000,
        {6: 2},
    )(hidden, down_z, up_z, grad_all, activated, slope, both)


def cross_back(back_attended, cross_query, text_pairs, shares, text_all, rows):
    tokens, share = cross_query.shape
    texts = text_all.shape[0]
    width = text_all.shape[1] // 2
    return local_call(
        functools.partial(cross_back_kernel, rows),
        "cross_back",
        2,
        (shape((tokens, share), bf16), shape((width, 4 * share), bf16)),
        [
            fixed(back_attended.shape),
            fixed(cross_query.shape),
            fixed(text_pairs.shape),
            fixed(shares.shape),
            moving((texts, width), lambda t: t),
        ],
        (fixed((tokens, share)), moving((width, 2 * share), lambda t: t)),
        [pltpu.VMEM((texts, 2 * share), bf16)],
        8 * texts * width * share,
        20_000_000,
    )(back_attended, cross_query, text_pairs, shares, text_all)


def outs_grad(attended1, carry1, attended2, carry2, n, n_dp):
    tokens, share = attended1.shape
    width = carry1.shape[1]
    chunk = share // n_dp
    return local_call(
        outs_grad_kernel,
        "outs_grad",
        2,
        shape((n_dp, n * chunk * 3 // 2, 4 * share), bf16),
        [fixed((tokens, share)), fixed((tokens, width))] * 2,
        pl.BlockSpec((n_dp, n * chunk // 4, 4 * share), lambda t: (0, 4 + t, 0)),
        [],
        4 * tokens * width * share,
        10_000_000,
    )(attended1, carry1, attended2, carry2)


def self_back(back_attended, projected, shares, hidden1, hidden2, back_cross, both, rows):
    tokens, width = hidden1.shape
    share = back_cross.shape[1]
    return local_call(
        functools.partial(self_back_kernel, rows),
        "self_back",
        4,
        (shape((tokens, 3 * share), bf16), shape(both.shape, bf16)),
        [
            fixed(back_attended.shape),
            fixed(projected.shape),
            fixed(shares.shape),
            fixed(hidden1.shape),
            fixed(hidden2.shape),
            fixed(back_cross.shape),
            in_place(),
        ],
        (
            fixed((tokens, 3 * share)),
            pl.BlockSpec((both.shape[0], both.shape[1] * 2 // 3, share), lambda t: (0, 0, t)),
        ),
        [pltpu.VMEM((3, tokens, share), bf16)],
        8 * tokens * width * share,
        25_000_000,
        {6: 1},
    )(back_attended, projected, shares, hidden1, hidden2, back_cross, both)


def block_slots(owners):
    owner = jnp.concatenate(owners)
    weight = jnp.concatenate([jnp.full(one.shape, at, jnp.int32) for at, one in enumerate(owners)])
    mark = owner + weight * 1024
    count = mark.shape[0]
    earlier = lax.broadcasted_iota(jnp.int32, (count, count), 1) < lax.broadcasted_iota(
        jnp.int32, (count, count), 0
    )
    same = jnp.logical_and(mark[:, None] == mark[None, :], earlier)
    return jnp.stack([owner, jnp.sum(same.astype(jnp.int32), axis=1)])


def slot_contents(owners, slots, places, capacities, firsts, n_dp):
    rows = []
    for owner, place, capacity, first in zip(owners, places, capacities, firsts):
        count = owner.shape[0]
        at = owner * capacity + slots[1, first : first + count]
        hit = at[None, :] == lax.broadcasted_iota(jnp.int32, (n_dp * capacity, count), 0)
        block = lax.broadcasted_iota(jnp.int32, (n_dp * capacity, count), 1)
        per_group, per_part, split = place_rule(place)
        part = block % per_group // per_part if split else block * 0
        column = block // per_group * per_part + block % per_part if split else block
        index = part * (count // (per_group // per_part)) + column if split else column
        rows.append(
            jnp.stack([jnp.sum(jnp.where(hit, value, 0), axis=1) for value in (index, block * 0 + 1)])
        )
    return jnp.concatenate(rows, axis=1)


def place_rule(place):
    parts = 1 + max(part for part, _ in place)
    if parts == 1:
        return 0, 0, False
    per_part = sum(1 for part, _ in place[:HEADS] if part == 0)
    return per_part * parts, per_part, True


def after(small, first):
    return lax.optimization_barrier((small, first))[0]


def body(
    tokens_in,
    text_in,
    seg_ids,
    capt_ids,
    grad_out,
    owner_query,
    owner_up,
    owner_outs,
    owner_text,
    owner_down,
    w_query,
    m_query,
    v_query,
    w_up,
    m_up,
    v_up,
    w_outs,
    m_outs,
    v_outs,
    w_text,
    m_text,
    v_text,
    w_down,
    m_down,
    v_down,
    norm_weight,
    m_norm,
    v_norm,
):
    n_dp = lax.axis_size("dp")
    n_z = lax.axis_size("fsdp")
    width = tokens_in.shape[1]
    own_rows = w_query.shape[0]
    chunk = own_rows // n_dp
    cap_big = w_query.shape[1] // BLK
    cap_out = w_outs.shape[1] // BLK
    heads_z = HEADS // n_z
    share = width // n_z
    owner_query, owner_up, owner_outs, owner_text, owner_down = (
        owner[:, 0] for owner in (owner_query, owner_up, owner_outs, owner_text, owner_down)
    )
    split_places = [split_place(b, heads_z, n_z) for b in range(owner_query.shape[0])]
    big_places = [flat_place(b) for b in range(owner_down.shape[0])]
    out_places = [flat_place(b) for b in range(owner_outs.shape[0])]
    owners = (owner_query, owner_outs, owner_text, owner_up, owner_down)
    places = (split_places, out_places, split_places, split_places, big_places)
    capacities = (cap_big, cap_out, cap_big, cap_big, cap_big)
    firsts = [sum(len(one) for one in places[:index]) for index in range(5)]
    slot_firsts = [sum(capacities[:index]) * n_dp for index in range(5)]
    slots = block_slots(owners)
    contents = slot_contents(owners, slots, places, capacities, firsts, n_dp)

    def spread(rows):
        return lax.all_gather(rows.reshape(-1, rows.shape[-1]), "dp", axis=0, tiled=True)

    def gather_sum(piece, parts):
        summed = lax.psum_scatter(piece, "dp", scatter_dimension=0, tiled=True)
        return summed.reshape(parts, chunk, -1)

    token_count = tokens_in.shape[0]
    marks = jnp.concatenate([seg_ids, capt_ids], axis=1)
    marks = jnp.pad(marks, ((0, 7), (0, 256 - marks.shape[1])))
    norms = jnp.pad(norm_weight, ((0, 2), (0, 0)))
    half = token_count // 2
    query_rows, grad_low, marks, norm_full = enter_call(
        "enter_query",
        0,
        slots,
        [(w_query, split_places, True, firsts[0])],
        [(grad_out[:half], False), (marks, False)],
        norms,
        True,
        False,
        n_z,
        n_dp,
        width,
    )
    outs_rows, hidden1, text_all = enter_call(
        "enter_outs",
        6,
        slots,
        [(w_outs, out_places, False, firsts[1])],
        [(tokens_in, True), (text_in, True)],
        norm_full[0:2],
        False,
        True,
        n_z,
        n_dp,
        width,
    )
    query_z, outs_z = spread(query_rows), spread(outs_rows)
    hidden1 = hidden1.reshape(-1, width)
    text_all = text_all.reshape(-1, text_in.shape[1])
    segment = marks[:, 0, :token_count]
    caption = marks[:, 0, token_count : token_count + capt_ids.shape[1]]
    self_mask = (segment[:, :, None] == segment[:, None, :]).astype(jnp.int32)
    text_row = lax.broadcasted_iota(jnp.int32, caption.shape, 0).reshape(1, 1, -1)
    packed_row = lax.broadcasted_iota(jnp.int32, (n_z, 1, 1), 0)
    cross_mask = jnp.logical_and(
        segment[:, :, None] == caption.reshape(1, 1, -1), packed_row == text_row
    ).astype(jnp.int32)

    projected, attended1, shares1 = self_forward(hidden1, query_z, self_mask)
    text_rows, grad_high = enter_call(
        "enter_text",
        7,
        after(slots, attended1),
        [(w_text, split_places, True, firsts[2])],
        [(grad_out[half:], False)],
        None,
        False,
        False,
        n_z,
        n_dp,
        width,
    )
    grad_all = jnp.concatenate([grad_low, grad_high], axis=1).reshape(-1, width)
    up_rows, down_rows, middle1, hidden2, cross_query = enter_call(
        "forward0",
        1,
        slots,
        [(w_up, split_places, True, firsts[3]), (w_down, big_places, False, firsts[4])],
        [],
        None,
        False,
        False,
        n_z,
        n_dp,
        width,
        forward_parts(
            attended1,
            outs_z,
            0,
            tokens_in,
            after(norm_full[2:4], text_rows),
            query_z,
            n_z,
            n_dp,
            False,
        ),
    )
    hidden2 = hidden2.reshape(-1, width)
    text_z, up_z, down_z = spread(text_rows), spread(up_rows), spread(down_rows)
    text_pairs, attended2, shares2 = cross_forward(cross_query, text_all, text_z, cross_mask)
    middle2, hidden3 = forward_call(
        attended2, outs_z, 1, middle1, norm_full[4:6], None, n_z, n_dp, 2
    )
    hidden3 = hidden3.reshape(-1, width)
    activated, slope, both = ffn(hidden3, up_z, grad_all, n_z, n_dp)
    branch3, part3, both = ffn_back(hidden3, down_z, up_z, grad_all, activated, slope, both)
    branch3 = branch3.reshape(n_z, token_count, width)
    part3 = part3.reshape(n_z, token_count, width)
    up_down_sum = gather_sum(both.reshape(-1, 4 * share), 2 * n_z)
    up_sum, down_sum = up_down_sum[:n_z], up_down_sum[n_z:]
    at_middle2, carry2, back_att2, term3 = back_call(
        part3, after(slots, part3), None, grad_out, middle2, norm_full[4:6], outs_z, 1, n_z, n_dp, 3
    )
    carry2 = carry2.reshape(-1, width)
    back_cross, text_part = cross_back(
        back_att2, cross_query, text_pairs, shares2, text_all, token_count
    )
    text_sum = gather_sum(text_part, n_z)
    at_middle1, carry1, back_att1, term2 = back_call(
        back_cross, query_z, 3, at_middle2, middle1, norm_full[2:4], outs_z, 0, n_z, n_dp, 4
    )
    carry1 = carry1.reshape(-1, width)
    both = outs_grad(attended1, after(carry1, up_down_sum), attended2, carry2, n_z, n_dp)
    back_projected, both = self_back(
        back_att1, projected, shares1, hidden1, hidden2, back_cross, both, token_count
    )
    query_outs_sum = gather_sum(both.reshape(-1, 4 * share), 3 * n_z // 2)
    down_grad, up_grad, text_grad, grad_in, result, term1 = leave_call(
        "leave_up",
        8,
        contents,
        [
            (down_sum, False, cap_big, slot_firsts[4], True),
            (up_sum, True, cap_big, slot_firsts[3], True),
            (text_sum, True, cap_big, slot_firsts[2], True),
        ],
        None,
        n_z,
        n_dp,
        last_parts(
            back_projected,
            query_z,
            at_middle1,
            tokens_in,
            norm_full[0:2],
            branch3,
            middle2,
            n_z,
            n_dp,
        ),
    )
    query_outs_sum = after(query_outs_sum, term1)
    query_sum, outs_sum = query_outs_sum[:n_z], query_outs_sum[n_z:]
    norm_term = jnp.concatenate([term1[:2], term2[:2], term3[:4]], axis=0)
    outs_slots, loose, norm_grad = leave_call(
        "leave_query",
        9,
        contents,
        [
            (outs_sum, False, cap_out, slot_firsts[1], True),
            (query_sum, True, cap_big, slot_firsts[0], False),
        ],
        norm_term,
        n_z,
        n_dp,
    )
    loose = lax.all_to_all(loose, "dp", 0, 0, tiled=True).reshape(own_rows, -1)
    outs_slots = outs_slots.reshape(own_rows, -1).astype(f32)
    query_grad = loose.astype(f32)
    norm_grad = norm_grad[:6]
    text_grad, up_grad, down_grad = (
        grad.reshape(own_rows, -1).astype(f32) for grad in (text_grad, up_grad, down_grad)
    )
    up_new = adamw_update(w_up, m_up, v_up, up_grad, rate_up, decay_rate)
    text_new = adamw_update(w_text, m_text, v_text, text_grad, rate_text, decay_rate)
    down_new = adamw_update(w_down, m_down, v_down, down_grad, rate_down, decay_rate)
    query_new = adamw_update(w_query, m_query, v_query, query_grad, rate_query, decay_rate)
    outs_new = adamw_update(w_outs, m_outs, v_outs, outs_slots, rate_outs, decay_rate)
    norm_new = adamw_update(norm_weight, m_norm, v_norm, norm_grad, rate_norm, 0.0)
    return (
        result,
        grad_in,
        *query_new,
        *up_new,
        *outs_new,
        *text_new,
        *down_new,
        *norm_new,
    )


def solution(mesh):
    rows = P(("dp", "fsdp"), None)
    slots = P("fsdp", "dp")
    norms = P(None, "dp")
    in_specs = (rows,) * 5 + (P(),) * 5 + (slots,) * 15 + (norms,) * 3
    out_specs = (rows,) * 2 + (slots,) * 15 + (norms,) * 3
    return jax.shard_map(body, mesh=mesh, in_specs=in_specs, out_specs=out_specs, check_vma=False)
```
